32 devices in a mesh: grp: 2 (over x), res: 16 (over z, y, core).
Axes of the slice: x: 2, y: 2, z: 4, core: 2. Of those that a mesh axis runs over, the one named last changes fastest.
Arguments:
- alignment_activations: bfloat16 [128, 512, 256], P(None, ('grp', 'res')), parts along dimension 1, may hold values from -6 to 6
- alignment_row_mask: int32 [128, 512], P(None, 'grp'), parts along dimension 1, may hold values from 0 to 1, as said below
- residue_mask_vector: int32 [512], P('grp'), parts along dimension 0, may hold values 0 or 1
- layer_norm_gain: float32 [256], replicated, may hold values from 0.25 to 1.75
- layer_norm_bias: float32 [256], replicated, may hold values from -3 to 3
- left_weight: bfloat16 [256, 32], replicated, may hold values from -0.375 to 0.375
- left_bias: float32 [32], replicated, may hold values from -3 to 3
- right_weight: bfloat16 [256, 32], replicated, may hold values from -0.375 to 0.375
- right_bias: float32 [32], replicated, may hold values from -3 to 3
- output_weight: bfloat16 [1024, 128], replicated, may hold values from -0.1875 to 0.1875
- output_bias: float32 [128], replicated, may hold values from -4 to 4
- pair_update_cotangent: bfloat16 [512, 256, 128], P(('grp', 'res')), parts along dimension 0, may hold values from -6 to 6
Outputs:
- pair_update_output: bfloat16 [512, 256, 128], P(('grp', 'res')), parts along dimension 0
- alignment_gradient: bfloat16 [128, 512, 256], P(None, ('grp', 'res')), parts along dimension 1
- left_weight_gradient: float32 [512, 32], P('grp'), parts along dimension 0
- left_bias_gradient: float32 [64], P('grp'), parts along dimension 0
- right_weight_gradient: float32 [512, 32], P('grp'), parts along dimension 0
- right_bias_gradient: float32 [64], P('grp'), parts along dimension 0
- w_out_grad: float32 [2048, 128], P('grp'), parts along dimension 0
- b_out_grad: float32 [256], P('grp'), parts along dimension 0
- norm_gain_gradient: float32 [512], P('grp'), parts along dimension 0
- norm_bias_gradient: float32 [512], P('grp'), parts along dimension 0
The draws below stay inside these ranges and needn't reach their ends.
There are 2 independent parts, one for each index of `grp`. The reference program is written for one: setup_inputs(seed, part) draws one part's arguments, and reference() takes and returns one part's arrays. A program takes and returns all parts, laid end to end along the dimension named above; an argument that names none is the same for every part. Nothing has to cross between parts.
Inputs may be any that keep to these rules, and one draw needn't show every extreme that they name: Sequence 0 covers every residue, so alignment_row_mask[0, i] = 1 for all i; other entries are 0 or 1, each sequence with its own coverage.
All inputs are finite; a program needn't handle non-finite values.
Results may differ from the reference program's by a relative error of at most 0.0075.
Values may be sent and summed in bfloat16 or wider, within the bound.
No kernel may reach another device: no remote copies, remote signals or barrier semaphores. Data moves between devices by JAX's collectives and lax.ppermute only.
A program may use at most 128 MiB of HBM per device.

```python
import math
import jax
import jax.numpy as jnp
from jax import lax

ALIGNMENT_WIDTH = 256
PROJECTION_SIZE = 32
CHANNELS = 128
SEQUENCE_COUNT = 128
CROP_RESIDUES = 256


def draw_alignment_row_mask(key, part):
    key = jax.random.fold_in(key, 11)
    first_key, second_key = jax.random.split(key)
    level = jax.random.randint(first_key, (SEQUENCE_COUNT, 1), 2, 11)
    coin = jax.random.randint(second_key, (SEQUENCE_COUNT, CROP_RESIDUES), 0, 10)
    kept = (coin < level).astype(jnp.int32)
    top_row = (jnp.arange(SEQUENCE_COUNT) == 0)[:, None]
    return jnp.where(top_row, 1, kept).astype(jnp.int32)


def set_ends(array, own_key, smallest, top_value):
    longest = array.shape.index(max(array.shape))
    spots = []
    for shift in (0, 1):
        where = [jax.random.randint(jax.random.fold_in(own_key, axis), (), 0, length) for axis, length in enumerate(array.shape)]
        where[longest] = (where[longest] + shift) % array.shape[longest]
        spots.append(tuple(where))
    return array.at[spots[0]].set(smallest).at[spots[1]].set(top_value)


def raised(result, own_key, source, target, parts, factor):
    def block_of(axis_at):
        return (jnp.arange(result.shape[axis_at]) // (result.shape[axis_at] // parts)).reshape((-1,) + (1,) * (result.ndim - 1 - axis_at))

    first = jax.random.permutation(own_key, parts)[block_of(target)]
    second = (block_of(target) + parts // 2) % parts
    return jnp.where((block_of(source) == first) | (block_of(source) == second), factor * result, result)


def steps_of(rng, extent, shards, smallest, top_value):
    def one(dim, blocks):
        steps = jax.random.uniform(jax.random.fold_in(jax.random.fold_in(rng, 6), dim), (blocks,), jnp.float32, smallest / len(shards), top_value / len(shards))
        return jnp.repeat(jnp.exp(steps), extent[dim] // blocks).reshape((-1,) + (1,) * (len(extent) - dim - 1))

    level = one(*shards[0])
    for cut in shards[1:]:
        level = level * one(*cut)
    return level


def centred(rng, dims, scale, reach, cuts=(), kind=jnp.bfloat16):
    entries = scale * jax.random.normal(rng, dims, jnp.float32)
    if cuts:
        entries = entries * steps_of(rng, dims, cuts, -0.22, 0.18)
    return jnp.clip(entries, -reach, reach).astype(kind)


def heavy_noise(key, shape, deviation, most, cuts, heavy, held_as=jnp.bfloat16):
    drawn = deviation * jax.random.normal(key, shape, jnp.float32)
    if cuts:
        drawn = drawn * steps_of(key, shape, cuts, -0.22, 0.18)
    return jnp.clip(raised(drawn, jax.random.fold_in(key, 3), *heavy), -most, most).astype(held_as)


def setup_inputs(seed: int = 0, part: int = 0) -> dict:
    key_of = jax.random.split(jax.random.key(seed), 13)
    part_splits = jax.random.split(jax.random.fold_in(key_of[12], part), 13)
    return {
        "alignment_activations": centred(part_splits[0], (SEQUENCE_COUNT, CROP_RESIDUES, ALIGNMENT_WIDTH), 1.0, 6.0, ((1, 16),)),
        "alignment_row_mask": draw_alignment_row_mask(jax.random.fold_in(jax.random.fold_in(key_of[12], part), 71), part),
        "residue_mask_vector": set_ends((jax.random.randint(part_splits[2], (CROP_RESIDUES,), 0, 8) < 7).astype(jnp.int32), jax.random.fold_in(part_splits[2], 1), 0, 1),
        "layer_norm_gain": jnp.clip(1.0 + 0.15 * jax.random.normal(key_of[3], (ALIGNMENT_WIDTH,), jnp.float32), 0.25, 1.75),
        "layer_norm_bias": centred(key_of[4], (ALIGNMENT_WIDTH,), 0.5, 3.0, (), jnp.float32),
        "left_weight": centred(key_of[5], (ALIGNMENT_WIDTH, PROJECTION_SIZE), ALIGNMENT_WIDTH ** -0.5, 0.375),
        "left_bias": centred(key_of[6], (PROJECTION_SIZE,), 0.5, 3.0, (), jnp.float32),
        "right_weight": centred(key_of[7], (ALIGNMENT_WIDTH, PROJECTION_SIZE), ALIGNMENT_WIDTH ** -0.5, 0.375),
        "right_bias": centred(key_of[8], (PROJECTION_SIZE,), 0.5, 3.0, (), jnp.float32),
        "output_weight": centred(key_of[9], (PROJECTION_SIZE * PROJECTION_SIZE, CHANNELS), (PROJECTION_SIZE * PROJECTION_SIZE) ** -0.5, 0.1875),
        "output_bias": centred(key_of[10], (CHANNELS,), 1.0, 4.0, (), jnp.float32),
        "pair_update_cotangent": heavy_noise(part_splits[11], (CROP_RESIDUES, CROP_RESIDUES, CHANNELS), 1.0, 6.0, ((0, 16),), (0, 1, 16, 2.0)),
    }


EPS = 1e-05

def apply_layer_norm(alignment_activations, layer_norm_gain, layer_norm_bias):
    value_entries = alignment_activations.astype(jnp.float32)
    center = lax.optimization_barrier(jnp.mean(value_entries, -1, keepdims=True))
    centered_input = value_entries - center
    spread = lax.optimization_barrier(jnp.mean(centered_input * centered_input, -1, keepdims=True))
    inverse_stddev = lax.rsqrt(spread + EPS)
    standardized_input = centered_input * inverse_stddev
    normalized_input = (standardized_input * layer_norm_gain + layer_norm_bias).astype(jnp.bfloat16)
    return (standardized_input, inverse_stddev, normalized_input)

def project(flat_rows, weight, bias, mask_vals):
    sequence_total, masked_row_count = mask_vals.shape
    linear = jnp.dot(flat_rows, weight, preferred_element_type=jnp.float32) + bias
    return (linear.reshape(sequence_total, masked_row_count, -1) * mask_vals[:, :, None]).astype(jnp.bfloat16)

def reference(alignment_activations, alignment_row_mask, residue_mask_vector, layer_norm_gain, layer_norm_bias, left_weight, left_bias, right_weight, right_bias, output_weight, output_bias, pair_update_cotangent):
    sequence_total, column_running_sum, feature_width = alignment_activations.shape
    proj_width = left_weight.shape[1]
    pair_width, chan_out = output_weight.shape
    full_sequence_mask = alignment_row_mask.astype(jnp.float32)
    resid_full = residue_mask_vector.astype(jnp.float32)
    standardized_input, inverse_stddev, normalized_input = apply_layer_norm(alignment_activations, layer_norm_gain, layer_norm_bias)
    flat_rows = normalized_input.reshape(-1, feature_width)
    left_proj = project(flat_rows, left_weight, left_bias, full_sequence_mask)
    right_proj = project(flat_rows, right_weight, right_bias, full_sequence_mask)
    right_wide = right_proj.astype(jnp.float32)
    block_rows = math.gcd(column_running_sum, 16)
    block_count = column_running_sum // block_rows

    def row_block(carry, block_idx):
        weight_running, bias_running, col_acc = carry
        begin = (block_idx * block_rows).astype(jnp.int32)
        left_rows = lax.dynamic_slice_in_dim(left_proj, begin, block_rows, 1)
        mask_rows = lax.dynamic_slice_in_dim(full_sequence_mask, begin, block_rows, 1)
        resid_rows = lax.dynamic_slice_in_dim(resid_full, begin, block_rows, 0)
        counted = jnp.dot(mask_rows.T, full_sequence_mask, preferred_element_type=jnp.float32)
        factor = resid_rows[:, None] * resid_full[None, :] / counted
        outer = jnp.einsum('sic,sje->ijce', left_rows.astype(jnp.float32), right_wide)
        outer = outer.reshape(-1, pair_width).astype(jnp.bfloat16)
        projected = jnp.dot(outer, output_weight, preferred_element_type=jnp.float32).reshape(block_rows, column_running_sum, chan_out) + output_bias
        scale = factor[:, :, None]
        pair_rows = (projected * scale).astype(jnp.bfloat16)
        grad_rows = lax.dynamic_slice_in_dim(pair_update_cotangent, begin, block_rows, 0)
        scaled = (grad_rows.astype(jnp.float32) * scale).astype(jnp.bfloat16).reshape(-1, chan_out)
        weight_running = weight_running + jnp.dot(outer.T, scaled, preferred_element_type=jnp.float32)
        bias_running = bias_running + lax.optimization_barrier(jnp.sum(scaled.astype(jnp.float32), 0))
        grad_outer = jnp.dot(scaled, output_weight.T, preferred_element_type=jnp.float32).astype(jnp.bfloat16)
        grad_outer = grad_outer.reshape(block_rows, column_running_sum, proj_width, proj_width).astype(jnp.float32)
        left_part = jnp.einsum('ijce,sje->sic', grad_outer, right_wide)
        col_acc = col_acc + jnp.einsum('sic,ijce->sje', left_rows.astype(jnp.float32), grad_outer)
        return ((weight_running, bias_running, col_acc), (pair_rows, left_part))
    init = (jnp.zeros((pair_width, chan_out), jnp.float32), jnp.zeros((chan_out,), jnp.float32), jnp.zeros((sequence_total, column_running_sum, proj_width), jnp.float32))
    (weight_running, bias_running, right_sum), (pair_blocks, left_blocks) = lax.scan(row_block, init, jnp.arange(block_count).astype(jnp.int32))
    pair_update_output = pair_blocks.reshape(column_running_sum, column_running_sum, chan_out)
    left_sum = jnp.transpose(left_blocks, (1, 0, 2, 3)).reshape(sequence_total, column_running_sum, proj_width)
    grad_left = (left_sum * full_sequence_mask[:, :, None]).astype(jnp.bfloat16).reshape(-1, proj_width)
    grad_right = (right_sum * full_sequence_mask[:, :, None]).astype(jnp.bfloat16).reshape(-1, proj_width)
    left_weight_gradient = jnp.dot(flat_rows.T, grad_left, preferred_element_type=jnp.float32)
    left_bias_gradient = lax.optimization_barrier(jnp.sum(grad_left.astype(jnp.float32), 0))
    right_weight_gradient = jnp.dot(flat_rows.T, grad_right, preferred_element_type=jnp.float32)
    right_bias_gradient = lax.optimization_barrier(jnp.sum(grad_right.astype(jnp.float32), 0))
    normalized_gradient = jnp.dot(grad_left, left_weight.T, preferred_element_type=jnp.float32) + jnp.dot(grad_right, right_weight.T, preferred_element_type=jnp.float32)
    standardized_flat_rows = standardized_input.reshape(-1, feature_width)
    norm_gain_gradient = lax.optimization_barrier(jnp.sum(normalized_gradient * standardized_flat_rows, 0))
    norm_bias_gradient = lax.optimization_barrier(jnp.sum(normalized_gradient, 0))
    gain_applied = normalized_gradient * layer_norm_gain
    alignment_gradient = (gain_applied - lax.optimization_barrier(jnp.mean(gain_applied, -1, keepdims=True)) - standardized_flat_rows * lax.optimization_barrier(jnp.mean(gain_applied * standardized_flat_rows, -1, keepdims=True))) * inverse_stddev.reshape(-1, 1)
    alignment_gradient = alignment_gradient.reshape(sequence_total, column_running_sum, feature_width).astype(jnp.bfloat16)
    return (pair_update_output, alignment_gradient, left_weight_gradient, left_bias_gradient, right_weight_gradient, right_bias_gradient, weight_running, bias_running, norm_gain_gradient, norm_bias_gradient)
```

```python
import functools

import jax
import jax.numpy as jnp
from jax import lax
from jax.experimental import pallas as pl
from jax.experimental.pallas import tpu as pltpu
from jax.sharding import PartitionSpec as P

EPS = 1e-05
LAST_DIMS = (((1,), (1,)), ((), ()))
FIRST_DIMS = (((0,), (0,)), ((), ()))
VMEM_LIMIT = 56 * 1024 * 1024
F32 = jnp.float32
BF16 = jnp.bfloat16


def call(kernel, out_shape, args, scratch=(), scalars=1, flops=0, moved=0):
    specs = [pl.BlockSpec(memory_space=pltpu.SMEM)] * scalars
    specs += [pl.BlockSpec(memory_space=pltpu.VMEM)] * (len(args) - scalars)
    out_specs = jax.tree.map(lambda _: pl.BlockSpec(memory_space=pltpu.VMEM), out_shape)
    return pl.pallas_call(
        kernel,
        out_shape=out_shape,
        in_specs=specs,
        out_specs=out_specs,
        scratch_shapes=list(scratch),
        compiler_params=pltpu.CompilerParams(vmem_limit_bytes=VMEM_LIMIT),
        cost_estimate=pl.CostEstimate(flops=flops, bytes_accessed=moved, transcendentals=0),
    )(*args)


def shape(dims, dtype):
    return jax.ShapeDtypeStruct(tuple(dims), dtype)


def dot(a, b, dims=(((1,), (0,)), ((), ()))):
    return lax.dot_general(a, b, dims, preferred_element_type=F32)


def normalize(x, gain, shift):
    centered = x - jnp.mean(x, -1, keepdims=True)
    inverse = lax.rsqrt(jnp.mean(centered * centered, -1, keepdims=True) + EPS)
    xhat = centered * inverse
    return xhat, inverse, (xhat * gain + shift).astype(BF16)


def project_kernel(
    index_ref, x_ref, mask_ref, gain_ref, shift_ref, w_ref, wb_ref,
    left_ref, right_ref, mask_own_ref, mask_t, proj, right_rows,
):
    seqs, rows, width = x_ref.shape
    proj_width = right_ref.shape[0]
    mask_t[...] = mask_ref[...].astype(F32).T
    begin = pl.multiple_of(index_ref[0] * rows, rows)
    mask_own_ref[...] = mask_t[pl.ds(begin, rows), :]
    step = 16
    for first in range(0, seqs, step):
        x = x_ref[first : first + step].astype(F32).reshape(step * rows, width)
        normalized = normalize(x, gain_ref[...], shift_ref[...])[2]
        proj[first * rows : (first + step) * rows, :] = dot(normalized, w_ref[...]) + wb_ref[...]
    for i in range(rows):
        block = proj[pl.ds(i, seqs, stride=rows), :].T * mask_own_ref[i : i + 1, :]
        left_ref[i * proj_width : (i + 1) * proj_width, :] = block[:proj_width].astype(BF16)
        right_rows[i * proj_width : (i + 1) * proj_width, :] = block[proj_width : 2 * proj_width]
    for e in range(proj_width):
        right_ref[e] = right_rows[pl.ds(e, rows, stride=proj_width), :].astype(BF16)


def right_kernel(
    index_ref, left_ref, mask_ref, mask_own_ref, resid_ref, cot_ref, w_ref,
    keep_ref, send_ref, scaled_ref, factor_ref, w2_ref, b_ref,
    wide, left_t, grad, resid_t, order,
):
    rows, cols, chan = cot_ref.shape
    seqs = left_ref.shape[1]
    proj_width = left_ref.shape[0] // rows
    devices = cols // rows
    index = index_ref[0]
    wide[...] = w_ref[...].astype(F32)
    for e in range(proj_width):
        w2_ref[e * proj_width : (e + 1) * proj_width, :] = wide[
            pl.ds(e, proj_width, stride=proj_width), :
        ].astype(BF16)
    left_t[...] = left_ref[...].astype(F32).T.astype(BF16)
    counted = dot(mask_own_ref[...].astype(BF16), mask_ref[...].astype(F32).astype(BF16))
    resid = resid_ref[...].astype(F32)
    resid_t[...] = jnp.broadcast_to(resid, (128, cols)).T
    resid_own = resid_t[pl.ds(pl.multiple_of(index * rows, rows), rows), :][:, :1]
    factor = resid_own * resid / counted
    factor_ref[...] = factor
    factor_t = factor.T
    bias_sum = jnp.zeros((1, chan), F32)
    for i in range(rows):
        scaled = (cot_ref[i].astype(F32) * factor_t[:, i : i + 1]).astype(BF16)
        scaled_ref[i] = scaled
        bias_sum = bias_sum + jnp.sum(scaled.astype(F32), 0, keepdims=True)
    b_ref[...] = bias_sum
    slots = rel_slots(devices)
    step = 256

    def grad_row(i, carry):
        for slot, rel in enumerate(slots):
            begin = pl.multiple_of((index ^ rel) * rows, rows)
            order[slot * rows : (slot + 1) * rows, :] = scaled_ref[i, pl.ds(begin, rows), :]
        for first in range(0, proj_width * proj_width, step):
            grad[i, first : first + step, :] = dot(
                w2_ref[first : first + step, :], order[...], LAST_DIMS
            ).astype(BF16)
        return carry

    lax.fori_loop(0, rows, grad_row, 0)
    half = devices // 2

    def part(e, carry):
        begin = pl.multiple_of(e * proj_width, proj_width)
        block = grad[:, pl.ds(begin, proj_width), :].reshape(rows * proj_width, cols)
        sums = dot(left_t[...], block).T.reshape(devices, rows, seqs)
        keep_ref[:, pl.ds(e, 1)] = sums[:half][:, None]
        send_ref[:, pl.ds(e, 1)] = sums[half:].astype(BF16)[:, None]
        return carry

    lax.fori_loop(0, proj_width, part, 0)


def rel_slots(devices):
    return [
        core + 2 * mid + 4 * high
        for core in (0, 1)
        for mid in (0, 1)
        for high in range(devices // 4)
    ]


def pair_kernel(
    index_ref, left_ref, w2_ref, scaled_ref, factor_ref, bias_ref, *refs, devices
):
    blocks = refs[:devices]
    pair_ref, w_own_ref, w_send_ref, left_sum_ref = refs[devices : devices + 4]
    right_all, outer, grad, w2_t, w_sum = refs[devices + 4 :]
    rows, cols, chan = scaled_ref.shape
    proj_width = left_ref.shape[0] // rows
    index = index_ref[0]
    for slot, rel in enumerate(rel_slots(devices)):
        begin = pl.multiple_of((index ^ rel) * rows, rows)
        right_all[:, pl.ds(begin, rows), :] = blocks[slot][...]
    w2_t[...] = w2_ref[...].astype(F32).T.astype(BF16)
    step = 256
    together = step // proj_width

    def grad_row(i, carry):
        for first in range(0, proj_width * proj_width, step):
            grad[i, first : first + step, :] = dot(
                w2_ref[first : first + step, :], scaled_ref[i], LAST_DIMS
            ).astype(BF16)
        return carry

    lax.fori_loop(0, rows, grad_row, 0)
    left_sum_ref[...] = jnp.zeros_like(left_sum_ref)

    def column(e, carry):
        begin = pl.multiple_of(e * proj_width, proj_width)
        right = right_all[e]
        for i in range(0, rows, together):
            span = slice(i * proj_width, i * proj_width + step)
            outer[i : i + together, pl.ds(begin, proj_width), :] = (
                dot(left_ref[span, :], right, LAST_DIMS)
                .astype(BF16)
                .reshape(together, proj_width, cols)
            )
            left_sum_ref[span, :] += dot(
                grad[i : i + together, pl.ds(begin, proj_width), :].reshape(step, cols), right
            )
        return carry

    lax.fori_loop(0, proj_width, column, 0)
    w_sum[...] = jnp.zeros_like(w_sum)
    bias = jnp.broadcast_to(bias_ref[...], (8, chan)).T[:, :1]

    def pair_row(i, carry):
        projected = dot(w2_t[...], outer[i]) + bias
        pair_ref[i] = (projected * factor_ref[pl.ds(i, 1), :]).T.astype(BF16)
        for first in range(0, proj_width * proj_width, step):
            w_sum[first : first + step, :] += dot(outer[i, first : first + step, :], scaled_ref[i])
        return carry

    lax.fori_loop(0, rows, pair_row, 0)
    share = w_sum.shape[0] // devices
    for rel in range(devices):
        begin = pl.multiple_of((index ^ rel) * share, share)
        value = w_sum[pl.ds(begin, share), :].astype(BF16)
        if rel < 4:
            w_own_ref[rel] = value
        else:
            w_send_ref[rel // 4 - 1, rel % 4] = value


def norm_kernel(
    x_ref, gain_ref, shift_ref, w_ref, mask_own_ref, left_sum_ref, b_ref, right_own_ref, *refs
):
    *right_refs, out_ref, pack_ref, right_sum, gathered = refs
    seqs, rows, width = x_ref.shape
    proj_width = right_own_ref.shape[0]
    total = right_own_ref[...]
    for ref in right_refs:
        total = total + ref[...].astype(F32)
    right_sum[...] = total.reshape(proj_width * rows, seqs)
    fill = jnp.zeros((128 - 2 * proj_width, seqs), F32)
    for i in range(rows):
        block = jnp.concatenate(
            [
                left_sum_ref[i * proj_width : (i + 1) * proj_width, :],
                right_sum[pl.ds(i, proj_width, stride=rows), :],
                fill,
            ],
            0,
        )
        gathered[pl.ds(i, seqs, stride=rows), :] = (block * mask_own_ref[i : i + 1, :]).T
    step = 16
    w_sum = jnp.zeros((128, width), F32)
    bias_sum = jnp.zeros((1, 128), F32)
    gain_sum = jnp.zeros((1, width), F32)
    shift_sum = jnp.zeros((1, width), F32)
    for first in range(0, seqs, step):
        x = x_ref[first : first + step].astype(F32).reshape(step * rows, width)
        xhat, inverse, normalized = normalize(x, gain_ref[...], shift_ref[...])
        grads = gathered[first * rows : (first + step) * rows, :].astype(BF16)
        bias_sum = bias_sum + jnp.sum(grads.astype(F32), 0, keepdims=True)
        w_sum = w_sum + dot(grads, normalized, FIRST_DIMS)
        grad_norm = dot(grads, w_ref[...], LAST_DIMS)
        gain_sum = gain_sum + jnp.sum(grad_norm * xhat, 0, keepdims=True)
        shift_sum = shift_sum + jnp.sum(grad_norm, 0, keepdims=True)
        g = grad_norm * gain_ref[...]
        result = (
            g - jnp.mean(g, -1, keepdims=True) - xhat * jnp.mean(g * xhat, -1, keepdims=True)
        ) * inverse
        out_ref[first : first + step] = result.astype(BF16).reshape(step, rows, width)
    tail = jnp.concatenate(
        [
            gain_sum,
            shift_sum,
            jnp.concatenate([bias_sum, b_ref[...]], 1),
            jnp.zeros((13, width), F32),
        ],
        0,
    )
    pack_ref[...] = jnp.concatenate([w_sum[: 2 * proj_width], tail], 0).astype(BF16)


def tree_sum(values):
    values = [value.astype(F32) for value in values]
    while len(values) > 1:
        values = [a + b for a, b in zip(values[::2], values[1::2])]
    return values[0]


def sum_kernel(*refs):
    *ins, out_ref = refs
    out_ref[...] = tree_sum([ref[...] for ref in ins]).astype(out_ref.dtype)


def unpack_kernel(*refs):
    ins = refs[:4]
    wl_ref, bl_ref, wr_ref, br_ref, b_ref, gain_ref, shift_ref = refs[4:]
    total = tree_sum([ref[...] for ref in ins])
    proj_width = wl_ref.shape[1]
    weights = total[: 2 * proj_width].T
    wl_ref[...] = weights[:, :proj_width]
    wr_ref[...] = weights[:, proj_width:]
    tail = total[2 * proj_width :]
    gain_ref[...] = tail[0:1]
    shift_ref[...] = tail[1:2]
    bl_ref[...] = tail[2:3, :proj_width]
    br_ref[...] = tail[2:3, proj_width : 2 * proj_width]
    b_ref[...] = tail[2:3, 128 : 128 + b_ref.shape[1]]


def place_kernel(index_ref, *refs):
    *ins, out_ref, rows_ref = refs
    count, share, chan = ins[0].shape
    proj_width = out_ref.shape[0]
    for high, ref in enumerate(ins):
        for low in range(count):
            begin = pl.multiple_of((index_ref[0] ^ (4 * high + low)) * share, share)
            rows_ref[pl.ds(begin, share), :] = ref[low].astype(F32)
    for c in range(proj_width):
        out_ref[c] = rows_ref[pl.ds(c, proj_width, stride=proj_width), :]


def body(
    devices,
    alignment_activations,
    alignment_row_mask,
    residue_mask_vector,
    layer_norm_gain,
    layer_norm_bias,
    left_weight,
    left_bias,
    right_weight,
    right_bias,
    output_weight,
    output_bias,
    pair_update_cotangent,
):
    seqs, rows, width = alignment_activations.shape
    cols = alignment_row_mask.shape[1]
    proj_width = left_weight.shape[1]
    pair_width, chan = output_weight.shape
    high = devices // 4
    index = lax.axis_index("res").astype(jnp.int32).reshape(1)
    gain = layer_norm_gain.reshape(1, width)
    shift = layer_norm_bias.reshape(1, width)
    fill = 128 - 2 * proj_width
    w_cat = jnp.concatenate([left_weight, right_weight, jnp.zeros((width, fill), BF16)], 1)
    b_cat = jnp.concatenate([left_bias, right_bias, jnp.zeros((fill,), F32)]).reshape(1, 128)

    def swap(value, rel):
        return lax.ppermute(value, "res", [(d, d ^ rel) for d in range(devices)])

    left, right, mask_own = call(
        project_kernel,
        (
            shape((rows * proj_width, seqs), BF16),
            shape((proj_width, rows, seqs), BF16),
            shape((rows, seqs), F32),
        ),
        (index, alignment_activations, alignment_row_mask, gain, shift, w_cat, b_cat),
        (
            pltpu.VMEM((cols, seqs), F32),
            pltpu.VMEM((seqs * rows, 128), F32),
            pltpu.VMEM((rows * proj_width, seqs), F32),
        ),
        flops=2 * seqs * rows * width * 128,
        moved=2 * seqs * rows * width,
    )
    blocks = {0: right}
    for k in range(1, high):
        blocks[4 * k] = swap(right, 4 * k)
    for k in range(high):
        blocks[2 + 4 * k] = swap(blocks[4 * k], 2)
    for k in range(high):
        for mid in (0, 2):
            blocks[1 + mid + 4 * k] = swap(blocks[mid + 4 * k], 1)

    half = devices // 2
    keep, send, scaled, factor, w2, b_part = call(
        right_kernel,
        (
            shape((half, proj_width, rows, seqs), F32),
            shape((half, proj_width, rows, seqs), BF16),
            shape((rows, cols, chan), BF16),
            shape((rows, cols), F32),
            shape((pair_width, chan), BF16),
            shape((1, chan), F32),
        ),
        (
            index,
            left,
            alignment_row_mask,
            mask_own,
            residue_mask_vector.reshape(1, cols),
            pair_update_cotangent,
            output_weight,
        ),
        (
            pltpu.VMEM((pair_width, chan), F32),
            pltpu.VMEM((seqs, rows * proj_width), BF16),
            pltpu.VMEM((rows, pair_width, cols), BF16),
            pltpu.VMEM((cols, 128), F32),
            pltpu.VMEM((cols, chan), BF16),
        ),
        flops=4 * rows * cols * pair_width * chan,
        moved=8 * rows * cols * chan,
    )
    first = keep + swap(send, 1).astype(F32)
    second = first[:high] + swap(first[high:].astype(BF16), 2).astype(F32)
    right_parts = [swap(second[k].astype(BF16), 4 * k) for k in range(1, high)]

    pair, w_own, w_send, left_sum = call(
        functools.partial(pair_kernel, devices=devices),
        (
            shape((rows, cols, chan), BF16),
            shape((4, pair_width // devices, chan), BF16),
            shape((high - 1, 4, pair_width // devices, chan), BF16),
            shape((rows * proj_width, seqs), F32),
        ),
        (index, left, w2, scaled, factor, output_bias.reshape(1, chan))
        + tuple(blocks[rel] for rel in rel_slots(devices)),
        (
            pltpu.VMEM((proj_width, cols, seqs), BF16),
            pltpu.VMEM((rows, pair_width, cols), BF16),
            pltpu.VMEM((rows, pair_width, cols), BF16),
            pltpu.VMEM((chan, pair_width), BF16),
            pltpu.VMEM((pair_width, chan), F32),
        ),
        flops=10 * rows * cols * pair_width * chan,
        moved=8 * rows * cols * chan,
    )
    share = pair_width // devices
    w_high = call(
        sum_kernel,
        shape((4, share, chan), BF16),
        (w_own,) + tuple(swap(w_send[k - 1], 4 * k) for k in range(1, high)),
        scalars=0,
    )
    w_low = call(
        sum_kernel,
        shape((share, chan), BF16),
        (w_high[0],) + tuple(swap(w_high[m], m) for m in range(1, 4)),
        scalars=0,
    )
    w_near = jnp.stack([w_low] + [swap(w_low, m) for m in range(1, 4)])
    w_out_grad = call(
        place_kernel,
        shape((proj_width, proj_width, chan), F32),
        (index, w_near) + tuple(swap(w_near, 4 * k) for k in range(1, high)),
        (pltpu.VMEM((pair_width, chan), F32),),
    ).reshape(pair_width, chan)

    alignment_gradient, pack = call(
        norm_kernel,
        (shape((seqs, rows, width), BF16), shape((2 * proj_width + 16, width), BF16)),
        (
            alignment_activations,
            gain,
            shift,
            w_cat,
            mask_own,
            left_sum,
            b_part,
            second[0],
        )
        + tuple(right_parts),
        (
            pltpu.VMEM((proj_width * rows, seqs), F32),
            pltpu.VMEM((seqs * rows, 128), F32),
        ),
        scalars=0,
        flops=4 * seqs * rows * width * 128,
        moved=4 * seqs * rows * width,
    )
    pack = call(
        sum_kernel,
        shape(pack.shape, BF16),
        (pack,) + tuple(swap(pack, 4 * k) for k in range(1, high)),
        scalars=0,
    )
    w_left, b_left, w_right, b_right, b_out, gain_grad, shift_grad = call(
        unpack_kernel,
        (
            shape((width, proj_width), F32),
            shape((1, proj_width), F32),
            shape((width, proj_width), F32),
            shape((1, proj_width), F32),
            shape((1, chan), F32),
            shape((1, width), F32),
            shape((1, width), F32),
        ),
        (pack,) + tuple(swap(pack, m) for m in range(1, 4)),
        scalars=0,
    )
    return (
        pair,
        alignment_gradient,
        w_left,
        b_left.reshape(-1),
        w_right,
        b_right.reshape(-1),
        w_out_grad,
        b_out.reshape(-1),
        gain_grad.reshape(-1),
        shift_grad.reshape(-1),
    )


def solution(mesh):
    return jax.shard_map(
        functools.partial(body, mesh.shape["res"]),
        mesh=mesh,
        in_specs=(
            P(None, ("grp", "res"), None),
            P(None, "grp"),
            P("grp"),
            P(),
            P(),
            P(),
            P(),
            P(),
            P(),
            P(),
            P(),
            P(("grp", "res"), None, None),
        ),
        out_specs=(
            P(("grp", "res"), None, None),
            P(None, ("grp", "res"), None),
            P("grp", None),
            P("grp"),
            P("grp", None),
            P("grp"),
            P("grp", None),
            P("grp"),
            P("grp"),
            P("grp"),
        ),
        check_vma=False,
    )
```

```python
import functools

import jax
import jax.numpy as jnp
from jax import lax
from jax.experimental import pallas as pl
from jax.experimental.pallas import tpu as pltpu
from jax.sharding import PartitionSpec as P

EPS = 1e-05
LAST_DIMS = (((1,), (1,)), ((), ()))
FIRST_DIMS = (((0,), (0,)), ((), ()))
VMEM_LIMIT = 56 * 1024 * 1024
LANES = 128
TAIL = 16
F32 = jnp.float32
BF16 = jnp.bfloat16


def call(kernel, out_shape, args, scratch=(), scalars=1, us=1.0, after=(), **static):
    specs = [pl.BlockSpec(memory_space=pltpu.SMEM)] * scalars
    specs += [pl.BlockSpec(memory_space=pltpu.VMEM)] * (len(args) - scalars)
    specs += [pl.BlockSpec(memory_space=pl.ANY)] * len(after)
    out_specs = jax.tree.map(lambda _: pl.BlockSpec(memory_space=pltpu.VMEM), out_shape)
    count = len(args)

    def run(*refs):
        kernel(*refs[:count], *refs[count + len(after) :], **static)

    run.__name__ = kernel.__name__
    return pl.pallas_call(
        run,
        name=kernel.__name__,
        out_shape=out_shape,
        in_specs=specs,
        out_specs=out_specs,
        scratch_shapes=list(scratch),
        compiler_params=pltpu.CompilerParams(vmem_limit_bytes=VMEM_LIMIT),
        cost_estimate=pl.CostEstimate(
            flops=int(us * 1.1e9), bytes_accessed=int(us * 1e5), transcendentals=0
        ),
    )(*args, *after)


def shape(dims, dtype):
    return jax.ShapeDtypeStruct(tuple(dims), dtype)


def dot(a, b, dims=(((1,), (0,)), ((), ()))):
    return lax.dot_general(a, b, dims, preferred_element_type=F32)


def normalize(x, gain, shift):
    centered = x - jnp.mean(x, -1, keepdims=True)
    inverse = lax.rsqrt(jnp.mean(centered * centered, -1, keepdims=True) + EPS)
    xhat = centered * inverse
    return xhat, inverse, (xhat * gain + shift).astype(BF16)


def column_of(row):
    return jnp.broadcast_to(row, (8, row.shape[1])).T[:, :1]


def project_kernel(
    index_ref, x_ref, mask_ref, gain_ref, shift_ref, wl_ref, wr_ref, bl_ref, br_ref,
    left_ref, right_ref, mask_t_ref, proj, right_rows, weights,
):
    seqs, rows, width = x_ref.shape
    proj_width = right_ref.shape[0]
    mask_t_ref[...] = mask_ref[...].astype(F32).T
    begin = pl.multiple_of(index_ref[0] * rows, rows)
    weights[:proj_width, :] = wl_ref[...]
    weights[proj_width : 2 * proj_width, :] = wr_ref[...]
    weights[2 * proj_width :, :] = jnp.zeros((LANES - 2 * proj_width, width), BF16)
    bias_left = column_of(bl_ref[...])
    bias_right = column_of(br_ref[...])
    step = 16
    for first in range(0, seqs, step):
        x = x_ref[first : first + step].astype(F32).reshape(step * rows, width)
        normalized = normalize(x, gain_ref[...], shift_ref[...])[2]
        proj[first * rows : (first + step) * rows, :] = dot(normalized, weights[...], LAST_DIMS)
    mask_own = mask_t_ref[pl.ds(begin, rows), :]
    for i in range(rows):
        block = proj[pl.ds(i, seqs, stride=rows), :].T
        mask_row = mask_own[i : i + 1, :]
        span = slice(i * proj_width, (i + 1) * proj_width)
        left_ref[span, :] = ((block[:proj_width] + bias_left) * mask_row).astype(BF16)
        right_rows[span, :] = (block[proj_width : 2 * proj_width] + bias_right) * mask_row
    for e in range(proj_width):
        right_ref[e] = right_rows[pl.ds(e, rows, stride=proj_width), :].astype(BF16)


def grad_columns(w2_ref, scaled_ref, grad):
    rows, cols, chan = scaled_ref.shape
    proj_width = grad.shape[0]
    for i in range(0, rows, 2):
        pair = scaled_ref[i : i + 2].reshape(2 * cols, chan)
        block = dot(w2_ref[...], pair, LAST_DIMS).astype(BF16)
        for e in range(proj_width):
            for sub in range(2):
                grad[e, (i + sub) * proj_width : (i + sub + 1) * proj_width, :] = block[
                    e * proj_width : (e + 1) * proj_width, sub * cols : (sub + 1) * cols
                ]


def right_columns(index_ref, left_t, grad, emit):
    proj_width, _, cols = grad.shape
    rows = left_t.shape[1] // proj_width
    slots = cols // rows
    own = index_ref[0] >> 1
    for e in range(0, proj_width, 2):
        block = jnp.concatenate([grad[e], grad[e + 1]], 1)
        sums = dot(left_t[...], block)
        for sub in range(2):
            part = sums[:, sub * cols : (sub + 1) * cols].T
            for q in range(slots):
                emit(e + sub, q ^ own, part[q * rows : (q + 1) * rows])


def scale_columns(half, mask_t_ref, mask_own, resid_t, resid_own, cot_ref, scaled_ref, factor_ref):
    rows = cot_ref.shape[0]
    cols = scaled_ref.shape[1]
    starts = [
        pl.multiple_of((2 * q + half) * rows, rows) for q in range(cols // rows)
    ]
    mask_cols = jnp.concatenate([mask_t_ref[pl.ds(s, rows), :] for s in starts], 0)
    resid_cols = jnp.concatenate([resid_t[pl.ds(s, rows), :] for s in starts], 0)
    counted = dot(mask_cols.astype(BF16), mask_own.astype(BF16), LAST_DIMS)
    factor_t = resid_cols[:, :1] * resid_own / counted
    factor_ref[...] = factor_t.T
    bias_sum = jnp.zeros((1, cot_ref.shape[2]), F32)
    for i in range(rows):
        cot = jnp.concatenate([cot_ref[i, pl.ds(s, rows), :] for s in starts], 0)
        scaled = (cot.astype(F32) * factor_t[:, i : i + 1]).astype(BF16)
        scaled_ref[i] = scaled
        bias_sum = bias_sum + jnp.sum(scaled.astype(F32), 0, keepdims=True)
    return bias_sum


def send_kernel(
    index_ref, left_ref, mask_t_ref, resid_ref, cot_ref, w_ref,
    send_ref, far_ref, near_ref, far_factor_ref, near_factor_ref, w2_ref, b_ref, left_t_ref,
    wide, grad, resid_t,
):
    rows, cols, chan = cot_ref.shape
    proj_width = left_ref.shape[0] // rows
    index = index_ref[0]
    wide[...] = w_ref[...].astype(F32)
    for e in range(proj_width):
        w2_ref[e * proj_width : (e + 1) * proj_width, :] = wide[
            pl.ds(e, proj_width, stride=proj_width), :
        ].astype(BF16)
    left_t_ref[...] = left_ref[...].astype(F32).T.astype(BF16)
    resid_t[...] = jnp.broadcast_to(resid_ref[...].astype(F32), (LANES, cols)).T
    begin = pl.multiple_of(index * rows, rows)
    mask_own = mask_t_ref[pl.ds(begin, rows), :]
    resid_own = resid_t[pl.ds(begin, rows), :].T[:1]
    side = index & 1
    shared = (mask_t_ref, mask_own, resid_t, resid_own, cot_ref)
    far_sum = scale_columns(1 - side, *shared, far_ref, far_factor_ref)
    near_sum = scale_columns(side, *shared, near_ref, near_factor_ref)
    b_ref[...] = far_sum + near_sum
    grad_columns(w2_ref, far_ref, grad)

    def emit(e, rel, value):
        send_ref[rel, e] = value.astype(BF16)

    right_columns(index_ref, left_t_ref, grad, emit)


def normal_kernel(x_ref, gain_ref, shift_ref, normal_ref):
    seqs, rows, width = x_ref.shape
    step = 16
    for first in range(0, seqs, step):
        x = x_ref[first : first + step].astype(F32).reshape(step * rows, width)
        xhat, _, normalized = normalize(x, gain_ref[...], shift_ref[...])
        span = slice(first * rows, (first + step) * rows)
        normal_ref[span, :width] = normalized
        normal_ref[span, width:] = xhat.astype(BF16)


def keep_kernel(index_ref, left_t_ref, w2_ref, near_ref, far_part_ref, keep_ref, send_ref, total, grad):
    grad_columns(w2_ref, near_ref, grad)

    def emit(e, rel, value):
        total[rel, e] = value

    right_columns(index_ref, left_t_ref, grad, emit)
    for k in range(keep_ref.shape[0]):
        keep_ref[k] = total[2 * k] + far_part_ref[2 * k].astype(F32)
        send_ref[k] = (total[2 * k + 1] + far_part_ref[2 * k + 1].astype(F32)).astype(BF16)


def high_kernel(keep_ref, other_ref, own_ref, *send_refs):
    own_ref[...] = keep_ref[0] + other_ref[0].astype(F32)
    for k, ref in enumerate(send_refs):
        ref[...] = (keep_ref[k + 1] + other_ref[k + 1].astype(F32)).astype(BF16)


def place_kernel(index_ref, *refs):
    *blocks, out_ref = refs
    rows = blocks[0].shape[1]
    own = index_ref[0] >> 1
    for rel, ref in enumerate(blocks):
        out_ref[:, pl.ds(pl.multiple_of((own ^ rel) * rows, rows), rows), :] = ref[...]


def outer_columns(left_ref, right_ref, outer):
    proj_width, cols, seqs = right_ref.shape
    rows = left_ref.shape[0] // proj_width
    for e in range(0, proj_width, 2):
        pair = right_ref[e : e + 2].reshape(2 * cols, seqs)
        block = dot(left_ref[...], pair, LAST_DIMS).astype(BF16)
        for i in range(rows):
            for sub in range(2):
                outer[
                    i // 2,
                    (e + sub) * proj_width : (e + sub + 1) * proj_width,
                    (i % 2) * cols : (i % 2 + 1) * cols,
                ] = block[i * proj_width : (i + 1) * proj_width, sub * cols : (sub + 1) * cols]


def weight_columns(left_ref, right_ref, scaled_ref, w_ref, outer):
    rows, cols, chan = scaled_ref.shape
    outer_columns(left_ref, right_ref, outer)
    for p in range(rows // 2):
        w_ref[...] += dot(outer[p], scaled_ref[2 * p : 2 * p + 2].reshape(2 * cols, chan))


def left_columns(w2_ref, scaled_ref, right_ref, left_sum_ref, grad):
    proj_width, cols, seqs = right_ref.shape
    grad_columns(w2_ref, scaled_ref, grad)
    for e in range(0, proj_width, 2):
        block = jnp.concatenate([grad[e], grad[e + 1]], 1)
        left_sum_ref[...] += dot(block, right_ref[e : e + 2].reshape(2 * cols, seqs))


def near_kernel(left_ref, w2_ref, scaled_ref, right_ref, w_sum_ref, left_sum_ref, outer, grad):
    w_sum_ref[...] = jnp.zeros_like(w_sum_ref)
    weight_columns(left_ref, right_ref, scaled_ref, w_sum_ref, outer)
    left_sum_ref[...] = jnp.zeros_like(left_sum_ref)
    left_columns(w2_ref, scaled_ref, right_ref, left_sum_ref, grad)


def far_weight_kernel(
    index_ref, left_ref, scaled_ref, right_ref, w_sum_ref, own_ref, *refs
):
    *send_refs, outer, total = refs
    high, share, _ = own_ref.shape
    total[...] = w_sum_ref[...]
    weight_columns(left_ref, right_ref, scaled_ref, total, outer)
    for low in range(4):
        for k in range(high):
            begin = pl.multiple_of((index_ref[0] ^ (4 * k + low)) * share, share)
            ref = own_ref if low == 0 else send_refs[low - 1]
            ref[k] = total[pl.ds(begin, share), :].astype(BF16)


def far_left_kernel(w2_ref, scaled_ref, right_ref, near_sum_ref, left_sum_ref, grad):
    left_sum_ref[...] = near_sum_ref[...]
    left_columns(w2_ref, scaled_ref, right_ref, left_sum_ref, grad)


def pair_kernel(
    index_ref, left_ref, w2_ref, bias_ref, near_ref, far_ref, near_factor_ref, far_factor_ref,
    out_ref, outer, w2_t,
):
    rows, _, chan = out_ref.shape
    w2_t[...] = w2_ref[...].astype(F32).T.astype(BF16)
    bias = column_of(bias_ref[...])
    side = index_ref[0] & 1
    for half, right_ref, factor_ref in (
        (side, near_ref, near_factor_ref),
        (1 - side, far_ref, far_factor_ref),
    ):
        cols = right_ref.shape[1]
        outer_columns(left_ref, right_ref, outer)
        for p in range(rows // 2):
            projected = dot(w2_t[...], outer[p]) + bias
            for sub in range(2):
                i = 2 * p + sub
                block = projected[:, sub * cols : (sub + 1) * cols] * factor_ref[i : i + 1, :]
                block = block.T.astype(BF16)
                for q in range(cols // rows):
                    begin = pl.multiple_of((2 * q + half) * rows, rows)
                    out_ref[i, pl.ds(begin, rows), :] = block[q * rows : (q + 1) * rows]


def sums_kernel(
    index_ref, normal_ref, wl_ref, wr_ref, mask_t_ref, left_sum_ref, b_ref, right_own_ref, *refs
):
    *right_refs, grads_ref, pack_ref, right_sum, gathered = refs
    seqs = mask_t_ref.shape[1]
    proj_width, rows, _ = right_own_ref.shape
    width = wl_ref.shape[1]
    total = right_own_ref[...]
    for ref in right_refs:
        total = total + ref[...].astype(F32)
    right_sum[...] = total.reshape(proj_width * rows, seqs)
    mask_own = mask_t_ref[pl.ds(pl.multiple_of(index_ref[0] * rows, rows), rows), :]
    fill = jnp.zeros((LANES - 2 * proj_width, seqs), F32)
    bias_cols = jnp.zeros((LANES, seqs), F32)
    for i in range(rows):
        block = jnp.concatenate(
            [
                left_sum_ref[i * proj_width : (i + 1) * proj_width, :],
                right_sum[pl.ds(i, proj_width, stride=rows), :],
                fill,
            ],
            0,
        )
        block = (block * mask_own[i : i + 1, :]).astype(BF16).astype(F32)
        bias_cols = bias_cols + block
        gathered[pl.ds(i, seqs, stride=rows), :] = block.T
    grads_ref[...] = gathered[...].astype(BF16)
    used = 2 * proj_width
    products = jnp.zeros((LANES, 2 * width), F32)
    step = 256
    for first in range(0, seqs * rows, step):
        products = products + dot(
            grads_ref[first : first + step, :], normal_ref[first : first + step, :], FIRST_DIMS
        )
    weights = jnp.concatenate([wl_ref[...], wr_ref[...]], 0).astype(F32)
    bias_sum = jnp.sum(bias_cols, 1, keepdims=True)
    gain_sum = jnp.sum(weights * products[:used, width:], 0, keepdims=True)
    shift_sum = jnp.sum(weights * bias_sum[:used], 0, keepdims=True)
    bias_row = jnp.broadcast_to(bias_sum, (LANES, LANES)).T[:1]
    pieces = [products[:used, k : k + LANES] for k in range(0, width, LANES)]
    pieces += [gain_sum[:, k : k + LANES] for k in range(0, width, LANES)]
    pieces += [shift_sum[:, k : k + LANES] for k in range(0, width, LANES)]
    pieces += [bias_row, b_ref[...]]
    pieces += [jnp.zeros((TAIL - 2 - 2 * (width // LANES), LANES), F32)]
    pack_ref[...] = jnp.concatenate(pieces, 0).astype(BF16)


def norm_kernel(x_ref, gain_ref, shift_ref, wl_ref, wr_ref, grads_ref, out_ref, weights):
    seqs, rows, width = x_ref.shape
    proj_width = wl_ref.shape[0]
    weights[...] = jnp.zeros_like(weights)
    weights[:proj_width, :] = wl_ref[...]
    weights[proj_width : 2 * proj_width, :] = wr_ref[...]
    step = 16
    for first in range(0, seqs, step):
        x = x_ref[first : first + step].astype(F32).reshape(step * rows, width)
        xhat, inverse, _ = normalize(x, gain_ref[...], shift_ref[...])
        g = dot(grads_ref[first * rows : (first + step) * rows, :], weights[...]) * gain_ref[...]
        result = (
            g - jnp.mean(g, -1, keepdims=True) - xhat * jnp.mean(g * xhat, -1, keepdims=True)
        ) * inverse
        out_ref[first : first + step] = result.astype(BF16).reshape(step, rows, width)


def tree_sum(values):
    values = [value.astype(F32) for value in values]
    while len(values) > 1:
        values = [a + b for a, b in zip(values[::2], values[1::2])]
    return values[0]


def share_kernel(*refs):
    ins, outs = refs[:4], refs[4:]
    total = tree_sum([ref[...] for ref in ins]).astype(BF16)
    for k, ref in enumerate(outs):
        ref[...] = total[k]


def total_kernel(pack_ref, *refs):
    *ins, out_ref = refs
    count = pack_ref.shape[0]
    out_ref[:count, :] = pack_ref[...]
    out_ref[count:, :] = tree_sum([ref[...] for ref in ins]).astype(BF16)


def merge_kernel(*refs):
    *ins, out_ref = refs
    rows = ins[0].shape[0]
    share = (out_ref.shape[0] - rows) // (len(ins) - 1)
    head = rows - share
    out_ref[:head, :] = tree_sum([ref[:head, :] for ref in ins]).astype(BF16)
    for k, ref in enumerate(ins):
        out_ref[head + k * share : head + (k + 1) * share, :] = ref[head:, :]


def unpack_kernel(index_ref, *refs, share):
    ins = refs[:4]
    wl_ref, bl_ref, wr_ref, br_ref, w_out_ref, b_ref, gain_ref, shift_ref, placed = refs[4:]
    proj_width, width = wl_ref.shape
    used = 2 * proj_width
    parts = width // LANES
    head = parts * used + TAIL
    total = tree_sum([ref[:head, :] for ref in ins])
    tail = total[parts * used :]
    for k in range(parts):
        span = slice(k * LANES, (k + 1) * LANES)
        wl_ref[:, span] = total[k * used : k * used + proj_width]
        wr_ref[:, span] = total[k * used + proj_width : (k + 1) * used]
        gain_ref[:, span] = tail[k : k + 1]
        shift_ref[:, span] = tail[parts + k : parts + k + 1]
    bl_ref[...] = tail[2 * parts : 2 * parts + 1, :proj_width]
    br_ref[...] = tail[2 * parts : 2 * parts + 1, proj_width:used]
    b_ref[...] = tail[2 * parts + 1 : 2 * parts + 2, :]
    for low, ref in enumerate(ins):
        for k in range((ref.shape[0] - head) // share):
            begin = pl.multiple_of((index_ref[0] ^ (4 * k + low)) * share, share)
            span = slice(head + k * share, head + (k + 1) * share)
            placed[pl.ds(begin, share), :] = ref[span, :].astype(F32)
    for c in range(proj_width):
        w_out_ref[c * proj_width : (c + 1) * proj_width, :] = placed[
            pl.ds(c, proj_width, stride=proj_width), :
        ]


def body(
    devices,
    alignment_activations,
    alignment_row_mask,
    residue_mask_vector,
    layer_norm_gain,
    layer_norm_bias,
    left_weight,
    left_bias,
    right_weight,
    right_bias,
    output_weight,
    output_bias,
    pair_update_cotangent,
):
    seqs, rows, width = alignment_activations.shape
    cols = alignment_row_mask.shape[1]
    proj_width = left_weight.shape[1]
    pair_width, chan = output_weight.shape
    high = devices // 4
    half = cols // 2
    share = pair_width // devices
    flat = rows * proj_width
    index = lax.axis_index("res").astype(jnp.int32).reshape(1)
    gain = layer_norm_gain.reshape(1, width)
    shift = layer_norm_bias.reshape(1, width)
    wl, wr = left_weight.T, right_weight.T
    piece = (proj_width, rows, seqs)

    def swap(value, rel):
        return lax.ppermute(value, "res", [(d, d ^ rel) for d in range(devices)])

    left, right, mask_t = call(
        project_kernel,
        (shape((flat, seqs), BF16), shape(piece, BF16), shape((cols, seqs), F32)),
        (index, alignment_activations, alignment_row_mask, gain, shift, wl, wr)
        + (left_bias.reshape(1, proj_width), right_bias.reshape(1, proj_width)),
        (
            pltpu.VMEM((seqs * rows, LANES), F32),
            pltpu.VMEM((flat, seqs), F32),
            pltpu.VMEM((LANES, width), BF16),
        ),
        us=4,
    )
    blocks = [None] * (2 * high)
    for k in range(high):
        blocks[2 * k] = swap(right, 4 * k) if k else right
    for k in range(high):
        blocks[2 * k + 1] = swap(blocks[2 * k], 2)

    send, far, near, far_factor, near_factor, w2, b_part, left_t = call(
        send_kernel,
        (
            shape((2 * high,) + piece, BF16),
            shape((rows, half, chan), BF16),
            shape((rows, half, chan), BF16),
            shape((rows, half), F32),
            shape((rows, half), F32),
            shape((pair_width, chan), BF16),
            shape((1, chan), F32),
            shape((seqs, flat), BF16),
        ),
        (
            index,
            left,
            mask_t,
            residue_mask_vector.reshape(1, cols),
            pair_update_cotangent,
            output_weight,
        ),
        (
            pltpu.VMEM((pair_width, chan), F32),
            pltpu.VMEM((proj_width, flat, half), BF16),
            pltpu.VMEM((cols, LANES), F32),
        ),
        us=6,
    )
    normal = call(
        normal_kernel,
        shape((seqs * rows, 2 * width), BF16),
        (alignment_activations, gain, shift),
        scalars=0,
        us=10,
        after=(left_t,) + tuple(blocks[1:][:1] + blocks[2::2]),
    )
    keep, send = call(
        keep_kernel,
        (shape((high,) + piece, F32), shape((high,) + piece, BF16)),
        (index, left_t, w2, near, swap(send, 1)),
        (
            pltpu.VMEM((2 * high,) + piece, F32),
            pltpu.VMEM((proj_width, flat, half), BF16),
        ),
        us=0.5,
        after=(normal,),
    )
    right_near = call(
        place_kernel,
        shape((proj_width, half, seqs), BF16),
        (index,) + tuple(blocks),
        after=(keep,),
    )
    right_far = swap(right_near, 1)
    outer_scratch = pltpu.VMEM((rows // 2, pair_width, 2 * half), BF16)
    grad_scratch = pltpu.VMEM((proj_width, flat, half), BF16)
    near_w, near_left = call(
        near_kernel,
        (shape((pair_width, chan), F32), shape((flat, seqs), F32)),
        (left, w2, near, right_near),
        (outer_scratch, grad_scratch),
        scalars=0,
        us=7,
    )
    right_own, *sends = call(
        high_kernel,
        (shape(piece, F32),) + (shape(piece, BF16),) * (high - 1),
        (keep, swap(send, 2)),
        scalars=0,
        after=(near_left,),
    )
    right_parts = tuple(swap(value, 4 * (k + 1)) for k, value in enumerate(sends))

    w_own, *w_sends = call(
        far_weight_kernel,
        (shape((high, share, chan), BF16),) * 4,
        (index, left, far, right_far, near_w),
        (outer_scratch, pltpu.VMEM((pair_width, chan), F32)),
        us=3.5,
        after=(right_own,),
    )
    left_sum = call(
        far_left_kernel,
        shape((flat, seqs), F32),
        (w2, far, right_far, near_left),
        (grad_scratch,),
        scalars=0,
        us=3.5,
        after=(w_own,),
    )
    grads, pack = call(
        sums_kernel,
        (
            shape((seqs * rows, LANES), BF16),
            shape((2 * proj_width * (width // LANES) + TAIL, LANES), BF16),
        ),
        (index, normal, wl, wr, mask_t, left_sum, b_part, right_own) + right_parts,
        (pltpu.VMEM((flat, seqs), F32), pltpu.VMEM((seqs * rows, LANES), F32)),
        us=3,
    )
    shares = call(
        share_kernel,
        (shape((share, chan), BF16),) * high,
        (w_own,) + tuple(swap(value, m + 1) for m, value in enumerate(w_sends)),
        scalars=0,
    )
    packed = call(
        total_kernel,
        shape((pack.shape[0] + share, LANES), BF16),
        (pack, shares[0]) + tuple(swap(shares[k], 4 * k) for k in range(1, high)),
        scalars=0,
    )
    alignment_gradient = call(
        norm_kernel,
        shape((seqs, rows, width), BF16),
        (alignment_activations, gain, shift, wl, wr, grads),
        (pltpu.VMEM((LANES, width), BF16),),
        scalars=0,
        us=4,
    )
    merged = call(
        merge_kernel,
        shape((pack.shape[0] + high * share, LANES), BF16),
        (packed,) + tuple(swap(packed, 4 * k) for k in range(1, high)),
        scalars=0,
        after=(alignment_gradient,),
    )
    pair = call(
        pair_kernel,
        shape((rows, cols, chan), BF16),
        (index, left, w2, output_bias.reshape(1, chan))
        + (right_near, right_far, near_factor, far_factor),
        (outer_scratch, pltpu.VMEM((chan, pair_width), BF16)),
        us=6,
        after=(merged,),
    )
    w_left, b_left, w_right, b_right, w_out_grad, b_out, gain_grad, shift_grad = call(
        unpack_kernel,
        (
            shape((proj_width, width), F32),
            shape((1, proj_width), F32),
            shape((proj_width, width), F32),
            shape((1, proj_width), F32),
            shape((pair_width, chan), F32),
            shape((1, chan), F32),
            shape((1, width), F32),
            shape((1, width), F32),
        ),
        (index, merged) + tuple(swap(merged, m) for m in range(1, 4)),
        (pltpu.VMEM((pair_width, chan), F32),),
        after=(pair,),
        share=share,
    )
    return (
        pair,
        alignment_gradient,
        w_left.T,
        b_left.reshape(-1),
        w_right.T,
        b_right.reshape(-1),
        w_out_grad,
        b_out.reshape(-1),
        gain_grad.reshape(-1),
        shift_grad.reshape(-1),
    )


def solution(mesh):
    return jax.shard_map(
        functools.partial(body, mesh.shape["res"]),
        mesh=mesh,
        in_specs=(
            P(None, ("grp", "res"), None),
            P(None, "grp"),
            P("grp"),
            P(),
            P(),
            P(),
            P(),
            P(),
            P(),
            P(),
            P(),
            P(("grp", "res"), None, None),
        ),
        out_specs=(
            P(("grp", "res"), None, None),
            P(None, ("grp", "res"), None),
            P("grp", None),
            P("grp"),
            P("grp", None),
            P("grp"),
            P("grp", None),
            P("grp"),
            P("grp"),
            P("grp"),
        ),
        check_vma=False,
    )
```

```python
import functools
import math

import jax
import jax.numpy as jnp
from jax import lax
from jax.experimental import pallas as pl
from jax.experimental.pallas import tpu as pltpu
from jax.sharding import PartitionSpec as P

EPS = 1e-05
LAST_DIMS = (((1,), (1,)), ((), ()))
FIRST_DIMS = (((0,), (0,)), ((), ()))
MIB = 1024 * 1024
LANES = 128
TAIL = 16
F32 = jnp.float32
BF16 = jnp.bfloat16


def tiled_bytes(dims, dtype):
    dims = tuple(dims)
    lanes = -(-dims[-1] // LANES) * LANES
    sublanes = -(-(dims[-2] if len(dims) > 1 else 1) // 16) * 16
    return math.prod(dims[:-2]) * sublanes * lanes * jnp.dtype(dtype).itemsize


def call(kernel, out_shape, args, scratch=(), scalars=1, us=1.0, after=(), **static):
    specs = [pl.BlockSpec(memory_space=pltpu.SMEM)] * scalars
    specs += [pl.BlockSpec(memory_space=pltpu.VMEM)] * (len(args) - scalars)
    specs += [pl.BlockSpec(memory_space=pl.ANY)] * len(after)
    out_specs = jax.tree.map(lambda _: pl.BlockSpec(memory_space=pltpu.VMEM), out_shape)
    count = len(args)
    held = list(args[scalars:]) + jax.tree.leaves(out_shape) + list(scratch)
    need = sum(tiled_bytes(value.shape, value.dtype) for value in held)

    def run(*refs):
        kernel(*refs[:count], *refs[count + len(after) :], **static)

    return pl.pallas_call(
        run,
        name=kernel.__name__,
        out_shape=out_shape,
        in_specs=specs,
        out_specs=out_specs,
        scratch_shapes=list(scratch),
        compiler_params=pltpu.CompilerParams(vmem_limit_bytes=min(need + 6 * MIB, 56 * MIB)),
        cost_estimate=pl.CostEstimate(
            flops=int(us * 1.1e9), bytes_accessed=int(us * 1e5), transcendentals=0
        ),
    )(*args, *after)


def shape(dims, dtype):
    return jax.ShapeDtypeStruct(tuple(dims), dtype)


def dot(a, b, dims=(((1,), (0,)), ((), ()))):
    return lax.dot_general(a, b, dims, preferred_element_type=F32)


def normalize(x, gain, shift):
    centered = x - jnp.mean(x, -1, keepdims=True)
    inverse = lax.rsqrt(jnp.mean(centered * centered, -1, keepdims=True) + EPS)
    xhat = centered * inverse
    return xhat, inverse, (xhat * gain + shift).astype(BF16)


def column_of(row):
    return jnp.broadcast_to(row, (8, row.shape[1])).T[:, :1]


def project_kernel(
    index_ref, x_ref, mask_ref, gain_ref, shift_ref, wl_ref, wr_ref, bl_ref, br_ref,
    left_ref, right_ref, mask_t_ref, normal_ref, inverse_ref, proj, right_rows, weights,
):
    seqs, rows, width = x_ref.shape
    high, proj_width = right_ref.shape[:2]
    mask_t_ref[...] = mask_ref[...].astype(F32).T
    begin = pl.multiple_of(index_ref[0] * rows, rows)
    weights[:proj_width, :] = wl_ref[...]
    weights[proj_width : 2 * proj_width, :] = wr_ref[...]
    weights[2 * proj_width :, :] = jnp.zeros((LANES - 2 * proj_width, width), BF16)
    bias_left = column_of(bl_ref[...])
    bias_right = column_of(br_ref[...])
    step = 16
    for first in range(0, seqs, step):
        x = x_ref[first : first + step].astype(F32).reshape(step * rows, width)
        xhat, inverse, normalized = normalize(x, gain_ref[...], shift_ref[...])
        span = slice(first * rows, (first + step) * rows)
        normal_ref[span, :width] = normalized
        normal_ref[span, width:] = xhat.astype(BF16)
        inverse_ref[span, :] = inverse
        proj[span, :] = dot(normalized, weights[...], LAST_DIMS)
    mask_own = mask_t_ref[pl.ds(begin, rows), :]
    for i in range(rows):
        block = proj[pl.ds(i, seqs, stride=rows), :].T
        mask_row = mask_own[i : i + 1, :]
        span = slice(i * proj_width, (i + 1) * proj_width)
        left_ref[span, :] = ((block[:proj_width] + bias_left) * mask_row).astype(BF16)
        right_rows[span, :] = (block[proj_width : 2 * proj_width] + bias_right) * mask_row
    for e in range(proj_width):
        value = right_rows[pl.ds(e, rows, stride=proj_width), :].astype(BF16)
        for k in range(high):
            right_ref[k, e] = value


def grad_columns(w2_ref, scaled_ref, grad):
    rows, cols, chan = scaled_ref.shape
    proj_width = grad.shape[0]
    for i in range(0, rows, 2):
        pair = scaled_ref[i : i + 2].reshape(2 * cols, chan)
        block = dot(w2_ref[...], pair, LAST_DIMS).astype(BF16)
        for e in range(proj_width):
            for sub in range(2):
                grad[e, (i + sub) * proj_width : (i + sub + 1) * proj_width, :] = block[
                    e * proj_width : (e + 1) * proj_width, sub * cols : (sub + 1) * cols
                ]


def right_columns(index_ref, left_t, grad, emit):
    proj_width, _, cols = grad.shape
    rows = left_t.shape[1] // proj_width
    high = cols // rows // 2
    own = (index_ref[0] >> 1) & 1
    for e in range(0, proj_width, 2):
        block = jnp.concatenate([grad[e], grad[e + 1]], 1)
        sums = dot(left_t[...], block)
        for sub in range(2):
            part = sums[:, sub * cols : (sub + 1) * cols].T
            for q in range(2 * high):
                slot = ((q & 1) ^ own) * high + (q >> 1)
                emit(e + sub, slot, part[q * rows : (q + 1) * rows])


def scale_columns(half, mask_t_ref, mask_own, resid_t, resid_own, cot_ref, scaled_ref, factor_ref):
    rows = cot_ref.shape[0]
    cols = scaled_ref.shape[1]
    starts = [
        pl.multiple_of((2 * q + half) * rows, rows) for q in range(cols // rows)
    ]
    mask_cols = jnp.concatenate([mask_t_ref[pl.ds(s, rows), :] for s in starts], 0)
    resid_cols = jnp.concatenate([resid_t[pl.ds(s, rows), :] for s in starts], 0)
    counted = dot(mask_cols.astype(BF16), mask_own.astype(BF16), LAST_DIMS)
    factor_t = resid_cols[:, :1] * resid_own / counted
    factor_ref[...] = factor_t.T
    bias_sum = jnp.zeros((1, cot_ref.shape[2]), F32)
    for i in range(rows):
        cot = jnp.concatenate([cot_ref[i, pl.ds(s, rows), :] for s in starts], 0)
        scaled = (cot.astype(F32) * factor_t[:, i : i + 1]).astype(BF16)
        scaled_ref[i] = scaled
        bias_sum = bias_sum + jnp.sum(scaled.astype(F32), 0, keepdims=True)
    return bias_sum


def send_kernel(
    index_ref, left_ref, mask_t_ref, resid_ref, cot_ref, w_ref,
    send_ref, far_ref, near_ref, far_factor_ref, near_factor_ref, w2_ref, b_ref, left_t_ref, grad,
    wide, resid_t,
):
    rows, cols, chan = cot_ref.shape
    proj_width = left_ref.shape[0] // rows
    index = index_ref[0]
    wide[...] = w_ref[...].astype(F32)
    for e in range(proj_width):
        w2_ref[e * proj_width : (e + 1) * proj_width, :] = wide[
            pl.ds(e, proj_width, stride=proj_width), :
        ].astype(BF16)
    left_t_ref[...] = left_ref[...].astype(F32).T.astype(BF16)
    resid_t[...] = jnp.broadcast_to(resid_ref[...].astype(F32), (LANES, cols)).T
    begin = pl.multiple_of(index * rows, rows)
    mask_own = mask_t_ref[pl.ds(begin, rows), :]
    resid_own = resid_t[pl.ds(begin, rows), :].T[:1]
    side = index & 1
    shared = (mask_t_ref, mask_own, resid_t, resid_own, cot_ref)
    far_sum = scale_columns(1 - side, *shared, far_ref, far_factor_ref)
    near_sum = scale_columns(side, *shared, near_ref, near_factor_ref)
    b_ref[...] = far_sum + near_sum
    grad_columns(w2_ref, far_ref, grad)

    def emit(e, slot, value):
        send_ref[slot, e] = value.astype(BF16)

    right_columns(index_ref, left_t_ref, grad, emit)


def keep_kernel(
    index_ref, left_t_ref, w2_ref, near_ref, far_part_ref, keep_ref, send_ref, grad, total
):
    high = keep_ref.shape[0]
    grad_columns(w2_ref, near_ref, grad)

    def emit(e, slot, value):
        total[slot, e] = value

    right_columns(index_ref, left_t_ref, grad, emit)
    keep_ref[...] = total[:high] + far_part_ref[:high].astype(F32)
    send_ref[...] = (total[high:] + far_part_ref[high:].astype(F32)).astype(BF16)


def add_kernel(keep_ref, other_ref, out_ref):
    out_ref[...] = (keep_ref[...] + other_ref[...].astype(F32)).astype(BF16)


def place_rows(index_ref, same_ref, other_ref, right):
    rows = same_ref.shape[2]
    own = (index_ref[0] >> 1) & 1
    for side, ref in ((own, same_ref), (1 - own, other_ref)):
        for k in range(ref.shape[0]):
            begin = pl.multiple_of((2 * k + side) * rows, rows)
            right[:, pl.ds(begin, rows), :] = ref[k]


def outer_columns(left_ref, right_ref, outer):
    proj_width, cols, seqs = right_ref.shape
    rows = left_ref.shape[0] // proj_width
    for e in range(0, proj_width, 2):
        pair = right_ref[e : e + 2].reshape(2 * cols, seqs)
        block = dot(left_ref[...], pair, LAST_DIMS).astype(BF16)
        for i in range(rows):
            for sub in range(2):
                outer[
                    i // 2,
                    (e + sub) * proj_width : (e + sub + 1) * proj_width,
                    (i % 2) * cols : (i % 2 + 1) * cols,
                ] = block[i * proj_width : (i + 1) * proj_width, sub * cols : (sub + 1) * cols]


def weight_columns(left_ref, right_ref, scaled_ref, w_ref, outer):
    rows, cols, chan = scaled_ref.shape
    outer_columns(left_ref, right_ref, outer)
    for p in range(rows // 2):
        w_ref[...] += dot(outer[p], scaled_ref[2 * p : 2 * p + 2].reshape(2 * cols, chan))


def left_columns(grad, right_ref, left_sum_ref):
    proj_width, cols, seqs = right_ref.shape
    for e in range(0, proj_width, 2):
        block = jnp.concatenate([grad[e], grad[e + 1]], 1)
        left_sum_ref[...] += dot(block, right_ref[e : e + 2].reshape(2 * cols, seqs))


def near_kernel(
    index_ref, left_ref, scaled_ref, grad_ref, same_ref, other_ref,
    w_sum_ref, left_sum_ref, outer_ref, right,
):
    place_rows(index_ref, same_ref, other_ref, right)
    w_sum_ref[...] = jnp.zeros_like(w_sum_ref)
    weight_columns(left_ref, right, scaled_ref, w_sum_ref, outer_ref)
    left_sum_ref[...] = jnp.zeros_like(left_sum_ref)
    left_columns(grad_ref, right, left_sum_ref)


def far_kernel(
    index_ref, left_ref, scaled_ref, grad_ref, same_ref, other_ref, w_sum_ref, near_sum_ref,
    w_send_ref, left_sum_ref, outer_ref, right, total,
):
    place_rows(index_ref, same_ref, other_ref, right)
    total[...] = w_sum_ref[...]
    weight_columns(left_ref, right, scaled_ref, total, outer_ref)
    w_send_ref[...] = total[...].astype(BF16).reshape(w_send_ref.shape)
    left_sum_ref[...] = near_sum_ref[...]
    left_columns(grad_ref, right, left_sum_ref)


def pair_kernel(
    index_ref, w2_ref, bias_ref, near_ref, far_ref, near_factor_ref, far_factor_ref, out_ref, w2_t
):
    rows = out_ref.shape[0]
    w2_t[...] = w2_ref[...].astype(F32).T.astype(BF16)
    bias = column_of(bias_ref[...])
    side = index_ref[0] & 1
    for half, outer, factor_ref in (
        (side, near_ref, near_factor_ref),
        (1 - side, far_ref, far_factor_ref),
    ):
        cols = outer.shape[2] // 2
        for p in range(rows // 2):
            projected = dot(w2_t[...], outer[p]) + bias
            for sub in range(2):
                i = 2 * p + sub
                block = projected[:, sub * cols : (sub + 1) * cols] * factor_ref[i : i + 1, :]
                block = block.T.astype(BF16)
                for q in range(cols // rows):
                    begin = pl.multiple_of((2 * q + half) * rows, rows)
                    out_ref[i, pl.ds(begin, rows), :] = block[q * rows : (q + 1) * rows]


def sums_kernel(
    index_ref, normal_ref, wl_ref, wr_ref, mask_t_ref, left_sum_ref, b_ref, right_ref, share_ref,
    grads_ref, pack_ref, right_sum, gathered,
):
    seqs = mask_t_ref.shape[1]
    high, proj_width, rows, _ = right_ref.shape
    width = wl_ref.shape[1]
    right_sum[...] = in_order([right_ref[k] for k in range(high)]).reshape(proj_width * rows, seqs)
    mask_own = mask_t_ref[pl.ds(pl.multiple_of(index_ref[0] * rows, rows), rows), :]
    fill = jnp.zeros((LANES - 2 * proj_width, seqs), F32)
    bias_cols = jnp.zeros((LANES, seqs), F32)
    for i in range(rows):
        block = jnp.concatenate(
            [
                left_sum_ref[i * proj_width : (i + 1) * proj_width, :],
                right_sum[pl.ds(i, proj_width, stride=rows), :],
                fill,
            ],
            0,
        )
        block = (block * mask_own[i : i + 1, :]).astype(BF16).astype(F32)
        bias_cols = bias_cols + block
        gathered[pl.ds(i, seqs, stride=rows), :] = block.T
    grads_ref[...] = gathered[...].astype(BF16)
    used = 2 * proj_width
    products = jnp.zeros((LANES, 2 * width), F32)
    step = 256
    for first in range(0, seqs * rows, step):
        products = products + dot(
            grads_ref[first : first + step, :], normal_ref[first : first + step, :], FIRST_DIMS
        )
    weights = jnp.concatenate([wl_ref[...], wr_ref[...]], 0).astype(F32)
    bias_sum = jnp.sum(bias_cols, 1, keepdims=True)
    gain_sum = jnp.sum(weights * products[:used, width:], 0, keepdims=True)
    shift_sum = jnp.sum(weights * bias_sum[:used], 0, keepdims=True)
    bias_row = jnp.broadcast_to(bias_sum, (LANES, LANES)).T[:1]
    pieces = [products[:used, k : k + LANES] for k in range(0, width, LANES)]
    pieces += [gain_sum[:, k : k + LANES] for k in range(0, width, LANES)]
    pieces += [shift_sum[:, k : k + LANES] for k in range(0, width, LANES)]
    pieces += [bias_row, b_ref[...]]
    pieces += [jnp.zeros((TAIL - 2 - 2 * (width // LANES), LANES), F32)]
    pieces += [in_order([share_ref[k] for k in range(high)])]
    packed = jnp.concatenate(pieces, 0).astype(BF16)
    for k in range(high):
        pack_ref[k] = packed


def norm_kernel(normal_ref, inverse_ref, gain_ref, wl_ref, wr_ref, grads_ref, out_ref, weights):
    seqs, rows, width = out_ref.shape
    proj_width = wl_ref.shape[0]
    weights[...] = jnp.zeros_like(weights)
    weights[:proj_width, :] = wl_ref[...]
    weights[proj_width : 2 * proj_width, :] = wr_ref[...]
    step = 16
    for first in range(0, seqs, step):
        span = slice(first * rows, (first + step) * rows)
        xhat = normal_ref[span, width:].astype(F32)
        g = dot(grads_ref[span, :], weights[...]) * gain_ref[...]
        result = (
            g - jnp.mean(g, -1, keepdims=True) - xhat * jnp.mean(g * xhat, -1, keepdims=True)
        ) * inverse_ref[span, :]
        out_ref[first : first + step] = result.astype(BF16).reshape(step, rows, width)


def in_order(values):
    total = values[0].astype(F32)
    for value in values[1:]:
        total = total + value.astype(F32)
    return total


def share_kernel(in_ref, out_ref):
    out_ref[...] = in_order([in_ref[k] for k in range(in_ref.shape[0])]).astype(BF16)


def merge_kernel(in_ref, out_ref, *, share):
    high, rows, _ = in_ref.shape
    head = rows - share
    total = in_order([in_ref[k, :head, :] for k in range(high)]).astype(BF16)
    for m in range(out_ref.shape[0]):
        out_ref[m, :head, :] = total
        for k in range(high):
            out_ref[m, head + k * share : head + (k + 1) * share, :] = in_ref[k, head:, :]


def unpack_kernel(
    in_ref, wl_ref, bl_ref, wr_ref, br_ref, w_out_ref, b_ref, gain_ref, shift_ref, placed
):
    count, size, _ = in_ref.shape
    proj_width, width = wl_ref.shape
    used = 2 * proj_width
    parts = width // LANES
    head = parts * used + TAIL
    total = in_order([in_ref[m, :head, :] for m in range(count)])
    tail = total[parts * used :]
    for k in range(parts):
        span = slice(k * LANES, (k + 1) * LANES)
        wl_ref[:, span] = total[k * used : k * used + proj_width]
        wr_ref[:, span] = total[k * used + proj_width : (k + 1) * used]
        gain_ref[:, span] = tail[k : k + 1]
        shift_ref[:, span] = tail[parts + k : parts + k + 1]
    bl_ref[...] = tail[2 * parts : 2 * parts + 1, :proj_width]
    br_ref[...] = tail[2 * parts : 2 * parts + 1, proj_width:used]
    b_ref[...] = tail[2 * parts + 1 : 2 * parts + 2, :]
    for m in range(count):
        placed[m * (size - head) : (m + 1) * (size - head), :] = in_ref[m, head:, :].astype(F32)
    for c in range(proj_width):
        w_out_ref[c * proj_width : (c + 1) * proj_width, :] = placed[
            pl.ds(c, proj_width, stride=proj_width), :
        ]


def body(
    devices,
    alignment_activations,
    alignment_row_mask,
    residue_mask_vector,
    layer_norm_gain,
    layer_norm_bias,
    left_weight,
    left_bias,
    right_weight,
    right_bias,
    output_weight,
    output_bias,
    pair_update_cotangent,
):
    seqs, rows, width = alignment_activations.shape
    cols = alignment_row_mask.shape[1]
    proj_width = left_weight.shape[1]
    pair_width, chan = output_weight.shape
    high = devices // 4
    half = cols // 2
    share = pair_width // devices
    flat = rows * proj_width
    index = lax.axis_index("res").astype(jnp.int32).reshape(1)
    gain = layer_norm_gain.reshape(1, width)
    shift = layer_norm_bias.reshape(1, width)
    wl, wr = left_weight.T, right_weight.T
    piece = (proj_width, rows, seqs)

    def swap(value, rel):
        return lax.ppermute(value, "res", [(d, d ^ rel) for d in range(devices)])

    def exchange(value, groups):
        return lax.all_to_all(
            value, "res", split_axis=0, concat_axis=0, axis_index_groups=groups, tiled=True
        )

    lines = [[4 * k + low for k in range(high)] for low in range(4)]
    squares = [[4 * k + low for low in range(4)] for k in range(high)]
    quarter = (high,) + piece

    left, right, mask_t, normal, inverse = call(
        project_kernel,
        (
            shape((flat, seqs), BF16),
            shape(quarter, BF16),
            shape((cols, seqs), F32),
            shape((seqs * rows, 2 * width), BF16),
            shape((seqs * rows, 1), F32),
        ),
        (index, alignment_activations, alignment_row_mask, gain, shift, wl, wr)
        + (left_bias.reshape(1, proj_width), right_bias.reshape(1, proj_width)),
        (
            pltpu.VMEM((seqs * rows, LANES), F32),
            pltpu.VMEM((flat, seqs), F32),
            pltpu.VMEM((LANES, width), BF16),
        ),
        us=4,
    )
    near_same = exchange(right, lines)
    near_other = swap(near_same, 2)
    far_same = swap(near_same, 1)
    far_other = swap(near_other, 1)

    grad_shape = shape((proj_width, flat, half), BF16)
    outer_shape = shape((rows // 2, pair_width, 2 * half), BF16)
    send, far, near, far_factor, near_factor, w2, b_part, left_t, far_grad = call(
        send_kernel,
        (
            shape((2 * high,) + piece, BF16),
            shape((rows, half, chan), BF16),
            shape((rows, half, chan), BF16),
            shape((rows, half), F32),
            shape((rows, half), F32),
            shape((pair_width, chan), BF16),
            shape((1, chan), F32),
            shape((seqs, flat), BF16),
            grad_shape,
        ),
        (
            index,
            left,
            mask_t,
            residue_mask_vector.reshape(1, cols),
            pair_update_cotangent,
            output_weight,
        ),
        (pltpu.VMEM((pair_width, chan), F32), pltpu.VMEM((cols, LANES), F32)),
        us=6,
    )
    keep, send, near_grad = call(
        keep_kernel,
        (shape(quarter, F32), shape(quarter, BF16), grad_shape),
        (index, left_t, w2, near, swap(send, 1)),
        (pltpu.VMEM((2 * high,) + piece, F32),),
        us=4,
        after=(near_same,),
    )
    right_place = pltpu.VMEM((proj_width, half, seqs), BF16)
    near_w, near_left, near_outer = call(
        near_kernel,
        (shape((pair_width, chan), F32), shape((flat, seqs), F32), outer_shape),
        (index, left, near, near_grad, near_same, near_other),
        (right_place,),
        us=7,
    )
    added = call(
        add_kernel,
        shape(quarter, BF16),
        (keep, swap(send, 2)),
        scalars=0,
        after=(near_left,),
    )
    right_parts = exchange(added, lines)
    w_send, left_sum, far_outer = call(
        far_kernel,
        (shape((4, high, share, chan), BF16), shape((flat, seqs), F32), outer_shape),
        (index, left, far, far_grad, far_same, far_other, near_w, near_left),
        (right_place, pltpu.VMEM((pair_width, chan), F32)),
        us=3,
        after=(added,),
    )
    shares = call(
        share_kernel, shape((high, share, chan), BF16), (exchange(w_send, squares),), scalars=0
    )
    pack_rows = 2 * proj_width * (width // LANES) + TAIL + share
    grads, pack = call(
        sums_kernel,
        (shape((seqs * rows, LANES), BF16), shape((high, pack_rows, LANES), BF16)),
        (index, normal, wl, wr, mask_t, left_sum, b_part, right_parts, exchange(shares, lines)),
        (pltpu.VMEM((flat, seqs), F32), pltpu.VMEM((seqs * rows, LANES), F32)),
        us=3,
    )
    alignment_gradient = call(
        norm_kernel,
        shape((seqs, rows, width), BF16),
        (normal, inverse, gain, wl, wr, grads),
        (pltpu.VMEM((LANES, width), BF16),),
        scalars=0,
        us=4,
    )
    merged = call(
        merge_kernel,
        shape((4, pack_rows + (high - 1) * share, LANES), BF16),
        (exchange(pack, lines),),
        scalars=0,
        after=(alignment_gradient,),
        share=share,
    )
    pair = call(
        pair_kernel,
        shape((rows, cols, chan), BF16),
        (index, w2, output_bias.reshape(1, chan), near_outer, far_outer, near_factor, far_factor),
        (pltpu.VMEM((chan, pair_width), BF16),),
        us=6,
        after=(merged,),
    )
    w_left, b_left, w_right, b_right, w_out_grad, b_out, gain_grad, shift_grad = call(
        unpack_kernel,
        (
            shape((proj_width, width), F32),
            shape((1, proj_width), F32),
            shape((proj_width, width), F32),
            shape((1, proj_width), F32),
            shape((pair_width, chan), F32),
            shape((1, chan), F32),
            shape((1, width), F32),
            shape((1, width), F32),
        ),
        (exchange(merged, squares),),
        (pltpu.VMEM((pair_width, chan), F32),),
        scalars=0,
        after=(pair,),
    )
    return (
        pair,
        alignment_gradient,
        w_left.T,
        b_left.reshape(-1),
        w_right.T,
        b_right.reshape(-1),
        w_out_grad,
        b_out.reshape(-1),
        gain_grad.reshape(-1),
        shift_grad.reshape(-1),
    )


def solution(mesh):
    return jax.shard_map(
        functools.partial(body, mesh.shape["res"]),
        mesh=mesh,
        in_specs=(
            P(None, ("grp", "res"), None),
            P(None, "grp"),
            P("grp"),
            P(),
            P(),
            P(),
            P(),
            P(),
            P(),
            P(),
            P(),
            P(("grp", "res"), None, None),
        ),
        out_specs=(
            P(("grp", "res"), None, None),
            P(None, ("grp", "res"), None),
            P("grp", None),
            P("grp"),
            P("grp", None),
            P("grp"),
            P("grp", None),
            P("grp"),
            P("grp"),
            P("grp"),
        ),
        check_vma=False,
    )
```

```python
import functools
import math

import jax
import jax.numpy as jnp
from jax import lax
from jax.experimental import pallas as pl
from jax.experimental.pallas import tpu as pltpu
from jax.sharding import PartitionSpec as P

EPS = 1e-05
LAST_DIMS = (((1,), (1,)), ((), ()))
FIRST_DIMS = (((0,), (0,)), ((), ()))
MIB = 1024 * 1024
LANES = 128
TAIL = 16
F32 = jnp.float32
BF16 = jnp.bfloat16


def tiled_bytes(dims, dtype):
    dims = tuple(dims)
    lanes = -(-dims[-1] // LANES) * LANES
    sublanes = -(-(dims[-2] if len(dims) > 1 else 1) // 16) * 16
    return math.prod(dims[:-2]) * sublanes * lanes * jnp.dtype(dtype).itemsize


def call(
    kernel, out_shape, args, scratch=(), scalars=1, us=1.0, after=(), fetched=(), token=False, grant=0, **static
):
    count = len(args)
    specs = [pl.BlockSpec(memory_space=pltpu.SMEM)] * scalars
    for k in range(scalars, count):
        specs.append(pl.BlockSpec(memory_space=pltpu.HBM if k in fetched else pltpu.VMEM))
    specs += [pl.BlockSpec(memory_space=pl.ANY)] * len(after)
    outs = list(out_shape) if isinstance(out_shape, (tuple, list)) else [out_shape]
    if token:
        outs.append(shape((8, LANES), F32))
    held = list(args[scalars:]) + outs + list(scratch)
    need = sum(tiled_bytes(value.shape, value.dtype) for value in held)
    places = [pltpu.VMEM(args[k].shape, args[k].dtype) for k in fetched]
    semaphores = [pltpu.SemaphoreType.DMA((len(fetched),))] if fetched else []

    def run(*refs):
        ins = list(refs[:count])
        rest = list(refs[count + len(after) :])
        if fetched:
            *rest, done = rest
            held_refs = rest[-len(fetched) :]
            rest = rest[: -len(fetched)]
            copies = [
                pltpu.make_async_copy(ins[k], ref, done.at[n])
                for n, (k, ref) in enumerate(zip(fetched, held_refs))
            ]
            for copy in copies:
                copy.start()
            for k, ref, copy in zip(fetched, held_refs, copies):
                ins[k] = Fetched(ref, copy)
        if token:
            rest.pop(len(outs) - 1)[...] = jnp.zeros((8, LANES), F32)
        kernel(*ins, *rest, **static)

    result = pl.pallas_call(
        run,
        name=kernel.__name__,
        out_shape=tuple(outs),
        in_specs=specs,
        out_specs=tuple([pl.BlockSpec(memory_space=pltpu.VMEM)] * len(outs)),
        scratch_shapes=list(scratch) + places + semaphores,
        compiler_params=pltpu.CompilerParams(vmem_limit_bytes=grant or min(need + 6 * MIB, 56 * MIB)),
        cost_estimate=pl.CostEstimate(
            flops=int(us * 1.1e9), bytes_accessed=int(us * 1e5), transcendentals=0
        ),
    )(*args, *after)
    return result if len(outs) > 1 else result[0]


class Fetched:
    def __init__(self, ref, copy):
        self.ref, self.copy, self.shape = ref, copy, ref.shape

    def __getitem__(self, index):
        if self.copy is not None:
            self.copy.wait()
            self.copy = None
        return self.ref[index]


def shape(dims, dtype):
    return jax.ShapeDtypeStruct(tuple(dims), dtype)


def dot(a, b, dims=(((1,), (0,)), ((), ()))):
    return lax.dot_general(a, b, dims, preferred_element_type=F32)


def normalize(x, gain, shift):
    centered = x - jnp.mean(x, -1, keepdims=True)
    inverse = lax.rsqrt(jnp.mean(centered * centered, -1, keepdims=True) + EPS)
    xhat = centered * inverse
    return xhat, inverse, (xhat * gain + shift).astype(BF16)


def column_of(row):
    return jnp.broadcast_to(row, (8, row.shape[1])).T[:, :1]


def project_kernel(
    index_ref, x_ref, mask_ref, gain_ref, shift_ref, wl_ref, wr_ref, bl_ref, br_ref,
    left_ref, right_ref, proj, right_rows, weights, mask_t,
):
    seqs, rows, width = x_ref.shape
    proj_width = right_ref.shape[0]
    begin = pl.multiple_of(index_ref[0] * rows, rows)
    weights[:proj_width, :] = wl_ref[...]
    weights[proj_width : 2 * proj_width, :] = wr_ref[...]
    weights[2 * proj_width :, :] = jnp.zeros((LANES - 2 * proj_width, width), BF16)
    bias_left = column_of(bl_ref[...])
    bias_right = column_of(br_ref[...])
    step = 16
    for first in range(0, seqs, step):
        x = x_ref[first : first + step].astype(F32).reshape(step * rows, width)
        normalized = normalize(x, gain_ref[...], shift_ref[...])[2]
        proj[first * rows : (first + step) * rows, :] = dot(normalized, weights[...], LAST_DIMS)
    mask_t[...] = mask_ref[...].astype(F32).T
    mask_own = mask_t[pl.ds(begin, rows), :]
    for i in range(rows):
        block = proj[pl.ds(i, seqs, stride=rows), :].T
        mask_row = mask_own[i : i + 1, :]
        span = slice(i * proj_width, (i + 1) * proj_width)
        left_ref[span, :] = ((block[:proj_width] + bias_left) * mask_row).astype(BF16)
        right_rows[span, :] = (block[proj_width : 2 * proj_width] + bias_right) * mask_row
    for e in range(proj_width):
        right_ref[e] = right_rows[pl.ds(e, rows, stride=proj_width), :].astype(BF16)


def grad_columns(w2_ref, scaled_ref, grad):
    rows, cols, chan = scaled_ref.shape
    proj_width = grad.shape[0]
    for i in range(0, rows, 2):
        pair = scaled_ref[i : i + 2].reshape(2 * cols, chan)
        block = dot(w2_ref[...], pair, LAST_DIMS).astype(BF16)
        for e in range(proj_width):
            for sub in range(2):
                grad[e, (i + sub) * proj_width : (i + sub + 1) * proj_width, :] = block[
                    e * proj_width : (e + 1) * proj_width, sub * cols : (sub + 1) * cols
                ]


def right_columns(index_ref, left_t, grad, emit):
    proj_width, _, cols = grad.shape
    rows = left_t.shape[1] // proj_width
    high = cols // rows // 2
    own = index_ref[0] >> 1
    for e in range(0, proj_width, 2):
        block = jnp.concatenate([grad[e], grad[e + 1]], 1)
        sums = dot(left_t[...], block)
        for sub in range(2):
            part = sums[:, sub * cols : (sub + 1) * cols].T
            for q in range(2 * high):
                rel = q ^ own
                emit(e + sub, (rel & 1) * high + (rel >> 1), part[q * rows : (q + 1) * rows])


def scale_columns(half, mask_t_ref, mask_own, resid_t, resid_own, cot_ref, scaled_ref, factor_ref):
    rows = cot_ref.shape[0]
    cols = scaled_ref.shape[1]
    starts = [
        pl.multiple_of((2 * q + half) * rows, rows) for q in range(cols // rows)
    ]
    mask_cols = jnp.concatenate([mask_t_ref[pl.ds(s, rows), :] for s in starts], 0)
    resid_cols = jnp.concatenate([resid_t[pl.ds(s, rows), :] for s in starts], 0)
    counted = dot(mask_cols.astype(BF16), mask_own.astype(BF16), LAST_DIMS)
    factor_t = resid_cols[:, :1] * resid_own / counted
    factor_ref[...] = factor_t.T
    bias_sum = jnp.zeros((1, cot_ref.shape[2]), F32)
    for i in range(rows):
        cot = jnp.concatenate([cot_ref[i, pl.ds(s, rows), :] for s in starts], 0)
        scaled = (cot.astype(F32) * factor_t[:, i : i + 1]).astype(BF16)
        scaled_ref[i] = scaled
        bias_sum = bias_sum + jnp.sum(scaled.astype(F32), 0, keepdims=True)
    return bias_sum


def send_kernel(
    index_ref, left_ref, mask_ref, resid_ref, cot_ref, w_ref,
    send_ref, far_ref, near_ref, far_factor_ref, near_factor_ref, w2_ref, b_ref, left_t_ref, grad,
    mask_own_ref, wide, resid_t, mask_t,
):
    rows, cols, chan = cot_ref.shape
    proj_width = left_ref.shape[0] // rows
    index = index_ref[0]
    wide[...] = w_ref[...].astype(F32)
    for e in range(proj_width):
        w2_ref[e * proj_width : (e + 1) * proj_width, :] = wide[
            pl.ds(e, proj_width, stride=proj_width), :
        ].astype(BF16)
    left_t_ref[...] = left_ref[...].astype(F32).T.astype(BF16)
    resid_t[...] = jnp.broadcast_to(resid_ref[...].astype(F32), (LANES, cols)).T
    begin = pl.multiple_of(index * rows, rows)
    mask_t[...] = mask_ref[...].astype(F32).T
    mask_own = mask_t[pl.ds(begin, rows), :]
    mask_own_ref[...] = mask_own
    resid_own = resid_t[pl.ds(begin, rows), :].T[:1]
    side = index & 1
    shared = (mask_t, mask_own, resid_t, resid_own, cot_ref)
    far_sum = scale_columns(1 - side, *shared, far_ref, far_factor_ref)
    near_sum = scale_columns(side, *shared, near_ref, near_factor_ref)
    b_ref[...] = far_sum + near_sum
    grad_columns(w2_ref, far_ref, grad)

    def emit(e, slot, value):
        send_ref[slot, e] = value.astype(BF16)

    right_columns(index_ref, left_t_ref, grad, emit)


def keep_kernel(
    index_ref, left_t_ref, w2_ref, near_ref, far_part_ref, keep_ref, send_ref, grad, total
):
    high = keep_ref.shape[0]
    grad_columns(w2_ref, near_ref, grad)

    def emit(e, slot, value):
        total[slot, e] = value

    right_columns(index_ref, left_t_ref, grad, emit)
    keep_ref[...] = total[:high] + far_part_ref[:high].astype(F32)
    send_ref[...] = (total[high:] + far_part_ref[high:].astype(F32)).astype(BF16)


def high_kernel(keep_ref, other_ref, own_ref, *send_refs):
    own_ref[...] = keep_ref[0] + other_ref[0].astype(F32)
    for k, ref in enumerate(send_refs):
        ref[...] = (keep_ref[k + 1] + other_ref[k + 1].astype(F32)).astype(BF16)


def normal_kernel(x_ref, gain_ref, shift_ref, normal_ref, inverse_ref):
    seqs, rows, width = x_ref.shape
    step = 16
    for first in range(0, seqs, step):
        x = x_ref[first : first + step].astype(F32).reshape(step * rows, width)
        xhat, inverse, normalized = normalize(x, gain_ref[...], shift_ref[...])
        span = slice(first * rows, (first + step) * rows)
        normal_ref[span, :width] = normalized
        normal_ref[span, width:] = xhat.astype(BF16)
        inverse_ref[span, :] = inverse


def line_kernel(*refs):
    *blocks, out_ref = refs
    for k, ref in enumerate(blocks):
        out_ref[k] = ref[...]


def place_kernel(index_ref, right_ref, line_ref, other_ref, line_other_ref, out_ref):
    rows = right_ref.shape[1]
    own = index_ref[0] >> 1

    def put(rel, value):
        out_ref[:, pl.ds(pl.multiple_of((own ^ rel) * rows, rows), rows), :] = value

    put(0, right_ref[...])
    put(1, other_ref[...])
    for k in range(line_ref.shape[0]):
        put(2 * k + 2, line_ref[k])
        put(2 * k + 3, line_other_ref[k])


def outer_columns(left_ref, right_ref, outer):
    proj_width, cols, seqs = right_ref.shape
    rows = left_ref.shape[0] // proj_width
    for e in range(0, proj_width, 2):
        pair = right_ref[e : e + 2].reshape(2 * cols, seqs)
        block = dot(left_ref[...], pair, LAST_DIMS).astype(BF16)
        for i in range(rows):
            for sub in range(2):
                outer[
                    i // 2,
                    (e + sub) * proj_width : (e + sub + 1) * proj_width,
                    (i % 2) * cols : (i % 2 + 1) * cols,
                ] = block[i * proj_width : (i + 1) * proj_width, sub * cols : (sub + 1) * cols]


def weight_columns(left_ref, right_ref, scaled_ref, w_ref, outer):
    rows, cols, chan = scaled_ref.shape
    outer_columns(left_ref, right_ref, outer)
    for p in range(rows // 2):
        w_ref[...] += dot(outer[p], scaled_ref[2 * p : 2 * p + 2].reshape(2 * cols, chan))


def left_columns(grad, right_ref, left_sum_ref):
    proj_width, cols, seqs = right_ref.shape
    for e in range(0, proj_width, 2):
        block = jnp.concatenate([grad[e], grad[e + 1]], 1)
        left_sum_ref[...] += dot(block, right_ref[e : e + 2].reshape(2 * cols, seqs))


def near_kernel(
    left_ref, scaled_ref, grad_ref, right_ref, w_sum_ref, left_sum_ref, outer_ref
):
    w_sum_ref[...] = jnp.zeros_like(w_sum_ref)
    weight_columns(left_ref, right_ref, scaled_ref, w_sum_ref, outer_ref)
    left_sum_ref[...] = jnp.zeros_like(left_sum_ref)
    left_columns(grad_ref, right_ref, left_sum_ref)


def far_kernel(index_ref, left_ref, scaled_ref, right_ref, w_sum_ref, outer_ref, *refs):
    *quarter_refs, total = refs
    total[...] = w_sum_ref[...]
    weight_columns(left_ref, right_ref, scaled_ref, total, outer_ref)
    quarter = quarter_refs[0].shape[0]
    for m, ref in enumerate(quarter_refs):
        begin = pl.multiple_of(((index_ref[0] & 3) ^ m) * quarter, quarter)
        ref[...] = total[pl.ds(begin, quarter), :].astype(BF16)


def left_kernel(grad_ref, right_ref, near_sum_ref, left_sum_ref):
    left_sum_ref[...] = near_sum_ref[...]
    left_columns(grad_ref, right_ref, left_sum_ref)


def pair_kernel(
    index_ref, w2_ref, bias_ref, near_ref, far_ref, near_factor_ref, far_factor_ref, out_ref, w2_t
):
    rows = out_ref.shape[0]
    w2_t[...] = w2_ref[...].astype(F32).T.astype(BF16)
    bias = column_of(bias_ref[...])
    side = index_ref[0] & 1
    for half, outer, factor_ref in (
        (side, near_ref, near_factor_ref),
        (1 - side, far_ref, far_factor_ref),
    ):
        cols = outer.shape[2] // 2
        for p in range(rows // 2):
            projected = dot(w2_t[...], outer[p]) + bias
            for sub in range(2):
                i = 2 * p + sub
                block = projected[:, sub * cols : (sub + 1) * cols] * factor_ref[i : i + 1, :]
                block = block.T.astype(BF16)
                for q in range(cols // rows):
                    begin = pl.multiple_of((2 * q + half) * rows, rows)
                    out_ref[i, pl.ds(begin, rows), :] = block[q * rows : (q + 1) * rows]


def sums_kernel(
    normal_ref, wl_ref, wr_ref, mask_own_ref, left_sum_ref, b_ref, right_own_ref, *refs
):
    *ins, grads_ref, pack_ref, right_sum, gathered = refs
    right_refs, quarter_refs = ins[:-4], ins[-4:]
    seqs = mask_own_ref.shape[1]
    proj_width, rows, _ = right_own_ref.shape
    width = wl_ref.shape[1]
    total = right_own_ref[...]
    for ref in right_refs:
        total = total + ref[...].astype(F32)
    right_sum[...] = total.reshape(proj_width * rows, seqs)
    fill = jnp.zeros((LANES - 2 * proj_width, seqs), F32)
    bias_cols = jnp.zeros((LANES, seqs), F32)
    for i in range(rows):
        block = jnp.concatenate(
            [
                left_sum_ref[i * proj_width : (i + 1) * proj_width, :],
                right_sum[pl.ds(i, proj_width, stride=rows), :],
                fill,
            ],
            0,
        )
        block = (block * mask_own_ref[i : i + 1, :]).astype(BF16).astype(F32)
        bias_cols = bias_cols + block
        gathered[pl.ds(i, seqs, stride=rows), :] = block.T
    grads_ref[...] = gathered[...].astype(BF16)
    used = 2 * proj_width
    products = jnp.zeros((LANES, 2 * width), F32)
    step = 256
    for first in range(0, seqs * rows, step):
        products = products + dot(
            grads_ref[first : first + step, :], normal_ref[first : first + step, :], FIRST_DIMS
        )
    weights = jnp.concatenate([wl_ref[...], wr_ref[...]], 0).astype(F32)
    bias_sum = jnp.sum(bias_cols, 1, keepdims=True)
    gain_sum = jnp.sum(weights * products[:used, width:], 0, keepdims=True)
    shift_sum = jnp.sum(weights * bias_sum[:used], 0, keepdims=True)
    bias_row = jnp.broadcast_to(bias_sum, (LANES, LANES)).T[:1]
    pieces = [products[:used, k : k + LANES] for k in range(0, width, LANES)]
    pieces += [gain_sum[:, k : k + LANES] for k in range(0, width, LANES)]
    pieces += [shift_sum[:, k : k + LANES] for k in range(0, width, LANES)]
    pieces += [bias_row, b_ref[...]]
    pieces += [jnp.zeros((TAIL - 2 - 2 * (width // LANES), LANES), F32)]
    pieces += [tree_sum([ref[...] for ref in quarter_refs])]
    pack_ref[...] = jnp.concatenate(pieces, 0).astype(BF16)


def norm_kernel(normal_ref, inverse_ref, gain_ref, wl_ref, wr_ref, grads_ref, out_ref, weights):
    seqs, rows, width = out_ref.shape
    proj_width = wl_ref.shape[0]
    weights[...] = jnp.zeros_like(weights)
    weights[:proj_width, :] = wl_ref[...]
    weights[proj_width : 2 * proj_width, :] = wr_ref[...]
    step = 16
    for first in range(0, seqs, step):
        span = slice(first * rows, (first + step) * rows)
        xhat = normal_ref[span, width:].astype(F32)
        g = dot(grads_ref[span, :], weights[...]) * gain_ref[...]
        result = (
            g - jnp.mean(g, -1, keepdims=True) - xhat * jnp.mean(g * xhat, -1, keepdims=True)
        ) * inverse_ref[span, :]
        out_ref[first : first + step] = result.astype(BF16).reshape(step, rows, width)


def tree_sum(values):
    values = [value.astype(F32) for value in values]
    while len(values) > 1:
        values = [a + b for a, b in zip(values[::2], values[1::2])]
    return values[0]


def merge_kernel(*refs):
    *ins, out_ref = refs
    out_ref[...] = tree_sum([ref[...] for ref in ins]).astype(BF16)


def unpack_kernel(index_ref, *refs):
    ins = refs[:4]
    wl_ref, bl_ref, wr_ref, br_ref, w_out_ref, b_ref, gain_ref, shift_ref, placed = refs[4:]
    proj_width, width = wl_ref.shape
    used = 2 * proj_width
    parts = width // LANES
    head = parts * used + TAIL
    total = tree_sum([ref[:head, :] for ref in ins])
    tail = total[parts * used :]
    for k in range(parts):
        span = slice(k * LANES, (k + 1) * LANES)
        wl_ref[:, span] = total[k * used : k * used + proj_width]
        wr_ref[:, span] = total[k * used + proj_width : (k + 1) * used]
        gain_ref[:, span] = tail[k : k + 1]
        shift_ref[:, span] = tail[parts + k : parts + k + 1]
    bl_ref[...] = tail[2 * parts : 2 * parts + 1, :proj_width]
    br_ref[...] = tail[2 * parts : 2 * parts + 1, proj_width:used]
    b_ref[...] = tail[2 * parts + 1 : 2 * parts + 2, :]
    quarter = placed.shape[0] // 4
    for m, ref in enumerate(ins):
        begin = pl.multiple_of(((index_ref[0] & 3) ^ m) * quarter, quarter)
        placed[pl.ds(begin, quarter), :] = ref[head:, :].astype(F32)
    for c in range(proj_width):
        w_out_ref[c * proj_width : (c + 1) * proj_width, :] = placed[
            pl.ds(c, proj_width, stride=proj_width), :
        ]


def body(
    devices,
    alignment_activations,
    alignment_row_mask,
    residue_mask_vector,
    layer_norm_gain,
    layer_norm_bias,
    left_weight,
    left_bias,
    right_weight,
    right_bias,
    output_weight,
    output_bias,
    pair_update_cotangent,
):
    seqs, rows, width = alignment_activations.shape
    cols = alignment_row_mask.shape[1]
    proj_width = left_weight.shape[1]
    pair_width, chan = output_weight.shape
    high = devices // 4
    half = cols // 2
    quarter = pair_width // 4
    flat = rows * proj_width
    index = lax.axis_index("res").astype(jnp.int32).reshape(1)
    gain = layer_norm_gain.reshape(1, width)
    shift = layer_norm_bias.reshape(1, width)
    wl, wr = left_weight.T, right_weight.T
    piece = (proj_width, rows, seqs)

    def swap(value, rel):
        return lax.ppermute(value, "res", [(d, d ^ rel) for d in range(devices)])

    slab = (high,) + piece
    left, right = call(
        project_kernel,
        (shape((flat, seqs), BF16), shape(piece, BF16)),
        (index, alignment_activations, alignment_row_mask, gain, shift, wl, wr)
        + (left_bias.reshape(1, proj_width), right_bias.reshape(1, proj_width)),
        (
            pltpu.VMEM((seqs * rows, LANES), F32),
            pltpu.VMEM((flat, seqs), F32),
            pltpu.VMEM((LANES, width), BF16),
            pltpu.VMEM((cols, seqs), F32),
        ),
        us=4,
        fetched=tuple(range(1, 9)),
        grant=60 * MIB,
    )
    line = tuple(swap(right, 4 * k) for k in range(1, high))
    right_other = swap(right, 2)
    grad_shape = shape((proj_width, flat, half), BF16)
    outer_shape = shape((rows // 2, pair_width, 2 * half), BF16)
    send, far, near, far_factor, near_factor, w2, b_part, left_t, far_grad, mask_own = call(
        send_kernel,
        (
            shape((2 * high,) + piece, BF16),
            shape((rows, half, chan), BF16),
            shape((rows, half, chan), BF16),
            shape((rows, half), F32),
            shape((rows, half), F32),
            shape((pair_width, chan), BF16),
            shape((1, chan), F32),
            shape((seqs, flat), BF16),
            grad_shape,
            shape((rows, seqs), F32),
        ),
        (
            index,
            left,
            alignment_row_mask,
            residue_mask_vector.reshape(1, cols),
            pair_update_cotangent,
            output_weight,
        ),
        (
            pltpu.VMEM((pair_width, chan), F32),
            pltpu.VMEM((cols, LANES), F32),
            pltpu.VMEM((cols, seqs), F32),
        ),
        us=6,
    )
    keep, send, near_grad = call(
        keep_kernel,
        (shape(slab, F32), shape(slab, BF16), grad_shape),
        (index, left_t, w2, near, swap(send, 1)),
        (pltpu.VMEM((2 * high,) + piece, F32),),
        us=4,
    )
    normal, inverse, normal_token = call(
        normal_kernel,
        (shape((seqs * rows, 2 * width), BF16), shape((seqs * rows, 1), F32)),
        (alignment_activations, gain, shift),
        scalars=0,
        us=10,
        after=(keep, right_other),
        token=True,
    )
    line = call(
        line_kernel,
        shape((high - 1,) + piece, BF16),
        line,
        scalars=0,
        us=0.1,
        after=(normal_token,),
    )
    right_own, *sends = call(
        high_kernel,
        (shape(piece, F32),) + (shape(piece, BF16),) * (high - 1),
        (keep, swap(send, 2)),
        scalars=0,
        after=(line,),
    )
    right_parts = tuple(swap(value, 4 * (k + 1)) for k, value in enumerate(sends))
    right_near = call(
        place_kernel,
        shape((proj_width, half, seqs), BF16),
        (index, right, line, right_other, swap(line, 2)),
        after=(right_own,),
    )
    right_far = swap(right_near, 1)
    near_w, near_left, near_outer = call(
        near_kernel,
        (shape((pair_width, chan), F32), shape((flat, seqs), F32), outer_shape),
        (left, near, near_grad, right_near),
        scalars=0,
        us=0.05,
    )
    far_outer, w_own, *w_sends = call(
        far_kernel,
        (outer_shape,) + (shape((quarter, chan), BF16),) * 4,
        (index, left, far, right_far, near_w),
        (pltpu.VMEM((pair_width, chan), F32),),
        us=0.02,
    )
    left_sum = call(
        left_kernel,
        shape((flat, seqs), F32),
        (far_grad, right_far, near_left),
        scalars=0,
        us=0.02,
        after=(w_own,),
    )
    pair, pair_token = call(
        pair_kernel,
        shape((rows, cols, chan), BF16),
        (index, w2, output_bias.reshape(1, chan), near_outer, far_outer, near_factor, far_factor),
        (pltpu.VMEM((chan, pair_width), BF16),),
        us=0.02,
        after=(w_own,),
        token=True,
    )
    pack_rows = 2 * proj_width * (width // LANES) + TAIL + quarter
    grads, pack = call(
        sums_kernel,
        (shape((seqs * rows, LANES), BF16), shape((pack_rows, LANES), BF16)),
        (normal, wl, wr, mask_own, left_sum, b_part, right_own)
        + right_parts
        + (w_own,)
        + tuple(swap(value, m + 1) for m, value in enumerate(w_sends)),
        (pltpu.VMEM((flat, seqs), F32), pltpu.VMEM((seqs * rows, LANES), F32)),
        scalars=0,
        us=2,
        after=(pair_token,),
    )
    alignment_gradient, norm_token = call(
        norm_kernel,
        shape((seqs, rows, width), BF16),
        (normal, inverse, gain, wl, wr, grads),
        (pltpu.VMEM((LANES, width), BF16),),
        scalars=0,
        us=2,
        token=True,
    )
    merged = call(
        merge_kernel,
        shape((pack_rows, LANES), BF16),
        (pack,) + tuple(swap(pack, 4 * k) for k in range(1, high)),
        scalars=0,
        after=(norm_token,),
    )
    w_left, b_left, w_right, b_right, w_out_grad, b_out, gain_grad, shift_grad = call(
        unpack_kernel,
        (
            shape((proj_width, width), F32),
            shape((1, proj_width), F32),
            shape((proj_width, width), F32),
            shape((1, proj_width), F32),
            shape((pair_width, chan), F32),
            shape((1, chan), F32),
            shape((1, width), F32),
            shape((1, width), F32),
        ),
        (index, merged) + tuple(swap(merged, m) for m in range(1, 4)),
        (pltpu.VMEM((pair_width, chan), F32),),
    )
    return (
        pair,
        alignment_gradient,
        w_left.T,
        b_left.reshape(-1),
        w_right.T,
        b_right.reshape(-1),
        w_out_grad,
        b_out.reshape(-1),
        gain_grad.reshape(-1),
        shift_grad.reshape(-1),
    )


def solution(mesh):
    return jax.shard_map(
        functools.partial(body, mesh.shape["res"]),
        mesh=mesh,
        in_specs=(
            P(None, ("grp", "res"), None),
            P(None, "grp"),
            P("grp"),
            P(),
            P(),
            P(),
            P(),
            P(),
            P(),
            P(),
            P(),
            P(("grp", "res"), None, None),
        ),
        out_specs=(
            P(("grp", "res"), None, None),
            P(None, ("grp", "res"), None),
            P("grp", None),
            P("grp"),
            P("grp", None),
            P("grp"),
            P("grp", None),
            P("grp"),
            P("grp"),
            P("grp"),
        ),
        check_vma=False,
    )
```

```python
import functools
import math

import jax
import jax.numpy as jnp
from jax import lax
from jax.experimental import pallas as pl
from jax.experimental.pallas import tpu as pltpu
from jax.sharding import PartitionSpec as P

EPS = 1e-05
LAST_DIMS = (((1,), (1,)), ((), ()))
FIRST_DIMS = (((0,), (0,)), ((), ()))
MIB = 1024 * 1024
LANES = 128
TAIL = 16
F32 = jnp.float32
BF16 = jnp.bfloat16


def tiled_bytes(dims, dtype):
    dims = tuple(dims)
    lanes = -(-dims[-1] // LANES) * LANES
    sublanes = -(-(dims[-2] if len(dims) > 1 else 1) // 16) * 16
    return math.prod(dims[:-2]) * sublanes * lanes * jnp.dtype(dtype).itemsize


def call(
    kernel, out_shape, args, scratch=(), scalars=1, us=1.0, after=(), fetched=(), token=False, grant=0, **static
):
    count = len(args)
    specs = [pl.BlockSpec(memory_space=pltpu.SMEM)] * scalars
    for k in range(scalars, count):
        specs.append(pl.BlockSpec(memory_space=pltpu.HBM if k in fetched else pltpu.VMEM))
    specs += [pl.BlockSpec(memory_space=pl.ANY)] * len(after)
    outs = list(out_shape) if isinstance(out_shape, (tuple, list)) else [out_shape]
    if token:
        outs.append(shape((8, LANES), F32))
    held = list(args[scalars:]) + outs + list(scratch)
    need = sum(tiled_bytes(value.shape, value.dtype) for value in held)
    places = [pltpu.VMEM(args[k].shape, args[k].dtype) for k in fetched]
    semaphores = [pltpu.SemaphoreType.DMA((len(fetched),))] if fetched else []

    def run(*refs):
        ins = list(refs[:count])
        rest = list(refs[count + len(after) :])
        if fetched:
            *rest, done = rest
            held_refs = rest[-len(fetched) :]
            rest = rest[: -len(fetched)]
            copies = [
                pltpu.make_async_copy(ins[k], ref, done.at[n])
                for n, (k, ref) in enumerate(zip(fetched, held_refs))
            ]
            for copy in copies:
                copy.start()
            for k, ref, copy in zip(fetched, held_refs, copies):
                ins[k] = Fetched(ref, copy)
        if token:
            rest.pop(len(outs) - 1)[...] = jnp.zeros((8, LANES), F32)
        kernel(*ins, *rest, **static)

    result = pl.pallas_call(
        run,
        name=kernel.__name__,
        out_shape=tuple(outs),
        in_specs=specs,
        out_specs=tuple([pl.BlockSpec(memory_space=pltpu.VMEM)] * len(outs)),
        scratch_shapes=list(scratch) + places + semaphores,
        compiler_params=pltpu.CompilerParams(vmem_limit_bytes=grant or min(need + 6 * MIB, 56 * MIB)),
        cost_estimate=pl.CostEstimate(
            flops=int(us * 1.1e9), bytes_accessed=int(us * 1e5), transcendentals=0
        ),
    )(*args, *after)
    return result if len(outs) > 1 else result[0]


class Fetched:
    def __init__(self, ref, copy):
        self.ref, self.copy, self.shape = ref, copy, ref.shape

    def __getitem__(self, index):
        if self.copy is not None:
            self.copy.wait()
            self.copy = None
        return self.ref[index]


def shape(dims, dtype):
    return jax.ShapeDtypeStruct(tuple(dims), dtype)


def dot(a, b, dims=(((1,), (0,)), ((), ()))):
    return lax.dot_general(a, b, dims, preferred_element_type=F32)


def normalize(x, gain, shift):
    centered = x - jnp.mean(x, -1, keepdims=True)
    inverse = lax.rsqrt(jnp.mean(centered * centered, -1, keepdims=True) + EPS)
    xhat = centered * inverse
    return xhat, inverse, (xhat * gain + shift).astype(BF16)


def column_of(row):
    return jnp.broadcast_to(row, (8, row.shape[1])).T[:, :1]


def project_kernel(
    index_ref, x_ref, mask_ref, gain_ref, shift_ref, wl_ref, wr_ref, bl_ref, br_ref,
    left_ref, right_ref, proj, right_rows, weights, mask_t,
):
    seqs, rows, width = x_ref.shape
    proj_width = right_ref.shape[0]
    begin = pl.multiple_of(index_ref[0] * rows, rows)
    weights[:proj_width, :] = wl_ref[...]
    weights[proj_width : 2 * proj_width, :] = wr_ref[...]
    weights[2 * proj_width :, :] = jnp.zeros((LANES - 2 * proj_width, width), BF16)
    bias_left = column_of(bl_ref[...])
    bias_right = column_of(br_ref[...])
    step = 16
    for first in range(0, seqs, step):
        x = x_ref[first : first + step].astype(F32).reshape(step * rows, width)
        normalized = normalize(x, gain_ref[...], shift_ref[...])[2]
        proj[first * rows : (first + step) * rows, :] = dot(normalized, weights[...], LAST_DIMS)
    mask_t[...] = mask_ref[...].astype(F32).T
    mask_own = mask_t[pl.ds(begin, rows), :]
    for i in range(rows):
        block = proj[pl.ds(i, seqs, stride=rows), :].T
        mask_row = mask_own[i : i + 1, :]
        span = slice(i * proj_width, (i + 1) * proj_width)
        left_ref[span, :] = ((block[:proj_width] + bias_left) * mask_row).astype(BF16)
        right_rows[span, :] = (block[proj_width : 2 * proj_width] + bias_right) * mask_row
    for e in range(proj_width):
        right_ref[e] = right_rows[pl.ds(e, rows, stride=proj_width), :].astype(BF16)


def grad_columns(w2_ref, scaled_ref, grad):
    rows, cols, chan = scaled_ref.shape
    proj_width = grad.shape[0]
    for i in range(0, rows, 2):
        pair = scaled_ref[i : i + 2].reshape(2 * cols, chan)
        block = dot(w2_ref[...], pair, LAST_DIMS).astype(BF16)
        for e in range(proj_width):
            for sub in range(2):
                grad[e, (i + sub) * proj_width : (i + sub + 1) * proj_width, :] = block[
                    e * proj_width : (e + 1) * proj_width, sub * cols : (sub + 1) * cols
                ]


def right_columns(index_ref, left_t, grad, emit):
    proj_width, _, cols = grad.shape
    rows = left_t.shape[1] // proj_width
    high = cols // rows // 2
    own = index_ref[0] >> 1
    for e in range(0, proj_width, 2):
        block = jnp.concatenate([grad[e], grad[e + 1]], 1)
        sums = dot(left_t[...], block)
        for sub in range(2):
            part = sums[:, sub * cols : (sub + 1) * cols].T
            for q in range(2 * high):
                rel = q ^ own
                emit(e + sub, (rel & 1) * high + (rel >> 1), part[q * rows : (q + 1) * rows])


def scale_columns(half, mask_t_ref, mask_own, resid_t, resid_own, cot_ref, scaled_ref, factor_ref):
    rows = cot_ref.shape[0]
    cols = scaled_ref.shape[1]
    starts = [
        pl.multiple_of((2 * q + half) * rows, rows) for q in range(cols // rows)
    ]
    mask_cols = jnp.concatenate([mask_t_ref[pl.ds(s, rows), :] for s in starts], 0)
    resid_cols = jnp.concatenate([resid_t[pl.ds(s, rows), :] for s in starts], 0)
    counted = dot(mask_cols.astype(BF16), mask_own.astype(BF16), LAST_DIMS)
    factor_t = resid_cols[:, :1] * resid_own / counted
    factor_ref[...] = factor_t.T
    bias_sum = jnp.zeros((1, cot_ref.shape[2]), F32)
    for i in range(rows):
        cot = jnp.concatenate([cot_ref[i, pl.ds(s, rows), :] for s in starts], 0)
        scaled = (cot.astype(F32) * factor_t[:, i : i + 1]).astype(BF16)
        scaled_ref[i] = scaled
        bias_sum = bias_sum + jnp.sum(scaled.astype(F32), 0, keepdims=True)
    return bias_sum


def send_kernel(
    index_ref, left_ref, mask_ref, resid_ref, cot_ref, w_ref,
    send_ref, far_ref, near_ref, far_factor_ref, near_factor_ref, w2_ref, b_ref, left_t_ref, grad,
    mask_own_ref, wide, resid_t, mask_t,
):
    rows, cols, chan = cot_ref.shape
    proj_width = left_ref.shape[0] // rows
    index = index_ref[0]
    wide[...] = w_ref[...].astype(F32)
    for e in range(proj_width):
        w2_ref[e * proj_width : (e + 1) * proj_width, :] = wide[
            pl.ds(e, proj_width, stride=proj_width), :
        ].astype(BF16)
    left_t_ref[...] = left_ref[...].astype(F32).T.astype(BF16)
    resid_t[...] = jnp.broadcast_to(resid_ref[...].astype(F32), (LANES, cols)).T
    begin = pl.multiple_of(index * rows, rows)
    mask_t[...] = mask_ref[...].astype(F32).T
    mask_own = mask_t[pl.ds(begin, rows), :]
    mask_own_ref[...] = mask_own
    resid_own = resid_t[pl.ds(begin, rows), :].T[:1]
    side = index & 1
    shared = (mask_t, mask_own, resid_t, resid_own, cot_ref)
    far_sum = scale_columns(1 - side, *shared, far_ref, far_factor_ref)
    near_sum = scale_columns(side, *shared, near_ref, near_factor_ref)
    b_ref[...] = far_sum + near_sum
    grad_columns(w2_ref, far_ref, grad)

    def emit(e, slot, value):
        send_ref[slot, e] = value.astype(BF16)

    right_columns(index_ref, left_t_ref, grad, emit)


def keep_kernel(
    index_ref, left_t_ref, w2_ref, near_ref, far_part_ref, right_ref,
    keep_ref, send_ref, grad, right_copy_ref, total,
):
    high = keep_ref.shape[0]
    right_copy_ref[...] = right_ref[...]
    grad_columns(w2_ref, near_ref, grad)

    def emit(e, slot, value):
        total[slot, e] = value

    right_columns(index_ref, left_t_ref, grad, emit)
    keep_ref[...] = total[:high] + far_part_ref[:high].astype(F32)
    send_ref[...] = (total[high:] + far_part_ref[high:].astype(F32)).astype(BF16)


def high_kernel(keep_ref, other_ref, own_ref, *send_refs):
    own_ref[...] = keep_ref[0] + other_ref[0].astype(F32)
    for k, ref in enumerate(send_refs):
        ref[...] = (keep_ref[k + 1] + other_ref[k + 1].astype(F32)).astype(BF16)


def normal_kernel(x_ref, gain_ref, shift_ref, normal_ref, inverse_ref):
    seqs, rows, width = x_ref.shape
    step = 16
    for first in range(0, seqs, step):
        x = x_ref[first : first + step].astype(F32).reshape(step * rows, width)
        xhat, inverse, normalized = normalize(x, gain_ref[...], shift_ref[...])
        span = slice(first * rows, (first + step) * rows)
        normal_ref[span, :width] = normalized
        normal_ref[span, width:] = xhat.astype(BF16)
        inverse_ref[span, :] = inverse


def line_kernel(*refs):
    *blocks, out_ref = refs
    for k, ref in enumerate(blocks):
        out_ref[k] = ref[...]


def place_kernel(
    index_ref, right_ref, other_ref, beside_ref, corner_ref, line_ref, line_other_ref, out_ref
):
    rows = right_ref.shape[1]
    own = index_ref[0] >> 1

    def put(rel, value):
        out_ref[:, pl.ds(pl.multiple_of((own ^ rel) * rows, rows), rows), :] = value

    for rel, ref in enumerate((right_ref, other_ref, beside_ref, corner_ref)):
        put(rel, ref[...])
    for k in range(line_ref.shape[0]):
        put(2 * k + 4, line_ref[k])
        put(2 * k + 5, line_other_ref[k])


def outer_columns(left_ref, right_ref, outer):
    proj_width, cols, seqs = right_ref.shape
    rows = left_ref.shape[0] // proj_width
    for e in range(0, proj_width, 2):
        pair = right_ref[e : e + 2].reshape(2 * cols, seqs)
        block = dot(left_ref[...], pair, LAST_DIMS).astype(BF16)
        for i in range(rows):
            for sub in range(2):
                outer[
                    i // 2,
                    (e + sub) * proj_width : (e + sub + 1) * proj_width,
                    (i % 2) * cols : (i % 2 + 1) * cols,
                ] = block[i * proj_width : (i + 1) * proj_width, sub * cols : (sub + 1) * cols]


def weight_columns(left_ref, right_ref, scaled_ref, w_ref, outer):
    rows, cols, chan = scaled_ref.shape
    outer_columns(left_ref, right_ref, outer)
    for p in range(rows // 2):
        w_ref[...] += dot(outer[p], scaled_ref[2 * p : 2 * p + 2].reshape(2 * cols, chan))


def left_columns(grad, right_ref, left_sum_ref):
    proj_width, cols, seqs = right_ref.shape
    for e in range(0, proj_width, 2):
        block = jnp.concatenate([grad[e], grad[e + 1]], 1)
        left_sum_ref[...] += dot(block, right_ref[e : e + 2].reshape(2 * cols, seqs))


def near_kernel(
    left_ref, scaled_ref, grad_ref, right_ref, w_sum_ref, left_sum_ref, outer_ref
):
    w_sum_ref[...] = jnp.zeros_like(w_sum_ref)
    weight_columns(left_ref, right_ref, scaled_ref, w_sum_ref, outer_ref)
    left_sum_ref[...] = jnp.zeros_like(left_sum_ref)
    left_columns(grad_ref, right_ref, left_sum_ref)


def far_kernel(index_ref, left_ref, scaled_ref, right_ref, w_sum_ref, outer_ref, *refs):
    *quarter_refs, total = refs
    total[...] = w_sum_ref[...]
    weight_columns(left_ref, right_ref, scaled_ref, total, outer_ref)
    quarter = quarter_refs[0].shape[0]
    for m, ref in enumerate(quarter_refs):
        begin = pl.multiple_of(((index_ref[0] & 3) ^ m) * quarter, quarter)
        ref[...] = total[pl.ds(begin, quarter), :].astype(BF16)


def left_kernel(grad_ref, right_ref, near_sum_ref, left_sum_ref):
    left_sum_ref[...] = near_sum_ref[...]
    left_columns(grad_ref, right_ref, left_sum_ref)


def pair_kernel(
    index_ref, w2_ref, bias_ref, near_ref, far_ref, near_factor_ref, far_factor_ref, out_ref, w2_t
):
    rows = out_ref.shape[0]
    w2_t[...] = w2_ref[...].astype(F32).T.astype(BF16)
    bias = column_of(bias_ref[...])
    side = index_ref[0] & 1
    for half, outer, factor_ref in (
        (side, near_ref, near_factor_ref),
        (1 - side, far_ref, far_factor_ref),
    ):
        cols = outer.shape[2] // 2
        for p in range(rows // 2):
            projected = dot(w2_t[...], outer[p]) + bias
            for sub in range(2):
                i = 2 * p + sub
                block = projected[:, sub * cols : (sub + 1) * cols] * factor_ref[i : i + 1, :]
                block = block.T.astype(BF16)
                for q in range(cols // rows):
                    begin = pl.multiple_of((2 * q + half) * rows, rows)
                    out_ref[i, pl.ds(begin, rows), :] = block[q * rows : (q + 1) * rows]


def sums_kernel(
    normal_ref, wl_ref, wr_ref, mask_own_ref, left_sum_ref, b_ref, right_own_ref, *refs
):
    *ins, grads_ref, pack_ref, right_sum, gathered = refs
    right_refs, quarter_refs = ins[:-4], ins[-4:]
    seqs = mask_own_ref.shape[1]
    proj_width, rows, _ = right_own_ref.shape
    width = wl_ref.shape[1]
    total = right_own_ref[...]
    for ref in right_refs:
        total = total + ref[...].astype(F32)
    right_sum[...] = total.reshape(proj_width * rows, seqs)
    fill = jnp.zeros((LANES - 2 * proj_width, seqs), F32)
    bias_cols = jnp.zeros((LANES, seqs), F32)
    for i in range(rows):
        block = jnp.concatenate(
            [
                left_sum_ref[i * proj_width : (i + 1) * proj_width, :],
                right_sum[pl.ds(i, proj_width, stride=rows), :],
                fill,
            ],
            0,
        )
        block = (block * mask_own_ref[i : i + 1, :]).astype(BF16).astype(F32)
        bias_cols = bias_cols + block
        gathered[pl.ds(i, seqs, stride=rows), :] = block.T
    grads_ref[...] = gathered[...].astype(BF16)
    used = 2 * proj_width
    products = jnp.zeros((LANES, 2 * width), F32)
    step = 256
    for first in range(0, seqs * rows, step):
        products = products + dot(
            grads_ref[first : first + step, :], normal_ref[first : first + step, :], FIRST_DIMS
        )
    weights = jnp.concatenate([wl_ref[...], wr_ref[...]], 0).astype(F32)
    bias_sum = jnp.sum(bias_cols, 1, keepdims=True)
    gain_sum = jnp.sum(weights * products[:used, width:], 0, keepdims=True)
    shift_sum = jnp.sum(weights * bias_sum[:used], 0, keepdims=True)
    bias_row = jnp.broadcast_to(bias_sum, (LANES, LANES)).T[:1]
    pieces = [products[:used, k : k + LANES] for k in range(0, width, LANES)]
    pieces += [gain_sum[:, k : k + LANES] for k in range(0, width, LANES)]
    pieces += [shift_sum[:, k : k + LANES] for k in range(0, width, LANES)]
    pieces += [bias_row, b_ref[...]]
    pieces += [jnp.zeros((TAIL - 2 - 2 * (width // LANES), LANES), F32)]
    pieces += [tree_sum([ref[...] for ref in quarter_refs])]
    pack_ref[...] = jnp.concatenate(pieces, 0).astype(BF16)


def norm_kernel(normal_ref, inverse_ref, gain_ref, wl_ref, wr_ref, grads_ref, out_ref, weights):
    seqs, rows, width = out_ref.shape
    proj_width = wl_ref.shape[0]
    weights[...] = jnp.zeros_like(weights)
    weights[:proj_width, :] = wl_ref[...]
    weights[proj_width : 2 * proj_width, :] = wr_ref[...]
    step = 16
    for first in range(0, seqs, step):
        span = slice(first * rows, (first + step) * rows)
        xhat = normal_ref[span, width:].astype(F32)
        g = dot(grads_ref[span, :], weights[...]) * gain_ref[...]
        result = (
            g - jnp.mean(g, -1, keepdims=True) - xhat * jnp.mean(g * xhat, -1, keepdims=True)
        ) * inverse_ref[span, :]
        out_ref[first : first + step] = result.astype(BF16).reshape(step, rows, width)


def tree_sum(values):
    values = [value.astype(F32) for value in values]
    while len(values) > 1:
        values = [a + b for a, b in zip(values[::2], values[1::2])]
    return values[0]


def merge_kernel(*refs):
    *ins, out_ref = refs
    out_ref[...] = tree_sum([ref[...] for ref in ins]).astype(BF16)


def unpack_kernel(index_ref, *refs):
    ins = refs[:4]
    wl_ref, bl_ref, wr_ref, br_ref, w_out_ref, b_ref, gain_ref, shift_ref, placed = refs[4:]
    proj_width, width = wl_ref.shape
    used = 2 * proj_width
    parts = width // LANES
    head = parts * used + TAIL
    total = tree_sum([ref[:head, :] for ref in ins])
    tail = total[parts * used :]
    for k in range(parts):
        span = slice(k * LANES, (k + 1) * LANES)
        wl_ref[:, span] = total[k * used : k * used + proj_width]
        wr_ref[:, span] = total[k * used + proj_width : (k + 1) * used]
        gain_ref[:, span] = tail[k : k + 1]
        shift_ref[:, span] = tail[parts + k : parts + k + 1]
    bl_ref[...] = tail[2 * parts : 2 * parts + 1, :proj_width]
    br_ref[...] = tail[2 * parts : 2 * parts + 1, proj_width:used]
    b_ref[...] = tail[2 * parts + 1 : 2 * parts + 2, :]
    quarter = placed.shape[0] // 4
    for m, ref in enumerate(ins):
        begin = pl.multiple_of(((index_ref[0] & 3) ^ m) * quarter, quarter)
        placed[pl.ds(begin, quarter), :] = ref[head:, :].astype(F32)
    for c in range(proj_width):
        w_out_ref[c * proj_width : (c + 1) * proj_width, :] = placed[
            pl.ds(c, proj_width, stride=proj_width), :
        ]


def body(
    devices,
    alignment_activations,
    alignment_row_mask,
    residue_mask_vector,
    layer_norm_gain,
    layer_norm_bias,
    left_weight,
    left_bias,
    right_weight,
    right_bias,
    output_weight,
    output_bias,
    pair_update_cotangent,
):
    seqs, rows, width = alignment_activations.shape
    cols = alignment_row_mask.shape[1]
    proj_width = left_weight.shape[1]
    pair_width, chan = output_weight.shape
    high = devices // 4
    half = cols // 2
    quarter = pair_width // 4
    flat = rows * proj_width
    index = lax.axis_index("res").astype(jnp.int32).reshape(1)
    gain = layer_norm_gain.reshape(1, width)
    shift = layer_norm_bias.reshape(1, width)
    wl, wr = left_weight.T, right_weight.T
    piece = (proj_width, rows, seqs)

    def swap(value, rel):
        return lax.ppermute(value, "res", [(d, d ^ rel) for d in range(devices)])

    slab = (high,) + piece
    left, right = call(
        project_kernel,
        (shape((flat, seqs), BF16), shape(piece, BF16)),
        (index, alignment_activations, alignment_row_mask, gain, shift, wl, wr)
        + (left_bias.reshape(1, proj_width), right_bias.reshape(1, proj_width)),
        (
            pltpu.VMEM((seqs * rows, LANES), F32),
            pltpu.VMEM((flat, seqs), F32),
            pltpu.VMEM((LANES, width), BF16),
            pltpu.VMEM((cols, seqs), F32),
        ),
        us=4,
        fetched=tuple(range(1, 9)),
        grant=60 * MIB,
    )
    other = swap(right, 2)
    corner = swap(right, 6)
    grad_shape = shape((proj_width, flat, half), BF16)
    outer_shape = shape((rows // 2, pair_width, 2 * half), BF16)
    send, far, near, far_factor, near_factor, w2, b_part, left_t, far_grad, mask_own = call(
        send_kernel,
        (
            shape((2 * high,) + piece, BF16),
            shape((rows, half, chan), BF16),
            shape((rows, half, chan), BF16),
            shape((rows, half), F32),
            shape((rows, half), F32),
            shape((pair_width, chan), BF16),
            shape((1, chan), F32),
            shape((seqs, flat), BF16),
            grad_shape,
            shape((rows, seqs), F32),
        ),
        (
            index,
            left,
            alignment_row_mask,
            residue_mask_vector.reshape(1, cols),
            pair_update_cotangent,
            output_weight,
        ),
        (
            pltpu.VMEM((pair_width, chan), F32),
            pltpu.VMEM((cols, LANES), F32),
            pltpu.VMEM((cols, seqs), F32),
        ),
        us=6,
    )
    keep, send, near_grad, right_copy = call(
        keep_kernel,
        (shape(slab, F32), shape(slab, BF16), grad_shape, shape(piece, BF16)),
        (index, left_t, w2, near, swap(send, 1), right),
        (pltpu.VMEM((2 * high,) + piece, F32),),
        us=4,
    )
    normal, inverse, normal_token = call(
        normal_kernel,
        (shape((seqs * rows, 2 * width), BF16), shape((seqs * rows, 1), F32)),
        (alignment_activations, gain, shift),
        scalars=0,
        us=10,
        after=(keep,),
        token=True,
    )
    beside = swap(right_copy, 4)
    line = tuple(swap(right_copy, 4 * k) for k in range(2, high))
    line = call(
        line_kernel,
        shape((high - 2,) + piece, BF16),
        line,
        scalars=0,
        us=0.1,
        after=(normal_token, other, corner),
    )
    right_own, *sends = call(
        high_kernel,
        (shape(piece, F32),) + (shape(piece, BF16),) * (high - 1),
        (keep, swap(send, 2)),
        scalars=0,
        after=(line,),
    )
    right_parts = tuple(swap(value, 4 * (k + 1)) for k, value in enumerate(sends))
    right_near = call(
        place_kernel,
        shape((proj_width, half, seqs), BF16),
        (index, right, other, beside, corner, line, swap(line, 2)),
        after=(right_own,),
    )
    right_far = swap(right_near, 1)
    near_w, near_left, near_outer = call(
        near_kernel,
        (shape((pair_width, chan), F32), shape((flat, seqs), F32), outer_shape),
        (left, near, near_grad, right_near),
        scalars=0,
        us=0.05,
    )
    far_outer, w_own, *w_sends = call(
        far_kernel,
        (outer_shape,) + (shape((quarter, chan), BF16),) * 4,
        (index, left, far, right_far, near_w),
        (pltpu.VMEM((pair_width, chan), F32),),
        us=0.02,
    )
    left_sum = call(
        left_kernel,
        shape((flat, seqs), F32),
        (far_grad, right_far, near_left),
        scalars=0,
        us=0.02,
        after=(w_own,) + right_parts,
    )
    pair, pair_token = call(
        pair_kernel,
        shape((rows, cols, chan), BF16),
        (index, w2, output_bias.reshape(1, chan), near_outer, far_outer, near_factor, far_factor),
        (pltpu.VMEM((chan, pair_width), BF16),),
        us=0.02,
        after=(w_own,),
        token=True,
    )
    pack_rows = 2 * proj_width * (width // LANES) + TAIL + quarter
    grads, pack = call(
        sums_kernel,
        (shape((seqs * rows, LANES), BF16), shape((pack_rows, LANES), BF16)),
        (normal, wl, wr, mask_own, left_sum, b_part, right_own)
        + right_parts
        + (w_own,)
        + tuple(swap(value, m + 1) for m, value in enumerate(w_sends)),
        (pltpu.VMEM((flat, seqs), F32), pltpu.VMEM((seqs * rows, LANES), F32)),
        scalars=0,
        us=2,
        after=(pair_token,),
    )
    alignment_gradient, norm_token = call(
        norm_kernel,
        shape((seqs, rows, width), BF16),
        (normal, inverse, gain, wl, wr, grads),
        (pltpu.VMEM((LANES, width), BF16),),
        scalars=0,
        us=2,
        token=True,
    )
    merged = call(
        merge_kernel,
        shape((pack_rows, LANES), BF16),
        (pack,) + tuple(swap(pack, 4 * k) for k in range(1, high)),
        scalars=0,
        after=(norm_token,),
    )
    w_left, b_left, w_right, b_right, w_out_grad, b_out, gain_grad, shift_grad = call(
        unpack_kernel,
        (
            shape((proj_width, width), F32),
            shape((1, proj_width), F32),
            shape((proj_width, width), F32),
            shape((1, proj_width), F32),
            shape((pair_width, chan), F32),
            shape((1, chan), F32),
            shape((1, width), F32),
            shape((1, width), F32),
        ),
        (index, merged) + tuple(swap(merged, m) for m in range(1, 4)),
        (pltpu.VMEM((pair_width, chan), F32),),
    )
    return (
        pair,
        alignment_gradient,
        w_left.T,
        b_left.reshape(-1),
        w_right.T,
        b_right.reshape(-1),
        w_out_grad,
        b_out.reshape(-1),
        gain_grad.reshape(-1),
        shift_grad.reshape(-1),
    )


def solution(mesh):
    return jax.shard_map(
        functools.partial(body, mesh.shape["res"]),
        mesh=mesh,
        in_specs=(
            P(None, ("grp", "res"), None),
            P(None, "grp"),
            P("grp"),
            P(),
            P(),
            P(),
            P(),
            P(),
            P(),
            P(),
            P(),
            P(("grp", "res"), None, None),
        ),
        out_specs=(
            P(("grp", "res"), None, None),
            P(None, ("grp", "res"), None),
            P("grp", None),
            P("grp"),
            P("grp", None),
            P("grp"),
            P("grp", None),
            P("grp"),
            P("grp"),
            P("grp"),
        ),
        check_vma=False,
    )
```

```python
import functools
import math

import jax
import jax.numpy as jnp
from jax import lax
from jax.experimental import pallas as pl
from jax.experimental.pallas import tpu as pltpu
from jax.sharding import PartitionSpec as P

EPS = 1e-05
LAST_DIMS = (((1,), (1,)), ((), ()))
FIRST_DIMS = (((0,), (0,)), ((), ()))
MIB = 1024 * 1024
LANES = 128
TAIL = 16
F32 = jnp.float32
BF16 = jnp.bfloat16


def tiled_bytes(dims, dtype):
    dims = tuple(dims)
    lanes = -(-dims[-1] // LANES) * LANES
    sublanes = -(-(dims[-2] if len(dims) > 1 else 1) // 16) * 16
    return math.prod(dims[:-2]) * sublanes * lanes * jnp.dtype(dtype).itemsize


def call(
    kernel, out_shape, args, scratch=(), scalars=1, us=1.0, after=(), fetched=(), token=False, grant=0, **static
):
    count = len(args)
    specs = [pl.BlockSpec(memory_space=pltpu.SMEM)] * scalars
    for k in range(scalars, count):
        specs.append(pl.BlockSpec(memory_space=pltpu.HBM if k in fetched else pltpu.VMEM))
    specs += [pl.BlockSpec(memory_space=pl.ANY)] * len(after)
    outs = list(out_shape) if isinstance(out_shape, (tuple, list)) else [out_shape]
    if token:
        outs.append(shape((8, LANES), F32))
    held = list(args[scalars:]) + outs + list(scratch)
    need = sum(tiled_bytes(value.shape, value.dtype) for value in held)
    places = [pltpu.VMEM(args[k].shape, args[k].dtype) for k in fetched]
    semaphores = [pltpu.SemaphoreType.DMA((len(fetched),))] if fetched else []

    def run(*refs):
        ins = list(refs[:count])
        rest = list(refs[count + len(after) :])
        if fetched:
            *rest, done = rest
            held_refs = rest[-len(fetched) :]
            rest = rest[: -len(fetched)]
            copies = [
                pltpu.make_async_copy(ins[k], ref, done.at[n])
                for n, (k, ref) in enumerate(zip(fetched, held_refs))
            ]
            for copy in copies:
                copy.start()
            for k, ref, copy in zip(fetched, held_refs, copies):
                ins[k] = Fetched(ref, copy)
        if token:
            rest.pop(len(outs) - 1)[...] = jnp.zeros((8, LANES), F32)
        kernel(*ins, *rest, **static)

    result = pl.pallas_call(
        run,
        name=kernel.__name__,
        out_shape=tuple(outs),
        in_specs=specs,
        out_specs=tuple([pl.BlockSpec(memory_space=pltpu.VMEM)] * len(outs)),
        scratch_shapes=list(scratch) + places + semaphores,
        compiler_params=pltpu.CompilerParams(vmem_limit_bytes=grant or min(need + 6 * MIB, 56 * MIB)),
        cost_estimate=pl.CostEstimate(
            flops=int(us * 1.1e9), bytes_accessed=int(us * 1e5), transcendentals=0
        ),
    )(*args, *after)
    return result if len(outs) > 1 else result[0]


class Fetched:
    def __init__(self, ref, copy):
        self.ref, self.copy, self.shape = ref, copy, ref.shape

    def __getitem__(self, index):
        if self.copy is not None:
            self.copy.wait()
            self.copy = None
        return self.ref[index]


def shape(dims, dtype):
    return jax.ShapeDtypeStruct(tuple(dims), dtype)


def dot(a, b, dims=(((1,), (0,)), ((), ()))):
    return lax.dot_general(a, b, dims, preferred_element_type=F32)


def normalize(x, gain, shift):
    centered = x - jnp.mean(x, -1, keepdims=True)
    inverse = lax.rsqrt(jnp.mean(centered * centered, -1, keepdims=True) + EPS)
    xhat = centered * inverse
    return xhat, inverse, (xhat * gain + shift).astype(BF16)


def column_of(row):
    return jnp.broadcast_to(row, (8, row.shape[1])).T[:, :1]


def project_kernel(
    index_ref, x_ref, mask_ref, gain_ref, shift_ref, wl_ref, wr_ref, bl_ref, br_ref,
    left_ref, right_ref, proj, right_rows, weights, mask_t,
):
    seqs, rows, width = x_ref.shape
    proj_width = right_ref.shape[0]
    begin = pl.multiple_of(index_ref[0] * rows, rows)
    weights[:proj_width, :] = wl_ref[...]
    weights[proj_width : 2 * proj_width, :] = wr_ref[...]
    weights[2 * proj_width :, :] = jnp.zeros((LANES - 2 * proj_width, width), BF16)
    bias_left = column_of(bl_ref[...])
    bias_right = column_of(br_ref[...])
    step = 16
    for first in range(0, seqs, step):
        x = x_ref[first : first + step].astype(F32).reshape(step * rows, width)
        normalized = normalize(x, gain_ref[...], shift_ref[...])[2]
        proj[first * rows : (first + step) * rows, :] = dot(normalized, weights[...], LAST_DIMS)
    mask_t[...] = mask_ref[...].astype(F32).T
    mask_own = mask_t[pl.ds(begin, rows), :]
    for i in range(rows):
        block = proj[pl.ds(i, seqs, stride=rows), :].T
        mask_row = mask_own[i : i + 1, :]
        span = slice(i * proj_width, (i + 1) * proj_width)
        left_ref[span, :] = ((block[:proj_width] + bias_left) * mask_row).astype(BF16)
        right_rows[span, :] = (block[proj_width : 2 * proj_width] + bias_right) * mask_row
    for e in range(proj_width):
        right_ref[e] = right_rows[pl.ds(e, rows, stride=proj_width), :].astype(BF16)


def grad_columns(w2_ref, scaled_ref, grad):
    rows, cols, chan = scaled_ref.shape
    proj_width = grad.shape[0]
    for i in range(0, rows, 2):
        pair = scaled_ref[i : i + 2].reshape(2 * cols, chan)
        block = dot(w2_ref[...], pair, LAST_DIMS).astype(BF16)
        for e in range(proj_width):
            for sub in range(2):
                grad[e, (i + sub) * proj_width : (i + sub + 1) * proj_width, :] = block[
                    e * proj_width : (e + 1) * proj_width, sub * cols : (sub + 1) * cols
                ]


def right_columns(index_ref, left_t, grad, emit):
    proj_width, _, cols = grad.shape
    rows = left_t.shape[1] // proj_width
    high = cols // rows // 2
    own = index_ref[0] >> 1
    for e in range(0, proj_width, 2):
        block = jnp.concatenate([grad[e], grad[e + 1]], 1)
        sums = dot(left_t[...], block)
        for sub in range(2):
            part = sums[:, sub * cols : (sub + 1) * cols].T
            for q in range(2 * high):
                rel = q ^ own
                emit(e + sub, (rel & 1) * high + (rel >> 1), part[q * rows : (q + 1) * rows])


def scale_columns(half, mask_t_ref, mask_own, resid_t, resid_own, cot_ref, scaled_ref, factor_ref):
    rows = cot_ref.shape[0]
    cols = scaled_ref.shape[1]
    starts = [
        pl.multiple_of((2 * q + half) * rows, rows) for q in range(cols // rows)
    ]
    mask_cols = jnp.concatenate([mask_t_ref[pl.ds(s, rows), :] for s in starts], 0)
    resid_cols = jnp.concatenate([resid_t[pl.ds(s, rows), :] for s in starts], 0)
    counted = dot(mask_cols.astype(BF16), mask_own.astype(BF16), LAST_DIMS)
    factor_t = resid_cols[:, :1] * resid_own / counted
    factor_ref[...] = factor_t.T
    bias_sum = jnp.zeros((1, cot_ref.shape[2]), F32)
    for i in range(rows):
        cot = jnp.concatenate([cot_ref[i, pl.ds(s, rows), :] for s in starts], 0)
        scaled = (cot.astype(F32) * factor_t[:, i : i + 1]).astype(BF16)
        scaled_ref[i] = scaled
        bias_sum = bias_sum + jnp.sum(scaled.astype(F32), 0, keepdims=True)
    return bias_sum


def send_kernel(
    index_ref, left_ref, mask_ref, resid_ref, cot_ref, w_ref,
    send_ref, far_ref, near_ref, far_factor_ref, near_factor_ref, w2_ref, b_ref, left_t_ref, grad,
    mask_own_ref, wide, resid_t, mask_t,
):
    rows, cols, chan = cot_ref.shape
    proj_width = left_ref.shape[0] // rows
    index = index_ref[0]
    wide[...] = w_ref[...].astype(F32)
    for e in range(proj_width):
        w2_ref[e * proj_width : (e + 1) * proj_width, :] = wide[
            pl.ds(e, proj_width, stride=proj_width), :
        ].astype(BF16)
    left_t_ref[...] = left_ref[...].astype(F32).T.astype(BF16)
    resid_t[...] = jnp.broadcast_to(resid_ref[...].astype(F32), (LANES, cols)).T
    begin = pl.multiple_of(index * rows, rows)
    mask_t[...] = mask_ref[...].astype(F32).T
    mask_own = mask_t[pl.ds(begin, rows), :]
    mask_own_ref[...] = mask_own
    resid_own = resid_t[pl.ds(begin, rows), :].T[:1]
    side = index & 1
    shared = (mask_t, mask_own, resid_t, resid_own, cot_ref)
    far_sum = scale_columns(1 - side, *shared, far_ref, far_factor_ref)
    near_sum = scale_columns(side, *shared, near_ref, near_factor_ref)
    b_ref[...] = far_sum + near_sum
    grad_columns(w2_ref, far_ref, grad)

    def emit(e, slot, value):
        send_ref[slot, e] = value.astype(BF16)

    right_columns(index_ref, left_t_ref, grad, emit)


def keep_kernel(
    index_ref, left_t_ref, w2_ref, near_ref, far_part_ref, keep_ref, send_ref, grad, total
):
    high = keep_ref.shape[0]
    grad_columns(w2_ref, near_ref, grad)

    def emit(e, slot, value):
        total[slot, e] = value

    right_columns(index_ref, left_t_ref, grad, emit)
    keep_ref[...] = total[:high] + far_part_ref[:high].astype(F32)
    send_ref[...] = (total[high:] + far_part_ref[high:].astype(F32)).astype(BF16)


def high_kernel(keep_ref, other_ref, own_ref, *send_refs):
    own_ref[...] = keep_ref[0] + other_ref[0].astype(F32)
    for k, ref in enumerate(send_refs):
        ref[...] = (keep_ref[k + 1] + other_ref[k + 1].astype(F32)).astype(BF16)


def normal_kernel(
    x_ref, gain_ref, shift_ref, right_ref, other_ref,
    normal_ref, inverse_ref, right_copy_ref, other_copy_ref,
):
    seqs, rows, width = x_ref.shape
    right_copy_ref[...] = right_ref[...]
    other_copy_ref[...] = other_ref[...]
    step = 16
    for first in range(0, seqs, step):
        x = x_ref[first : first + step].astype(F32).reshape(step * rows, width)
        xhat, inverse, normalized = normalize(x, gain_ref[...], shift_ref[...])
        span = slice(first * rows, (first + step) * rows)
        normal_ref[span, :width] = normalized
        normal_ref[span, width:] = xhat.astype(BF16)
        inverse_ref[span, :] = inverse


def line_kernel(*refs):
    count = len(refs) // 2
    for k in range(count):
        refs[count + k][...] = refs[k][...]
    refs[-1][...] = jnp.zeros_like(refs[-1])


def place_kernel(index_ref, *refs):
    *blocks, out_ref = refs
    rows = blocks[0].shape[1]
    own = index_ref[0] >> 1
    for rel, ref in enumerate(blocks):
        out_ref[:, pl.ds(pl.multiple_of((own ^ rel) * rows, rows), rows), :] = ref[...]


def outer_columns(left_ref, right_ref, outer):
    proj_width, cols, seqs = right_ref.shape
    rows = left_ref.shape[0] // proj_width
    for e in range(0, proj_width, 2):
        pair = right_ref[e : e + 2].reshape(2 * cols, seqs)
        block = dot(left_ref[...], pair, LAST_DIMS).astype(BF16)
        for i in range(rows):
            for sub in range(2):
                outer[
                    i // 2,
                    (e + sub) * proj_width : (e + sub + 1) * proj_width,
                    (i % 2) * cols : (i % 2 + 1) * cols,
                ] = block[i * proj_width : (i + 1) * proj_width, sub * cols : (sub + 1) * cols]


def weight_columns(left_ref, right_ref, scaled_ref, w_ref, outer):
    rows, cols, chan = scaled_ref.shape
    outer_columns(left_ref, right_ref, outer)
    for p in range(rows // 2):
        w_ref[...] += dot(outer[p], scaled_ref[2 * p : 2 * p + 2].reshape(2 * cols, chan))


def left_columns(grad, right_ref, left_sum_ref):
    proj_width, cols, seqs = right_ref.shape
    for e in range(0, proj_width, 2):
        block = jnp.concatenate([grad[e], grad[e + 1]], 1)
        left_sum_ref[...] += dot(block, right_ref[e : e + 2].reshape(2 * cols, seqs))


def near_kernel(
    left_ref, scaled_ref, grad_ref, right_ref, w_sum_ref, left_sum_ref, outer_ref
):
    w_sum_ref[...] = jnp.zeros_like(w_sum_ref)
    weight_columns(left_ref, right_ref, scaled_ref, w_sum_ref, outer_ref)
    left_sum_ref[...] = jnp.zeros_like(left_sum_ref)
    left_columns(grad_ref, right_ref, left_sum_ref)


def far_kernel(index_ref, left_ref, scaled_ref, right_ref, w_sum_ref, outer_ref, *refs):
    *quarter_refs, total = refs
    total[...] = w_sum_ref[...]
    weight_columns(left_ref, right_ref, scaled_ref, total, outer_ref)
    quarter = quarter_refs[0].shape[0]
    for m, ref in enumerate(quarter_refs):
        begin = pl.multiple_of(((index_ref[0] & 3) ^ m) * quarter, quarter)
        ref[...] = total[pl.ds(begin, quarter), :].astype(BF16)


def left_kernel(grad_ref, right_ref, near_sum_ref, left_sum_ref):
    left_sum_ref[...] = near_sum_ref[...]
    left_columns(grad_ref, right_ref, left_sum_ref)


def pair_kernel(
    index_ref, w2_ref, bias_ref, near_ref, far_ref, near_factor_ref, far_factor_ref, out_ref, w2_t
):
    rows = out_ref.shape[0]
    w2_t[...] = w2_ref[...].astype(F32).T.astype(BF16)
    bias = column_of(bias_ref[...])
    side = index_ref[0] & 1
    for half, outer, factor_ref in (
        (side, near_ref, near_factor_ref),
        (1 - side, far_ref, far_factor_ref),
    ):
        cols = outer.shape[2] // 2
        for p in range(rows // 2):
            projected = dot(w2_t[...], outer[p]) + bias
            for sub in range(2):
                i = 2 * p + sub
                block = projected[:, sub * cols : (sub + 1) * cols] * factor_ref[i : i + 1, :]
                block = block.T.astype(BF16)
                for q in range(cols // rows):
                    begin = pl.multiple_of((2 * q + half) * rows, rows)
                    out_ref[i, pl.ds(begin, rows), :] = block[q * rows : (q + 1) * rows]


def sums_kernel(
    normal_ref, wl_ref, wr_ref, mask_own_ref, left_sum_ref, b_ref, right_own_ref, *refs
):
    *ins, grads_ref, pack_ref, right_sum, gathered = refs
    right_refs, quarter_refs = ins[:-4], ins[-4:]
    seqs = mask_own_ref.shape[1]
    proj_width, rows, _ = right_own_ref.shape
    width = wl_ref.shape[1]
    total = right_own_ref[...]
    for ref in right_refs:
        total = total + ref[...].astype(F32)
    right_sum[...] = total.reshape(proj_width * rows, seqs)
    fill = jnp.zeros((LANES - 2 * proj_width, seqs), F32)
    bias_cols = jnp.zeros((LANES, seqs), F32)
    for i in range(rows):
        block = jnp.concatenate(
            [
                left_sum_ref[i * proj_width : (i + 1) * proj_width, :],
                right_sum[pl.ds(i, proj_width, stride=rows), :],
                fill,
            ],
            0,
        )
        block = (block * mask_own_ref[i : i + 1, :]).astype(BF16).astype(F32)
        bias_cols = bias_cols + block
        gathered[pl.ds(i, seqs, stride=rows), :] = block.T
    grads_ref[...] = gathered[...].astype(BF16)
    used = 2 * proj_width
    products = jnp.zeros((LANES, 2 * width), F32)
    step = 256
    for first in range(0, seqs * rows, step):
        products = products + dot(
            grads_ref[first : first + step, :], normal_ref[first : first + step, :], FIRST_DIMS
        )
    weights = jnp.concatenate([wl_ref[...], wr_ref[...]], 0).astype(F32)
    bias_sum = jnp.sum(bias_cols, 1, keepdims=True)
    gain_sum = jnp.sum(weights * products[:used, width:], 0, keepdims=True)
    shift_sum = jnp.sum(weights * bias_sum[:used], 0, keepdims=True)
    bias_row = jnp.broadcast_to(bias_sum, (LANES, LANES)).T[:1]
    pieces = [products[:used, k : k + LANES] for k in range(0, width, LANES)]
    pieces += [gain_sum[:, k : k + LANES] for k in range(0, width, LANES)]
    pieces += [shift_sum[:, k : k + LANES] for k in range(0, width, LANES)]
    pieces += [bias_row, b_ref[...]]
    pieces += [jnp.zeros((TAIL - 2 - 2 * (width // LANES), LANES), F32)]
    pieces += [tree_sum([ref[...] for ref in quarter_refs])]
    pack_ref[...] = jnp.concatenate(pieces, 0).astype(BF16)


def norm_kernel(normal_ref, inverse_ref, gain_ref, wl_ref, wr_ref, grads_ref, out_ref, weights):
    seqs, rows, width = out_ref.shape
    proj_width = wl_ref.shape[0]
    weights[...] = jnp.zeros_like(weights)
    weights[:proj_width, :] = wl_ref[...]
    weights[proj_width : 2 * proj_width, :] = wr_ref[...]
    step = 16
    for first in range(0, seqs, step):
        span = slice(first * rows, (first + step) * rows)
        xhat = normal_ref[span, width:].astype(F32)
        g = dot(grads_ref[span, :], weights[...]) * gain_ref[...]
        result = (
            g - jnp.mean(g, -1, keepdims=True) - xhat * jnp.mean(g * xhat, -1, keepdims=True)
        ) * inverse_ref[span, :]
        out_ref[first : first + step] = result.astype(BF16).reshape(step, rows, width)


def tree_sum(values):
    values = [value.astype(F32) for value in values]
    while len(values) > 1:
        values = [a + b for a, b in zip(values[::2], values[1::2])]
    return values[0]


def merge_kernel(*refs):
    *ins, out_ref = refs
    out_ref[...] = tree_sum([ref[...] for ref in ins]).astype(BF16)


def unpack_kernel(index_ref, *refs):
    ins = refs[:4]
    wl_ref, bl_ref, wr_ref, br_ref, w_out_ref, b_ref, gain_ref, shift_ref, placed = refs[4:]
    proj_width, width = wl_ref.shape
    used = 2 * proj_width
    parts = width // LANES
    head = parts * used + TAIL
    total = tree_sum([ref[:head, :] for ref in ins])
    tail = total[parts * used :]
    for k in range(parts):
        span = slice(k * LANES, (k + 1) * LANES)
        wl_ref[:, span] = total[k * used : k * used + proj_width]
        wr_ref[:, span] = total[k * used + proj_width : (k + 1) * used]
        gain_ref[:, span] = tail[k : k + 1]
        shift_ref[:, span] = tail[parts + k : parts + k + 1]
    bl_ref[...] = tail[2 * parts : 2 * parts + 1, :proj_width]
    br_ref[...] = tail[2 * parts : 2 * parts + 1, proj_width:used]
    b_ref[...] = tail[2 * parts + 1 : 2 * parts + 2, :]
    quarter = placed.shape[0] // 4
    for m, ref in enumerate(ins):
        begin = pl.multiple_of(((index_ref[0] & 3) ^ m) * quarter, quarter)
        placed[pl.ds(begin, quarter), :] = ref[head:, :].astype(F32)
    for c in range(proj_width):
        w_out_ref[c * proj_width : (c + 1) * proj_width, :] = placed[
            pl.ds(c, proj_width, stride=proj_width), :
        ]


def body(
    devices,
    alignment_activations,
    alignment_row_mask,
    residue_mask_vector,
    layer_norm_gain,
    layer_norm_bias,
    left_weight,
    left_bias,
    right_weight,
    right_bias,
    output_weight,
    output_bias,
    pair_update_cotangent,
):
    seqs, rows, width = alignment_activations.shape
    cols = alignment_row_mask.shape[1]
    proj_width = left_weight.shape[1]
    pair_width, chan = output_weight.shape
    high = devices // 4
    half = cols // 2
    quarter = pair_width // 4
    flat = rows * proj_width
    index = lax.axis_index("res").astype(jnp.int32).reshape(1)
    gain = layer_norm_gain.reshape(1, width)
    shift = layer_norm_bias.reshape(1, width)
    wl, wr = left_weight.T, right_weight.T
    piece = (proj_width, rows, seqs)

    def swap(value, rel):
        return lax.ppermute(value, "res", [(d, d ^ rel) for d in range(devices)])

    slab = (high,) + piece
    left, right = call(
        project_kernel,
        (shape((flat, seqs), BF16), shape(piece, BF16)),
        (index, alignment_activations, alignment_row_mask, gain, shift, wl, wr)
        + (left_bias.reshape(1, proj_width), right_bias.reshape(1, proj_width)),
        (
            pltpu.VMEM((seqs * rows, LANES), F32),
            pltpu.VMEM((flat, seqs), F32),
            pltpu.VMEM((LANES, width), BF16),
            pltpu.VMEM((cols, seqs), F32),
        ),
        us=4,
        fetched=tuple(range(1, 9)),
        grant=60 * MIB,
    )
    blocks = {0: right, 2: swap(right, 2)}
    for k in range(2, high):
        blocks[4 * k] = swap(right, 4 * k)
    grad_shape = shape((proj_width, flat, half), BF16)
    outer_shape = shape((rows // 2, pair_width, 2 * half), BF16)
    send, far, near, far_factor, near_factor, w2, b_part, left_t, far_grad, mask_own = call(
        send_kernel,
        (
            shape((2 * high,) + piece, BF16),
            shape((rows, half, chan), BF16),
            shape((rows, half, chan), BF16),
            shape((rows, half), F32),
            shape((rows, half), F32),
            shape((pair_width, chan), BF16),
            shape((1, chan), F32),
            shape((seqs, flat), BF16),
            grad_shape,
            shape((rows, seqs), F32),
        ),
        (
            index,
            left,
            alignment_row_mask,
            residue_mask_vector.reshape(1, cols),
            pair_update_cotangent,
            output_weight,
        ),
        (
            pltpu.VMEM((pair_width, chan), F32),
            pltpu.VMEM((cols, LANES), F32),
            pltpu.VMEM((cols, seqs), F32),
        ),
        us=6,
    )
    keep, send, near_grad = call(
        keep_kernel,
        (shape(slab, F32), shape(slab, BF16), grad_shape),
        (index, left_t, w2, near, swap(send, 1)),
        (pltpu.VMEM((2 * high,) + piece, F32),),
        us=4,
    )
    normal, inverse, right_copy, other_copy, normal_token = call(
        normal_kernel,
        (shape((seqs * rows, 2 * width), BF16), shape((seqs * rows, 1), F32))
        + (shape(piece, BF16),) * 2,
        (alignment_activations, gain, shift, right, blocks[2]),
        scalars=0,
        us=10,
        after=(keep,),
        token=True,
    )
    blocks[4] = swap(right_copy, 4)
    blocks[6] = swap(other_copy, 4)
    blocks[10] = swap(other_copy, 8)
    line = call(
        line_kernel,
        (shape(piece, BF16),) * (high - 3) + (shape((8, LANES), F32),),
        tuple(blocks[4 * k] for k in range(3, high)),
        scalars=0,
        us=10,
        after=(normal_token, blocks[8]),
    )
    for k in range(3, high):
        blocks[4 * k + 2] = swap(line[k - 3], 2)
    right_own, *sends = call(
        high_kernel,
        (shape(piece, F32),) + (shape(piece, BF16),) * (high - 1),
        (keep, swap(send, 2)),
        scalars=0,
        us=0.1,
        after=(line[-1],),
    )
    right_parts = tuple(swap(value, 4 * (k + 1)) for k, value in enumerate(sends))
    right_near = call(
        place_kernel,
        shape((proj_width, half, seqs), BF16),
        (index,) + tuple(blocks[rel] for rel in range(0, devices, 2)),
        after=(right_own,),
    )
    right_far = swap(right_near, 1)
    near_w, near_left, near_outer = call(
        near_kernel,
        (shape((pair_width, chan), F32), shape((flat, seqs), F32), outer_shape),
        (left, near, near_grad, right_near),
        scalars=0,
        us=0.05,
    )
    far_outer, w_own, *w_sends = call(
        far_kernel,
        (outer_shape,) + (shape((quarter, chan), BF16),) * 4,
        (index, left, far, right_far, near_w),
        (pltpu.VMEM((pair_width, chan), F32),),
        us=0.02,
    )
    left_sum = call(
        left_kernel,
        shape((flat, seqs), F32),
        (far_grad, right_far, near_left),
        scalars=0,
        us=0.02,
        after=(w_own,) + right_parts,
    )
    pack_rows = 2 * proj_width * (width // LANES) + TAIL + quarter
    grads, pack = call(
        sums_kernel,
        (shape((seqs * rows, LANES), BF16), shape((pack_rows, LANES), BF16)),
        (normal, wl, wr, mask_own, left_sum, b_part, right_own)
        + right_parts
        + (w_own,)
        + tuple(swap(value, m + 1) for m, value in enumerate(w_sends)),
        (pltpu.VMEM((flat, seqs), F32), pltpu.VMEM((seqs * rows, LANES), F32)),
        scalars=0,
        us=2,
    )
    alignment_gradient, norm_token = call(
        norm_kernel,
        shape((seqs, rows, width), BF16),
        (normal, inverse, gain, wl, wr, grads),
        (pltpu.VMEM((LANES, width), BF16),),
        scalars=0,
        us=2,
        token=True,
    )
    pair, pair_token = call(
        pair_kernel,
        shape((rows, cols, chan), BF16),
        (index, w2, output_bias.reshape(1, chan), near_outer, far_outer, near_factor, far_factor),
        (pltpu.VMEM((chan, pair_width), BF16),),
        us=0.02,
        after=(norm_token,),
        token=True,
    )
    merged = call(
        merge_kernel,
        shape((pack_rows, LANES), BF16),
        (pack,) + tuple(swap(pack, 4 * k) for k in range(1, high)),
        scalars=0,
        after=(pair_token,),
    )
    w_left, b_left, w_right, b_right, w_out_grad, b_out, gain_grad, shift_grad = call(
        unpack_kernel,
        (
            shape((proj_width, width), F32),
            shape((1, proj_width), F32),
            shape((proj_width, width), F32),
            shape((1, proj_width), F32),
            shape((pair_width, chan), F32),
            shape((1, chan), F32),
            shape((1, width), F32),
            shape((1, width), F32),
        ),
        (index, merged) + tuple(swap(merged, m) for m in range(1, 4)),
        (pltpu.VMEM((pair_width, chan), F32),),
    )
    return (
        pair,
        alignment_gradient,
        w_left.T,
        b_left.reshape(-1),
        w_right.T,
        b_right.reshape(-1),
        w_out_grad,
        b_out.reshape(-1),
        gain_grad.reshape(-1),
        shift_grad.reshape(-1),
    )


def solution(mesh):
    return jax.shard_map(
        functools.partial(body, mesh.shape["res"]),
        mesh=mesh,
        in_specs=(
            P(None, ("grp", "res"), None),
            P(None, "grp"),
            P("grp"),
            P(),
            P(),
            P(),
            P(),
            P(),
            P(),
            P(),
            P(),
            P(("grp", "res"), None, None),
        ),
        out_specs=(
            P(("grp", "res"), None, None),
            P(None, ("grp", "res"), None),
            P("grp", None),
            P("grp"),
            P("grp", None),
            P("grp"),
            P("grp", None),
            P("grp"),
            P("grp"),
            P("grp"),
        ),
        check_vma=False,
    )
```

```python
import functools
import math

import jax
import jax.numpy as jnp
from jax import lax
from jax.experimental import pallas as pl
from jax.experimental.pallas import tpu as pltpu
from jax.sharding import PartitionSpec as P

EPS = 1e-05
LAST_DIMS = (((1,), (1,)), ((), ()))
FIRST_DIMS = (((0,), (0,)), ((), ()))
MIB = 1024 * 1024
LANES = 128
TAIL = 16
F32 = jnp.float32
BF16 = jnp.bfloat16


def tiled_bytes(dims, dtype):
    dims = tuple(dims)
    lanes = -(-dims[-1] // LANES) * LANES
    sublanes = -(-(dims[-2] if len(dims) > 1 else 1) // 16) * 16
    return math.prod(dims[:-2]) * sublanes * lanes * jnp.dtype(dtype).itemsize


def call(
    kernel, out_shape, args, scratch=(), scalars=1, us=1.0, after=(), fetched=(), token=False, grant=0, **static
):
    count = len(args)
    specs = [pl.BlockSpec(memory_space=pl.ANY)] * len(after)
    specs += [pl.BlockSpec(memory_space=pltpu.SMEM)] * scalars
    for k in range(scalars, count):
        specs.append(pl.BlockSpec(memory_space=pltpu.HBM if k in fetched else pltpu.VMEM))
    outs = list(out_shape) if isinstance(out_shape, (tuple, list)) else [out_shape]
    if token:
        outs.append(shape((8, LANES), F32))
    held = list(args[scalars:]) + outs + list(scratch)
    need = sum(tiled_bytes(value.shape, value.dtype) for value in held)
    places = [pltpu.VMEM(args[k].shape, args[k].dtype) for k in fetched]
    semaphores = [pltpu.SemaphoreType.DMA((len(fetched),))] if fetched else []

    def run(*refs):
        ins = list(refs[len(after) : len(after) + count])
        rest = list(refs[len(after) + count :])
        if fetched:
            *rest, done = rest
            held_refs = rest[-len(fetched) :]
            rest = rest[: -len(fetched)]
            copies = [
                pltpu.make_async_copy(ins[k], ref, done.at[n])
                for n, (k, ref) in enumerate(zip(fetched, held_refs))
            ]
            for copy in copies:
                copy.start()
            for k, ref, copy in zip(fetched, held_refs, copies):
                ins[k] = Fetched(ref, copy)
        if token:
            rest.pop(len(outs) - 1)[...] = jnp.zeros((8, LANES), F32)
        kernel(*ins, *rest, **static)

    result = pl.pallas_call(
        run,
        name=kernel.__name__,
        out_shape=tuple(outs),
        in_specs=specs,
        out_specs=tuple([pl.BlockSpec(memory_space=pltpu.VMEM)] * len(outs)),
        scratch_shapes=list(scratch) + places + semaphores,
        compiler_params=pltpu.CompilerParams(vmem_limit_bytes=grant or min(need + 6 * MIB, 56 * MIB)),
        cost_estimate=pl.CostEstimate(
            flops=int(us * 1.1e9), bytes_accessed=int(us * 1e5), transcendentals=0
        ),
    )(*after, *args)
    return result if len(outs) > 1 else result[0]


class Fetched:
    def __init__(self, ref, copy):
        self.ref, self.copy, self.shape = ref, copy, ref.shape

    def __getitem__(self, index):
        if self.copy is not None:
            self.copy.wait()
            self.copy = None
        return self.ref[index]


def shape(dims, dtype):
    return jax.ShapeDtypeStruct(tuple(dims), dtype)


def dot(a, b, dims=(((1,), (0,)), ((), ()))):
    return lax.dot_general(a, b, dims, preferred_element_type=F32)


def normalize(x, gain, shift):
    centered = x - jnp.mean(x, -1, keepdims=True)
    inverse = lax.rsqrt(jnp.mean(centered * centered, -1, keepdims=True) + EPS)
    xhat = centered * inverse
    return xhat, inverse, (xhat * gain + shift).astype(BF16)


def column_of(row):
    return jnp.broadcast_to(row, (8, row.shape[1])).T[:, :1]


def project_kernel(
    index_ref, x_ref, mask_ref, gain_ref, shift_ref, wl_ref, wr_ref, bl_ref, br_ref,
    left_ref, right_ref, proj, right_rows, weights, mask_t,
):
    seqs, rows, width = x_ref.shape
    proj_width = right_ref.shape[0]
    begin = pl.multiple_of(index_ref[0] * rows, rows)
    weights[:proj_width, :] = wl_ref[...]
    weights[proj_width : 2 * proj_width, :] = wr_ref[...]
    weights[2 * proj_width :, :] = jnp.zeros((LANES - 2 * proj_width, width), BF16)
    bias_left = column_of(bl_ref[...])
    bias_right = column_of(br_ref[...])
    step = 16
    for first in range(0, seqs, step):
        x = x_ref[first : first + step].astype(F32).reshape(step * rows, width)
        normalized = normalize(x, gain_ref[...], shift_ref[...])[2]
        proj[first * rows : (first + step) * rows, :] = dot(normalized, weights[...], LAST_DIMS)
    mask_t[...] = mask_ref[...].astype(F32).T
    mask_own = mask_t[pl.ds(begin, rows), :]
    for i in range(rows):
        block = proj[pl.ds(i, seqs, stride=rows), :].T
        mask_row = mask_own[i : i + 1, :]
        span = slice(i * proj_width, (i + 1) * proj_width)
        left_ref[span, :] = ((block[:proj_width] + bias_left) * mask_row).astype(BF16)
        right_rows[span, :] = (block[proj_width : 2 * proj_width] + bias_right) * mask_row
    for e in range(proj_width):
        right_ref[e] = right_rows[pl.ds(e, rows, stride=proj_width), :].astype(BF16)


def grad_columns(w2_ref, scaled_ref, grad):
    rows, cols, chan = scaled_ref.shape
    proj_width = grad.shape[0]
    for i in range(0, rows, 2):
        pair = scaled_ref[i : i + 2].reshape(2 * cols, chan)
        block = dot(w2_ref[...], pair, LAST_DIMS).astype(BF16)
        for e in range(proj_width):
            for sub in range(2):
                grad[e, (i + sub) * proj_width : (i + sub + 1) * proj_width, :] = block[
                    e * proj_width : (e + 1) * proj_width, sub * cols : (sub + 1) * cols
                ]


def right_columns(index_ref, left_t, grad, emit):
    proj_width, _, cols = grad.shape
    rows = left_t.shape[1] // proj_width
    high = cols // rows // 2
    own = index_ref[0] >> 1
    for e in range(0, proj_width, 2):
        block = jnp.concatenate([grad[e], grad[e + 1]], 1)
        sums = dot(left_t[...], block)
        for sub in range(2):
            part = sums[:, sub * cols : (sub + 1) * cols].T
            for q in range(2 * high):
                rel = q ^ own
                emit(e + sub, (rel & 1) * high + (rel >> 1), part[q * rows : (q + 1) * rows])


def scale_columns(half, mask_t_ref, mask_own, resid_t, resid_own, cot_ref, scaled_ref, factor_ref):
    rows = cot_ref.shape[0]
    cols = scaled_ref.shape[1]
    starts = [
        pl.multiple_of((2 * q + half) * rows, rows) for q in range(cols // rows)
    ]
    mask_cols = jnp.concatenate([mask_t_ref[pl.ds(s, rows), :] for s in starts], 0)
    resid_cols = jnp.concatenate([resid_t[pl.ds(s, rows), :] for s in starts], 0)
    counted = dot(mask_cols.astype(BF16), mask_own.astype(BF16), LAST_DIMS)
    factor_t = resid_cols[:, :1] * resid_own / counted
    factor_ref[...] = factor_t.T
    bias_sum = jnp.zeros((1, cot_ref.shape[2]), F32)
    for i in range(rows):
        cot = jnp.concatenate([cot_ref[i, pl.ds(s, rows), :] for s in starts], 0)
        scaled = (cot.astype(F32) * factor_t[:, i : i + 1]).astype(BF16)
        scaled_ref[i] = scaled
        bias_sum = bias_sum + jnp.sum(scaled.astype(F32), 0, keepdims=True)
    return bias_sum


def send_kernel(
    index_ref, left_ref, mask_ref, resid_ref, cot_ref, w_ref,
    send_ref, far_ref, near_ref, far_factor_ref, near_factor_ref, w2_ref, b_ref, left_t_ref, grad,
    mask_own_ref, wide, resid_t, mask_t,
):
    rows, cols, chan = cot_ref.shape
    proj_width = left_ref.shape[0] // rows
    index = index_ref[0]
    wide[...] = w_ref[...].astype(F32)
    for e in range(proj_width):
        w2_ref[e * proj_width : (e + 1) * proj_width, :] = wide[
            pl.ds(e, proj_width, stride=proj_width), :
        ].astype(BF16)
    left_t_ref[...] = left_ref[...].astype(F32).T.astype(BF16)
    resid_t[...] = jnp.broadcast_to(resid_ref[...].astype(F32), (LANES, cols)).T
    begin = pl.multiple_of(index * rows, rows)
    mask_t[...] = mask_ref[...].astype(F32).T
    mask_own = mask_t[pl.ds(begin, rows), :]
    mask_own_ref[...] = mask_own
    resid_own = resid_t[pl.ds(begin, rows), :].T[:1]
    side = index & 1
    shared = (mask_t, mask_own, resid_t, resid_own, cot_ref)
    far_sum = scale_columns(1 - side, *shared, far_ref, far_factor_ref)
    near_sum = scale_columns(side, *shared, near_ref, near_factor_ref)
    b_ref[...] = far_sum + near_sum
    grad_columns(w2_ref, far_ref, grad)

    def emit(e, slot, value):
        send_ref[slot, e] = value.astype(BF16)

    right_columns(index_ref, left_t_ref, grad, emit)


def keep_kernel(
    index_ref, left_t_ref, w2_ref, near_ref, far_part_ref, keep_ref, send_ref, grad, total
):
    high = keep_ref.shape[0]
    grad_columns(w2_ref, near_ref, grad)

    def emit(e, slot, value):
        total[slot, e] = value

    right_columns(index_ref, left_t_ref, grad, emit)
    keep_ref[...] = total[:high] + far_part_ref[:high].astype(F32)
    send_ref[...] = (total[high:] + far_part_ref[high:].astype(F32)).astype(BF16)


def high_kernel(keep_ref, other_ref, own_ref, *send_refs):
    own_ref[...] = keep_ref[0] + other_ref[0].astype(F32)
    for k, ref in enumerate(send_refs):
        ref[...] = (keep_ref[k + 1] + other_ref[k + 1].astype(F32)).astype(BF16)


def normal_kernel(
    x_ref, gain_ref, shift_ref, right_ref, other_ref,
    normal_ref, inverse_ref, right_copy_ref, other_copy_ref,
):
    seqs, rows, width = x_ref.shape
    right_copy_ref[...] = right_ref[...]
    other_copy_ref[...] = other_ref[...]
    step = 16
    for first in range(0, seqs, step):
        x = x_ref[first : first + step].astype(F32).reshape(step * rows, width)
        xhat, inverse, normalized = normalize(x, gain_ref[...], shift_ref[...])
        span = slice(first * rows, (first + step) * rows)
        normal_ref[span, :width] = normalized
        normal_ref[span, width:] = xhat.astype(BF16)
        inverse_ref[span, :] = inverse


def line_kernel(*refs):
    count = len(refs) // 2
    for k in range(count):
        refs[count + k][...] = refs[k][...]
    refs[-1][...] = jnp.zeros_like(refs[-1])


def place_kernel(index_ref, *refs):
    *blocks, out_ref = refs
    rows = blocks[0].shape[1]
    own = index_ref[0] >> 1
    for rel, ref in enumerate(blocks):
        out_ref[:, pl.ds(pl.multiple_of((own ^ rel) * rows, rows), rows), :] = ref[...]


def outer_columns(left_ref, right_ref, outer):
    proj_width, cols, seqs = right_ref.shape
    rows = left_ref.shape[0] // proj_width
    for e in range(0, proj_width, 2):
        pair = right_ref[e : e + 2].reshape(2 * cols, seqs)
        block = dot(left_ref[...], pair, LAST_DIMS).astype(BF16)
        for i in range(rows):
            for sub in range(2):
                outer[
                    i // 2,
                    (e + sub) * proj_width : (e + sub + 1) * proj_width,
                    (i % 2) * cols : (i % 2 + 1) * cols,
                ] = block[i * proj_width : (i + 1) * proj_width, sub * cols : (sub + 1) * cols]


def weight_columns(left_ref, right_ref, scaled_ref, w_ref, outer):
    rows, cols, chan = scaled_ref.shape
    outer_columns(left_ref, right_ref, outer)
    for p in range(rows // 2):
        w_ref[...] += dot(outer[p], scaled_ref[2 * p : 2 * p + 2].reshape(2 * cols, chan))


def left_columns(grad, right_ref, left_sum_ref):
    proj_width, cols, seqs = right_ref.shape
    for e in range(0, proj_width, 2):
        block = jnp.concatenate([grad[e], grad[e + 1]], 1)
        left_sum_ref[...] += dot(block, right_ref[e : e + 2].reshape(2 * cols, seqs))


def near_kernel(
    left_ref, scaled_ref, grad_ref, right_ref, w_sum_ref, left_sum_ref, outer_ref
):
    w_sum_ref[...] = jnp.zeros_like(w_sum_ref)
    weight_columns(left_ref, right_ref, scaled_ref, w_sum_ref, outer_ref)
    left_sum_ref[...] = jnp.zeros_like(left_sum_ref)
    left_columns(grad_ref, right_ref, left_sum_ref)


def far_kernel(index_ref, left_ref, scaled_ref, right_ref, w_sum_ref, outer_ref, *refs):
    *quarter_refs, total = refs
    total[...] = w_sum_ref[...]
    weight_columns(left_ref, right_ref, scaled_ref, total, outer_ref)
    quarter = quarter_refs[0].shape[0]
    for m, ref in enumerate(quarter_refs):
        begin = pl.multiple_of(((index_ref[0] & 3) ^ m) * quarter, quarter)
        ref[...] = total[pl.ds(begin, quarter), :].astype(BF16)


def left_kernel(grad_ref, right_ref, near_sum_ref, left_sum_ref):
    left_sum_ref[...] = near_sum_ref[...]
    left_columns(grad_ref, right_ref, left_sum_ref)


def pair_kernel(
    index_ref, w2_ref, bias_ref, near_ref, far_ref, near_factor_ref, far_factor_ref, out_ref, w2_t
):
    rows = out_ref.shape[0]
    w2_t[...] = w2_ref[...].astype(F32).T.astype(BF16)
    bias = column_of(bias_ref[...])
    side = index_ref[0] & 1
    for half, outer, factor_ref in (
        (side, near_ref, near_factor_ref),
        (1 - side, far_ref, far_factor_ref),
    ):
        cols = outer.shape[2] // 2
        for p in range(rows // 2):
            projected = dot(w2_t[...], outer[p]) + bias
            for sub in range(2):
                i = 2 * p + sub
                block = projected[:, sub * cols : (sub + 1) * cols] * factor_ref[i : i + 1, :]
                block = block.T.astype(BF16)
                for q in range(cols // rows):
                    begin = pl.multiple_of((2 * q + half) * rows, rows)
                    out_ref[i, pl.ds(begin, rows), :] = block[q * rows : (q + 1) * rows]


def sums_kernel(
    right_own_ref, *refs
):
    *ins, grads_ref, pack_ref, right_sum, gathered = refs
    right_refs, quarter_refs = ins[:-10], ins[-4:]
    normal_ref, wl_ref, wr_ref, mask_own_ref, left_sum_ref, b_ref = ins[-10:-4]
    seqs = mask_own_ref.shape[1]
    proj_width, rows, _ = right_own_ref.shape
    width = wl_ref.shape[1]
    total = right_own_ref[...]
    for ref in right_refs:
        total = total + ref[...].astype(F32)
    right_sum[...] = total.reshape(proj_width * rows, seqs)
    fill = jnp.zeros((LANES - 2 * proj_width, seqs), F32)
    bias_cols = jnp.zeros((LANES, seqs), F32)
    for i in range(rows):
        block = jnp.concatenate(
            [
                left_sum_ref[i * proj_width : (i + 1) * proj_width, :],
                right_sum[pl.ds(i, proj_width, stride=rows), :],
                fill,
            ],
            0,
        )
        block = (block * mask_own_ref[i : i + 1, :]).astype(BF16).astype(F32)
        bias_cols = bias_cols + block
        gathered[pl.ds(i, seqs, stride=rows), :] = block.T
    grads_ref[...] = gathered[...].astype(BF16)
    used = 2 * proj_width
    products = jnp.zeros((LANES, 2 * width), F32)
    step = 256
    for first in range(0, seqs * rows, step):
        products = products + dot(
            grads_ref[first : first + step, :], normal_ref[first : first + step, :], FIRST_DIMS
        )
    weights = jnp.concatenate([wl_ref[...], wr_ref[...]], 0).astype(F32)
    bias_sum = jnp.sum(bias_cols, 1, keepdims=True)
    gain_sum = jnp.sum(weights * products[:used, width:], 0, keepdims=True)
    shift_sum = jnp.sum(weights * bias_sum[:used], 0, keepdims=True)
    bias_row = jnp.broadcast_to(bias_sum, (LANES, LANES)).T[:1]
    pieces = [products[:used, k : k + LANES] for k in range(0, width, LANES)]
    pieces += [gain_sum[:, k : k + LANES] for k in range(0, width, LANES)]
    pieces += [shift_sum[:, k : k + LANES] for k in range(0, width, LANES)]
    pieces += [bias_row, b_ref[...]]
    pieces += [jnp.zeros((TAIL - 2 - 2 * (width // LANES), LANES), F32)]
    pieces += [tree_sum([ref[...] for ref in quarter_refs])]
    pack_ref[...] = jnp.concatenate(pieces, 0).astype(BF16)


def norm_kernel(normal_ref, inverse_ref, gain_ref, wl_ref, wr_ref, grads_ref, out_ref, weights):
    seqs, rows, width = out_ref.shape
    proj_width = wl_ref.shape[0]
    weights[...] = jnp.zeros_like(weights)
    weights[:proj_width, :] = wl_ref[...]
    weights[proj_width : 2 * proj_width, :] = wr_ref[...]
    step = 16
    for first in range(0, seqs, step):
        span = slice(first * rows, (first + step) * rows)
        xhat = normal_ref[span, width:].astype(F32)
        g = dot(grads_ref[span, :], weights[...]) * gain_ref[...]
        result = (
            g - jnp.mean(g, -1, keepdims=True) - xhat * jnp.mean(g * xhat, -1, keepdims=True)
        ) * inverse_ref[span, :]
        out_ref[first : first + step] = result.astype(BF16).reshape(step, rows, width)


def tree_sum(values):
    values = [value.astype(F32) for value in values]
    while len(values) > 1:
        values = [a + b for a, b in zip(values[::2], values[1::2])]
    return values[0]


def merge_kernel(*refs):
    *ins, out_ref = refs
    out_ref[...] = tree_sum([ref[...] for ref in ins]).astype(BF16)


def unpack_kernel(index_ref, *refs):
    ins = refs[:4]
    wl_ref, bl_ref, wr_ref, br_ref, w_out_ref, b_ref, gain_ref, shift_ref, placed = refs[4:]
    proj_width, width = wl_ref.shape
    used = 2 * proj_width
    parts = width // LANES
    head = parts * used + TAIL
    total = tree_sum([ref[:head, :] for ref in ins])
    tail = total[parts * used :]
    for k in range(parts):
        span = slice(k * LANES, (k + 1) * LANES)
        wl_ref[:, span] = total[k * used : k * used + proj_width]
        wr_ref[:, span] = total[k * used + proj_width : (k + 1) * used]
        gain_ref[:, span] = tail[k : k + 1]
        shift_ref[:, span] = tail[parts + k : parts + k + 1]
    bl_ref[...] = tail[2 * parts : 2 * parts + 1, :proj_width]
    br_ref[...] = tail[2 * parts : 2 * parts + 1, proj_width:used]
    b_ref[...] = tail[2 * parts + 1 : 2 * parts + 2, :]
    quarter = placed.shape[0] // 4
    for m, ref in enumerate(ins):
        begin = pl.multiple_of(((index_ref[0] & 3) ^ m) * quarter, quarter)
        placed[pl.ds(begin, quarter), :] = ref[head:, :].astype(F32)
    for c in range(proj_width):
        w_out_ref[c * proj_width : (c + 1) * proj_width, :] = placed[
            pl.ds(c, proj_width, stride=proj_width), :
        ]


def body(
    devices,
    alignment_activations,
    alignment_row_mask,
    residue_mask_vector,
    layer_norm_gain,
    layer_norm_bias,
    left_weight,
    left_bias,
    right_weight,
    right_bias,
    output_weight,
    output_bias,
    pair_update_cotangent,
):
    seqs, rows, width = alignment_activations.shape
    cols = alignment_row_mask.shape[1]
    proj_width = left_weight.shape[1]
    pair_width, chan = output_weight.shape
    high = devices // 4
    half = cols // 2
    quarter = pair_width // 4
    flat = rows * proj_width
    index = lax.axis_index("res").astype(jnp.int32).reshape(1)
    gain = layer_norm_gain.reshape(1, width)
    shift = layer_norm_bias.reshape(1, width)
    wl, wr = left_weight.T, right_weight.T
    piece = (proj_width, rows, seqs)

    def swap(value, rel):
        return lax.ppermute(value, "res", [(d, d ^ rel) for d in range(devices)])

    slab = (high,) + piece
    left, right = call(
        project_kernel,
        (shape((flat, seqs), BF16), shape(piece, BF16)),
        (index, alignment_activations, alignment_row_mask, gain, shift, wl, wr)
        + (left_bias.reshape(1, proj_width), right_bias.reshape(1, proj_width)),
        (
            pltpu.VMEM((seqs * rows, LANES), F32),
            pltpu.VMEM((flat, seqs), F32),
            pltpu.VMEM((LANES, width), BF16),
            pltpu.VMEM((cols, seqs), F32),
        ),
        us=4,
        fetched=tuple(range(1, 9)),
        grant=60 * MIB,
    )
    blocks = {0: right, 2: swap(right, 2)}
    for k in range(2, high):
        blocks[4 * k] = swap(right, 4 * k)
    grad_shape = shape((proj_width, flat, half), BF16)
    outer_shape = shape((rows // 2, pair_width, 2 * half), BF16)
    send, far, near, far_factor, near_factor, w2, b_part, left_t, far_grad, mask_own = call(
        send_kernel,
        (
            shape((2 * high,) + piece, BF16),
            shape((rows, half, chan), BF16),
            shape((rows, half, chan), BF16),
            shape((rows, half), F32),
            shape((rows, half), F32),
            shape((pair_width, chan), BF16),
            shape((1, chan), F32),
            shape((seqs, flat), BF16),
            grad_shape,
            shape((rows, seqs), F32),
        ),
        (
            index,
            left,
            alignment_row_mask,
            residue_mask_vector.reshape(1, cols),
            pair_update_cotangent,
            output_weight,
        ),
        (
            pltpu.VMEM((pair_width, chan), F32),
            pltpu.VMEM((cols, LANES), F32),
            pltpu.VMEM((cols, seqs), F32),
        ),
        us=6,
    )
    keep, send, near_grad = call(
        keep_kernel,
        (shape(slab, F32), shape(slab, BF16), grad_shape),
        (index, left_t, w2, near, swap(send, 1)),
        (pltpu.VMEM((2 * high,) + piece, F32),),
        us=4,
    )
    normal, inverse, right_copy, other_copy, normal_token = call(
        normal_kernel,
        (shape((seqs * rows, 2 * width), BF16), shape((seqs * rows, 1), F32))
        + (shape(piece, BF16),) * 2,
        (alignment_activations, gain, shift, right, blocks[2]),
        scalars=0,
        us=10,
        after=(keep,),
        token=True,
    )
    blocks[4] = swap(right_copy, 4)
    blocks[6] = swap(other_copy, 4)
    blocks[10] = swap(other_copy, 8)
    line = call(
        line_kernel,
        (shape(piece, BF16),) * (high - 3) + (shape((8, LANES), F32),),
        tuple(blocks[4 * k] for k in range(3, high)),
        scalars=0,
        us=0.1,
        after=(normal_token, blocks[8], blocks[4]),
    )
    for k in range(3, high):
        blocks[4 * k + 2] = swap(line[k - 3], 2)
    right_own, *sends = call(
        high_kernel,
        (shape(piece, F32),) + (shape(piece, BF16),) * (high - 1),
        (keep, swap(send, 2)),
        scalars=0,
        us=10,
        after=(line[-1],),
    )
    right_parts = tuple(swap(value, 4 * (k + 1)) for k, value in enumerate(sends))
    right_near = call(
        place_kernel,
        shape((proj_width, half, seqs), BF16),
        (index,) + tuple(blocks[rel] for rel in range(0, devices, 2)),
        after=(right_own,),
    )
    right_far = swap(right_near, 1)
    near_w, near_left, near_outer = call(
        near_kernel,
        (shape((pair_width, chan), F32), shape((flat, seqs), F32), outer_shape),
        (left, near, near_grad, right_near),
        scalars=0,
        us=0.05,
    )
    far_outer, w_own, *w_sends = call(
        far_kernel,
        (outer_shape,) + (shape((quarter, chan), BF16),) * 4,
        (index, left, far, right_far, near_w),
        (pltpu.VMEM((pair_width, chan), F32),),
        us=0.02,
    )
    left_sum = call(
        left_kernel,
        shape((flat, seqs), F32),
        (far_grad, right_far, near_left),
        scalars=0,
        us=0.02,
        after=(w_own,) + right_parts,
    )
    pack_rows = 2 * proj_width * (width // LANES) + TAIL + quarter
    grads, pack = call(
        sums_kernel,
        (shape((seqs * rows, LANES), BF16), shape((pack_rows, LANES), BF16)),
        (right_own,)
        + right_parts
        + (normal, wl, wr, mask_own, left_sum, b_part, w_own)
        + tuple(swap(value, m + 1) for m, value in enumerate(w_sends)),
        (pltpu.VMEM((flat, seqs), F32), pltpu.VMEM((seqs * rows, LANES), F32)),
        scalars=0,
        us=2,
    )
    alignment_gradient, norm_token = call(
        norm_kernel,
        shape((seqs, rows, width), BF16),
        (normal, inverse, gain, wl, wr, grads),
        (pltpu.VMEM((LANES, width), BF16),),
        scalars=0,
        us=2,
        token=True,
    )
    pair, pair_token = call(
        pair_kernel,
        shape((rows, cols, chan), BF16),
        (index, w2, output_bias.reshape(1, chan), near_outer, far_outer, near_factor, far_factor),
        (pltpu.VMEM((chan, pair_width), BF16),),
        us=0.02,
        after=(norm_token,),
        token=True,
    )
    merged = call(
        merge_kernel,
        shape((pack_rows, LANES), BF16),
        (pack,) + tuple(swap(pack, 4 * k) for k in range(1, high)),
        scalars=0,
        after=(pair_token,),
    )
    w_left, b_left, w_right, b_right, w_out_grad, b_out, gain_grad, shift_grad = call(
        unpack_kernel,
        (
            shape((proj_width, width), F32),
            shape((1, proj_width), F32),
            shape((proj_width, width), F32),
            shape((1, proj_width), F32),
            shape((pair_width, chan), F32),
            shape((1, chan), F32),
            shape((1, width), F32),
            shape((1, width), F32),
        ),
        (index, merged) + tuple(swap(merged, m) for m in range(1, 4)),
        (pltpu.VMEM((pair_width, chan), F32),),
    )
    return (
        pair,
        alignment_gradient,
        w_left.T,
        b_left.reshape(-1),
        w_right.T,
        b_right.reshape(-1),
        w_out_grad,
        b_out.reshape(-1),
        gain_grad.reshape(-1),
        shift_grad.reshape(-1),
    )


def solution(mesh):
    return jax.shard_map(
        functools.partial(body, mesh.shape["res"]),
        mesh=mesh,
        in_specs=(
            P(None, ("grp", "res"), None),
            P(None, "grp"),
            P("grp"),
            P(),
            P(),
            P(),
            P(),
            P(),
            P(),
            P(),
            P(),
            P(("grp", "res"), None, None),
        ),
        out_specs=(
            P(("grp", "res"), None, None),
            P(None, ("grp", "res"), None),
            P("grp", None),
            P("grp"),
            P("grp", None),
            P("grp"),
            P("grp", None),
            P("grp"),
            P("grp"),
            P("grp"),
        ),
        check_vma=False,
    )
```

```python
import functools
import math

import jax
import jax.numpy as jnp
from jax import lax
from jax.experimental import pallas as pl
from jax.experimental.pallas import tpu as pltpu
from jax.sharding import PartitionSpec as P

EPS = 1e-05
LAST_DIMS = (((1,), (1,)), ((), ()))
FIRST_DIMS = (((0,), (0,)), ((), ()))
MIB = 1024 * 1024
LANES = 128
TAIL = 16
F32 = jnp.float32
BF16 = jnp.bfloat16


def tiled_bytes(dims, dtype):
    dims = tuple(dims)
    lanes = -(-dims[-1] // LANES) * LANES
    sublanes = -(-(dims[-2] if len(dims) > 1 else 1) // 16) * 16
    return math.prod(dims[:-2]) * sublanes * lanes * jnp.dtype(dtype).itemsize


def call(
    kernel, out_shape, args, scratch=(), scalars=1, us=1.0, after=(), fetched=(), token=False, grant=0, **static
):
    count = len(args)
    specs = [pl.BlockSpec(memory_space=pl.ANY)] * len(after)
    specs += [pl.BlockSpec(memory_space=pltpu.SMEM)] * scalars
    for k in range(scalars, count):
        specs.append(pl.BlockSpec(memory_space=pltpu.HBM if k in fetched else pltpu.VMEM))
    outs = list(out_shape) if isinstance(out_shape, (tuple, list)) else [out_shape]
    if token:
        outs.append(shape((8, LANES), F32))
    held = list(args[scalars:]) + outs + list(scratch)
    need = sum(tiled_bytes(value.shape, value.dtype) for value in held)
    places = [pltpu.VMEM(args[k].shape, args[k].dtype) for k in fetched]
    semaphores = [pltpu.SemaphoreType.DMA((len(fetched),))] if fetched else []

    def run(*refs):
        ins = list(refs[len(after) : len(after) + count])
        rest = list(refs[len(after) + count :])
        if fetched:
            *rest, done = rest
            held_refs = rest[-len(fetched) :]
            rest = rest[: -len(fetched)]
            copies = [
                pltpu.make_async_copy(ins[k], ref, done.at[n])
                for n, (k, ref) in enumerate(zip(fetched, held_refs))
            ]
            for copy in copies:
                copy.start()
            for k, ref, copy in zip(fetched, held_refs, copies):
                ins[k] = Fetched(ref, copy)
        if token:
            rest.pop(len(outs) - 1)[...] = jnp.zeros((8, LANES), F32)
        kernel(*ins, *rest, **static)

    result = pl.pallas_call(
        run,
        name=kernel.__name__,
        out_shape=tuple(outs),
        in_specs=specs,
        out_specs=tuple([pl.BlockSpec(memory_space=pltpu.VMEM)] * len(outs)),
        scratch_shapes=list(scratch) + places + semaphores,
        compiler_params=pltpu.CompilerParams(vmem_limit_bytes=grant or min(need + 6 * MIB, 56 * MIB)),
        cost_estimate=pl.CostEstimate(
            flops=int(us * 1.1e9), bytes_accessed=int(us * 1e5), transcendentals=0
        ),
    )(*after, *args)
    return result if len(outs) > 1 else result[0]


class Fetched:
    def __init__(self, ref, copy):
        self.ref, self.copy, self.shape = ref, copy, ref.shape

    def __getitem__(self, index):
        if self.copy is not None:
            self.copy.wait()
            self.copy = None
        return self.ref[index]


def shape(dims, dtype):
    return jax.ShapeDtypeStruct(tuple(dims), dtype)


def dot(a, b, dims=(((1,), (0,)), ((), ()))):
    return lax.dot_general(a, b, dims, preferred_element_type=F32)


def normalize(x, gain, shift):
    centered = x - jnp.mean(x, -1, keepdims=True)
    inverse = lax.rsqrt(jnp.mean(centered * centered, -1, keepdims=True) + EPS)
    xhat = centered * inverse
    return xhat, inverse, (xhat * gain + shift).astype(BF16)


def column_of(row):
    return jnp.broadcast_to(row, (8, row.shape[1])).T[:, :1]


def project_kernel(
    index_ref, x_ref, mask_ref, gain_ref, shift_ref, wl_ref, wr_ref, bl_ref, br_ref,
    left_ref, right_ref, proj, right_rows, weights, mask_t,
):
    seqs, rows, width = x_ref.shape
    proj_width = right_ref.shape[0]
    begin = pl.multiple_of(index_ref[0] * rows, rows)
    weights[:proj_width, :] = wl_ref[...]
    weights[proj_width : 2 * proj_width, :] = wr_ref[...]
    weights[2 * proj_width :, :] = jnp.zeros((LANES - 2 * proj_width, width), BF16)
    bias_left = column_of(bl_ref[...])
    bias_right = column_of(br_ref[...])
    step = 16
    for first in range(0, seqs, step):
        x = x_ref[first : first + step].astype(F32).reshape(step * rows, width)
        normalized = normalize(x, gain_ref[...], shift_ref[...])[2]
        proj[first * rows : (first + step) * rows, :] = dot(normalized, weights[...], LAST_DIMS)
    mask_t[...] = mask_ref[...].astype(F32).T
    mask_own = mask_t[pl.ds(begin, rows), :]
    for i in range(rows):
        block = proj[pl.ds(i, seqs, stride=rows), :].T
        mask_row = mask_own[i : i + 1, :]
        span = slice(i * proj_width, (i + 1) * proj_width)
        left_ref[span, :] = ((block[:proj_width] + bias_left) * mask_row).astype(BF16)
        right_rows[span, :] = (block[proj_width : 2 * proj_width] + bias_right) * mask_row
    for e in range(proj_width):
        right_ref[e] = right_rows[pl.ds(e, rows, stride=proj_width), :].astype(BF16)


def grad_columns(w2_ref, scaled_ref, grad):
    rows, cols, chan = scaled_ref.shape
    proj_width = grad.shape[0]
    for i in range(0, rows, 2):
        pair = scaled_ref[i : i + 2].reshape(2 * cols, chan)
        block = dot(w2_ref[...], pair, LAST_DIMS).astype(BF16)
        for e in range(proj_width):
            for sub in range(2):
                grad[e, (i + sub) * proj_width : (i + sub + 1) * proj_width, :] = block[
                    e * proj_width : (e + 1) * proj_width, sub * cols : (sub + 1) * cols
                ]


def right_columns(index_ref, left_t, grad, emit):
    proj_width, _, cols = grad.shape
    rows = left_t.shape[1] // proj_width
    high = cols // rows // 2
    own = index_ref[0] >> 1
    for e in range(0, proj_width, 2):
        block = jnp.concatenate([grad[e], grad[e + 1]], 1)
        sums = dot(left_t[...], block)
        for sub in range(2):
            part = sums[:, sub * cols : (sub + 1) * cols].T
            for q in range(2 * high):
                rel = q ^ own
                emit(e + sub, (rel & 1) * high + (rel >> 1), part[q * rows : (q + 1) * rows])


def scale_columns(half, mask_t_ref, mask_own, resid_t, resid_own, cot_ref, scaled_ref, factor_ref):
    rows = cot_ref.shape[0]
    cols = scaled_ref.shape[1]
    starts = [
        pl.multiple_of((2 * q + half) * rows, rows) for q in range(cols // rows)
    ]
    mask_cols = jnp.concatenate([mask_t_ref[pl.ds(s, rows), :] for s in starts], 0)
    resid_cols = jnp.concatenate([resid_t[pl.ds(s, rows), :] for s in starts], 0)
    counted = dot(mask_cols.astype(BF16), mask_own.astype(BF16), LAST_DIMS)
    factor_t = resid_cols[:, :1] * resid_own / counted
    factor_ref[...] = factor_t.T
    bias_sum = jnp.zeros((1, cot_ref.shape[2]), F32)
    for i in range(rows):
        cot = jnp.concatenate([cot_ref[i, pl.ds(s, rows), :] for s in starts], 0)
        scaled = (cot.astype(F32) * factor_t[:, i : i + 1]).astype(BF16)
        scaled_ref[i] = scaled
        bias_sum = bias_sum + jnp.sum(scaled.astype(F32), 0, keepdims=True)
    return bias_sum


def send_kernel(
    index_ref, left_ref, mask_ref, resid_ref, cot_ref, w_ref,
    send_ref, far_ref, near_ref, far_factor_ref, near_factor_ref, w2_ref, b_ref, left_t_ref, grad,
    mask_own_ref, wide, resid_t, mask_t,
):
    rows, cols, chan = cot_ref.shape
    proj_width = left_ref.shape[0] // rows
    index = index_ref[0]
    wide[...] = w_ref[...].astype(F32)
    for e in range(proj_width):
        w2_ref[e * proj_width : (e + 1) * proj_width, :] = wide[
            pl.ds(e, proj_width, stride=proj_width), :
        ].astype(BF16)
    left_t_ref[...] = left_ref[...].astype(F32).T.astype(BF16)
    resid_t[...] = jnp.broadcast_to(resid_ref[...].astype(F32), (LANES, cols)).T
    begin = pl.multiple_of(index * rows, rows)
    mask_t[...] = mask_ref[...].astype(F32).T
    mask_own = mask_t[pl.ds(begin, rows), :]
    mask_own_ref[...] = mask_own
    resid_own = resid_t[pl.ds(begin, rows), :].T[:1]
    side = index & 1
    shared = (mask_t, mask_own, resid_t, resid_own, cot_ref)
    far_sum = scale_columns(1 - side, *shared, far_ref, far_factor_ref)
    near_sum = scale_columns(side, *shared, near_ref, near_factor_ref)
    b_ref[...] = far_sum + near_sum
    grad_columns(w2_ref, far_ref, grad)

    def emit(e, slot, value):
        send_ref[slot, e] = value.astype(BF16)

    right_columns(index_ref, left_t_ref, grad, emit)


def keep_kernel(
    index_ref, left_t_ref, w2_ref, near_ref, far_part_ref, keep_ref, send_ref, grad, total
):
    high = keep_ref.shape[0]
    grad_columns(w2_ref, near_ref, grad)

    def emit(e, slot, value):
        total[slot, e] = value

    right_columns(index_ref, left_t_ref, grad, emit)
    keep_ref[...] = total[:high] + far_part_ref[:high].astype(F32)
    send_ref[...] = (total[high:] + far_part_ref[high:].astype(F32)).astype(BF16)


def high_kernel(keep_ref, other_ref, own_ref, *send_refs):
    own_ref[...] = keep_ref[0] + other_ref[0].astype(F32)
    for k, ref in enumerate(send_refs):
        ref[...] = (keep_ref[k + 1] + other_ref[k + 1].astype(F32)).astype(BF16)


def normal_kernel(
    x_ref, gain_ref, shift_ref, right_ref, other_ref,
    normal_ref, inverse_ref, right_copy_ref, other_copy_ref,
):
    seqs, rows, width = x_ref.shape
    right_copy_ref[...] = right_ref[...]
    other_copy_ref[...] = other_ref[...]
    step = 16
    for first in range(0, seqs, step):
        x = x_ref[first : first + step].astype(F32).reshape(step * rows, width)
        xhat, inverse, normalized = normalize(x, gain_ref[...], shift_ref[...])
        span = slice(first * rows, (first + step) * rows)
        normal_ref[span, :width] = normalized
        normal_ref[span, width:] = xhat.astype(BF16)
        inverse_ref[span, :] = inverse


def line_kernel(*refs):
    count = len(refs) // 2
    for k in range(count):
        refs[count + k][...] = refs[k][...]
    refs[-1][...] = jnp.zeros_like(refs[-1])


def place_kernel(index_ref, *refs):
    *blocks, out_ref = refs
    rows = blocks[0].shape[1]
    own = index_ref[0] >> 1
    for rel, ref in enumerate(blocks):
        out_ref[:, pl.ds(pl.multiple_of((own ^ rel) * rows, rows), rows), :] = ref[...]


def outer_columns(left_ref, right_ref, outer):
    proj_width, cols, seqs = right_ref.shape
    rows = left_ref.shape[0] // proj_width
    for e in range(0, proj_width, 2):
        pair = right_ref[e : e + 2].reshape(2 * cols, seqs)
        block = dot(left_ref[...], pair, LAST_DIMS).astype(BF16)
        for i in range(rows):
            for sub in range(2):
                outer[
                    i // 2,
                    (e + sub) * proj_width : (e + sub + 1) * proj_width,
                    (i % 2) * cols : (i % 2 + 1) * cols,
                ] = block[i * proj_width : (i + 1) * proj_width, sub * cols : (sub + 1) * cols]


def weight_columns(left_ref, right_ref, scaled_ref, w_ref, outer):
    rows, cols, chan = scaled_ref.shape
    outer_columns(left_ref, right_ref, outer)
    for p in range(rows // 2):
        w_ref[...] += dot(outer[p], scaled_ref[2 * p : 2 * p + 2].reshape(2 * cols, chan))


def left_columns(grad, right_ref, left_sum_ref):
    proj_width, cols, seqs = right_ref.shape
    for e in range(0, proj_width, 2):
        block = jnp.concatenate([grad[e], grad[e + 1]], 1)
        left_sum_ref[...] += dot(block, right_ref[e : e + 2].reshape(2 * cols, seqs))


def near_kernel(left_ref, scaled_ref, right_ref, w_sum_ref, outer_ref):
    w_sum_ref[...] = jnp.zeros_like(w_sum_ref)
    weight_columns(left_ref, right_ref, scaled_ref, w_sum_ref, outer_ref)


def far_kernel(index_ref, left_ref, scaled_ref, right_ref, w_sum_ref, outer_ref, *refs):
    *quarter_refs, total = refs
    total[...] = w_sum_ref[...]
    weight_columns(left_ref, right_ref, scaled_ref, total, outer_ref)
    quarter = quarter_refs[0].shape[0]
    for m, ref in enumerate(quarter_refs):
        begin = pl.multiple_of(((index_ref[0] & 3) ^ m) * quarter, quarter)
        ref[...] = total[pl.ds(begin, quarter), :].astype(BF16)


def left_kernel(near_grad_ref, near_ref, far_grad_ref, far_ref, left_sum_ref):
    left_sum_ref[...] = jnp.zeros_like(left_sum_ref)
    left_columns(near_grad_ref, near_ref, left_sum_ref)
    left_columns(far_grad_ref, far_ref, left_sum_ref)


def pair_kernel(
    index_ref, w2_ref, bias_ref, near_ref, far_ref, near_factor_ref, far_factor_ref, out_ref, w2_t
):
    rows = out_ref.shape[0]
    w2_t[...] = w2_ref[...].astype(F32).T.astype(BF16)
    bias = column_of(bias_ref[...])
    side = index_ref[0] & 1
    for half, outer, factor_ref in (
        (side, near_ref, near_factor_ref),
        (1 - side, far_ref, far_factor_ref),
    ):
        cols = outer.shape[2] // 2
        for p in range(rows // 2):
            projected = dot(w2_t[...], outer[p]) + bias
            for sub in range(2):
                i = 2 * p + sub
                block = projected[:, sub * cols : (sub + 1) * cols] * factor_ref[i : i + 1, :]
                block = block.T.astype(BF16)
                for q in range(cols // rows):
                    begin = pl.multiple_of((2 * q + half) * rows, rows)
                    out_ref[i, pl.ds(begin, rows), :] = block[q * rows : (q + 1) * rows]


def sums_kernel(
    right_own_ref, *refs
):
    *ins, grads_ref, pack_ref, right_sum, gathered = refs
    right_refs, quarter_refs = ins[:-10], ins[-4:]
    normal_ref, wl_ref, wr_ref, mask_own_ref, left_sum_ref, b_ref = ins[-10:-4]
    seqs = mask_own_ref.shape[1]
    proj_width, rows, _ = right_own_ref.shape
    width = wl_ref.shape[1]
    total = right_own_ref[...]
    for ref in right_refs:
        total = total + ref[...].astype(F32)
    right_sum[...] = total.reshape(proj_width * rows, seqs)
    fill = jnp.zeros((LANES - 2 * proj_width, seqs), F32)
    bias_cols = jnp.zeros((LANES, seqs), F32)
    for i in range(rows):
        block = jnp.concatenate(
            [
                left_sum_ref[i * proj_width : (i + 1) * proj_width, :],
                right_sum[pl.ds(i, proj_width, stride=rows), :],
                fill,
            ],
            0,
        )
        block = (block * mask_own_ref[i : i + 1, :]).astype(BF16).astype(F32)
        bias_cols = bias_cols + block
        gathered[pl.ds(i, seqs, stride=rows), :] = block.T
    grads_ref[...] = gathered[...].astype(BF16)
    used = 2 * proj_width
    products = jnp.zeros((LANES, 2 * width), F32)
    step = 256
    for first in range(0, seqs * rows, step):
        products = products + dot(
            grads_ref[first : first + step, :], normal_ref[first : first + step, :], FIRST_DIMS
        )
    weights = jnp.concatenate([wl_ref[...], wr_ref[...]], 0).astype(F32)
    bias_sum = jnp.sum(bias_cols, 1, keepdims=True)
    gain_sum = jnp.sum(weights * products[:used, width:], 0, keepdims=True)
    shift_sum = jnp.sum(weights * bias_sum[:used], 0, keepdims=True)
    bias_row = jnp.broadcast_to(bias_sum, (LANES, LANES)).T[:1]
    pieces = [products[:used, k : k + LANES] for k in range(0, width, LANES)]
    pieces += [gain_sum[:, k : k + LANES] for k in range(0, width, LANES)]
    pieces += [shift_sum[:, k : k + LANES] for k in range(0, width, LANES)]
    pieces += [bias_row, b_ref[...]]
    pieces += [jnp.zeros((TAIL - 2 - 2 * (width // LANES), LANES), F32)]
    pieces += [tree_sum([ref[...] for ref in quarter_refs])]
    pack_ref[...] = jnp.concatenate(pieces, 0).astype(BF16)


def norm_kernel(normal_ref, inverse_ref, gain_ref, wl_ref, wr_ref, grads_ref, out_ref, weights):
    seqs, rows, width = out_ref.shape
    proj_width = wl_ref.shape[0]
    weights[...] = jnp.zeros_like(weights)
    weights[:proj_width, :] = wl_ref[...]
    weights[proj_width : 2 * proj_width, :] = wr_ref[...]
    step = 16
    for first in range(0, seqs, step):
        span = slice(first * rows, (first + step) * rows)
        xhat = normal_ref[span, width:].astype(F32)
        g = dot(grads_ref[span, :], weights[...]) * gain_ref[...]
        result = (
            g - jnp.mean(g, -1, keepdims=True) - xhat * jnp.mean(g * xhat, -1, keepdims=True)
        ) * inverse_ref[span, :]
        out_ref[first : first + step] = result.astype(BF16).reshape(step, rows, width)


def tree_sum(values):
    values = [value.astype(F32) for value in values]
    while len(values) > 1:
        values = [a + b for a, b in zip(values[::2], values[1::2])]
    return values[0]


def merge_kernel(own_ref, other_ref, out_ref):
    out_ref[...] = tree_sum([own_ref[...], other_ref[...]]).astype(BF16)


def side_kernel(own_ref, other_ref, out_ref, *, head):
    rows = own_ref.shape[0]
    out_ref[:head, :] = tree_sum([own_ref[:head, :], other_ref[:head, :]]).astype(BF16)
    out_ref[head:rows, :] = own_ref[head:, :]
    out_ref[rows:, :] = other_ref[head:, :]


def unpack_kernel(index_ref, *refs):
    ins = refs[:2]
    wl_ref, bl_ref, wr_ref, br_ref, w_out_ref, b_ref, gain_ref, shift_ref, placed = refs[2:]
    proj_width, width = wl_ref.shape
    used = 2 * proj_width
    parts = width // LANES
    head = parts * used + TAIL
    total = tree_sum([ref[:head, :] for ref in ins])
    tail = total[parts * used :]
    for k in range(parts):
        span = slice(k * LANES, (k + 1) * LANES)
        wl_ref[:, span] = total[k * used : k * used + proj_width]
        wr_ref[:, span] = total[k * used + proj_width : (k + 1) * used]
        gain_ref[:, span] = tail[k : k + 1]
        shift_ref[:, span] = tail[parts + k : parts + k + 1]
    bl_ref[...] = tail[2 * parts : 2 * parts + 1, :proj_width]
    br_ref[...] = tail[2 * parts : 2 * parts + 1, proj_width:used]
    b_ref[...] = tail[2 * parts + 1 : 2 * parts + 2, :]
    quarter = placed.shape[0] // 4
    for core, ref in enumerate(ins):
        for side in range(2):
            begin = pl.multiple_of(((index_ref[0] & 3) ^ (core + 2 * side)) * quarter, quarter)
            span = slice(head + side * quarter, head + (side + 1) * quarter)
            placed[pl.ds(begin, quarter), :] = ref[span, :].astype(F32)
    for c in range(proj_width):
        w_out_ref[c * proj_width : (c + 1) * proj_width, :] = placed[
            pl.ds(c, proj_width, stride=proj_width), :
        ]


def body(
    devices,
    alignment_activations,
    alignment_row_mask,
    residue_mask_vector,
    layer_norm_gain,
    layer_norm_bias,
    left_weight,
    left_bias,
    right_weight,
    right_bias,
    output_weight,
    output_bias,
    pair_update_cotangent,
):
    seqs, rows, width = alignment_activations.shape
    cols = alignment_row_mask.shape[1]
    proj_width = left_weight.shape[1]
    pair_width, chan = output_weight.shape
    high = devices // 4
    half = cols // 2
    quarter = pair_width // 4
    flat = rows * proj_width
    index = lax.axis_index("res").astype(jnp.int32).reshape(1)
    gain = layer_norm_gain.reshape(1, width)
    shift = layer_norm_bias.reshape(1, width)
    wl, wr = left_weight.T, right_weight.T
    piece = (proj_width, rows, seqs)

    def swap(value, rel):
        return lax.ppermute(value, "res", [(d, d ^ rel) for d in range(devices)])

    slab = (high,) + piece
    left, right = call(
        project_kernel,
        (shape((flat, seqs), BF16), shape(piece, BF16)),
        (index, alignment_activations, alignment_row_mask, gain, shift, wl, wr)
        + (left_bias.reshape(1, proj_width), right_bias.reshape(1, proj_width)),
        (
            pltpu.VMEM((seqs * rows, LANES), F32),
            pltpu.VMEM((flat, seqs), F32),
            pltpu.VMEM((LANES, width), BF16),
            pltpu.VMEM((cols, seqs), F32),
        ),
        us=4,
        fetched=tuple(range(1, 9)),
        grant=60 * MIB,
    )
    blocks = {0: right, 2: swap(right, 2)}
    for k in range(2, high):
        blocks[4 * k] = swap(right, 4 * k)
    grad_shape = shape((proj_width, flat, half), BF16)
    outer_shape = shape((rows // 2, pair_width, 2 * half), BF16)
    send, far, near, far_factor, near_factor, w2, b_part, left_t, far_grad, mask_own = call(
        send_kernel,
        (
            shape((2 * high,) + piece, BF16),
            shape((rows, half, chan), BF16),
            shape((rows, half, chan), BF16),
            shape((rows, half), F32),
            shape((rows, half), F32),
            shape((pair_width, chan), BF16),
            shape((1, chan), F32),
            shape((seqs, flat), BF16),
            grad_shape,
            shape((rows, seqs), F32),
        ),
        (
            index,
            left,
            alignment_row_mask,
            residue_mask_vector.reshape(1, cols),
            pair_update_cotangent,
            output_weight,
        ),
        (
            pltpu.VMEM((pair_width, chan), F32),
            pltpu.VMEM((cols, LANES), F32),
            pltpu.VMEM((cols, seqs), F32),
        ),
        us=6,
    )
    keep, send, near_grad = call(
        keep_kernel,
        (shape(slab, F32), shape(slab, BF16), grad_shape),
        (index, left_t, w2, near, swap(send, 1)),
        (pltpu.VMEM((2 * high,) + piece, F32),),
        us=4,
    )
    normal, inverse, right_copy, other_copy, normal_token = call(
        normal_kernel,
        (shape((seqs * rows, 2 * width), BF16), shape((seqs * rows, 1), F32))
        + (shape(piece, BF16),) * 2,
        (alignment_activations, gain, shift, right, blocks[2]),
        scalars=0,
        us=10,
        after=(keep,),
        token=True,
    )
    blocks[4] = swap(right_copy, 4)
    blocks[6] = swap(other_copy, 4)
    blocks[10] = swap(other_copy, 8)
    line = call(
        line_kernel,
        (shape(piece, BF16),) * (high - 3) + (shape((8, LANES), F32),),
        tuple(blocks[4 * k] for k in range(3, high)),
        scalars=0,
        us=0.1,
        after=(normal_token, blocks[8]),
    )
    for k in range(3, high):
        blocks[4 * k + 2] = swap(line[k - 3], 2)
    right_own, *sends = call(
        high_kernel,
        (shape(piece, F32),) + (shape(piece, BF16),) * (high - 1),
        (keep, swap(send, 2)),
        scalars=0,
        us=10,
        after=(line[-1], blocks[4], blocks[6], blocks[10]),
    )
    right_parts = tuple(swap(value, 4 * (k + 1)) for k, value in enumerate(sends))
    right_near = call(
        place_kernel,
        shape((proj_width, half, seqs), BF16),
        (index,) + tuple(blocks[rel] for rel in range(0, devices, 2)),
        after=(right_own,),
    )
    right_far = swap(right_near, 1)
    near_w, near_outer = call(
        near_kernel,
        (shape((pair_width, chan), F32), outer_shape),
        (left, near, right_near),
        scalars=0,
        us=0.05,
    )
    far_outer, w_own, *w_sends = call(
        far_kernel,
        (outer_shape,) + (shape((quarter, chan), BF16),) * 4,
        (index, left, far, right_far, near_w),
        (pltpu.VMEM((pair_width, chan), F32),),
        us=0.02,
    )
    left_sum = call(
        left_kernel,
        shape((flat, seqs), F32),
        (near_grad, right_near, far_grad, right_far),
        scalars=0,
        us=0.02,
        after=(w_own,) + right_parts,
    )
    pack_rows = 2 * proj_width * (width // LANES) + TAIL + quarter
    grads, pack = call(
        sums_kernel,
        (shape((seqs * rows, LANES), BF16), shape((pack_rows, LANES), BF16)),
        (right_own,)
        + right_parts
        + (normal, wl, wr, mask_own, left_sum, b_part, w_own)
        + tuple(swap(value, m + 1) for m, value in enumerate(w_sends)),
        (pltpu.VMEM((flat, seqs), F32), pltpu.VMEM((seqs * rows, LANES), F32)),
        scalars=0,
        us=2,
    )
    alignment_gradient, norm_token = call(
        norm_kernel,
        shape((seqs, rows, width), BF16),
        (normal, inverse, gain, wl, wr, grads),
        (pltpu.VMEM((LANES, width), BF16),),
        scalars=0,
        us=2,
        token=True,
    )
    pair, pair_token = call(
        pair_kernel,
        shape((rows, cols, chan), BF16),
        (index, w2, output_bias.reshape(1, chan), near_outer, far_outer, near_factor, far_factor),
        (pltpu.VMEM((chan, pair_width), BF16),),
        us=2,
        after=(norm_token,),
        token=True,
    )
    far_step, *steps = [devices // 2 >> n for n in range(high.bit_length() - 1)]
    merged = call(
        merge_kernel,
        shape((pack_rows, LANES), BF16),
        (pack, swap(pack, far_step)),
        scalars=0,
        after=(norm_token,),
    )
    for step in steps:
        merged = call(
            merge_kernel,
            shape((pack_rows, LANES), BF16),
            (merged, swap(merged, step)),
            scalars=0,
            after=(pair_token,),
        )
    merged = call(
        side_kernel,
        shape((pack_rows + quarter, LANES), BF16),
        (merged, swap(merged, 2)),
        scalars=0,
        head=pack_rows - quarter,
    )
    w_left, b_left, w_right, b_right, w_out_grad, b_out, gain_grad, shift_grad = call(
        unpack_kernel,
        (
            shape((proj_width, width), F32),
            shape((1, proj_width), F32),
            shape((proj_width, width), F32),
            shape((1, proj_width), F32),
            shape((pair_width, chan), F32),
            shape((1, chan), F32),
            shape((1, width), F32),
            shape((1, width), F32),
        ),
        (index, merged, swap(merged, 1)),
        (pltpu.VMEM((pair_width, chan), F32),),
    )
    return (
        pair,
        alignment_gradient,
        w_left.T,
        b_left.reshape(-1),
        w_right.T,
        b_right.reshape(-1),
        w_out_grad,
        b_out.reshape(-1),
        gain_grad.reshape(-1),
        shift_grad.reshape(-1),
    )


def solution(mesh):
    return jax.shard_map(
        functools.partial(body, mesh.shape["res"]),
        mesh=mesh,
        in_specs=(
            P(None, ("grp", "res"), None),
            P(None, "grp"),
            P("grp"),
            P(),
            P(),
            P(),
            P(),
            P(),
            P(),
            P(),
            P(),
            P(("grp", "res"), None, None),
        ),
        out_specs=(
            P(("grp", "res"), None, None),
            P(None, ("grp", "res"), None),
            P("grp", None),
            P("grp"),
            P("grp", None),
            P("grp"),
            P("grp", None),
            P("grp"),
            P("grp"),
            P("grp"),
        ),
        check_vma=False,
    )
```

```python
import functools
import math

import jax
import jax.numpy as jnp
from jax import lax
from jax.experimental import pallas as pl
from jax.experimental.pallas import tpu as pltpu
from jax.sharding import PartitionSpec as P

EPS = 1e-05
LAST_DIMS = (((1,), (1,)), ((), ()))
FIRST_DIMS = (((0,), (0,)), ((), ()))
MIB = 1024 * 1024
LANES = 128
TAIL = 16
F32 = jnp.float32
BF16 = jnp.bfloat16


def tiled_bytes(dims, dtype):
    dims = tuple(dims)
    lanes = -(-dims[-1] // LANES) * LANES
    sublanes = -(-(dims[-2] if len(dims) > 1 else 1) // 16) * 16
    return math.prod(dims[:-2]) * sublanes * lanes * jnp.dtype(dtype).itemsize


def call(
    kernel, out_shape, args, scratch=(), scalars=1, us=1.0, after=(), fetched=(), token=False, grant=0, **static
):
    count = len(args)
    specs = [pl.BlockSpec(memory_space=pl.ANY)] * len(after)
    specs += [pl.BlockSpec(memory_space=pltpu.SMEM)] * scalars
    for k in range(scalars, count):
        specs.append(pl.BlockSpec(memory_space=pltpu.HBM if k in fetched else pltpu.VMEM))
    outs = list(out_shape) if isinstance(out_shape, (tuple, list)) else [out_shape]
    if token:
        outs.append(shape((8, LANES), F32))
    held = list(args[scalars:]) + outs + list(scratch)
    need = sum(tiled_bytes(value.shape, value.dtype) for value in held)
    places = [pltpu.VMEM(args[k].shape, args[k].dtype) for k in fetched]
    semaphores = [pltpu.SemaphoreType.DMA((len(fetched),))] if fetched else []

    def run(*refs):
        ins = list(refs[len(after) : len(after) + count])
        rest = list(refs[len(after) + count :])
        if fetched:
            *rest, done = rest
            held_refs = rest[-len(fetched) :]
            rest = rest[: -len(fetched)]
            copies = [
                pltpu.make_async_copy(ins[k], ref, done.at[n])
                for n, (k, ref) in enumerate(zip(fetched, held_refs))
            ]
            for copy in copies:
                copy.start()
            for k, ref, copy in zip(fetched, held_refs, copies):
                ins[k] = Fetched(ref, copy)
        if token:
            rest.pop(len(outs) - 1)[...] = jnp.zeros((8, LANES), F32)
        kernel(*ins, *rest, **static)

    result = pl.pallas_call(
        run,
        name=kernel.__name__,
        out_shape=tuple(outs),
        in_specs=specs,
        out_specs=tuple([pl.BlockSpec(memory_space=pltpu.VMEM)] * len(outs)),
        scratch_shapes=list(scratch) + places + semaphores,
        compiler_params=pltpu.CompilerParams(vmem_limit_bytes=grant or min(need + 6 * MIB, 56 * MIB)),
        cost_estimate=pl.CostEstimate(
            flops=int(us * 1.1e9), bytes_accessed=int(us * 1e5), transcendentals=0
        ),
    )(*after, *args)
    return result if len(outs) > 1 else result[0]


class Fetched:
    def __init__(self, ref, copy):
        self.ref, self.copy, self.shape = ref, copy, ref.shape

    def __getitem__(self, index):
        if self.copy is not None:
            self.copy.wait()
            self.copy = None
        return self.ref[index]


def shape(dims, dtype):
    return jax.ShapeDtypeStruct(tuple(dims), dtype)


def dot(a, b, dims=(((1,), (0,)), ((), ()))):
    return lax.dot_general(a, b, dims, preferred_element_type=F32)


def normalize(x, gain, shift):
    centered = x - jnp.mean(x, -1, keepdims=True)
    inverse = lax.rsqrt(jnp.mean(centered * centered, -1, keepdims=True) + EPS)
    xhat = centered * inverse
    return xhat, inverse, (xhat * gain + shift).astype(BF16)


def column_of(row):
    return jnp.broadcast_to(row, (8, row.shape[1])).T[:, :1]


def project_kernel(
    index_ref, x_ref, mask_ref, gain_ref, shift_ref, wl_ref, wr_ref, bl_ref, br_ref,
    left_ref, right_ref, proj, right_rows, weights, mask_t,
):
    seqs, rows, width = x_ref.shape
    proj_width = right_ref.shape[0]
    begin = pl.multiple_of(index_ref[0] * rows, rows)
    weights[:proj_width, :] = wl_ref[...]
    weights[proj_width : 2 * proj_width, :] = wr_ref[...]
    weights[2 * proj_width :, :] = jnp.zeros((LANES - 2 * proj_width, width), BF16)
    bias_left = column_of(bl_ref[...])
    bias_right = column_of(br_ref[...])
    step = 16
    for first in range(0, seqs, step):
        x = x_ref[first : first + step].astype(F32).reshape(step * rows, width)
        normalized = normalize(x, gain_ref[...], shift_ref[...])[2]
        proj[first * rows : (first + step) * rows, :] = dot(normalized, weights[...], LAST_DIMS)
    mask_t[...] = mask_ref[...].astype(F32).T
    mask_own = mask_t[pl.ds(begin, rows), :]
    for i in range(rows):
        block = proj[pl.ds(i, seqs, stride=rows), :].T
        mask_row = mask_own[i : i + 1, :]
        span = slice(i * proj_width, (i + 1) * proj_width)
        left_ref[span, :] = ((block[:proj_width] + bias_left) * mask_row).astype(BF16)
        right_rows[span, :] = (block[proj_width : 2 * proj_width] + bias_right) * mask_row
    for e in range(proj_width):
        right_ref[e] = right_rows[pl.ds(e, rows, stride=proj_width), :].astype(BF16)


def grad_columns(w2_ref, scaled_ref, grad):
    rows, cols, chan = scaled_ref.shape
    proj_width = grad.shape[0]
    for i in range(0, rows, 2):
        pair = scaled_ref[i : i + 2].reshape(2 * cols, chan)
        block = dot(w2_ref[...], pair, LAST_DIMS).astype(BF16)
        for e in range(proj_width):
            for sub in range(2):
                grad[e, (i + sub) * proj_width : (i + sub + 1) * proj_width, :] = block[
                    e * proj_width : (e + 1) * proj_width, sub * cols : (sub + 1) * cols
                ]


def right_columns(index_ref, left_t, grad, emit):
    proj_width, _, cols = grad.shape
    rows = left_t.shape[1] // proj_width
    high = cols // rows // 2
    own = index_ref[0] >> 1
    for e in range(0, proj_width, 2):
        block = jnp.concatenate([grad[e], grad[e + 1]], 1)
        sums = dot(left_t[...], block)
        for sub in range(2):
            part = sums[:, sub * cols : (sub + 1) * cols].T
            for q in range(2 * high):
                rel = q ^ own
                emit(e + sub, (rel & 1) * high + (rel >> 1), part[q * rows : (q + 1) * rows])


def scale_columns(half, mask_t_ref, mask_own, resid_t, resid_own, cot_ref, scaled_ref, factor_ref):
    rows = cot_ref.shape[0]
    cols = scaled_ref.shape[1]
    starts = [
        pl.multiple_of((2 * q + half) * rows, rows) for q in range(cols // rows)
    ]
    mask_cols = jnp.concatenate([mask_t_ref[pl.ds(s, rows), :] for s in starts], 0)
    resid_cols = jnp.concatenate([resid_t[pl.ds(s, rows), :] for s in starts], 0)
    counted = dot(mask_cols.astype(BF16), mask_own.astype(BF16), LAST_DIMS)
    factor_t = resid_cols[:, :1] * resid_own / counted
    factor_ref[...] = factor_t.T
    bias_sum = jnp.zeros((1, cot_ref.shape[2]), F32)
    for i in range(rows):
        cot = jnp.concatenate([cot_ref[i, pl.ds(s, rows), :] for s in starts], 0)
        scaled = (cot.astype(F32) * factor_t[:, i : i + 1]).astype(BF16)
        scaled_ref[i] = scaled
        bias_sum = bias_sum + jnp.sum(scaled.astype(F32), 0, keepdims=True)
    return bias_sum


def send_kernel(
    index_ref, left_ref, mask_ref, resid_ref, cot_ref, w_ref,
    send_ref, far_ref, near_ref, far_factor_ref, near_factor_ref, w2_ref, b_ref, left_t_ref, grad,
    mask_own_ref, wide, resid_t, mask_t,
):
    rows, cols, chan = cot_ref.shape
    proj_width = left_ref.shape[0] // rows
    index = index_ref[0]
    wide[...] = w_ref[...].astype(F32)
    for e in range(proj_width):
        w2_ref[e * proj_width : (e + 1) * proj_width, :] = wide[
            pl.ds(e, proj_width, stride=proj_width), :
        ].astype(BF16)
    left_t_ref[...] = left_ref[...].astype(F32).T.astype(BF16)
    resid_t[...] = jnp.broadcast_to(resid_ref[...].astype(F32), (LANES, cols)).T
    begin = pl.multiple_of(index * rows, rows)
    mask_t[...] = mask_ref[...].astype(F32).T
    mask_own = mask_t[pl.ds(begin, rows), :]
    mask_own_ref[...] = mask_own
    resid_own = resid_t[pl.ds(begin, rows), :].T[:1]
    side = index & 1
    shared = (mask_t, mask_own, resid_t, resid_own, cot_ref)
    far_sum = scale_columns(1 - side, *shared, far_ref, far_factor_ref)
    near_sum = scale_columns(side, *shared, near_ref, near_factor_ref)
    b_ref[...] = far_sum + near_sum
    grad_columns(w2_ref, far_ref, grad)

    def emit(e, slot, value):
        send_ref[slot, e] = value.astype(BF16)

    right_columns(index_ref, left_t_ref, grad, emit)


def keep_kernel(
    index_ref, left_t_ref, w2_ref, near_ref, far_part_ref, keep_ref, send_ref, grad, total
):
    high = keep_ref.shape[0]
    grad_columns(w2_ref, near_ref, grad)

    def emit(e, slot, value):
        total[slot, e] = value

    right_columns(index_ref, left_t_ref, grad, emit)
    keep_ref[...] = total[:high] + far_part_ref[:high].astype(F32)
    send_ref[...] = (total[high:] + far_part_ref[high:].astype(F32)).astype(BF16)


def high_kernel(keep_ref, other_ref, own_ref, *send_refs):
    own_ref[...] = keep_ref[0] + other_ref[0].astype(F32)
    for k, ref in enumerate(send_refs):
        ref[...] = (keep_ref[k + 1] + other_ref[k + 1].astype(F32)).astype(BF16)


def normal_kernel(
    x_ref, gain_ref, shift_ref, right_ref, other_ref,
    normal_ref, inverse_ref, right_copy_ref, other_copy_ref,
):
    seqs, rows, width = x_ref.shape
    right_copy_ref[...] = right_ref[...]
    other_copy_ref[...] = other_ref[...]
    step = 16
    for first in range(0, seqs, step):
        x = x_ref[first : first + step].astype(F32).reshape(step * rows, width)
        xhat, inverse, normalized = normalize(x, gain_ref[...], shift_ref[...])
        span = slice(first * rows, (first + step) * rows)
        normal_ref[span, :width] = normalized
        normal_ref[span, width:] = xhat.astype(BF16)
        inverse_ref[span, :] = inverse


def line_kernel(*refs):
    count = len(refs) // 2
    for k in range(count):
        refs[count + k][...] = refs[k][...]
    refs[-1][...] = jnp.zeros_like(refs[-1])


def place_kernel(index_ref, *refs):
    *blocks, out_ref = refs
    rows = blocks[0].shape[1]
    own = index_ref[0] >> 1
    for rel, ref in enumerate(blocks):
        out_ref[:, pl.ds(pl.multiple_of((own ^ rel) * rows, rows), rows), :] = ref[...]


def outer_columns(left_ref, right_ref, outer):
    proj_width, cols, seqs = right_ref.shape
    rows = left_ref.shape[0] // proj_width
    for e in range(0, proj_width, 2):
        pair = right_ref[e : e + 2].reshape(2 * cols, seqs)
        block = dot(left_ref[...], pair, LAST_DIMS).astype(BF16)
        for i in range(rows):
            for sub in range(2):
                outer[
                    i // 2,
                    (e + sub) * proj_width : (e + sub + 1) * proj_width,
                    (i % 2) * cols : (i % 2 + 1) * cols,
                ] = block[i * proj_width : (i + 1) * proj_width, sub * cols : (sub + 1) * cols]


def weight_columns(left_ref, right_ref, scaled_ref, w_ref, outer):
    rows, cols, chan = scaled_ref.shape
    outer_columns(left_ref, right_ref, outer)
    for p in range(rows // 2):
        w_ref[...] += dot(outer[p], scaled_ref[2 * p : 2 * p + 2].reshape(2 * cols, chan))


def left_columns(grad, right_ref, left_sum_ref):
    proj_width, cols, seqs = right_ref.shape
    for e in range(0, proj_width, 2):
        block = jnp.concatenate([grad[e], grad[e + 1]], 1)
        left_sum_ref[...] += dot(block, right_ref[e : e + 2].reshape(2 * cols, seqs))


def near_kernel(left_ref, scaled_ref, right_ref, w_sum_ref, outer_ref):
    w_sum_ref[...] = jnp.zeros_like(w_sum_ref)
    weight_columns(left_ref, right_ref, scaled_ref, w_sum_ref, outer_ref)


def far_kernel(index_ref, left_ref, scaled_ref, right_ref, w_sum_ref, outer_ref, *refs):
    *quarter_refs, total = refs
    total[...] = w_sum_ref[...]
    weight_columns(left_ref, right_ref, scaled_ref, total, outer_ref)
    quarter = quarter_refs[0].shape[0]
    for m, ref in enumerate(quarter_refs):
        begin = pl.multiple_of(((index_ref[0] & 3) ^ m) * quarter, quarter)
        ref[...] = total[pl.ds(begin, quarter), :].astype(BF16)


def left_kernel(near_grad_ref, near_ref, far_grad_ref, far_ref, left_sum_ref):
    left_sum_ref[...] = jnp.zeros_like(left_sum_ref)
    left_columns(near_grad_ref, near_ref, left_sum_ref)
    left_columns(far_grad_ref, far_ref, left_sum_ref)


def pair_kernel(
    index_ref, w2_ref, bias_ref, near_ref, far_ref, near_factor_ref, far_factor_ref, out_ref, w2_t
):
    rows = out_ref.shape[0]
    w2_t[...] = w2_ref[...].astype(F32).T.astype(BF16)
    bias = column_of(bias_ref[...])
    side = index_ref[0] & 1
    for half, outer, factor_ref in (
        (side, near_ref, near_factor_ref),
        (1 - side, far_ref, far_factor_ref),
    ):
        cols = outer.shape[2] // 2
        for p in range(rows // 2):
            projected = dot(w2_t[...], outer[p]) + bias
            for sub in range(2):
                i = 2 * p + sub
                block = projected[:, sub * cols : (sub + 1) * cols] * factor_ref[i : i + 1, :]
                block = block.T.astype(BF16)
                for q in range(cols // rows):
                    begin = pl.multiple_of((2 * q + half) * rows, rows)
                    out_ref[i, pl.ds(begin, rows), :] = block[q * rows : (q + 1) * rows]


def sums_kernel(
    right_own_ref, *refs
):
    *ins, grads_ref, pack_ref, right_sum, gathered = refs
    *right_refs, normal_ref, wl_ref, wr_ref, mask_own_ref, left_sum_ref, b_ref = ins
    seqs = mask_own_ref.shape[1]
    proj_width, rows, _ = right_own_ref.shape
    width = wl_ref.shape[1]
    total = right_own_ref[...]
    for ref in right_refs:
        total = total + ref[...].astype(F32)
    right_sum[...] = total.reshape(proj_width * rows, seqs)
    fill = jnp.zeros((LANES - 2 * proj_width, seqs), F32)
    bias_cols = jnp.zeros((LANES, seqs), F32)
    for i in range(rows):
        block = jnp.concatenate(
            [
                left_sum_ref[i * proj_width : (i + 1) * proj_width, :],
                right_sum[pl.ds(i, proj_width, stride=rows), :],
                fill,
            ],
            0,
        )
        block = (block * mask_own_ref[i : i + 1, :]).astype(BF16).astype(F32)
        bias_cols = bias_cols + block
        gathered[pl.ds(i, seqs, stride=rows), :] = block.T
    grads_ref[...] = gathered[...].astype(BF16)
    used = 2 * proj_width
    products = jnp.zeros((LANES, 2 * width), F32)
    step = 256
    for first in range(0, seqs * rows, step):
        products = products + dot(
            grads_ref[first : first + step, :], normal_ref[first : first + step, :], FIRST_DIMS
        )
    weights = jnp.concatenate([wl_ref[...], wr_ref[...]], 0).astype(F32)
    bias_sum = jnp.sum(bias_cols, 1, keepdims=True)
    gain_sum = jnp.sum(weights * products[:used, width:], 0, keepdims=True)
    shift_sum = jnp.sum(weights * bias_sum[:used], 0, keepdims=True)
    bias_row = jnp.broadcast_to(bias_sum, (LANES, LANES)).T[:1]
    pieces = [products[:used, k : k + LANES] for k in range(0, width, LANES)]
    pieces += [gain_sum[:, k : k + LANES] for k in range(0, width, LANES)]
    pieces += [shift_sum[:, k : k + LANES] for k in range(0, width, LANES)]
    pieces += [bias_row, b_ref[...]]
    pieces += [jnp.zeros((TAIL - 2 - 2 * (width // LANES), LANES), F32)]
    pack_ref[...] = jnp.concatenate(pieces, 0).astype(BF16)


def norm_kernel(normal_ref, inverse_ref, gain_ref, wl_ref, wr_ref, grads_ref, out_ref, weights):
    seqs, rows, width = out_ref.shape
    proj_width = wl_ref.shape[0]
    weights[...] = jnp.zeros_like(weights)
    weights[:proj_width, :] = wl_ref[...]
    weights[proj_width : 2 * proj_width, :] = wr_ref[...]
    step = 16
    for first in range(0, seqs, step):
        span = slice(first * rows, (first + step) * rows)
        xhat = normal_ref[span, width:].astype(F32)
        g = dot(grads_ref[span, :], weights[...]) * gain_ref[...]
        result = (
            g - jnp.mean(g, -1, keepdims=True) - xhat * jnp.mean(g * xhat, -1, keepdims=True)
        ) * inverse_ref[span, :]
        out_ref[first : first + step] = result.astype(BF16).reshape(step, rows, width)


def tree_sum(values):
    values = [value.astype(F32) for value in values]
    while len(values) > 1:
        values = [a + b for a, b in zip(values[::2], values[1::2])]
    return values[0]


def merge_kernel(*refs):
    *ins, out_ref = refs
    out_ref[...] = tree_sum([ref[...] for ref in ins]).astype(BF16)


def join_kernel(own_ref, other_ref, out_ref):
    out_ref[0] = own_ref[...]
    out_ref[1] = other_ref[...]


def weight_kernel(index_ref, own_ref, other_ref, out_ref, placed):
    quarter = own_ref.shape[1]
    proj_width = math.isqrt(out_ref.shape[0])
    for core, ref in enumerate((own_ref, other_ref)):
        for side in range(2):
            begin = pl.multiple_of(((index_ref[0] & 3) ^ (core + 2 * side)) * quarter, quarter)
            placed[pl.ds(begin, quarter), :] = ref[side].astype(F32)
    for c in range(proj_width):
        out_ref[c * proj_width : (c + 1) * proj_width, :] = placed[
            pl.ds(c, proj_width, stride=proj_width), :
        ]


def unpack_kernel(
    own_ref, other_ref, wl_ref, bl_ref, wr_ref, br_ref, b_ref, gain_ref, shift_ref
):
    proj_width, width = wl_ref.shape
    used = 2 * proj_width
    parts = width // LANES
    total = tree_sum([own_ref[...], other_ref[...]])
    tail = total[parts * used :]
    for k in range(parts):
        span = slice(k * LANES, (k + 1) * LANES)
        wl_ref[:, span] = total[k * used : k * used + proj_width]
        wr_ref[:, span] = total[k * used + proj_width : (k + 1) * used]
        gain_ref[:, span] = tail[k : k + 1]
        shift_ref[:, span] = tail[parts + k : parts + k + 1]
    bl_ref[...] = tail[2 * parts : 2 * parts + 1, :proj_width]
    br_ref[...] = tail[2 * parts : 2 * parts + 1, proj_width:used]
    b_ref[...] = tail[2 * parts + 1 : 2 * parts + 2, :]


def body(
    devices,
    alignment_activations,
    alignment_row_mask,
    residue_mask_vector,
    layer_norm_gain,
    layer_norm_bias,
    left_weight,
    left_bias,
    right_weight,
    right_bias,
    output_weight,
    output_bias,
    pair_update_cotangent,
):
    seqs, rows, width = alignment_activations.shape
    cols = alignment_row_mask.shape[1]
    proj_width = left_weight.shape[1]
    pair_width, chan = output_weight.shape
    high = devices // 4
    half = cols // 2
    quarter = pair_width // 4
    flat = rows * proj_width
    index = lax.axis_index("res").astype(jnp.int32).reshape(1)
    gain = layer_norm_gain.reshape(1, width)
    shift = layer_norm_bias.reshape(1, width)
    wl, wr = left_weight.T, right_weight.T
    piece = (proj_width, rows, seqs)

    def swap(value, rel):
        return lax.ppermute(value, "res", [(d, d ^ rel) for d in range(devices)])

    slab = (high,) + piece
    left, right = call(
        project_kernel,
        (shape((flat, seqs), BF16), shape(piece, BF16)),
        (index, alignment_activations, alignment_row_mask, gain, shift, wl, wr)
        + (left_bias.reshape(1, proj_width), right_bias.reshape(1, proj_width)),
        (
            pltpu.VMEM((seqs * rows, LANES), F32),
            pltpu.VMEM((flat, seqs), F32),
            pltpu.VMEM((LANES, width), BF16),
            pltpu.VMEM((cols, seqs), F32),
        ),
        us=4,
        fetched=tuple(range(1, 9)),
        grant=60 * MIB,
    )
    blocks = {0: right, 2: swap(right, 2)}
    for k in range(2, high):
        blocks[4 * k] = swap(right, 4 * k)
    grad_shape = shape((proj_width, flat, half), BF16)
    outer_shape = shape((rows // 2, pair_width, 2 * half), BF16)
    send, far, near, far_factor, near_factor, w2, b_part, left_t, far_grad, mask_own = call(
        send_kernel,
        (
            shape((2 * high,) + piece, BF16),
            shape((rows, half, chan), BF16),
            shape((rows, half, chan), BF16),
            shape((rows, half), F32),
            shape((rows, half), F32),
            shape((pair_width, chan), BF16),
            shape((1, chan), F32),
            shape((seqs, flat), BF16),
            grad_shape,
            shape((rows, seqs), F32),
        ),
        (
            index,
            left,
            alignment_row_mask,
            residue_mask_vector.reshape(1, cols),
            pair_update_cotangent,
            output_weight,
        ),
        (
            pltpu.VMEM((pair_width, chan), F32),
            pltpu.VMEM((cols, LANES), F32),
            pltpu.VMEM((cols, seqs), F32),
        ),
        us=6,
    )
    keep, send, near_grad = call(
        keep_kernel,
        (shape(slab, F32), shape(slab, BF16), grad_shape),
        (index, left_t, w2, near, swap(send, 1)),
        (pltpu.VMEM((2 * high,) + piece, F32),),
        us=4,
    )
    normal, inverse, right_copy, other_copy, normal_token = call(
        normal_kernel,
        (shape((seqs * rows, 2 * width), BF16), shape((seqs * rows, 1), F32))
        + (shape(piece, BF16),) * 2,
        (alignment_activations, gain, shift, right, blocks[2]),
        scalars=0,
        us=10,
        after=(keep,),
        token=True,
    )
    blocks[4] = swap(right_copy, 4)
    blocks[6] = swap(other_copy, 4)
    blocks[10] = swap(other_copy, 8)
    line = call(
        line_kernel,
        (shape(piece, BF16),) * (high - 3) + (shape((8, LANES), F32),),
        tuple(blocks[4 * k] for k in range(3, high)),
        scalars=0,
        us=0.1,
        after=(normal_token, blocks[8]),
    )
    for k in range(3, high):
        blocks[4 * k + 2] = swap(line[k - 3], 2)
    right_own, *sends = call(
        high_kernel,
        (shape(piece, F32),) + (shape(piece, BF16),) * (high - 1),
        (keep, swap(send, 2)),
        scalars=0,
        us=10,
        after=(line[-1], blocks[4], blocks[6], blocks[10]),
    )
    right_parts = tuple(swap(sends[k - 1], 4 * k) for k in range(high - 1, 0, -1))
    right_near = call(
        place_kernel,
        shape((proj_width, half, seqs), BF16),
        (index,) + tuple(blocks[rel] for rel in range(0, devices, 2)),
        after=(right_own,),
    )
    right_far = swap(right_near, 1)
    near_w, near_outer = call(
        near_kernel,
        (shape((pair_width, chan), F32), outer_shape),
        (left, near, right_near),
        scalars=0,
        us=0.05,
    )
    far_outer, w_own, *w_sends = call(
        far_kernel,
        (outer_shape,) + (shape((quarter, chan), BF16),) * 4,
        (index, left, far, right_far, near_w),
        (pltpu.VMEM((pair_width, chan), F32),),
        us=0.02,
    )
    left_sum = call(
        left_kernel,
        shape((flat, seqs), F32),
        (near_grad, right_near, far_grad, right_far),
        scalars=0,
        us=0.02,
        after=(w_own,) + right_parts,
    )
    distances = [devices // 2 >> n for n in range(high.bit_length() - 1)]
    weights = call(
        merge_kernel,
        shape((quarter, chan), BF16),
        (w_own,) + tuple(swap(value, m + 1) for m, value in enumerate(w_sends)),
        scalars=0,
        us=0.1,
        after=(left_sum,),
    )
    for distance in distances:
        weights = call(
            merge_kernel,
            shape((quarter, chan), BF16),
            (weights, swap(weights, distance)),
            scalars=0,
            us=0.1,
        )
    weights = call(
        join_kernel,
        shape((2, quarter, chan), BF16),
        (weights, swap(weights, 2)),
        scalars=0,
        us=0.1,
    )
    w_out_grad = call(
        weight_kernel,
        shape((pair_width, chan), F32),
        (index, weights, swap(weights, 1)),
        (pltpu.VMEM((pair_width, chan), F32),),
        us=0.1,
    )

    pack_shape = shape((2 * proj_width * (width // LANES) + TAIL, LANES), BF16)
    grads, pack = call(
        sums_kernel,
        (shape((seqs * rows, LANES), BF16), pack_shape),
        (right_own,) + right_parts + (normal, wl, wr, mask_own, left_sum, b_part),
        (pltpu.VMEM((flat, seqs), F32), pltpu.VMEM((seqs * rows, LANES), F32)),
        scalars=0,
        us=2,
    )
    alignment_gradient, norm_token = call(
        norm_kernel,
        shape((seqs, rows, width), BF16),
        (normal, inverse, gain, wl, wr, grads),
        (pltpu.VMEM((LANES, width), BF16),),
        scalars=0,
        us=2,
        token=True,
    )
    pair, pair_token = call(
        pair_kernel,
        shape((rows, cols, chan), BF16),
        (index, w2, output_bias.reshape(1, chan), near_outer, far_outer, near_factor, far_factor),
        (pltpu.VMEM((chan, pair_width), BF16),),
        us=2,
        after=(norm_token,),
        token=True,
    )
    tokens = [norm_token] + [pair_token] * len(distances)
    for distance, token in zip(distances + [2], tokens):
        pack = call(
            merge_kernel,
            pack_shape,
            (pack, swap(pack, distance)),
            scalars=0,
            us=0.1,
            after=(token,),
        )
    w_left, b_left, w_right, b_right, b_out, gain_grad, shift_grad = call(
        unpack_kernel,
        (
            shape((proj_width, width), F32),
            shape((1, proj_width), F32),
            shape((proj_width, width), F32),
            shape((1, proj_width), F32),
            shape((1, chan), F32),
            shape((1, width), F32),
            shape((1, width), F32),
        ),
        (pack, swap(pack, 1)),
        scalars=0,
    )
    return (
        pair,
        alignment_gradient,
        w_left.T,
        b_left.reshape(-1),
        w_right.T,
        b_right.reshape(-1),
        w_out_grad,
        b_out.reshape(-1),
        gain_grad.reshape(-1),
        shift_grad.reshape(-1),
    )


def solution(mesh):
    return jax.shard_map(
        functools.partial(body, mesh.shape["res"]),
        mesh=mesh,
        in_specs=(
            P(None, ("grp", "res"), None),
            P(None, "grp"),
            P("grp"),
            P(),
            P(),
            P(),
            P(),
            P(),
            P(),
            P(),
            P(),
            P(("grp", "res"), None, None),
        ),
        out_specs=(
            P(("grp", "res"), None, None),
            P(None, ("grp", "res"), None),
            P("grp", None),
            P("grp"),
            P("grp", None),
            P("grp"),
            P("grp", None),
            P("grp"),
            P("grp"),
            P("grp"),
        ),
        check_vma=False,
    )
```

```python
import functools
import math

import jax
import jax.numpy as jnp
from jax import lax
from jax.experimental import pallas as pl
from jax.experimental.pallas import tpu as pltpu
from jax.sharding import PartitionSpec as P

EPS = 1e-05
LAST_DIMS = (((1,), (1,)), ((), ()))
FIRST_DIMS = (((0,), (0,)), ((), ()))
MIB = 1024 * 1024
LANES = 128
TAIL = 16
F32 = jnp.float32
BF16 = jnp.bfloat16


def tiled_bytes(dims, dtype):
    dims = tuple(dims)
    lanes = -(-dims[-1] // LANES) * LANES
    sublanes = -(-(dims[-2] if len(dims) > 1 else 1) // 16) * 16
    return math.prod(dims[:-2]) * sublanes * lanes * jnp.dtype(dtype).itemsize


def call(
    kernel, out_shape, args, scratch=(), scalars=1, us=1.0, after=(), fetched=(), token=False, grant=0, **static
):
    count = len(args)
    specs = [pl.BlockSpec(memory_space=pl.ANY)] * len(after)
    specs += [pl.BlockSpec(memory_space=pltpu.SMEM)] * scalars
    for k in range(scalars, count):
        specs.append(pl.BlockSpec(memory_space=pltpu.HBM if k in fetched else pltpu.VMEM))
    outs = list(out_shape) if isinstance(out_shape, (tuple, list)) else [out_shape]
    if token:
        outs.append(shape((8, LANES), F32))
    held = list(args[scalars:]) + outs + list(scratch)
    need = sum(tiled_bytes(value.shape, value.dtype) for value in held)
    places = [pltpu.VMEM(args[k].shape, args[k].dtype) for k in fetched]
    semaphores = [pltpu.SemaphoreType.DMA((len(fetched),))] if fetched else []

    def run(*refs):
        ins = list(refs[len(after) : len(after) + count])
        rest = list(refs[len(after) + count :])
        if fetched:
            *rest, done = rest
            held_refs = rest[-len(fetched) :]
            rest = rest[: -len(fetched)]
            copies = [
                pltpu.make_async_copy(ins[k], ref, done.at[n])
                for n, (k, ref) in enumerate(zip(fetched, held_refs))
            ]
            for copy in copies:
                copy.start()
            for k, ref, copy in zip(fetched, held_refs, copies):
                ins[k] = Fetched(ref, copy)
        if token:
            rest.pop(len(outs) - 1)[...] = jnp.zeros((8, LANES), F32)
        kernel(*ins, *rest, **static)

    result = pl.pallas_call(
        run,
        name=kernel.__name__,
        out_shape=tuple(outs),
        in_specs=specs,
        out_specs=tuple([pl.BlockSpec(memory_space=pltpu.VMEM)] * len(outs)),
        scratch_shapes=list(scratch) + places + semaphores,
        compiler_params=pltpu.CompilerParams(vmem_limit_bytes=grant or min(need + 6 * MIB, 56 * MIB)),
        cost_estimate=pl.CostEstimate(
            flops=int(us * 1.1e9), bytes_accessed=int(us * 1e5), transcendentals=0
        ),
    )(*after, *args)
    return result if len(outs) > 1 else result[0]


class Fetched:
    def __init__(self, ref, copy):
        self.ref, self.copy, self.shape = ref, copy, ref.shape

    def __getitem__(self, index):
        if self.copy is not None:
            self.copy.wait()
            self.copy = None
        return self.ref[index]


def shape(dims, dtype):
    return jax.ShapeDtypeStruct(tuple(dims), dtype)


def dot(a, b, dims=(((1,), (0,)), ((), ()))):
    return lax.dot_general(a, b, dims, preferred_element_type=F32)


def normalize(x, gain, shift):
    centered = x - jnp.mean(x, -1, keepdims=True)
    inverse = lax.rsqrt(jnp.mean(centered * centered, -1, keepdims=True) + EPS)
    xhat = centered * inverse
    return xhat, inverse, (xhat * gain + shift).astype(BF16)


def column_of(row):
    return jnp.broadcast_to(row, (8, row.shape[1])).T[:, :1]


def project_kernel(
    index_ref, x_ref, mask_ref, gain_ref, shift_ref, wl_ref, wr_ref, bl_ref, br_ref,
    left_ref, right_ref, proj, right_rows, weights, mask_t,
):
    seqs, rows, width = x_ref.shape
    proj_width = right_ref.shape[0]
    begin = pl.multiple_of(index_ref[0] * rows, rows)
    weights[:proj_width, :] = wl_ref[...]
    weights[proj_width : 2 * proj_width, :] = wr_ref[...]
    weights[2 * proj_width :, :] = jnp.zeros((LANES - 2 * proj_width, width), BF16)
    bias_left = column_of(bl_ref[...])
    bias_right = column_of(br_ref[...])
    step = 16
    for first in range(0, seqs, step):
        x = x_ref[first : first + step].astype(F32).reshape(step * rows, width)
        normalized = normalize(x, gain_ref[...], shift_ref[...])[2]
        proj[first * rows : (first + step) * rows, :] = dot(normalized, weights[...], LAST_DIMS)
    mask_t[...] = mask_ref[...].astype(F32).T
    mask_own = mask_t[pl.ds(begin, rows), :]
    for i in range(rows):
        block = proj[pl.ds(i, seqs, stride=rows), :].T
        mask_row = mask_own[i : i + 1, :]
        span = slice(i * proj_width, (i + 1) * proj_width)
        left_ref[span, :] = ((block[:proj_width] + bias_left) * mask_row).astype(BF16)
        right_rows[span, :] = (block[proj_width : 2 * proj_width] + bias_right) * mask_row
    for e in range(proj_width):
        right_ref[e] = right_rows[pl.ds(e, rows, stride=proj_width), :].astype(BF16)


def grad_columns(w2_ref, scaled_ref, grad):
    rows, cols, chan = scaled_ref.shape
    proj_width = grad.shape[0]
    for i in range(0, rows, 2):
        pair = scaled_ref[i : i + 2].reshape(2 * cols, chan)
        block = dot(w2_ref[...], pair, LAST_DIMS).astype(BF16)
        for e in range(proj_width):
            for sub in range(2):
                grad[e, (i + sub) * proj_width : (i + sub + 1) * proj_width, :] = block[
                    e * proj_width : (e + 1) * proj_width, sub * cols : (sub + 1) * cols
                ]


def right_columns(index_ref, left_t, grad, emit):
    proj_width, _, cols = grad.shape
    rows = left_t.shape[1] // proj_width
    high = cols // rows // 2
    own = index_ref[0] >> 1
    for e in range(0, proj_width, 2):
        block = jnp.concatenate([grad[e], grad[e + 1]], 1)
        sums = dot(left_t[...], block)
        for sub in range(2):
            part = sums[:, sub * cols : (sub + 1) * cols].T
            for q in range(2 * high):
                rel = q ^ own
                emit(e + sub, (rel & 1) * high + (rel >> 1), part[q * rows : (q + 1) * rows])


def scale_columns(half, mask_t_ref, mask_own, resid_t, resid_own, cot_ref, scaled_ref, factor_ref):
    rows = cot_ref.shape[0]
    cols = scaled_ref.shape[1]
    starts = [
        pl.multiple_of((2 * q + half) * rows, rows) for q in range(cols // rows)
    ]
    mask_cols = jnp.concatenate([mask_t_ref[pl.ds(s, rows), :] for s in starts], 0)
    resid_cols = jnp.concatenate([resid_t[pl.ds(s, rows), :] for s in starts], 0)
    counted = dot(mask_cols.astype(BF16), mask_own.astype(BF16), LAST_DIMS)
    factor_t = resid_cols[:, :1] * resid_own / counted
    factor_ref[...] = factor_t.T
    bias_sum = jnp.zeros((1, cot_ref.shape[2]), F32)
    for i in range(rows):
        cot = jnp.concatenate([cot_ref[i, pl.ds(s, rows), :] for s in starts], 0)
        scaled = (cot.astype(F32) * factor_t[:, i : i + 1]).astype(BF16)
        scaled_ref[i] = scaled
        bias_sum = bias_sum + jnp.sum(scaled.astype(F32), 0, keepdims=True)
    return bias_sum


def send_kernel(
    index_ref, left_ref, mask_ref, resid_ref, cot_ref, w_ref,
    send_ref, far_ref, near_ref, far_factor_ref, near_factor_ref, w2_ref, b_ref, left_t_ref, grad,
    mask_own_ref, wide, resid_t, mask_t,
):
    rows, cols, chan = cot_ref.shape
    proj_width = left_ref.shape[0] // rows
    index = index_ref[0]
    wide[...] = w_ref[...].astype(F32)
    for e in range(proj_width):
        w2_ref[e * proj_width : (e + 1) * proj_width, :] = wide[
            pl.ds(e, proj_width, stride=proj_width), :
        ].astype(BF16)
    left_t_ref[...] = left_ref[...].astype(F32).T.astype(BF16)
    resid_t[...] = jnp.broadcast_to(resid_ref[...].astype(F32), (LANES, cols)).T
    begin = pl.multiple_of(index * rows, rows)
    mask_t[...] = mask_ref[...].astype(F32).T
    mask_own = mask_t[pl.ds(begin, rows), :]
    mask_own_ref[...] = mask_own
    resid_own = resid_t[pl.ds(begin, rows), :].T[:1]
    side = index & 1
    shared = (mask_t, mask_own, resid_t, resid_own, cot_ref)
    far_sum = scale_columns(1 - side, *shared, far_ref, far_factor_ref)
    near_sum = scale_columns(side, *shared, near_ref, near_factor_ref)
    b_ref[...] = far_sum + near_sum
    grad_columns(w2_ref, far_ref, grad)

    def emit(e, slot, value):
        send_ref[slot, e] = value.astype(BF16)

    right_columns(index_ref, left_t_ref, grad, emit)


def keep_kernel(
    index_ref, left_t_ref, w2_ref, near_ref, far_part_ref, keep_ref, send_ref, grad, total
):
    high = keep_ref.shape[0]
    grad_columns(w2_ref, near_ref, grad)

    def emit(e, slot, value):
        total[slot, e] = value

    right_columns(index_ref, left_t_ref, grad, emit)
    keep_ref[...] = total[:high] + far_part_ref[:high].astype(F32)
    send_ref[...] = (total[high:] + far_part_ref[high:].astype(F32)).astype(BF16)


def high_kernel(keep_ref, other_ref, own_ref, *send_refs):
    own_ref[...] = keep_ref[0] + other_ref[0].astype(F32)
    for k, ref in enumerate(send_refs):
        ref[...] = (keep_ref[k + 1] + other_ref[k + 1].astype(F32)).astype(BF16)


def normal_kernel(
    x_ref, gain_ref, shift_ref, right_ref, other_ref,
    normal_ref, inverse_ref, right_copy_ref, other_copy_ref,
):
    seqs, rows, width = x_ref.shape
    right_copy_ref[...] = right_ref[...]
    other_copy_ref[...] = other_ref[...]
    step = 16
    for first in range(0, seqs, step):
        x = x_ref[first : first + step].astype(F32).reshape(step * rows, width)
        xhat, inverse, normalized = normalize(x, gain_ref[...], shift_ref[...])
        span = slice(first * rows, (first + step) * rows)
        normal_ref[span, :width] = normalized
        normal_ref[span, width:] = xhat.astype(BF16)
        inverse_ref[span, :] = inverse


def line_kernel(*refs):
    count = len(refs) // 2
    for k in range(count):
        refs[count + k][...] = refs[k][...]
    refs[-1][...] = jnp.zeros_like(refs[-1])


def place_kernel(index_ref, *refs):
    *blocks, out_ref = refs
    rows = blocks[0].shape[1]
    own = index_ref[0] >> 1
    for rel, ref in enumerate(blocks):
        out_ref[:, pl.ds(pl.multiple_of((own ^ rel) * rows, rows), rows), :] = ref[...]


def outer_columns(left_ref, right_ref, outer):
    proj_width, cols, seqs = right_ref.shape
    rows = left_ref.shape[0] // proj_width
    for e in range(0, proj_width, 2):
        pair = right_ref[e : e + 2].reshape(2 * cols, seqs)
        block = dot(left_ref[...], pair, LAST_DIMS).astype(BF16)
        for i in range(rows):
            for sub in range(2):
                outer[
                    i // 2,
                    (e + sub) * proj_width : (e + sub + 1) * proj_width,
                    (i % 2) * cols : (i % 2 + 1) * cols,
                ] = block[i * proj_width : (i + 1) * proj_width, sub * cols : (sub + 1) * cols]


def weight_columns(left_ref, right_ref, scaled_ref, w_ref, outer):
    rows, cols, chan = scaled_ref.shape
    outer_columns(left_ref, right_ref, outer)
    for p in range(rows // 2):
        w_ref[...] += dot(outer[p], scaled_ref[2 * p : 2 * p + 2].reshape(2 * cols, chan))


def left_columns(grad, right_ref, left_sum_ref):
    proj_width, cols, seqs = right_ref.shape
    for e in range(0, proj_width, 2):
        block = jnp.concatenate([grad[e], grad[e + 1]], 1)
        left_sum_ref[...] += dot(block, right_ref[e : e + 2].reshape(2 * cols, seqs))


def near_kernel(left_ref, scaled_ref, right_ref, w_sum_ref, outer_ref):
    w_sum_ref[...] = jnp.zeros_like(w_sum_ref)
    weight_columns(left_ref, right_ref, scaled_ref, w_sum_ref, outer_ref)


def far_kernel(
    index_ref, left_ref, scaled_ref, w_sum_ref, near_grad_ref, near_ref, far_grad_ref, far_ref,
    outer_ref, left_sum_ref, *refs,
):
    *quarter_refs, total = refs
    total[...] = w_sum_ref[...]
    weight_columns(left_ref, far_ref, scaled_ref, total, outer_ref)
    quarter = quarter_refs[0].shape[0]
    for m, ref in enumerate(quarter_refs):
        begin = pl.multiple_of(((index_ref[0] & 3) ^ m) * quarter, quarter)
        ref[...] = total[pl.ds(begin, quarter), :].astype(BF16)
    left_sum_ref[...] = jnp.zeros_like(left_sum_ref)
    left_columns(near_grad_ref, near_ref, left_sum_ref)
    left_columns(far_grad_ref, far_ref, left_sum_ref)


def pair_kernel(
    index_ref, w2_ref, bias_ref, near_ref, far_ref, near_factor_ref, far_factor_ref, out_ref, w2_t
):
    rows = out_ref.shape[0]
    w2_t[...] = w2_ref[...].astype(F32).T.astype(BF16)
    bias = column_of(bias_ref[...])
    side = index_ref[0] & 1
    for half, outer, factor_ref in (
        (side, near_ref, near_factor_ref),
        (1 - side, far_ref, far_factor_ref),
    ):
        cols = outer.shape[2] // 2
        for p in range(rows // 2):
            projected = dot(w2_t[...], outer[p]) + bias
            for sub in range(2):
                i = 2 * p + sub
                block = projected[:, sub * cols : (sub + 1) * cols] * factor_ref[i : i + 1, :]
                block = block.T.astype(BF16)
                for q in range(cols // rows):
                    begin = pl.multiple_of((2 * q + half) * rows, rows)
                    out_ref[i, pl.ds(begin, rows), :] = block[q * rows : (q + 1) * rows]


def sums_kernel(
    right_own_ref, *refs
):
    *ins, grads_ref, pack_ref, right_sum, gathered = refs
    *right_refs, normal_ref, wl_ref, wr_ref, mask_own_ref, left_sum_ref, b_ref = ins
    seqs = mask_own_ref.shape[1]
    proj_width, rows, _ = right_own_ref.shape
    width = wl_ref.shape[1]
    total = right_own_ref[...]
    for ref in right_refs:
        total = total + ref[...].astype(F32)
    right_sum[...] = total.reshape(proj_width * rows, seqs)
    fill = jnp.zeros((LANES - 2 * proj_width, seqs), F32)
    bias_cols = jnp.zeros((LANES, seqs), F32)
    for i in range(rows):
        block = jnp.concatenate(
            [
                left_sum_ref[i * proj_width : (i + 1) * proj_width, :],
                right_sum[pl.ds(i, proj_width, stride=rows), :],
                fill,
            ],
            0,
        )
        block = (block * mask_own_ref[i : i + 1, :]).astype(BF16).astype(F32)
        bias_cols = bias_cols + block
        gathered[pl.ds(i, seqs, stride=rows), :] = block.T
    grads_ref[...] = gathered[...].astype(BF16)
    used = 2 * proj_width
    products = jnp.zeros((LANES, 2 * width), F32)
    step = 256
    for first in range(0, seqs * rows, step):
        products = products + dot(
            grads_ref[first : first + step, :], normal_ref[first : first + step, :], FIRST_DIMS
        )
    weights = jnp.concatenate([wl_ref[...], wr_ref[...]], 0).astype(F32)
    bias_sum = jnp.sum(bias_cols, 1, keepdims=True)
    gain_sum = jnp.sum(weights * products[:used, width:], 0, keepdims=True)
    shift_sum = jnp.sum(weights * bias_sum[:used], 0, keepdims=True)
    bias_row = jnp.broadcast_to(bias_sum, (LANES, LANES)).T[:1]
    pieces = [products[:used, k : k + LANES] for k in range(0, width, LANES)]
    pieces += [gain_sum[:, k : k + LANES] for k in range(0, width, LANES)]
    pieces += [shift_sum[:, k : k + LANES] for k in range(0, width, LANES)]
    pieces += [bias_row, b_ref[...]]
    pieces += [jnp.zeros((TAIL - 2 - 2 * (width // LANES), LANES), F32)]
    pack_ref[...] = jnp.concatenate(pieces, 0).astype(BF16)


def norm_kernel(normal_ref, inverse_ref, gain_ref, wl_ref, wr_ref, grads_ref, out_ref, weights):
    seqs, rows, width = out_ref.shape
    proj_width = wl_ref.shape[0]
    weights[...] = jnp.zeros_like(weights)
    weights[:proj_width, :] = wl_ref[...]
    weights[proj_width : 2 * proj_width, :] = wr_ref[...]
    step = 16
    for first in range(0, seqs, step):
        span = slice(first * rows, (first + step) * rows)
        xhat = normal_ref[span, width:].astype(F32)
        g = dot(grads_ref[span, :], weights[...]) * gain_ref[...]
        result = (
            g - jnp.mean(g, -1, keepdims=True) - xhat * jnp.mean(g * xhat, -1, keepdims=True)
        ) * inverse_ref[span, :]
        out_ref[first : first + step] = result.astype(BF16).reshape(step, rows, width)


def tree_sum(values):
    values = [value.astype(F32) for value in values]
    while len(values) > 1:
        values = [a + b for a, b in zip(values[::2], values[1::2])]
    return values[0]


def merge_kernel(*refs):
    *ins, out_ref = refs
    out_ref[...] = tree_sum([ref[...] for ref in ins]).astype(BF16)


def join_kernel(own_ref, other_ref, out_ref):
    out_ref[0] = own_ref[...]
    out_ref[1] = other_ref[...]


def weight_kernel(index_ref, own_ref, other_ref, out_ref, placed):
    quarter = own_ref.shape[1]
    proj_width = math.isqrt(out_ref.shape[0])
    for core, ref in enumerate((own_ref, other_ref)):
        for side in range(2):
            begin = pl.multiple_of(((index_ref[0] & 3) ^ (core + 2 * side)) * quarter, quarter)
            placed[pl.ds(begin, quarter), :] = ref[side].astype(F32)
    for c in range(proj_width):
        out_ref[c * proj_width : (c + 1) * proj_width, :] = placed[
            pl.ds(c, proj_width, stride=proj_width), :
        ]


def unpack_kernel(
    own_ref, other_ref, wl_ref, bl_ref, wr_ref, br_ref, b_ref, gain_ref, shift_ref
):
    proj_width, width = wl_ref.shape
    used = 2 * proj_width
    parts = width // LANES
    total = tree_sum([own_ref[...], other_ref[...]])
    tail = total[parts * used :]
    for k in range(parts):
        span = slice(k * LANES, (k + 1) * LANES)
        wl_ref[:, span] = total[k * used : k * used + proj_width]
        wr_ref[:, span] = total[k * used + proj_width : (k + 1) * used]
        gain_ref[:, span] = tail[k : k + 1]
        shift_ref[:, span] = tail[parts + k : parts + k + 1]
    bl_ref[...] = tail[2 * parts : 2 * parts + 1, :proj_width]
    br_ref[...] = tail[2 * parts : 2 * parts + 1, proj_width:used]
    b_ref[...] = tail[2 * parts + 1 : 2 * parts + 2, :]


def body(
    devices,
    alignment_activations,
    alignment_row_mask,
    residue_mask_vector,
    layer_norm_gain,
    layer_norm_bias,
    left_weight,
    left_bias,
    right_weight,
    right_bias,
    output_weight,
    output_bias,
    pair_update_cotangent,
):
    seqs, rows, width = alignment_activations.shape
    cols = alignment_row_mask.shape[1]
    proj_width = left_weight.shape[1]
    pair_width, chan = output_weight.shape
    high = devices // 4
    half = cols // 2
    quarter = pair_width // 4
    flat = rows * proj_width
    index = lax.axis_index("res").astype(jnp.int32).reshape(1)
    gain = layer_norm_gain.reshape(1, width)
    shift = layer_norm_bias.reshape(1, width)
    wl, wr = left_weight.T, right_weight.T
    piece = (proj_width, rows, seqs)

    def swap(value, rel):
        return lax.ppermute(value, "res", [(d, d ^ rel) for d in range(devices)])

    slab = (high,) + piece
    left, right = call(
        project_kernel,
        (shape((flat, seqs), BF16), shape(piece, BF16)),
        (index, alignment_activations, alignment_row_mask, gain, shift, wl, wr)
        + (left_bias.reshape(1, proj_width), right_bias.reshape(1, proj_width)),
        (
            pltpu.VMEM((seqs * rows, LANES), F32),
            pltpu.VMEM((flat, seqs), F32),
            pltpu.VMEM((LANES, width), BF16),
            pltpu.VMEM((cols, seqs), F32),
        ),
        us=4,
        fetched=tuple(range(1, 9)),
        grant=60 * MIB,
    )
    blocks = {0: right, 2: swap(right, 2)}
    for k in range(2, high):
        blocks[4 * k] = swap(right, 4 * k)
    grad_shape = shape((proj_width, flat, half), BF16)
    outer_shape = shape((rows // 2, pair_width, 2 * half), BF16)
    send, far, near, far_factor, near_factor, w2, b_part, left_t, far_grad, mask_own = call(
        send_kernel,
        (
            shape((2 * high,) + piece, BF16),
            shape((rows, half, chan), BF16),
            shape((rows, half, chan), BF16),
            shape((rows, half), F32),
            shape((rows, half), F32),
            shape((pair_width, chan), BF16),
            shape((1, chan), F32),
            shape((seqs, flat), BF16),
            grad_shape,
            shape((rows, seqs), F32),
        ),
        (
            index,
            left,
            alignment_row_mask,
            residue_mask_vector.reshape(1, cols),
            pair_update_cotangent,
            output_weight,
        ),
        (
            pltpu.VMEM((pair_width, chan), F32),
            pltpu.VMEM((cols, LANES), F32),
            pltpu.VMEM((cols, seqs), F32),
        ),
        us=6,
    )
    keep, send, near_grad = call(
        keep_kernel,
        (shape(slab, F32), shape(slab, BF16), grad_shape),
        (index, left_t, w2, near, swap(send, 1)),
        (pltpu.VMEM((2 * high,) + piece, F32),),
        us=4,
    )
    normal, inverse, right_copy, other_copy, normal_token = call(
        normal_kernel,
        (shape((seqs * rows, 2 * width), BF16), shape((seqs * rows, 1), F32))
        + (shape(piece, BF16),) * 2,
        (alignment_activations, gain, shift, right, blocks[2]),
        scalars=0,
        us=10,
        after=(keep,),
        token=True,
    )
    blocks[4] = swap(right_copy, 4)
    blocks[6] = swap(other_copy, 4)
    blocks[10] = swap(other_copy, 8)
    line = call(
        line_kernel,
        (shape(piece, BF16),) * (high - 3) + (shape((8, LANES), F32),),
        tuple(blocks[4 * k] for k in range(3, high)),
        scalars=0,
        us=0.1,
        after=(normal_token, blocks[8]),
    )
    for k in range(3, high):
        blocks[4 * k + 2] = swap(line[k - 3], 2)
    right_own, *sends = call(
        high_kernel,
        (shape(piece, F32),) + (shape(piece, BF16),) * (high - 1),
        (keep, swap(send, 2)),
        scalars=0,
        us=10,
        after=(line[-1], blocks[4], blocks[10]),
    )
    right_parts = tuple(swap(sends[k - 1], 4 * k) for k in range(high - 1, 0, -1))
    right_near = call(
        place_kernel,
        shape((proj_width, half, seqs), BF16),
        (index,) + tuple(blocks[rel] for rel in range(0, devices, 2)),
        after=(right_own,),
    )
    right_far = swap(right_near, 1)
    near_w, near_outer = call(
        near_kernel,
        (shape((pair_width, chan), F32), outer_shape),
        (left, near, right_near),
        scalars=0,
        us=100,
    )
    far_outer, left_sum, w_own, *w_sends = call(
        far_kernel,
        (outer_shape, shape((flat, seqs), F32)) + (shape((quarter, chan), BF16),) * 4,
        (index, left, far, near_w, near_grad, right_near, far_grad, right_far),
        (pltpu.VMEM((pair_width, chan), F32),),
        us=0.02,
    )
    distances = [devices // 2 >> n for n in range(high.bit_length() - 1)]
    weights = call(
        merge_kernel,
        shape((quarter, chan), BF16),
        (w_own,) + tuple(swap(value, m + 1) for m, value in enumerate(w_sends)),
        scalars=0,
        us=0.1,
        after=right_parts,
    )
    for distance in distances:
        weights = call(
            merge_kernel,
            shape((quarter, chan), BF16),
            (weights, swap(weights, distance)),
            scalars=0,
            us=0.1,
        )
    weights = call(
        join_kernel,
        shape((2, quarter, chan), BF16),
        (weights, swap(weights, 2)),
        scalars=0,
        us=0.1,
    )
    w_out_grad = call(
        weight_kernel,
        shape((pair_width, chan), F32),
        (index, weights, swap(weights, 1)),
        (pltpu.VMEM((pair_width, chan), F32),),
        us=0.1,
    )

    pack_shape = shape((2 * proj_width * (width // LANES) + TAIL, LANES), BF16)
    grads, pack = call(
        sums_kernel,
        (shape((seqs * rows, LANES), BF16), pack_shape),
        (right_own,) + right_parts + (normal, wl, wr, mask_own, left_sum, b_part),
        (pltpu.VMEM((flat, seqs), F32), pltpu.VMEM((seqs * rows, LANES), F32)),
        scalars=0,
        us=2,
    )
    alignment_gradient, norm_token = call(
        norm_kernel,
        shape((seqs, rows, width), BF16),
        (normal, inverse, gain, wl, wr, grads),
        (pltpu.VMEM((LANES, width), BF16),),
        scalars=0,
        us=2,
        token=True,
    )
    pair, pair_token = call(
        pair_kernel,
        shape((rows, cols, chan), BF16),
        (index, w2, output_bias.reshape(1, chan), near_outer, far_outer, near_factor, far_factor),
        (pltpu.VMEM((chan, pair_width), BF16),),
        us=2,
        after=(norm_token,),
        token=True,
    )
    tokens = [norm_token] + [pair_token] * len(distances)
    for distance, token in zip(distances + [2], tokens):
        pack = call(
            merge_kernel,
            pack_shape,
            (pack, swap(pack, distance)),
            scalars=0,
            us=0.1,
            after=(token,),
        )
    w_left, b_left, w_right, b_right, b_out, gain_grad, shift_grad = call(
        unpack_kernel,
        (
            shape((proj_width, width), F32),
            shape((1, proj_width), F32),
            shape((proj_width, width), F32),
            shape((1, proj_width), F32),
            shape((1, chan), F32),
            shape((1, width), F32),
            shape((1, width), F32),
        ),
        (pack, swap(pack, 1)),
        scalars=0,
    )
    return (
        pair,
        alignment_gradient,
        w_left.T,
        b_left.reshape(-1),
        w_right.T,
        b_right.reshape(-1),
        w_out_grad,
        b_out.reshape(-1),
        gain_grad.reshape(-1),
        shift_grad.reshape(-1),
    )


def solution(mesh):
    return jax.shard_map(
        functools.partial(body, mesh.shape["res"]),
        mesh=mesh,
        in_specs=(
            P(None, ("grp", "res"), None),
            P(None, "grp"),
            P("grp"),
            P(),
            P(),
            P(),
            P(),
            P(),
            P(),
            P(),
            P(),
            P(("grp", "res"), None, None),
        ),
        out_specs=(
            P(("grp", "res"), None, None),
            P(None, ("grp", "res"), None),
            P("grp", None),
            P("grp"),
            P("grp", None),
            P("grp"),
            P("grp", None),
            P("grp"),
            P("grp"),
            P("grp"),
        ),
        check_vma=False,
    )
```

```python
import functools
import math

import jax
import jax.numpy as jnp
from jax import lax
from jax.experimental import pallas as pl
from jax.experimental.pallas import tpu as pltpu
from jax.sharding import PartitionSpec as P

EPS = 1e-05
LAST_DIMS = (((1,), (1,)), ((), ()))
FIRST_DIMS = (((0,), (0,)), ((), ()))
MIB = 1024 * 1024
LANES = 128
TAIL = 16
F32 = jnp.float32
BF16 = jnp.bfloat16


def tiled_bytes(dims, dtype):
    dims = tuple(dims)
    lanes = -(-dims[-1] // LANES) * LANES
    sublanes = -(-(dims[-2] if len(dims) > 1 else 1) // 16) * 16
    return math.prod(dims[:-2]) * sublanes * lanes * jnp.dtype(dtype).itemsize


def call(
    kernel, out_shape, args, scratch=(), scalars=1, us=1.0, after=(), fetched=(), token=False, grant=0, **static
):
    count = len(args)
    specs = [pl.BlockSpec(memory_space=pl.ANY)] * len(after)
    specs += [pl.BlockSpec(memory_space=pltpu.SMEM)] * scalars
    for k in range(scalars, count):
        specs.append(pl.BlockSpec(memory_space=pltpu.HBM if k in fetched else pltpu.VMEM))
    outs = list(out_shape) if isinstance(out_shape, (tuple, list)) else [out_shape]
    if token:
        outs.append(shape((8, LANES), F32))
    held = list(args[scalars:]) + outs + list(scratch)
    need = sum(tiled_bytes(value.shape, value.dtype) for value in held)
    places = [pltpu.VMEM(args[k].shape, args[k].dtype) for k in fetched]
    semaphores = [pltpu.SemaphoreType.DMA((len(fetched),))] if fetched else []

    def run(*refs):
        ins = list(refs[len(after) : len(after) + count])
        rest = list(refs[len(after) + count :])
        if fetched:
            *rest, done = rest
            held_refs = rest[-len(fetched) :]
            rest = rest[: -len(fetched)]
            copies = [
                pltpu.make_async_copy(ins[k], ref, done.at[n])
                for n, (k, ref) in enumerate(zip(fetched, held_refs))
            ]
            for copy in copies:
                copy.start()
            for k, ref, copy in zip(fetched, held_refs, copies):
                ins[k] = Fetched(ref, copy)
        if token:
            rest.pop(len(outs) - 1)[...] = jnp.zeros((8, LANES), F32)
        kernel(*ins, *rest, **static)

    result = pl.pallas_call(
        run,
        name=kernel.__name__,
        out_shape=tuple(outs),
        in_specs=specs,
        out_specs=tuple([pl.BlockSpec(memory_space=pltpu.VMEM)] * len(outs)),
        scratch_shapes=list(scratch) + places + semaphores,
        compiler_params=pltpu.CompilerParams(vmem_limit_bytes=grant or min(need + 6 * MIB, 56 * MIB)),
        cost_estimate=pl.CostEstimate(
            flops=int(us * 1.1e9), bytes_accessed=int(us * 1e5), transcendentals=0
        ),
    )(*after, *args)
    return result if len(outs) > 1 else result[0]


class Fetched:
    def __init__(self, ref, copy):
        self.ref, self.copy, self.shape = ref, copy, ref.shape

    def __getitem__(self, index):
        if self.copy is not None:
            self.copy.wait()
            self.copy = None
        return self.ref[index]


def shape(dims, dtype):
    return jax.ShapeDtypeStruct(tuple(dims), dtype)


def dot(a, b, dims=(((1,), (0,)), ((), ()))):
    return lax.dot_general(a, b, dims, preferred_element_type=F32)


def normalize(x, gain, shift):
    centered = x - jnp.mean(x, -1, keepdims=True)
    inverse = lax.rsqrt(jnp.mean(centered * centered, -1, keepdims=True) + EPS)
    xhat = centered * inverse
    return xhat, inverse, (xhat * gain + shift).astype(BF16)


def column_of(row):
    return jnp.broadcast_to(row, (8, row.shape[1])).T[:, :1]


def project_kernel(
    index_ref, x_ref, mask_ref, gain_ref, shift_ref, wl_ref, wr_ref, bl_ref, br_ref,
    left_ref, right_ref, proj, right_rows, weights, mask_t,
):
    seqs, rows, width = x_ref.shape
    proj_width = right_ref.shape[0]
    begin = pl.multiple_of(index_ref[0] * rows, rows)
    weights[:proj_width, :] = wl_ref[...]
    weights[proj_width : 2 * proj_width, :] = wr_ref[...]
    weights[2 * proj_width :, :] = jnp.zeros((LANES - 2 * proj_width, width), BF16)
    bias_left = column_of(bl_ref[...])
    bias_right = column_of(br_ref[...])
    step = 16
    for first in range(0, seqs, step):
        x = x_ref[first : first + step].astype(F32).reshape(step * rows, width)
        normalized = normalize(x, gain_ref[...], shift_ref[...])[2]
        proj[first * rows : (first + step) * rows, :] = dot(normalized, weights[...], LAST_DIMS)
    mask_t[...] = mask_ref[...].astype(F32).T
    mask_own = mask_t[pl.ds(begin, rows), :]
    for i in range(rows):
        block = proj[pl.ds(i, seqs, stride=rows), :].T
        mask_row = mask_own[i : i + 1, :]
        span = slice(i * proj_width, (i + 1) * proj_width)
        left_ref[span, :] = ((block[:proj_width] + bias_left) * mask_row).astype(BF16)
        right_rows[span, :] = (block[proj_width : 2 * proj_width] + bias_right) * mask_row
    for e in range(proj_width):
        right_ref[e] = right_rows[pl.ds(e, rows, stride=proj_width), :].astype(BF16)


def grad_columns(w2_ref, scaled_ref, grad):
    rows, cols, chan = scaled_ref.shape
    proj_width = grad.shape[0]
    for i in range(0, rows, 2):
        pair = scaled_ref[i : i + 2].reshape(2 * cols, chan)
        block = dot(w2_ref[...], pair, LAST_DIMS).astype(BF16)
        for e in range(proj_width):
            for sub in range(2):
                grad[e, (i + sub) * proj_width : (i + sub + 1) * proj_width, :] = block[
                    e * proj_width : (e + 1) * proj_width, sub * cols : (sub + 1) * cols
                ]


def right_columns(index_ref, left_t, grad, emit):
    proj_width, _, cols = grad.shape
    rows = left_t.shape[1] // proj_width
    high = cols // rows // 2
    own = index_ref[0] >> 1
    for e in range(0, proj_width, 2):
        block = jnp.concatenate([grad[e], grad[e + 1]], 1)
        sums = dot(left_t[...], block)
        for sub in range(2):
            part = sums[:, sub * cols : (sub + 1) * cols].T
            for q in range(2 * high):
                rel = q ^ own
                emit(e + sub, (rel & 1) * high + (rel >> 1), part[q * rows : (q + 1) * rows])


def scale_columns(half, mask_t_ref, mask_own, resid_t, resid_own, cot_ref, scaled_ref, factor_ref):
    rows = cot_ref.shape[0]
    cols = scaled_ref.shape[1]
    starts = [
        pl.multiple_of((2 * q + half) * rows, rows) for q in range(cols // rows)
    ]
    mask_cols = jnp.concatenate([mask_t_ref[pl.ds(s, rows), :] for s in starts], 0)
    resid_cols = jnp.concatenate([resid_t[pl.ds(s, rows), :] for s in starts], 0)
    counted = dot(mask_cols.astype(BF16), mask_own.astype(BF16), LAST_DIMS)
    factor_t = resid_cols[:, :1] * resid_own / counted
    factor_ref[...] = factor_t.T
    bias_sum = jnp.zeros((1, cot_ref.shape[2]), F32)
    for i in range(rows):
        cot = jnp.concatenate([cot_ref[i, pl.ds(s, rows), :] for s in starts], 0)
        scaled = (cot.astype(F32) * factor_t[:, i : i + 1]).astype(BF16)
        scaled_ref[i] = scaled
        bias_sum = bias_sum + jnp.sum(scaled.astype(F32), 0, keepdims=True)
    return bias_sum


def send_kernel(
    index_ref, left_ref, mask_ref, resid_ref, cot_ref, w_ref,
    send_ref, far_ref, near_ref, far_factor_ref, near_factor_ref, w2_ref, b_ref, left_t_ref, grad,
    mask_own_ref, wide, resid_t, mask_t,
):
    rows, cols, chan = cot_ref.shape
    proj_width = left_ref.shape[0] // rows
    index = index_ref[0]
    wide[...] = w_ref[...].astype(F32)
    for e in range(proj_width):
        w2_ref[e * proj_width : (e + 1) * proj_width, :] = wide[
            pl.ds(e, proj_width, stride=proj_width), :
        ].astype(BF16)
    left_t_ref[...] = left_ref[...].astype(F32).T.astype(BF16)
    resid_t[...] = jnp.broadcast_to(resid_ref[...].astype(F32), (LANES, cols)).T
    begin = pl.multiple_of(index * rows, rows)
    mask_t[...] = mask_ref[...].astype(F32).T
    mask_own = mask_t[pl.ds(begin, rows), :]
    mask_own_ref[...] = mask_own
    resid_own = resid_t[pl.ds(begin, rows), :].T[:1]
    side = index & 1
    shared = (mask_t, mask_own, resid_t, resid_own, cot_ref)
    far_sum = scale_columns(1 - side, *shared, far_ref, far_factor_ref)
    near_sum = scale_columns(side, *shared, near_ref, near_factor_ref)
    b_ref[...] = far_sum + near_sum
    grad_columns(w2_ref, far_ref, grad)

    def emit(e, slot, value):
        send_ref[slot, e] = value.astype(BF16)

    right_columns(index_ref, left_t_ref, grad, emit)


def keep_kernel(
    index_ref, left_t_ref, w2_ref, near_ref, far_part_ref, keep_ref, send_ref, grad, total
):
    high = keep_ref.shape[0]
    grad_columns(w2_ref, near_ref, grad)

    def emit(e, slot, value):
        total[slot, e] = value

    right_columns(index_ref, left_t_ref, grad, emit)
    keep_ref[...] = total[:high] + far_part_ref[:high].astype(F32)
    send_ref[...] = (total[high:] + far_part_ref[high:].astype(F32)).astype(BF16)


def high_kernel(keep_ref, other_ref, own_ref, *send_refs):
    own_ref[...] = keep_ref[0] + other_ref[0].astype(F32)
    for k, ref in enumerate(send_refs):
        ref[...] = (keep_ref[k + 1] + other_ref[k + 1].astype(F32)).astype(BF16)


def normal_kernel(
    x_ref, gain_ref, shift_ref, right_ref, other_ref,
    normal_ref, inverse_ref, right_copy_ref, other_copy_ref,
):
    seqs, rows, width = x_ref.shape
    right_copy_ref[...] = right_ref[...]
    other_copy_ref[...] = other_ref[...]
    step = 16
    for first in range(0, seqs, step):
        x = x_ref[first : first + step].astype(F32).reshape(step * rows, width)
        xhat, inverse, normalized = normalize(x, gain_ref[...], shift_ref[...])
        span = slice(first * rows, (first + step) * rows)
        normal_ref[span, :width] = normalized
        normal_ref[span, width:] = xhat.astype(BF16)
        inverse_ref[span, :] = inverse


def line_kernel(*refs):
    count = len(refs) // 2
    for k in range(count):
        refs[count + k][...] = refs[k][...]
    refs[-1][...] = jnp.zeros_like(refs[-1])


def place_kernel(index_ref, *refs):
    *blocks, out_ref = refs
    rows = blocks[0].shape[1]
    own = index_ref[0] >> 1
    for rel, ref in enumerate(blocks):
        out_ref[:, pl.ds(pl.multiple_of((own ^ rel) * rows, rows), rows), :] = ref[...]


def outer_columns(left_ref, right_ref, outer):
    proj_width, cols, seqs = right_ref.shape
    rows = left_ref.shape[0] // proj_width
    for e in range(0, proj_width, 2):
        pair = right_ref[e : e + 2].reshape(2 * cols, seqs)
        block = dot(left_ref[...], pair, LAST_DIMS).astype(BF16)
        for i in range(rows):
            for sub in range(2):
                outer[
                    i // 2,
                    (e + sub) * proj_width : (e + sub + 1) * proj_width,
                    (i % 2) * cols : (i % 2 + 1) * cols,
                ] = block[i * proj_width : (i + 1) * proj_width, sub * cols : (sub + 1) * cols]


def weight_columns(left_ref, right_ref, scaled_ref, w_ref, outer):
    rows, cols, chan = scaled_ref.shape
    outer_columns(left_ref, right_ref, outer)
    for p in range(rows // 2):
        w_ref[...] += dot(outer[p], scaled_ref[2 * p : 2 * p + 2].reshape(2 * cols, chan))


def left_columns(grad, right_ref, left_sum_ref):
    proj_width, cols, seqs = right_ref.shape
    for e in range(0, proj_width, 2):
        block = jnp.concatenate([grad[e], grad[e + 1]], 1)
        left_sum_ref[...] += dot(block, right_ref[e : e + 2].reshape(2 * cols, seqs))


def near_kernel(left_ref, scaled_ref, right_ref, w_sum_ref, outer_ref):
    w_sum_ref[...] = jnp.zeros_like(w_sum_ref)
    weight_columns(left_ref, right_ref, scaled_ref, w_sum_ref, outer_ref)


def far_kernel(
    index_ref, left_ref, scaled_ref, w_sum_ref, near_grad_ref, near_ref, far_grad_ref, far_ref,
    outer_ref, left_sum_ref, *refs,
):
    *quarter_refs, total = refs
    total[...] = w_sum_ref[...]
    weight_columns(left_ref, far_ref, scaled_ref, total, outer_ref)
    quarter = quarter_refs[0].shape[0]
    for m, ref in enumerate(quarter_refs):
        begin = pl.multiple_of(((index_ref[0] & 3) ^ m) * quarter, quarter)
        ref[...] = total[pl.ds(begin, quarter), :].astype(BF16)
    left_sum_ref[...] = jnp.zeros_like(left_sum_ref)
    left_columns(near_grad_ref, near_ref, left_sum_ref)
    left_columns(far_grad_ref, far_ref, left_sum_ref)


def pair_kernel(
    index_ref, w2_ref, bias_ref, near_ref, far_ref, near_factor_ref, far_factor_ref, out_ref, w2_t
):
    rows = out_ref.shape[0]
    w2_t[...] = w2_ref[...].astype(F32).T.astype(BF16)
    bias = column_of(bias_ref[...])
    side = index_ref[0] & 1
    for half, outer, factor_ref in (
        (side, near_ref, near_factor_ref),
        (1 - side, far_ref, far_factor_ref),
    ):
        cols = outer.shape[2] // 2
        for p in range(rows // 2):
            projected = dot(w2_t[...], outer[p]) + bias
            for sub in range(2):
                i = 2 * p + sub
                block = projected[:, sub * cols : (sub + 1) * cols] * factor_ref[i : i + 1, :]
                block = block.T.astype(BF16)
                for q in range(cols // rows):
                    begin = pl.multiple_of((2 * q + half) * rows, rows)
                    out_ref[i, pl.ds(begin, rows), :] = block[q * rows : (q + 1) * rows]


def sums_kernel(
    right_own_ref, *refs
):
    *ins, grads_ref, pack_ref, right_sum, gathered = refs
    *right_refs, normal_ref, wl_ref, wr_ref, mask_own_ref, left_sum_ref, b_ref = ins
    seqs = mask_own_ref.shape[1]
    proj_width, rows, _ = right_own_ref.shape
    width = wl_ref.shape[1]
    total = right_own_ref[...]
    for ref in right_refs:
        total = total + ref[...].astype(F32)
    right_sum[...] = total.reshape(proj_width * rows, seqs)
    fill = jnp.zeros((LANES - 2 * proj_width, seqs), F32)
    bias_cols = jnp.zeros((LANES, seqs), F32)
    for i in range(rows):
        block = jnp.concatenate(
            [
                left_sum_ref[i * proj_width : (i + 1) * proj_width, :],
                right_sum[pl.ds(i, proj_width, stride=rows), :],
                fill,
            ],
            0,
        )
        block = (block * mask_own_ref[i : i + 1, :]).astype(BF16).astype(F32)
        bias_cols = bias_cols + block
        gathered[pl.ds(i, seqs, stride=rows), :] = block.T
    grads_ref[...] = gathered[...].astype(BF16)
    used = 2 * proj_width
    products = jnp.zeros((LANES, 2 * width), F32)
    step = 256
    for first in range(0, seqs * rows, step):
        products = products + dot(
            grads_ref[first : first + step, :], normal_ref[first : first + step, :], FIRST_DIMS
        )
    weights = jnp.concatenate([wl_ref[...], wr_ref[...]], 0).astype(F32)
    bias_sum = jnp.sum(bias_cols, 1, keepdims=True)
    gain_sum = jnp.sum(weights * products[:used, width:], 0, keepdims=True)
    shift_sum = jnp.sum(weights * bias_sum[:used], 0, keepdims=True)
    bias_row = jnp.broadcast_to(bias_sum, (LANES, LANES)).T[:1]
    pieces = [products[:used, k : k + LANES] for k in range(0, width, LANES)]
    pieces += [gain_sum[:, k : k + LANES] for k in range(0, width, LANES)]
    pieces += [shift_sum[:, k : k + LANES] for k in range(0, width, LANES)]
    pieces += [bias_row, b_ref[...]]
    pieces += [jnp.zeros((TAIL - 2 - 2 * (width // LANES), LANES), F32)]
    pack_ref[...] = jnp.concatenate(pieces, 0).astype(BF16)


def norm_kernel(normal_ref, inverse_ref, gain_ref, wl_ref, wr_ref, grads_ref, out_ref, weights):
    seqs, rows, width = out_ref.shape
    proj_width = wl_ref.shape[0]
    weights[...] = jnp.zeros_like(weights)
    weights[:proj_width, :] = wl_ref[...]
    weights[proj_width : 2 * proj_width, :] = wr_ref[...]
    step = 16
    for first in range(0, seqs, step):
        span = slice(first * rows, (first + step) * rows)
        xhat = normal_ref[span, width:].astype(F32)
        g = dot(grads_ref[span, :], weights[...]) * gain_ref[...]
        result = (
            g - jnp.mean(g, -1, keepdims=True) - xhat * jnp.mean(g * xhat, -1, keepdims=True)
        ) * inverse_ref[span, :]
        out_ref[first : first + step] = result.astype(BF16).reshape(step, rows, width)


def tree_sum(values):
    values = [value.astype(F32) for value in values]
    while len(values) > 1:
        values = [a + b for a, b in zip(values[::2], values[1::2])]
    return values[0]


def merge_kernel(*refs):
    *ins, out_ref = refs
    out_ref[...] = tree_sum([ref[...] for ref in ins]).astype(BF16)


def join_kernel(own_ref, other_ref, out_ref):
    out_ref[0] = own_ref[...]
    out_ref[1] = other_ref[...]


def weight_kernel(index_ref, own_ref, other_ref, out_ref, placed):
    quarter = own_ref.shape[1]
    proj_width = math.isqrt(out_ref.shape[0])
    for core, ref in enumerate((own_ref, other_ref)):
        for side in range(2):
            begin = pl.multiple_of(((index_ref[0] & 3) ^ (core + 2 * side)) * quarter, quarter)
            placed[pl.ds(begin, quarter), :] = ref[side].astype(F32)
    for c in range(proj_width):
        out_ref[c * proj_width : (c + 1) * proj_width, :] = placed[
            pl.ds(c, proj_width, stride=proj_width), :
        ]


def unpack_kernel(
    own_ref, other_ref, wl_ref, bl_ref, wr_ref, br_ref, b_ref, gain_ref, shift_ref
):
    proj_width, width = wl_ref.shape
    used = 2 * proj_width
    parts = width // LANES
    total = tree_sum([own_ref[...], other_ref[...]])
    tail = total[parts * used :]
    for k in range(parts):
        span = slice(k * LANES, (k + 1) * LANES)
        wl_ref[:, span] = total[k * used : k * used + proj_width]
        wr_ref[:, span] = total[k * used + proj_width : (k + 1) * used]
        gain_ref[:, span] = tail[k : k + 1]
        shift_ref[:, span] = tail[parts + k : parts + k + 1]
    bl_ref[...] = tail[2 * parts : 2 * parts + 1, :proj_width]
    br_ref[...] = tail[2 * parts : 2 * parts + 1, proj_width:used]
    b_ref[...] = tail[2 * parts + 1 : 2 * parts + 2, :]


def body(
    devices,
    alignment_activations,
    alignment_row_mask,
    residue_mask_vector,
    layer_norm_gain,
    layer_norm_bias,
    left_weight,
    left_bias,
    right_weight,
    right_bias,
    output_weight,
    output_bias,
    pair_update_cotangent,
):
    seqs, rows, width = alignment_activations.shape
    cols = alignment_row_mask.shape[1]
    proj_width = left_weight.shape[1]
    pair_width, chan = output_weight.shape
    high = devices // 4
    half = cols // 2
    quarter = pair_width // 4
    flat = rows * proj_width
    index = lax.axis_index("res").astype(jnp.int32).reshape(1)
    gain = layer_norm_gain.reshape(1, width)
    shift = layer_norm_bias.reshape(1, width)
    wl, wr = left_weight.T, right_weight.T
    piece = (proj_width, rows, seqs)

    def swap(value, rel):
        return lax.ppermute(value, "res", [(d, d ^ rel) for d in range(devices)])

    slab = (high,) + piece
    left, right = call(
        project_kernel,
        (shape((flat, seqs), BF16), shape(piece, BF16)),
        (index, alignment_activations, alignment_row_mask, gain, shift, wl, wr)
        + (left_bias.reshape(1, proj_width), right_bias.reshape(1, proj_width)),
        (
            pltpu.VMEM((seqs * rows, LANES), F32),
            pltpu.VMEM((flat, seqs), F32),
            pltpu.VMEM((LANES, width), BF16),
            pltpu.VMEM((cols, seqs), F32),
        ),
        us=4,
        fetched=tuple(range(1, 9)),
        grant=60 * MIB,
    )
    blocks = {0: right, 2: swap(right, 2)}
    for k in range(2, high):
        blocks[4 * k] = swap(right, 4 * k)
    grad_shape = shape((proj_width, flat, half), BF16)
    outer_shape = shape((rows // 2, pair_width, 2 * half), BF16)
    send, far, near, far_factor, near_factor, w2, b_part, left_t, far_grad, mask_own = call(
        send_kernel,
        (
            shape((2 * high,) + piece, BF16),
            shape((rows, half, chan), BF16),
            shape((rows, half, chan), BF16),
            shape((rows, half), F32),
            shape((rows, half), F32),
            shape((pair_width, chan), BF16),
            shape((1, chan), F32),
            shape((seqs, flat), BF16),
            grad_shape,
            shape((rows, seqs), F32),
        ),
        (
            index,
            left,
            alignment_row_mask,
            residue_mask_vector.reshape(1, cols),
            pair_update_cotangent,
            output_weight,
        ),
        (
            pltpu.VMEM((pair_width, chan), F32),
            pltpu.VMEM((cols, LANES), F32),
            pltpu.VMEM((cols, seqs), F32),
        ),
        us=6,
    )
    keep, send, near_grad = call(
        keep_kernel,
        (shape(slab, F32), shape(slab, BF16), grad_shape),
        (index, left_t, w2, near, swap(send, 1)),
        (pltpu.VMEM((2 * high,) + piece, F32),),
        us=4,
    )
    normal, inverse, right_copy, other_copy, normal_token = call(
        normal_kernel,
        (shape((seqs * rows, 2 * width), BF16), shape((seqs * rows, 1), F32))
        + (shape(piece, BF16),) * 2,
        (alignment_activations, gain, shift, right, blocks[2]),
        scalars=0,
        us=10,
        after=(keep,),
        token=True,
    )
    blocks[4] = swap(right_copy, 4)
    blocks[6] = swap(other_copy, 4)
    blocks[10] = swap(other_copy, 8)
    line = call(
        line_kernel,
        (shape(piece, BF16),) * (high - 3) + (shape((8, LANES), F32),),
        tuple(blocks[4 * k] for k in range(3, high)),
        scalars=0,
        us=0.1,
        after=(normal_token, blocks[8]),
    )
    for k in range(3, high):
        blocks[4 * k + 2] = swap(line[k - 3], 2)
    right_own, *sends = call(
        high_kernel,
        (shape(piece, F32),) + (shape(piece, BF16),) * (high - 1),
        (keep, swap(send, 2)),
        scalars=0,
        us=10,
        after=(line[-1], blocks[4], blocks[10]),
    )
    right_parts = tuple(swap(sends[k - 1], 4 * k) for k in range(high - 1, 0, -1))
    right_near = call(
        place_kernel,
        shape((proj_width, half, seqs), BF16),
        (index,) + tuple(blocks[rel] for rel in range(0, devices, 2)),
        after=(right_own,),
    )
    right_far = swap(right_near, 1)
    near_w, near_outer = call(
        near_kernel,
        (shape((pair_width, chan), F32), outer_shape),
        (left, near, right_near),
        scalars=0,
        us=100,
    )
    far_outer, left_sum, w_own, *w_sends = call(
        far_kernel,
        (outer_shape, shape((flat, seqs), F32)) + (shape((quarter, chan), BF16),) * 4,
        (index, left, far, near_w, near_grad, right_near, far_grad, right_far),
        (pltpu.VMEM((pair_width, chan), F32),),
        us=0.02,
    )
    pack_shape = shape((2 * proj_width * (width // LANES) + TAIL, LANES), BF16)
    grads, pack = call(
        sums_kernel,
        (shape((seqs * rows, LANES), BF16), pack_shape),
        (right_own,) + right_parts + (normal, wl, wr, mask_own, left_sum, b_part),
        (pltpu.VMEM((flat, seqs), F32), pltpu.VMEM((seqs * rows, LANES), F32)),
        scalars=0,
        us=2,
    )
    pair, pair_token = call(
        pair_kernel,
        shape((rows, cols, chan), BF16),
        (index, w2, output_bias.reshape(1, chan), near_outer, far_outer, near_factor, far_factor),
        (pltpu.VMEM((chan, pair_width), BF16),),
        us=0.02,
        after=(pack,),
        token=True,
    )
    distances = [devices // 2 >> n for n in range(high.bit_length() - 1)]
    packs = [pack]

    def merge_pack(after):
        last = packs[-1]
        packs.append(
            call(
                merge_kernel,
                pack_shape,
                (last, swap(last, (distances + [2])[len(packs) - 1])),
                scalars=0,
                us=0.1,
                after=after,
            )
        )

    merge_pack(())
    weights = call(
        merge_kernel,
        shape((quarter, chan), BF16),
        (w_own,) + tuple(swap(value, m + 1) for m, value in enumerate(w_sends)),
        scalars=0,
        us=0.1,
        after=(pair_token, packs[1]),
    )
    alignment_gradient, norm_token = call(
        norm_kernel,
        shape((seqs, rows, width), BF16),
        (normal, inverse, gain, wl, wr, grads),
        (pltpu.VMEM((LANES, width), BF16),),
        scalars=0,
        us=0.02,
        after=(packs[1],),
        token=True,
    )
    while len(packs) < len(distances) + 2:
        merge_pack(())
    for n, distance in enumerate(distances):
        weights = call(
            merge_kernel,
            shape((quarter, chan), BF16),
            (weights, swap(weights, distance)),
            scalars=0,
            us=0.1,
            after=(norm_token, packs[n + 2]),
        )
    weights = call(
        join_kernel,
        shape((2, quarter, chan), BF16),
        (weights, swap(weights, 2)),
        scalars=0,
        us=0.1,
    )
    w_out_grad = call(
        weight_kernel,
        shape((pair_width, chan), F32),
        (index, weights, swap(weights, 1)),
        (pltpu.VMEM((pair_width, chan), F32),),
        us=0.1,
    )

    w_left, b_left, w_right, b_right, b_out, gain_grad, shift_grad = call(
        unpack_kernel,
        (
            shape((proj_width, width), F32),
            shape((1, proj_width), F32),
            shape((proj_width, width), F32),
            shape((1, proj_width), F32),
            shape((1, chan), F32),
            shape((1, width), F32),
            shape((1, width), F32),
        ),
        (packs[-1], swap(packs[-1], 1)),
        scalars=0,
    )
    return (
        pair,
        alignment_gradient,
        w_left.T,
        b_left.reshape(-1),
        w_right.T,
        b_right.reshape(-1),
        w_out_grad,
        b_out.reshape(-1),
        gain_grad.reshape(-1),
        shift_grad.reshape(-1),
    )


def solution(mesh):
    return jax.shard_map(
        functools.partial(body, mesh.shape["res"]),
        mesh=mesh,
        in_specs=(
            P(None, ("grp", "res"), None),
            P(None, "grp"),
            P("grp"),
            P(),
            P(),
            P(),
            P(),
            P(),
            P(),
            P(),
            P(),
            P(("grp", "res"), None, None),
        ),
        out_specs=(
            P(("grp", "res"), None, None),
            P(None, ("grp", "res"), None),
            P("grp", None),
            P("grp"),
            P("grp", None),
            P("grp"),
            P("grp", None),
            P("grp"),
            P("grp"),
            P("grp"),
        ),
        check_vma=False,
    )
```

```python
import functools
import math

import jax
import jax.numpy as jnp
from jax import lax
from jax.experimental import pallas as pl
from jax.experimental.pallas import tpu as pltpu
from jax.sharding import PartitionSpec as P

EPS = 1e-05
LAST_DIMS = (((1,), (1,)), ((), ()))
FIRST_DIMS = (((0,), (0,)), ((), ()))
MIB = 1024 * 1024
LANES = 128
TAIL = 16
F32 = jnp.float32
BF16 = jnp.bfloat16


def tiled_bytes(dims, dtype):
    dims = tuple(dims)
    lanes = -(-dims[-1] // LANES) * LANES
    sublanes = -(-(dims[-2] if len(dims) > 1 else 1) // 16) * 16
    return math.prod(dims[:-2]) * sublanes * lanes * jnp.dtype(dtype).itemsize


def call(
    kernel, out_shape, args, scratch=(), scalars=1, us=1.0, after=(), fetched=(), token=False, grant=0, **static
):
    count = len(args)
    specs = [pl.BlockSpec(memory_space=pl.ANY)] * len(after)
    specs += [pl.BlockSpec(memory_space=pltpu.SMEM)] * scalars
    for k in range(scalars, count):
        specs.append(pl.BlockSpec(memory_space=pltpu.HBM if k in fetched else pltpu.VMEM))
    outs = list(out_shape) if isinstance(out_shape, (tuple, list)) else [out_shape]
    if token:
        outs.append(shape((8, LANES), F32))
    held = list(args[scalars:]) + outs + list(scratch)
    need = sum(tiled_bytes(value.shape, value.dtype) for value in held)
    places = [pltpu.VMEM(args[k].shape, args[k].dtype) for k in fetched]
    semaphores = [pltpu.SemaphoreType.DMA((len(fetched),))] if fetched else []

    def run(*refs):
        ins = list(refs[len(after) : len(after) + count])
        rest = list(refs[len(after) + count :])
        if fetched:
            *rest, done = rest
            held_refs = rest[-len(fetched) :]
            rest = rest[: -len(fetched)]
            copies = [
                pltpu.make_async_copy(ins[k], ref, done.at[n])
                for n, (k, ref) in enumerate(zip(fetched, held_refs))
            ]
            for copy in copies:
                copy.start()
            for k, ref, copy in zip(fetched, held_refs, copies):
                ins[k] = Fetched(ref, copy)
        if token:
            rest.pop(len(outs) - 1)[...] = jnp.zeros((8, LANES), F32)
        kernel(*ins, *rest, **static)

    result = pl.pallas_call(
        run,
        name=kernel.__name__,
        out_shape=tuple(outs),
        in_specs=specs,
        out_specs=tuple([pl.BlockSpec(memory_space=pltpu.VMEM)] * len(outs)),
        scratch_shapes=list(scratch) + places + semaphores,
        compiler_params=pltpu.CompilerParams(vmem_limit_bytes=grant or min(need + 6 * MIB, 56 * MIB)),
        cost_estimate=pl.CostEstimate(
            flops=int(us * 1.1e9), bytes_accessed=int(us * 1e5), transcendentals=0
        ),
    )(*after, *args)
    return result if len(outs) > 1 else result[0]


class Fetched:
    def __init__(self, ref, copy):
        self.ref, self.copy, self.shape = ref, copy, ref.shape

    def __getitem__(self, index):
        if self.copy is not None:
            self.copy.wait()
            self.copy = None
        return self.ref[index]


def shape(dims, dtype):
    return jax.ShapeDtypeStruct(tuple(dims), dtype)


def dot(a, b, dims=(((1,), (0,)), ((), ()))):
    return lax.dot_general(a, b, dims, preferred_element_type=F32)


def normalize(x, gain, shift):
    centered = x - jnp.mean(x, -1, keepdims=True)
    inverse = lax.rsqrt(jnp.mean(centered * centered, -1, keepdims=True) + EPS)
    xhat = centered * inverse
    return xhat, inverse, (xhat * gain + shift).astype(BF16)


def column_of(row):
    return jnp.broadcast_to(row, (8, row.shape[1])).T[:, :1]


def project_kernel(
    index_ref, x_ref, mask_ref, gain_ref, shift_ref, wl_ref, wr_ref, bl_ref, br_ref,
    left_ref, right_ref, proj, right_rows, weights, mask_t,
):
    seqs, rows, width = x_ref.shape
    proj_width = right_ref.shape[0]
    begin = pl.multiple_of(index_ref[0] * rows, rows)
    weights[:proj_width, :] = wl_ref[...]
    weights[proj_width : 2 * proj_width, :] = wr_ref[...]
    weights[2 * proj_width :, :] = jnp.zeros((LANES - 2 * proj_width, width), BF16)
    bias_left = column_of(bl_ref[...])
    bias_right = column_of(br_ref[...])
    step = 16
    for first in range(0, seqs, step):
        x = x_ref[first : first + step].astype(F32).reshape(step * rows, width)
        normalized = normalize(x, gain_ref[...], shift_ref[...])[2]
        proj[first * rows : (first + step) * rows, :] = dot(normalized, weights[...], LAST_DIMS)
    mask_t[...] = mask_ref[...].astype(F32).T
    mask_own = mask_t[pl.ds(begin, rows), :]
    for i in range(rows):
        block = proj[pl.ds(i, seqs, stride=rows), :].T
        mask_row = mask_own[i : i + 1, :]
        span = slice(i * proj_width, (i + 1) * proj_width)
        left_ref[span, :] = ((block[:proj_width] + bias_left) * mask_row).astype(BF16)
        right_rows[span, :] = (block[proj_width : 2 * proj_width] + bias_right) * mask_row
    for e in range(proj_width):
        right_ref[e] = right_rows[pl.ds(e, rows, stride=proj_width), :].astype(BF16)


def grad_columns(w2_ref, scaled_ref, grad):
    rows, cols, chan = scaled_ref.shape
    proj_width = grad.shape[0]
    for i in range(0, rows, 2):
        pair = scaled_ref[i : i + 2].reshape(2 * cols, chan)
        block = dot(w2_ref[...], pair, LAST_DIMS).astype(BF16)
        for e in range(proj_width):
            for sub in range(2):
                grad[e, (i + sub) * proj_width : (i + sub + 1) * proj_width, :] = block[
                    e * proj_width : (e + 1) * proj_width, sub * cols : (sub + 1) * cols
                ]


def right_columns(index_ref, left_t, grad, emit):
    proj_width, _, cols = grad.shape
    rows = left_t.shape[1] // proj_width
    high = cols // rows // 2
    own = index_ref[0] >> 1
    for e in range(0, proj_width, 2):
        block = jnp.concatenate([grad[e], grad[e + 1]], 1)
        sums = dot(left_t[...], block)
        for sub in range(2):
            part = sums[:, sub * cols : (sub + 1) * cols].T
            for q in range(2 * high):
                rel = q ^ own
                emit(e + sub, (rel & 1) * high + (rel >> 1), part[q * rows : (q + 1) * rows])


def scale_columns(half, mask_t_ref, mask_own, resid_t, resid_own, cot_ref, scaled_ref, factor_ref):
    rows = cot_ref.shape[0]
    cols = scaled_ref.shape[1]
    starts = [
        pl.multiple_of((2 * q + half) * rows, rows) for q in range(cols // rows)
    ]
    mask_cols = jnp.concatenate([mask_t_ref[pl.ds(s, rows), :] for s in starts], 0)
    resid_cols = jnp.concatenate([resid_t[pl.ds(s, rows), :] for s in starts], 0)
    counted = dot(mask_cols.astype(BF16), mask_own.astype(BF16), LAST_DIMS)
    factor_t = resid_cols[:, :1] * resid_own / counted
    factor_ref[...] = factor_t.T
    bias_sum = jnp.zeros((1, cot_ref.shape[2]), F32)
    for i in range(rows):
        cot = jnp.concatenate([cot_ref[i, pl.ds(s, rows), :] for s in starts], 0)
        scaled = (cot.astype(F32) * factor_t[:, i : i + 1]).astype(BF16)
        scaled_ref[i] = scaled
        bias_sum = bias_sum + jnp.sum(scaled.astype(F32), 0, keepdims=True)
    return bias_sum


def send_kernel(
    index_ref, left_ref, mask_ref, resid_ref, cot_ref, w_ref,
    send_ref, far_ref, near_ref, far_factor_ref, near_factor_ref, w2_ref, b_ref, left_t_ref, grad,
    mask_own_ref, wide, resid_t, mask_t,
):
    rows, cols, chan = cot_ref.shape
    proj_width = left_ref.shape[0] // rows
    index = index_ref[0]
    wide[...] = w_ref[...].astype(F32)
    for e in range(proj_width):
        w2_ref[e * proj_width : (e + 1) * proj_width, :] = wide[
            pl.ds(e, proj_width, stride=proj_width), :
        ].astype(BF16)
    left_t_ref[...] = left_ref[...].astype(F32).T.astype(BF16)
    resid_t[...] = jnp.broadcast_to(resid_ref[...].astype(F32), (LANES, cols)).T
    begin = pl.multiple_of(index * rows, rows)
    mask_t[...] = mask_ref[...].astype(F32).T
    mask_own = mask_t[pl.ds(begin, rows), :]
    mask_own_ref[...] = mask_own
    resid_own = resid_t[pl.ds(begin, rows), :].T[:1]
    side = index & 1
    shared = (mask_t, mask_own, resid_t, resid_own, cot_ref)
    far_sum = scale_columns(1 - side, *shared, far_ref, far_factor_ref)
    near_sum = scale_columns(side, *shared, near_ref, near_factor_ref)
    b_ref[...] = far_sum + near_sum
    grad_columns(w2_ref, far_ref, grad)

    def emit(e, slot, value):
        send_ref[slot, e] = value.astype(BF16)

    right_columns(index_ref, left_t_ref, grad, emit)


def keep_kernel(
    index_ref, left_t_ref, w2_ref, near_ref, far_part_ref, keep_ref, send_ref, grad, total
):
    high = keep_ref.shape[0]
    grad_columns(w2_ref, near_ref, grad)

    def emit(e, slot, value):
        total[slot, e] = value

    right_columns(index_ref, left_t_ref, grad, emit)
    keep_ref[...] = total[:high] + far_part_ref[:high].astype(F32)
    send_ref[...] = (total[high:] + far_part_ref[high:].astype(F32)).astype(BF16)


def high_kernel(keep_ref, other_ref, own_ref, *send_refs):
    own_ref[...] = keep_ref[0] + other_ref[0].astype(F32)
    for k, ref in enumerate(send_refs):
        ref[...] = (keep_ref[k + 1] + other_ref[k + 1].astype(F32)).astype(BF16)


def normal_kernel(
    x_ref, gain_ref, shift_ref, right_ref, other_ref,
    normal_ref, inverse_ref, right_copy_ref, other_copy_ref,
):
    seqs, rows, width = x_ref.shape
    right_copy_ref[...] = right_ref[...]
    other_copy_ref[...] = other_ref[...]
    step = 16
    for first in range(0, seqs, step):
        x = x_ref[first : first + step].astype(F32).reshape(step * rows, width)
        xhat, inverse, normalized = normalize(x, gain_ref[...], shift_ref[...])
        span = slice(first * rows, (first + step) * rows)
        normal_ref[span, :width] = normalized
        normal_ref[span, width:] = xhat.astype(BF16)
        inverse_ref[span, :] = inverse


def line_kernel(*refs):
    count = len(refs) // 2
    for k in range(count):
        refs[count + k][...] = refs[k][...]
    refs[-1][...] = jnp.zeros_like(refs[-1])


def place_kernel(index_ref, *refs):
    *blocks, out_ref = refs
    rows = blocks[0].shape[1]
    own = index_ref[0] >> 1
    for rel, ref in enumerate(blocks):
        out_ref[:, pl.ds(pl.multiple_of((own ^ rel) * rows, rows), rows), :] = ref[...]


def outer_columns(left_ref, right_ref, outer):
    proj_width, cols, seqs = right_ref.shape
    rows = left_ref.shape[0] // proj_width
    for e in range(0, proj_width, 2):
        pair = right_ref[e : e + 2].reshape(2 * cols, seqs)
        block = dot(left_ref[...], pair, LAST_DIMS).astype(BF16)
        for i in range(rows):
            for sub in range(2):
                outer[
                    i // 2,
                    (e + sub) * proj_width : (e + sub + 1) * proj_width,
                    (i % 2) * cols : (i % 2 + 1) * cols,
                ] = block[i * proj_width : (i + 1) * proj_width, sub * cols : (sub + 1) * cols]


def weight_columns(left_ref, right_ref, scaled_ref, w_ref, outer):
    rows, cols, chan = scaled_ref.shape
    outer_columns(left_ref, right_ref, outer)
    for p in range(rows // 2):
        w_ref[...] += dot(outer[p], scaled_ref[2 * p : 2 * p + 2].reshape(2 * cols, chan))


def left_columns(grad, right_ref, left_sum_ref):
    proj_width, cols, seqs = right_ref.shape
    for e in range(0, proj_width, 2):
        block = jnp.concatenate([grad[e], grad[e + 1]], 1)
        left_sum_ref[...] += dot(block, right_ref[e : e + 2].reshape(2 * cols, seqs))


def near_kernel(left_ref, scaled_ref, grad_ref, right_ref, w_sum_ref, left_sum_ref, outer_ref):
    w_sum_ref[...] = jnp.zeros_like(w_sum_ref)
    weight_columns(left_ref, right_ref, scaled_ref, w_sum_ref, outer_ref)
    left_sum_ref[...] = jnp.zeros_like(left_sum_ref)
    left_columns(grad_ref, right_ref, left_sum_ref)


def far_kernel(index_ref, left_ref, scaled_ref, w_sum_ref, right_ref, outer_ref, *refs):
    *quarter_refs, total = refs
    total[...] = w_sum_ref[...]
    weight_columns(left_ref, right_ref, scaled_ref, total, outer_ref)
    quarter = quarter_refs[0].shape[0]
    for m, ref in enumerate(quarter_refs):
        begin = pl.multiple_of(((index_ref[0] & 3) ^ m) * quarter, quarter)
        ref[...] = total[pl.ds(begin, quarter), :].astype(BF16)


def left_kernel(near_sum_ref, grad_ref, right_ref, left_sum_ref):
    left_sum_ref[...] = near_sum_ref[...]
    left_columns(grad_ref, right_ref, left_sum_ref)


def pair_kernel(
    index_ref, w2_ref, bias_ref, near_ref, far_ref, near_factor_ref, far_factor_ref, out_ref, w2_t
):
    rows = out_ref.shape[0]
    w2_t[...] = w2_ref[...].astype(F32).T.astype(BF16)
    bias = column_of(bias_ref[...])
    side = index_ref[0] & 1
    for half, outer, factor_ref in (
        (side, near_ref, near_factor_ref),
        (1 - side, far_ref, far_factor_ref),
    ):
        cols = outer.shape[2] // 2
        for p in range(rows // 2):
            projected = dot(w2_t[...], outer[p]) + bias
            for sub in range(2):
                i = 2 * p + sub
                block = projected[:, sub * cols : (sub + 1) * cols] * factor_ref[i : i + 1, :]
                block = block.T.astype(BF16)
                for q in range(cols // rows):
                    begin = pl.multiple_of((2 * q + half) * rows, rows)
                    out_ref[i, pl.ds(begin, rows), :] = block[q * rows : (q + 1) * rows]


def sums_kernel(
    right_own_ref, *refs
):
    *ins, grads_ref, pack_ref, right_sum, gathered = refs
    *right_refs, normal_ref, wl_ref, wr_ref, mask_own_ref, left_sum_ref, b_ref = ins
    seqs = mask_own_ref.shape[1]
    proj_width, rows, _ = right_own_ref.shape
    width = wl_ref.shape[1]
    total = right_own_ref[...]
    for ref in right_refs:
        total = total + ref[...].astype(F32)
    right_sum[...] = total.reshape(proj_width * rows, seqs)
    fill = jnp.zeros((LANES - 2 * proj_width, seqs), F32)
    bias_cols = jnp.zeros((LANES, seqs), F32)
    for i in range(rows):
        block = jnp.concatenate(
            [
                left_sum_ref[i * proj_width : (i + 1) * proj_width, :],
                right_sum[pl.ds(i, proj_width, stride=rows), :],
                fill,
            ],
            0,
        )
        block = (block * mask_own_ref[i : i + 1, :]).astype(BF16).astype(F32)
        bias_cols = bias_cols + block
        gathered[pl.ds(i, seqs, stride=rows), :] = block.T
    grads_ref[...] = gathered[...].astype(BF16)
    used = 2 * proj_width
    products = jnp.zeros((LANES, 2 * width), F32)
    step = 256
    for first in range(0, seqs * rows, step):
        products = products + dot(
            grads_ref[first : first + step, :], normal_ref[first : first + step, :], FIRST_DIMS
        )
    weights = jnp.concatenate([wl_ref[...], wr_ref[...]], 0).astype(F32)
    bias_sum = jnp.sum(bias_cols, 1, keepdims=True)
    gain_sum = jnp.sum(weights * products[:used, width:], 0, keepdims=True)
    shift_sum = jnp.sum(weights * bias_sum[:used], 0, keepdims=True)
    bias_row = jnp.broadcast_to(bias_sum, (LANES, LANES)).T[:1]
    pieces = [products[:used, k : k + LANES] for k in range(0, width, LANES)]
    pieces += [gain_sum[:, k : k + LANES] for k in range(0, width, LANES)]
    pieces += [shift_sum[:, k : k + LANES] for k in range(0, width, LANES)]
    pieces += [bias_row, b_ref[...]]
    pieces += [jnp.zeros((TAIL - 2 - 2 * (width // LANES), LANES), F32)]
    pack_ref[...] = jnp.concatenate(pieces, 0).astype(BF16)


def norm_kernel(normal_ref, inverse_ref, gain_ref, wl_ref, wr_ref, grads_ref, out_ref, weights):
    seqs, rows, width = out_ref.shape
    proj_width = wl_ref.shape[0]
    weights[...] = jnp.zeros_like(weights)
    weights[:proj_width, :] = wl_ref[...]
    weights[proj_width : 2 * proj_width, :] = wr_ref[...]
    step = 16
    for first in range(0, seqs, step):
        span = slice(first * rows, (first + step) * rows)
        xhat = normal_ref[span, width:].astype(F32)
        g = dot(grads_ref[span, :], weights[...]) * gain_ref[...]
        result = (
            g - jnp.mean(g, -1, keepdims=True) - xhat * jnp.mean(g * xhat, -1, keepdims=True)
        ) * inverse_ref[span, :]
        out_ref[first : first + step] = result.astype(BF16).reshape(step, rows, width)


def tree_sum(values):
    values = [value.astype(F32) for value in values]
    while len(values) > 1:
        values = [a + b for a, b in zip(values[::2], values[1::2])]
    return values[0]


def merge_kernel(*refs):
    *ins, out_ref = refs
    out_ref[...] = tree_sum([ref[...] for ref in ins]).astype(BF16)


def join_kernel(own_ref, other_ref, out_ref):
    out_ref[0] = own_ref[...]
    out_ref[1] = other_ref[...]


def weight_kernel(index_ref, own_ref, other_ref, out_ref, placed):
    quarter = own_ref.shape[1]
    proj_width = math.isqrt(out_ref.shape[0])
    for core, ref in enumerate((own_ref, other_ref)):
        for side in range(2):
            begin = pl.multiple_of(((index_ref[0] & 3) ^ (core + 2 * side)) * quarter, quarter)
            placed[pl.ds(begin, quarter), :] = ref[side].astype(F32)
    for c in range(proj_width):
        out_ref[c * proj_width : (c + 1) * proj_width, :] = placed[
            pl.ds(c, proj_width, stride=proj_width), :
        ]


def unpack_kernel(
    own_ref, other_ref, wl_ref, bl_ref, wr_ref, br_ref, b_ref, gain_ref, shift_ref
):
    proj_width, width = wl_ref.shape
    used = 2 * proj_width
    parts = width // LANES
    total = tree_sum([own_ref[...], other_ref[...]])
    tail = total[parts * used :]
    for k in range(parts):
        span = slice(k * LANES, (k + 1) * LANES)
        wl_ref[:, span] = total[k * used : k * used + proj_width]
        wr_ref[:, span] = total[k * used + proj_width : (k + 1) * used]
        gain_ref[:, span] = tail[k : k + 1]
        shift_ref[:, span] = tail[parts + k : parts + k + 1]
    bl_ref[...] = tail[2 * parts : 2 * parts + 1, :proj_width]
    br_ref[...] = tail[2 * parts : 2 * parts + 1, proj_width:used]
    b_ref[...] = tail[2 * parts + 1 : 2 * parts + 2, :]


def body(
    devices,
    alignment_activations,
    alignment_row_mask,
    residue_mask_vector,
    layer_norm_gain,
    layer_norm_bias,
    left_weight,
    left_bias,
    right_weight,
    right_bias,
    output_weight,
    output_bias,
    pair_update_cotangent,
):
    seqs, rows, width = alignment_activations.shape
    cols = alignment_row_mask.shape[1]
    proj_width = left_weight.shape[1]
    pair_width, chan = output_weight.shape
    high = devices // 4
    half = cols // 2
    quarter = pair_width // 4
    flat = rows * proj_width
    index = lax.axis_index("res").astype(jnp.int32).reshape(1)
    gain = layer_norm_gain.reshape(1, width)
    shift = layer_norm_bias.reshape(1, width)
    wl, wr = left_weight.T, right_weight.T
    piece = (proj_width, rows, seqs)

    def swap(value, rel):
        return lax.ppermute(value, "res", [(d, d ^ rel) for d in range(devices)])

    slab = (high,) + piece
    left, right = call(
        project_kernel,
        (shape((flat, seqs), BF16), shape(piece, BF16)),
        (index, alignment_activations, alignment_row_mask, gain, shift, wl, wr)
        + (left_bias.reshape(1, proj_width), right_bias.reshape(1, proj_width)),
        (
            pltpu.VMEM((seqs * rows, LANES), F32),
            pltpu.VMEM((flat, seqs), F32),
            pltpu.VMEM((LANES, width), BF16),
            pltpu.VMEM((cols, seqs), F32),
        ),
        us=4,
        fetched=tuple(range(1, 9)),
        grant=60 * MIB,
    )
    blocks = {0: right, 2: swap(right, 2)}
    for k in range(2, high):
        blocks[4 * k] = swap(right, 4 * k)
    grad_shape = shape((proj_width, flat, half), BF16)
    outer_shape = shape((rows // 2, pair_width, 2 * half), BF16)
    send, far, near, far_factor, near_factor, w2, b_part, left_t, far_grad, mask_own = call(
        send_kernel,
        (
            shape((2 * high,) + piece, BF16),
            shape((rows, half, chan), BF16),
            shape((rows, half, chan), BF16),
            shape((rows, half), F32),
            shape((rows, half), F32),
            shape((pair_width, chan), BF16),
            shape((1, chan), F32),
            shape((seqs, flat), BF16),
            grad_shape,
            shape((rows, seqs), F32),
        ),
        (
            index,
            left,
            alignment_row_mask,
            residue_mask_vector.reshape(1, cols),
            pair_update_cotangent,
            output_weight,
        ),
        (
            pltpu.VMEM((pair_width, chan), F32),
            pltpu.VMEM((cols, LANES), F32),
            pltpu.VMEM((cols, seqs), F32),
        ),
        us=6,
    )
    keep, send, near_grad = call(
        keep_kernel,
        (shape(slab, F32), shape(slab, BF16), grad_shape),
        (index, left_t, w2, near, swap(send, 1)),
        (pltpu.VMEM((2 * high,) + piece, F32),),
        us=4,
    )
    normal, inverse, right_copy, other_copy, normal_token = call(
        normal_kernel,
        (shape((seqs * rows, 2 * width), BF16), shape((seqs * rows, 1), F32))
        + (shape(piece, BF16),) * 2,
        (alignment_activations, gain, shift, right, blocks[2]),
        scalars=0,
        us=10,
        after=(keep,),
        token=True,
    )
    blocks[4] = swap(right_copy, 4)
    blocks[6] = swap(other_copy, 4)
    blocks[10] = swap(other_copy, 8)
    line = call(
        line_kernel,
        (shape(piece, BF16),) * (high - 3) + (shape((8, LANES), F32),),
        tuple(blocks[4 * k] for k in range(3, high)),
        scalars=0,
        us=0.1,
        after=(normal_token, blocks[8]),
    )
    for k in range(3, high):
        blocks[4 * k + 2] = swap(line[k - 3], 2)
    right_own, *sends = call(
        high_kernel,
        (shape(piece, F32),) + (shape(piece, BF16),) * (high - 1),
        (keep, swap(send, 2)),
        scalars=0,
        us=10,
        after=(line[-1], blocks[4], blocks[10]),
    )
    right_parts = tuple(swap(sends[k - 1], 4 * k) for k in range(high - 1, 0, -1))
    right_near = call(
        place_kernel,
        shape((proj_width, half, seqs), BF16),
        (index,) + tuple(blocks[rel] for rel in range(0, devices, 2)),
        after=(right_own,),
    )
    right_far = swap(right_near, 1)
    near_w, near_left, near_outer = call(
        near_kernel,
        (shape((pair_width, chan), F32), shape((flat, seqs), F32), outer_shape),
        (left, near, near_grad, right_near),
        scalars=0,
        us=100,
    )
    far_outer, w_own, *w_sends = call(
        far_kernel,
        (outer_shape,) + (shape((quarter, chan), BF16),) * 4,
        (index, left, far, near_w, right_far),
        (pltpu.VMEM((pair_width, chan), F32),),
        us=0.02,
    )
    left_sum = call(
        left_kernel,
        shape((flat, seqs), F32),
        (near_left, far_grad, right_far),
        scalars=0,
        us=0.02,
        after=(w_own,),
    )
    pack_shape = shape((2 * proj_width * (width // LANES) + TAIL, LANES), BF16)
    grads, pack = call(
        sums_kernel,
        (shape((seqs * rows, LANES), BF16), pack_shape),
        (right_own,) + right_parts + (normal, wl, wr, mask_own, left_sum, b_part),
        (pltpu.VMEM((flat, seqs), F32), pltpu.VMEM((seqs * rows, LANES), F32)),
        scalars=0,
        us=2,
    )
    distances = [devices // 2 >> n for n in range(high.bit_length() - 1)]
    packs = [pack]

    def merge_pack(after):
        last = packs[-1]
        packs.append(
            call(
                merge_kernel,
                pack_shape,
                (last, swap(last, (distances + [2])[len(packs) - 1])),
                scalars=0,
                us=0.1,
                after=after,
            )
        )

    weights = call(
        merge_kernel,
        shape((quarter, chan), BF16),
        (w_own,) + tuple(swap(value, m + 1) for m, value in enumerate(w_sends)),
        scalars=0,
        us=0.1,
        after=(pack,),
    )
    alignment_gradient, norm_token = call(
        norm_kernel,
        shape((seqs, rows, width), BF16),
        (normal, inverse, gain, wl, wr, grads),
        (pltpu.VMEM((LANES, width), BF16),),
        scalars=0,
        us=0.02,
        after=(weights,),
        token=True,
    )
    merge_pack((norm_token,))
    merge_pack(())
    pair, pair_token = call(
        pair_kernel,
        shape((rows, cols, chan), BF16),
        (index, w2, output_bias.reshape(1, chan), near_outer, far_outer, near_factor, far_factor),
        (pltpu.VMEM((chan, pair_width), BF16),),
        us=0.02,
        after=(packs[2],),
        token=True,
    )
    while len(packs) < len(distances) + 2:
        merge_pack((pair_token,))
    for n, distance in enumerate(distances):
        weights = call(
            merge_kernel,
            shape((quarter, chan), BF16),
            (weights, swap(weights, distance)),
            scalars=0,
            us=0.1,
            after=(packs[n + 1],),
        )
    weights = call(
        join_kernel,
        shape((2, quarter, chan), BF16),
        (weights, swap(weights, 2)),
        scalars=0,
        us=0.1,
    )
    w_out_grad = call(
        weight_kernel,
        shape((pair_width, chan), F32),
        (index, weights, swap(weights, 1)),
        (pltpu.VMEM((pair_width, chan), F32),),
        us=0.1,
    )

    w_left, b_left, w_right, b_right, b_out, gain_grad, shift_grad = call(
        unpack_kernel,
        (
            shape((proj_width, width), F32),
            shape((1, proj_width), F32),
            shape((proj_width, width), F32),
            shape((1, proj_width), F32),
            shape((1, chan), F32),
            shape((1, width), F32),
            shape((1, width), F32),
        ),
        (packs[-1], swap(packs[-1], 1)),
        scalars=0,
    )
    return (
        pair,
        alignment_gradient,
        w_left.T,
        b_left.reshape(-1),
        w_right.T,
        b_right.reshape(-1),
        w_out_grad,
        b_out.reshape(-1),
        gain_grad.reshape(-1),
        shift_grad.reshape(-1),
    )


def solution(mesh):
    return jax.shard_map(
        functools.partial(body, mesh.shape["res"]),
        mesh=mesh,
        in_specs=(
            P(None, ("grp", "res"), None),
            P(None, "grp"),
            P("grp"),
            P(),
            P(),
            P(),
            P(),
            P(),
            P(),
            P(),
            P(),
            P(("grp", "res"), None, None),
        ),
        out_specs=(
            P(("grp", "res"), None, None),
            P(None, ("grp", "res"), None),
            P("grp", None),
            P("grp"),
            P("grp", None),
            P("grp"),
            P("grp", None),
            P("grp"),
            P("grp"),
            P("grp"),
        ),
        check_vma=False,
    )
```

```python
import functools
import math

import jax
import jax.numpy as jnp
from jax import lax
from jax.experimental import pallas as pl
from jax.experimental.pallas import tpu as pltpu
from jax.sharding import PartitionSpec as P

EPS = 1e-05
LAST_DIMS = (((1,), (1,)), ((), ()))
FIRST_DIMS = (((0,), (0,)), ((), ()))
MIB = 1024 * 1024
LANES = 128
TAIL = 16
F32 = jnp.float32
BF16 = jnp.bfloat16


def tiled_bytes(dims, dtype):
    dims = tuple(dims)
    lanes = -(-dims[-1] // LANES) * LANES
    sublanes = -(-(dims[-2] if len(dims) > 1 else 1) // 16) * 16
    return math.prod(dims[:-2]) * sublanes * lanes * jnp.dtype(dtype).itemsize


def call(
    kernel, out_shape, args, scratch=(), scalars=1, us=1.0, after=(), fetched=(), token=False, grant=0, **static
):
    count = len(args)
    specs = [pl.BlockSpec(memory_space=pl.ANY)] * len(after)
    specs += [pl.BlockSpec(memory_space=pltpu.SMEM)] * scalars
    for k in range(scalars, count):
        specs.append(pl.BlockSpec(memory_space=pltpu.HBM if k in fetched else pltpu.VMEM))
    outs = list(out_shape) if isinstance(out_shape, (tuple, list)) else [out_shape]
    if token:
        outs.append(shape((8, LANES), F32))
    held = list(args[scalars:]) + outs + list(scratch)
    need = sum(tiled_bytes(value.shape, value.dtype) for value in held)
    places = [pltpu.VMEM(args[k].shape, args[k].dtype) for k in fetched]
    semaphores = [pltpu.SemaphoreType.DMA((len(fetched),))] if fetched else []

    def run(*refs):
        ins = list(refs[len(after) : len(after) + count])
        rest = list(refs[len(after) + count :])
        if fetched:
            *rest, done = rest
            held_refs = rest[-len(fetched) :]
            rest = rest[: -len(fetched)]
            copies = [
                pltpu.make_async_copy(ins[k], ref, done.at[n])
                for n, (k, ref) in enumerate(zip(fetched, held_refs))
            ]
            for copy in copies:
                copy.start()
            for k, ref, copy in zip(fetched, held_refs, copies):
                ins[k] = Fetched(ref, copy)
        if token:
            rest.pop(len(outs) - 1)[...] = jnp.zeros((8, LANES), F32)
        kernel(*ins, *rest, **static)

    result = pl.pallas_call(
        run,
        name=kernel.__name__,
        out_shape=tuple(outs),
        in_specs=specs,
        out_specs=tuple([pl.BlockSpec(memory_space=pltpu.VMEM)] * len(outs)),
        scratch_shapes=list(scratch) + places + semaphores,
        compiler_params=pltpu.CompilerParams(vmem_limit_bytes=grant or min(need + 6 * MIB, 56 * MIB)),
        cost_estimate=pl.CostEstimate(
            flops=int(us * 1.1e9), bytes_accessed=int(us * 1e5), transcendentals=0
        ),
    )(*after, *args)
    return result if len(outs) > 1 else result[0]


class Fetched:
    def __init__(self, ref, copy):
        self.ref, self.copy, self.shape = ref, copy, ref.shape

    def __getitem__(self, index):
        if self.copy is not None:
            self.copy.wait()
            self.copy = None
        return self.ref[index]


def shape(dims, dtype):
    return jax.ShapeDtypeStruct(tuple(dims), dtype)


def dot(a, b, dims=(((1,), (0,)), ((), ()))):
    return lax.dot_general(a, b, dims, preferred_element_type=F32)


def normalize(x, gain, shift):
    centered = x - jnp.mean(x, -1, keepdims=True)
    inverse = lax.rsqrt(jnp.mean(centered * centered, -1, keepdims=True) + EPS)
    xhat = centered * inverse
    return xhat, inverse, (xhat * gain + shift).astype(BF16)


def column_of(row):
    return jnp.broadcast_to(row, (8, row.shape[1])).T[:, :1]


def project_kernel(
    index_ref, x_ref, mask_ref, gain_ref, shift_ref, wl_ref, wr_ref, bl_ref, br_ref,
    left_ref, right_ref, proj, right_rows, weights, mask_t,
):
    seqs, rows, width = x_ref.shape
    proj_width = right_ref.shape[0]
    begin = pl.multiple_of(index_ref[0] * rows, rows)
    weights[:proj_width, :] = wl_ref[...]
    weights[proj_width : 2 * proj_width, :] = wr_ref[...]
    weights[2 * proj_width :, :] = jnp.zeros((LANES - 2 * proj_width, width), BF16)
    bias_left = column_of(bl_ref[...])
    bias_right = column_of(br_ref[...])
    step = 16
    for first in range(0, seqs, step):
        x = x_ref[first : first + step].astype(F32).reshape(step * rows, width)
        normalized = normalize(x, gain_ref[...], shift_ref[...])[2]
        proj[first * rows : (first + step) * rows, :] = dot(normalized, weights[...], LAST_DIMS)
    mask_t[...] = mask_ref[...].astype(F32).T
    mask_own = mask_t[pl.ds(begin, rows), :]
    for i in range(rows):
        block = proj[pl.ds(i, seqs, stride=rows), :].T
        mask_row = mask_own[i : i + 1, :]
        span = slice(i * proj_width, (i + 1) * proj_width)
        left_ref[span, :] = ((block[:proj_width] + bias_left) * mask_row).astype(BF16)
        right_rows[span, :] = (block[proj_width : 2 * proj_width] + bias_right) * mask_row
    for e in range(proj_width):
        right_ref[e] = right_rows[pl.ds(e, rows, stride=proj_width), :].astype(BF16)


def grad_columns(w2_ref, scaled_ref, grad):
    rows, cols, chan = scaled_ref.shape
    proj_width = grad.shape[0]
    for i in range(0, rows, 2):
        pair = scaled_ref[i : i + 2].reshape(2 * cols, chan)
        block = dot(w2_ref[...], pair, LAST_DIMS).astype(BF16)
        for e in range(proj_width):
            for sub in range(2):
                grad[e, (i + sub) * proj_width : (i + sub + 1) * proj_width, :] = block[
                    e * proj_width : (e + 1) * proj_width, sub * cols : (sub + 1) * cols
                ]


def right_columns(index_ref, left_t, grad, emit):
    proj_width, _, cols = grad.shape
    rows = left_t.shape[1] // proj_width
    high = cols // rows // 2
    own = index_ref[0] >> 1
    for e in range(0, proj_width, 2):
        block = jnp.concatenate([grad[e], grad[e + 1]], 1)
        sums = dot(left_t[...], block)
        for sub in range(2):
            part = sums[:, sub * cols : (sub + 1) * cols].T
            for q in range(2 * high):
                rel = q ^ own
                emit(e + sub, (rel & 1) * high + (rel >> 1), part[q * rows : (q + 1) * rows])


def scale_columns(half, mask_t_ref, mask_own, resid_t, resid_own, cot_ref, scaled_ref, factor_ref):
    rows = cot_ref.shape[0]
    cols = scaled_ref.shape[1]
    starts = [
        pl.multiple_of((2 * q + half) * rows, rows) for q in range(cols // rows)
    ]
    mask_cols = jnp.concatenate([mask_t_ref[pl.ds(s, rows), :] for s in starts], 0)
    resid_cols = jnp.concatenate([resid_t[pl.ds(s, rows), :] for s in starts], 0)
    counted = dot(mask_cols.astype(BF16), mask_own.astype(BF16), LAST_DIMS)
    factor_t = resid_cols[:, :1] * resid_own / counted
    factor_ref[...] = factor_t.T
    bias_sum = jnp.zeros((1, cot_ref.shape[2]), F32)
    for i in range(rows):
        cot = jnp.concatenate([cot_ref[i, pl.ds(s, rows), :] for s in starts], 0)
        scaled = (cot.astype(F32) * factor_t[:, i : i + 1]).astype(BF16)
        scaled_ref[i] = scaled
        bias_sum = bias_sum + jnp.sum(scaled.astype(F32), 0, keepdims=True)
    return bias_sum


def send_kernel(
    index_ref, left_ref, mask_ref, resid_ref, cot_ref, w_ref,
    send_ref, far_ref, near_ref, far_factor_ref, near_factor_ref, w2_ref, b_ref, left_t_ref, grad,
    mask_own_ref, wide, resid_t, mask_t,
):
    rows, cols, chan = cot_ref.shape
    proj_width = left_ref.shape[0] // rows
    index = index_ref[0]
    wide[...] = w_ref[...].astype(F32)
    for e in range(proj_width):
        w2_ref[e * proj_width : (e + 1) * proj_width, :] = wide[
            pl.ds(e, proj_width, stride=proj_width), :
        ].astype(BF16)
    left_t_ref[...] = left_ref[...].astype(F32).T.astype(BF16)
    resid_t[...] = jnp.broadcast_to(resid_ref[...].astype(F32), (LANES, cols)).T
    begin = pl.multiple_of(index * rows, rows)
    mask_t[...] = mask_ref[...].astype(F32).T
    mask_own = mask_t[pl.ds(begin, rows), :]
    mask_own_ref[...] = mask_own
    resid_own = resid_t[pl.ds(begin, rows), :].T[:1]
    side = index & 1
    shared = (mask_t, mask_own, resid_t, resid_own, cot_ref)
    far_sum = scale_columns(1 - side, *shared, far_ref, far_factor_ref)
    near_sum = scale_columns(side, *shared, near_ref, near_factor_ref)
    b_ref[...] = far_sum + near_sum
    grad_columns(w2_ref, far_ref, grad)

    def emit(e, slot, value):
        send_ref[slot, e] = value.astype(BF16)

    right_columns(index_ref, left_t_ref, grad, emit)


def keep_kernel(
    index_ref, left_t_ref, w2_ref, near_ref, far_part_ref, keep_ref, send_ref, grad, total
):
    high = keep_ref.shape[0]
    grad_columns(w2_ref, near_ref, grad)

    def emit(e, slot, value):
        total[slot, e] = value

    right_columns(index_ref, left_t_ref, grad, emit)
    keep_ref[...] = total[:high] + far_part_ref[:high].astype(F32)
    send_ref[...] = (total[high:] + far_part_ref[high:].astype(F32)).astype(BF16)


def high_kernel(keep_ref, other_ref, own_ref, *send_refs):
    own_ref[...] = keep_ref[0] + other_ref[0].astype(F32)
    for k, ref in enumerate(send_refs):
        ref[...] = (keep_ref[k + 1] + other_ref[k + 1].astype(F32)).astype(BF16)


def normal_kernel(
    x_ref, gain_ref, shift_ref, right_ref, other_ref,
    normal_ref, inverse_ref, right_copy_ref, other_copy_ref,
):
    seqs, rows, width = x_ref.shape
    right_copy_ref[...] = right_ref[...]
    other_copy_ref[...] = other_ref[...]
    step = 16
    for first in range(0, seqs, step):
        x = x_ref[first : first + step].astype(F32).reshape(step * rows, width)
        xhat, inverse, normalized = normalize(x, gain_ref[...], shift_ref[...])
        span = slice(first * rows, (first + step) * rows)
        normal_ref[span, :width] = normalized
        normal_ref[span, width:] = xhat.astype(BF16)
        inverse_ref[span, :] = inverse


def line_kernel(*refs):
    count = len(refs) // 2
    for k in range(count):
        refs[count + k][...] = refs[k][...]
    refs[-1][...] = jnp.zeros_like(refs[-1])


def place_kernel(index_ref, *refs):
    *blocks, out_ref = refs
    rows = blocks[0].shape[1]
    own = index_ref[0] >> 1
    for rel, ref in enumerate(blocks):
        out_ref[:, pl.ds(pl.multiple_of((own ^ rel) * rows, rows), rows), :] = ref[...]


def outer_columns(left_ref, right_ref, outer):
    proj_width, cols, seqs = right_ref.shape
    rows = left_ref.shape[0] // proj_width
    for e in range(0, proj_width, 2):
        pair = right_ref[e : e + 2].reshape(2 * cols, seqs)
        block = dot(left_ref[...], pair, LAST_DIMS).astype(BF16)
        for i in range(rows):
            for sub in range(2):
                outer[
                    i // 2,
                    (e + sub) * proj_width : (e + sub + 1) * proj_width,
                    (i % 2) * cols : (i % 2 + 1) * cols,
                ] = block[i * proj_width : (i + 1) * proj_width, sub * cols : (sub + 1) * cols]


def weight_columns(left_ref, right_ref, scaled_ref, w_ref, outer):
    rows, cols, chan = scaled_ref.shape
    outer_columns(left_ref, right_ref, outer)
    for p in range(rows // 2):
        w_ref[...] += dot(outer[p], scaled_ref[2 * p : 2 * p + 2].reshape(2 * cols, chan))


def left_columns(grad, right_ref, left_sum_ref):
    proj_width, cols, seqs = right_ref.shape
    for e in range(0, proj_width, 2):
        block = jnp.concatenate([grad[e], grad[e + 1]], 1)
        left_sum_ref[...] += dot(block, right_ref[e : e + 2].reshape(2 * cols, seqs))


def near_kernel(left_ref, scaled_ref, grad_ref, right_ref, w_sum_ref, left_sum_ref, outer_ref):
    w_sum_ref[...] = jnp.zeros_like(w_sum_ref)
    weight_columns(left_ref, right_ref, scaled_ref, w_sum_ref, outer_ref)
    left_sum_ref[...] = jnp.zeros_like(left_sum_ref)
    left_columns(grad_ref, right_ref, left_sum_ref)


def far_kernel(index_ref, left_ref, scaled_ref, w_sum_ref, right_ref, outer_ref, *refs):
    *quarter_refs, total = refs
    total[...] = w_sum_ref[...]
    weight_columns(left_ref, right_ref, scaled_ref, total, outer_ref)
    quarter = quarter_refs[0].shape[0]
    for m, ref in enumerate(quarter_refs):
        begin = pl.multiple_of(((index_ref[0] & 3) ^ m) * quarter, quarter)
        ref[...] = total[pl.ds(begin, quarter), :].astype(BF16)


def left_kernel(near_sum_ref, grad_ref, right_ref, left_sum_ref):
    left_sum_ref[...] = near_sum_ref[...]
    left_columns(grad_ref, right_ref, left_sum_ref)


def pair_kernel(
    index_ref, w2_ref, bias_ref, near_ref, far_ref, near_factor_ref, far_factor_ref, out_ref, w2_t
):
    rows = out_ref.shape[0]
    w2_t[...] = w2_ref[...].astype(F32).T.astype(BF16)
    bias = column_of(bias_ref[...])
    side = index_ref[0] & 1
    for half, outer, factor_ref in (
        (side, near_ref, near_factor_ref),
        (1 - side, far_ref, far_factor_ref),
    ):
        cols = outer.shape[2] // 2
        for p in range(rows // 2):
            projected = dot(w2_t[...], outer[p]) + bias
            for sub in range(2):
                i = 2 * p + sub
                block = projected[:, sub * cols : (sub + 1) * cols] * factor_ref[i : i + 1, :]
                block = block.T.astype(BF16)
                for q in range(cols // rows):
                    begin = pl.multiple_of((2 * q + half) * rows, rows)
                    out_ref[i, pl.ds(begin, rows), :] = block[q * rows : (q + 1) * rows]


def sums_kernel(
    right_own_ref, *refs
):
    *ins, grads_ref, pack_ref, right_sum, gathered = refs
    *right_refs, normal_ref, wl_ref, wr_ref, mask_own_ref, left_sum_ref, b_ref = ins
    seqs = mask_own_ref.shape[1]
    proj_width, rows, _ = right_own_ref.shape
    width = wl_ref.shape[1]
    total = right_own_ref[...]
    for ref in right_refs:
        total = total + ref[...].astype(F32)
    right_sum[...] = total.reshape(proj_width * rows, seqs)
    fill = jnp.zeros((LANES - 2 * proj_width, seqs), F32)
    bias_cols = jnp.zeros((LANES, seqs), F32)
    for i in range(rows):
        block = jnp.concatenate(
            [
                left_sum_ref[i * proj_width : (i + 1) * proj_width, :],
                right_sum[pl.ds(i, proj_width, stride=rows), :],
                fill,
            ],
            0,
        )
        block = (block * mask_own_ref[i : i + 1, :]).astype(BF16).astype(F32)
        bias_cols = bias_cols + block
        gathered[pl.ds(i, seqs, stride=rows), :] = block.T
    grads_ref[...] = gathered[...].astype(BF16)
    used = 2 * proj_width
    products = jnp.zeros((LANES, 2 * width), F32)
    step = 256
    for first in range(0, seqs * rows, step):
        products = products + dot(
            grads_ref[first : first + step, :], normal_ref[first : first + step, :], FIRST_DIMS
        )
    weights = jnp.concatenate([wl_ref[...], wr_ref[...]], 0).astype(F32)
    bias_sum = jnp.sum(bias_cols, 1, keepdims=True)
    gain_sum = jnp.sum(weights * products[:used, width:], 0, keepdims=True)
    shift_sum = jnp.sum(weights * bias_sum[:used], 0, keepdims=True)
    bias_row = jnp.broadcast_to(bias_sum, (LANES, LANES)).T[:1]
    pieces = [products[:used, k : k + LANES] for k in range(0, width, LANES)]
    pieces += [gain_sum[:, k : k + LANES] for k in range(0, width, LANES)]
    pieces += [shift_sum[:, k : k + LANES] for k in range(0, width, LANES)]
    pieces += [bias_row, b_ref[...]]
    pieces += [jnp.zeros((TAIL - 2 - 2 * (width // LANES), LANES), F32)]
    pack_ref[...] = jnp.concatenate(pieces, 0).astype(BF16)


def norm_kernel(normal_ref, inverse_ref, gain_ref, wl_ref, wr_ref, grads_ref, out_ref, weights):
    seqs, rows, width = out_ref.shape
    proj_width = wl_ref.shape[0]
    weights[...] = jnp.zeros_like(weights)
    weights[:proj_width, :] = wl_ref[...]
    weights[proj_width : 2 * proj_width, :] = wr_ref[...]
    step = 16
    for first in range(0, seqs, step):
        span = slice(first * rows, (first + step) * rows)
        xhat = normal_ref[span, width:].astype(F32)
        g = dot(grads_ref[span, :], weights[...]) * gain_ref[...]
        result = (
            g - jnp.mean(g, -1, keepdims=True) - xhat * jnp.mean(g * xhat, -1, keepdims=True)
        ) * inverse_ref[span, :]
        out_ref[first : first + step] = result.astype(BF16).reshape(step, rows, width)


def tree_sum(values):
    values = [value.astype(F32) for value in values]
    while len(values) > 1:
        values = [a + b for a, b in zip(values[::2], values[1::2])]
    return values[0]


def merge_kernel(*refs):
    *ins, out_ref = refs
    out_ref[...] = tree_sum([ref[...] for ref in ins]).astype(BF16)


def join_kernel(own_ref, other_ref, out_ref):
    out_ref[0] = own_ref[...]
    out_ref[1] = other_ref[...]


def weight_kernel(index_ref, own_ref, other_ref, out_ref, placed):
    quarter = own_ref.shape[1]
    proj_width = math.isqrt(out_ref.shape[0])
    for core, ref in enumerate((own_ref, other_ref)):
        for side in range(2):
            begin = pl.multiple_of(((index_ref[0] & 3) ^ (core + 2 * side)) * quarter, quarter)
            placed[pl.ds(begin, quarter), :] = ref[side].astype(F32)
    for c in range(proj_width):
        out_ref[c * proj_width : (c + 1) * proj_width, :] = placed[
            pl.ds(c, proj_width, stride=proj_width), :
        ]


def unpack_kernel(
    own_ref, other_ref, wl_ref, bl_ref, wr_ref, br_ref, b_ref, gain_ref, shift_ref
):
    proj_width, width = wl_ref.shape
    used = 2 * proj_width
    parts = width // LANES
    total = tree_sum([own_ref[...], other_ref[...]])
    tail = total[parts * used :]
    for k in range(parts):
        span = slice(k * LANES, (k + 1) * LANES)
        wl_ref[:, span] = total[k * used : k * used + proj_width]
        wr_ref[:, span] = total[k * used + proj_width : (k + 1) * used]
        gain_ref[:, span] = tail[k : k + 1]
        shift_ref[:, span] = tail[parts + k : parts + k + 1]
    bl_ref[...] = tail[2 * parts : 2 * parts + 1, :proj_width]
    br_ref[...] = tail[2 * parts : 2 * parts + 1, proj_width:used]
    b_ref[...] = tail[2 * parts + 1 : 2 * parts + 2, :]


def body(
    devices,
    alignment_activations,
    alignment_row_mask,
    residue_mask_vector,
    layer_norm_gain,
    layer_norm_bias,
    left_weight,
    left_bias,
    right_weight,
    right_bias,
    output_weight,
    output_bias,
    pair_update_cotangent,
):
    seqs, rows, width = alignment_activations.shape
    cols = alignment_row_mask.shape[1]
    proj_width = left_weight.shape[1]
    pair_width, chan = output_weight.shape
    high = devices // 4
    half = cols // 2
    quarter = pair_width // 4
    flat = rows * proj_width
    index = lax.axis_index("res").astype(jnp.int32).reshape(1)
    gain = layer_norm_gain.reshape(1, width)
    shift = layer_norm_bias.reshape(1, width)
    wl, wr = left_weight.T, right_weight.T
    piece = (proj_width, rows, seqs)

    def swap(value, rel):
        return lax.ppermute(value, "res", [(d, d ^ rel) for d in range(devices)])

    slab = (high,) + piece
    left, right = call(
        project_kernel,
        (shape((flat, seqs), BF16), shape(piece, BF16)),
        (index, alignment_activations, alignment_row_mask, gain, shift, wl, wr)
        + (left_bias.reshape(1, proj_width), right_bias.reshape(1, proj_width)),
        (
            pltpu.VMEM((seqs * rows, LANES), F32),
            pltpu.VMEM((flat, seqs), F32),
            pltpu.VMEM((LANES, width), BF16),
            pltpu.VMEM((cols, seqs), F32),
        ),
        us=4,
        fetched=tuple(range(1, 9)),
        grant=60 * MIB,
    )
    blocks = {0: right, 2: swap(right, 2)}
    for k in range(2, high):
        blocks[4 * k] = swap(right, 4 * k)
    grad_shape = shape((proj_width, flat, half), BF16)
    outer_shape = shape((rows // 2, pair_width, 2 * half), BF16)
    send, far, near, far_factor, near_factor, w2, b_part, left_t, far_grad, mask_own = call(
        send_kernel,
        (
            shape((2 * high,) + piece, BF16),
            shape((rows, half, chan), BF16),
            shape((rows, half, chan), BF16),
            shape((rows, half), F32),
            shape((rows, half), F32),
            shape((pair_width, chan), BF16),
            shape((1, chan), F32),
            shape((seqs, flat), BF16),
            grad_shape,
            shape((rows, seqs), F32),
        ),
        (
            index,
            left,
            alignment_row_mask,
            residue_mask_vector.reshape(1, cols),
            pair_update_cotangent,
            output_weight,
        ),
        (
            pltpu.VMEM((pair_width, chan), F32),
            pltpu.VMEM((cols, LANES), F32),
            pltpu.VMEM((cols, seqs), F32),
        ),
        us=6,
    )
    keep, send, near_grad = call(
        keep_kernel,
        (shape(slab, F32), shape(slab, BF16), grad_shape),
        (index, left_t, w2, near, swap(send, 1)),
        (pltpu.VMEM((2 * high,) + piece, F32),),
        us=4,
    )
    normal, inverse, right_copy, other_copy, normal_token = call(
        normal_kernel,
        (shape((seqs * rows, 2 * width), BF16), shape((seqs * rows, 1), F32))
        + (shape(piece, BF16),) * 2,
        (alignment_activations, gain, shift, right, blocks[2]),
        scalars=0,
        us=10,
        after=(keep,),
        token=True,
    )
    blocks[4] = swap(right_copy, 4)
    blocks[6] = swap(other_copy, 4)
    blocks[10] = swap(other_copy, 8)
    line = call(
        line_kernel,
        (shape(piece, BF16),) * (high - 3) + (shape((8, LANES), F32),),
        tuple(blocks[4 * k] for k in range(3, high)),
        scalars=0,
        us=0.1,
        after=(normal_token, blocks[8]),
    )
    for k in range(3, high):
        blocks[4 * k + 2] = swap(line[k - 3], 2)
    right_own, *sends = call(
        high_kernel,
        (shape(piece, F32),) + (shape(piece, BF16),) * (high - 1),
        (keep, swap(send, 2)),
        scalars=0,
        us=10,
        after=(line[-1], blocks[4], blocks[10]),
    )
    right_parts = tuple(swap(sends[k - 1], 4 * k) for k in range(high - 1, 0, -1))
    right_near = call(
        place_kernel,
        shape((proj_width, half, seqs), BF16),
        (index,) + tuple(blocks[rel] for rel in range(0, devices, 2)),
        after=(right_own,),
    )
    right_far = swap(right_near, 1)
    near_w, near_left, near_outer = call(
        near_kernel,
        (shape((pair_width, chan), F32), shape((flat, seqs), F32), outer_shape),
        (left, near, near_grad, right_near),
        scalars=0,
        us=100,
    )
    far_outer, w_own, *w_sends = call(
        far_kernel,
        (outer_shape,) + (shape((quarter, chan), BF16),) * 4,
        (index, left, far, near_w, right_far),
        (pltpu.VMEM((pair_width, chan), F32),),
        us=0.02,
    )
    left_sum = call(
        left_kernel,
        shape((flat, seqs), F32),
        (near_left, far_grad, right_far),
        scalars=0,
        us=0.02,
        after=(w_own,),
    )
    pack_shape = shape((2 * proj_width * (width // LANES) + TAIL, LANES), BF16)
    grads, pack = call(
        sums_kernel,
        (shape((seqs * rows, LANES), BF16), pack_shape),
        (right_own,) + right_parts + (normal, wl, wr, mask_own, left_sum, b_part),
        (pltpu.VMEM((flat, seqs), F32), pltpu.VMEM((seqs * rows, LANES), F32)),
        scalars=0,
        us=2,
    )
    distances = [devices // 2 >> n for n in range(high.bit_length() - 1)]
    packs = [pack]

    def merge_pack(after):
        last = packs[-1]
        packs.append(
            call(
                merge_kernel,
                pack_shape,
                (last, swap(last, (distances + [2])[len(packs) - 1])),
                scalars=0,
                us=0.1,
                after=after,
            )
        )

    weights = call(
        merge_kernel,
        shape((quarter, chan), BF16),
        (w_own,) + tuple(swap(value, m + 1) for m, value in enumerate(w_sends)),
        scalars=0,
        us=0.1,
        after=(pack,),
    )
    alignment_gradient, norm_token = call(
        norm_kernel,
        shape((seqs, rows, width), BF16),
        (normal, inverse, gain, wl, wr, grads),
        (pltpu.VMEM((LANES, width), BF16),),
        scalars=0,
        us=0.02,
        after=(weights,),
        token=True,
    )
    pair, pair_token = call(
        pair_kernel,
        shape((rows, cols, chan), BF16),
        (index, w2, output_bias.reshape(1, chan), near_outer, far_outer, near_factor, far_factor),
        (pltpu.VMEM((chan, pair_width), BF16),),
        us=0.02,
        after=(norm_token,),
        token=True,
    )
    merge_pack((pair_token,))
    while len(packs) < len(distances) + 2:
        merge_pack(())
    for n, distance in enumerate(distances):
        weights = call(
            merge_kernel,
            shape((quarter, chan), BF16),
            (weights, swap(weights, distance)),
            scalars=0,
            us=0.1,
            after=(packs[n + 1],),
        )
    weights = call(
        join_kernel,
        shape((2, quarter, chan), BF16),
        (weights, swap(weights, 2)),
        scalars=0,
        us=0.1,
    )
    w_out_grad = call(
        weight_kernel,
        shape((pair_width, chan), F32),
        (index, weights, swap(weights, 1)),
        (pltpu.VMEM((pair_width, chan), F32),),
        us=0.1,
    )

    w_left, b_left, w_right, b_right, b_out, gain_grad, shift_grad = call(
        unpack_kernel,
        (
            shape((proj_width, width), F32),
            shape((1, proj_width), F32),
            shape((proj_width, width), F32),
            shape((1, proj_width), F32),
            shape((1, chan), F32),
            shape((1, width), F32),
            shape((1, width), F32),
        ),
        (packs[-1], swap(packs[-1], 1)),
        scalars=0,
    )
    return (
        pair,
        alignment_gradient,
        w_left.T,
        b_left.reshape(-1),
        w_right.T,
        b_right.reshape(-1),
        w_out_grad,
        b_out.reshape(-1),
        gain_grad.reshape(-1),
        shift_grad.reshape(-1),
    )


def solution(mesh):
    return jax.shard_map(
        functools.partial(body, mesh.shape["res"]),
        mesh=mesh,
        in_specs=(
            P(None, ("grp", "res"), None),
            P(None, "grp"),
            P("grp"),
            P(),
            P(),
            P(),
            P(),
            P(),
            P(),
            P(),
            P(),
            P(("grp", "res"), None, None),
        ),
        out_specs=(
            P(("grp", "res"), None, None),
            P(None, ("grp", "res"), None),
            P("grp", None),
            P("grp"),
            P("grp", None),
            P("grp"),
            P("grp", None),
            P("grp"),
            P("grp"),
            P("grp"),
        ),
        check_vma=False,
    )
```

```python
import functools
import math

import jax
import jax.numpy as jnp
from jax import lax
from jax.experimental import pallas as pl
from jax.experimental.pallas import tpu as pltpu
from jax.sharding import PartitionSpec as P

EPS = 1e-05
LAST_DIMS = (((1,), (1,)), ((), ()))
FIRST_DIMS = (((0,), (0,)), ((), ()))
MIB = 1024 * 1024
LANES = 128
TAIL = 16
F32 = jnp.float32
BF16 = jnp.bfloat16


def tiled_bytes(dims, dtype):
    dims = tuple(dims)
    lanes = -(-dims[-1] // LANES) * LANES
    sublanes = -(-(dims[-2] if len(dims) > 1 else 1) // 16) * 16
    return math.prod(dims[:-2]) * sublanes * lanes * jnp.dtype(dtype).itemsize


def call(
    kernel, out_shape, args, scratch=(), scalars=1, us=1.0, after=(), fetched=(), token=False, grant=0, **static
):
    count = len(args)
    specs = [pl.BlockSpec(memory_space=pl.ANY)] * len(after)
    specs += [pl.BlockSpec(memory_space=pltpu.SMEM)] * scalars
    for k in range(scalars, count):
        specs.append(pl.BlockSpec(memory_space=pltpu.HBM if k in fetched else pltpu.VMEM))
    outs = list(out_shape) if isinstance(out_shape, (tuple, list)) else [out_shape]
    if token:
        outs.append(shape((8, LANES), F32))
    held = list(args[scalars:]) + outs + list(scratch)
    need = sum(tiled_bytes(value.shape, value.dtype) for value in held)
    places = [pltpu.VMEM(args[k].shape, args[k].dtype) for k in fetched]
    semaphores = [pltpu.SemaphoreType.DMA((len(fetched),))] if fetched else []

    def run(*refs):
        ins = list(refs[len(after) : len(after) + count])
        rest = list(refs[len(after) + count :])
        if fetched:
            *rest, done = rest
            held_refs = rest[-len(fetched) :]
            rest = rest[: -len(fetched)]
            copies = [
                pltpu.make_async_copy(ins[k], ref, done.at[n])
                for n, (k, ref) in enumerate(zip(fetched, held_refs))
            ]
            for copy in copies:
                copy.start()
            for k, ref, copy in zip(fetched, held_refs, copies):
                ins[k] = Fetched(ref, copy)
        if token:
            rest.pop(len(outs) - 1)[...] = jnp.zeros((8, LANES), F32)
        kernel(*ins, *rest, **static)

    result = pl.pallas_call(
        run,
        name=kernel.__name__,
        out_shape=tuple(outs),
        in_specs=specs,
        out_specs=tuple([pl.BlockSpec(memory_space=pltpu.VMEM)] * len(outs)),
        scratch_shapes=list(scratch) + places + semaphores,
        compiler_params=pltpu.CompilerParams(vmem_limit_bytes=grant or min(need + 6 * MIB, 56 * MIB)),
        cost_estimate=pl.CostEstimate(
            flops=int(us * 1.1e9), bytes_accessed=int(us * 1e5), transcendentals=0
        ),
    )(*after, *args)
    return result if len(outs) > 1 else result[0]


class Fetched:
    def __init__(self, ref, copy):
        self.ref, self.copy, self.shape = ref, copy, ref.shape

    def __getitem__(self, index):
        if self.copy is not None:
            self.copy.wait()
            self.copy = None
        return self.ref[index]


def shape(dims, dtype):
    return jax.ShapeDtypeStruct(tuple(dims), dtype)


def dot(a, b, dims=(((1,), (0,)), ((), ()))):
    return lax.dot_general(a, b, dims, preferred_element_type=F32)


def normalize(x, gain, shift):
    centered = x - jnp.mean(x, -1, keepdims=True)
    inverse = lax.rsqrt(jnp.mean(centered * centered, -1, keepdims=True) + EPS)
    xhat = centered * inverse
    return xhat, inverse, (xhat * gain + shift).astype(BF16)


def column_of(row):
    return jnp.broadcast_to(row, (8, row.shape[1])).T[:, :1]


def project_kernel(
    index_ref, x_ref, mask_ref, gain_ref, shift_ref, wl_ref, wr_ref, bl_ref, br_ref,
    left_ref, right_ref, proj, right_rows, weights, mask_t,
):
    seqs, rows, width = x_ref.shape
    proj_width = right_ref.shape[0]
    begin = pl.multiple_of(index_ref[0] * rows, rows)
    weights[:proj_width, :] = wl_ref[...]
    weights[proj_width : 2 * proj_width, :] = wr_ref[...]
    weights[2 * proj_width :, :] = jnp.zeros((LANES - 2 * proj_width, width), BF16)
    bias_left = column_of(bl_ref[...])
    bias_right = column_of(br_ref[...])
    step = 16
    for first in range(0, seqs, step):
        x = x_ref[first : first + step].astype(F32).reshape(step * rows, width)
        normalized = normalize(x, gain_ref[...], shift_ref[...])[2]
        proj[first * rows : (first + step) * rows, :] = dot(normalized, weights[...], LAST_DIMS)
    mask_t[...] = mask_ref[...].astype(F32).T
    mask_own = mask_t[pl.ds(begin, rows), :]
    for i in range(rows):
        block = proj[pl.ds(i, seqs, stride=rows), :].T
        mask_row = mask_own[i : i + 1, :]
        span = slice(i * proj_width, (i + 1) * proj_width)
        left_ref[span, :] = ((block[:proj_width] + bias_left) * mask_row).astype(BF16)
        right_rows[span, :] = (block[proj_width : 2 * proj_width] + bias_right) * mask_row
    for e in range(proj_width):
        right_ref[e] = right_rows[pl.ds(e, rows, stride=proj_width), :].astype(BF16)


def grad_columns(w2_ref, scaled_ref, grad):
    rows, cols, chan = scaled_ref.shape
    proj_width = grad.shape[0]
    for i in range(0, rows, 2):
        pair = scaled_ref[i : i + 2].reshape(2 * cols, chan)
        block = dot(w2_ref[...], pair, LAST_DIMS).astype(BF16)
        for e in range(proj_width):
            for sub in range(2):
                grad[e, (i + sub) * proj_width : (i + sub + 1) * proj_width, :] = block[
                    e * proj_width : (e + 1) * proj_width, sub * cols : (sub + 1) * cols
                ]


def right_columns(index_ref, left_t, grad, emit):
    proj_width, _, cols = grad.shape
    rows = left_t.shape[1] // proj_width
    high = cols // rows // 2
    own = index_ref[0] >> 1
    for e in range(0, proj_width, 2):
        block = jnp.concatenate([grad[e], grad[e + 1]], 1)
        sums = dot(left_t[...], block)
        for sub in range(2):
            part = sums[:, sub * cols : (sub + 1) * cols].T
            for q in range(2 * high):
                rel = q ^ own
                emit(e + sub, (rel & 1) * high + (rel >> 1), part[q * rows : (q + 1) * rows])


def scale_columns(half, mask_t_ref, mask_own, resid_t, resid_own, cot_ref, scaled_ref, factor_ref):
    rows = cot_ref.shape[0]
    cols = scaled_ref.shape[1]
    starts = [
        pl.multiple_of((2 * q + half) * rows, rows) for q in range(cols // rows)
    ]
    mask_cols = jnp.concatenate([mask_t_ref[pl.ds(s, rows), :] for s in starts], 0)
    resid_cols = jnp.concatenate([resid_t[pl.ds(s, rows), :] for s in starts], 0)
    counted = dot(mask_cols.astype(BF16), mask_own.astype(BF16), LAST_DIMS)
    factor_t = resid_cols[:, :1] * resid_own / counted
    factor_ref[...] = factor_t.T
    bias_sum = jnp.zeros((1, cot_ref.shape[2]), F32)
    for i in range(rows):
        cot = jnp.concatenate([cot_ref[i, pl.ds(s, rows), :] for s in starts], 0)
        scaled = (cot.astype(F32) * factor_t[:, i : i + 1]).astype(BF16)
        scaled_ref[i] = scaled
        bias_sum = bias_sum + jnp.sum(scaled.astype(F32), 0, keepdims=True)
    return bias_sum


def send_kernel(
    index_ref, left_ref, mask_ref, resid_ref, cot_ref, w_ref,
    send_ref, far_ref, near_ref, far_factor_ref, near_factor_ref, w2_ref, b_ref, left_t_ref, grad,
    mask_own_ref, wide, resid_t, mask_t,
):
    rows, cols, chan = cot_ref.shape
    proj_width = left_ref.shape[0] // rows
    index = index_ref[0]
    wide[...] = w_ref[...].astype(F32)
    for e in range(proj_width):
        w2_ref[e * proj_width : (e + 1) * proj_width, :] = wide[
            pl.ds(e, proj_width, stride=proj_width), :
        ].astype(BF16)
    left_t_ref[...] = left_ref[...].astype(F32).T.astype(BF16)
    resid_t[...] = jnp.broadcast_to(resid_ref[...].astype(F32), (LANES, cols)).T
    begin = pl.multiple_of(index * rows, rows)
    mask_t[...] = mask_ref[...].astype(F32).T
    mask_own = mask_t[pl.ds(begin, rows), :]
    mask_own_ref[...] = mask_own
    resid_own = resid_t[pl.ds(begin, rows), :].T[:1]
    side = index & 1
    shared = (mask_t, mask_own, resid_t, resid_own, cot_ref)
    far_sum = scale_columns(1 - side, *shared, far_ref, far_factor_ref)
    near_sum = scale_columns(side, *shared, near_ref, near_factor_ref)
    b_ref[...] = far_sum + near_sum
    grad_columns(w2_ref, far_ref, grad)

    def emit(e, slot, value):
        send_ref[slot, e] = value.astype(BF16)

    right_columns(index_ref, left_t_ref, grad, emit)


def keep_kernel(
    index_ref, left_t_ref, w2_ref, near_ref, far_part_ref, keep_ref, send_ref, grad, total
):
    high = keep_ref.shape[0]
    grad_columns(w2_ref, near_ref, grad)

    def emit(e, slot, value):
        total[slot, e] = value

    right_columns(index_ref, left_t_ref, grad, emit)
    keep_ref[...] = total[:high] + far_part_ref[:high].astype(F32)
    send_ref[...] = (total[high:] + far_part_ref[high:].astype(F32)).astype(BF16)


def high_kernel(keep_ref, other_ref, own_ref, *send_refs):
    own_ref[...] = keep_ref[0] + other_ref[0].astype(F32)
    for k, ref in enumerate(send_refs):
        ref[...] = (keep_ref[k + 1] + other_ref[k + 1].astype(F32)).astype(BF16)


def normal_kernel(
    x_ref, gain_ref, shift_ref, right_ref, other_ref,
    normal_ref, inverse_ref, right_copy_ref, other_copy_ref,
):
    seqs, rows, width = x_ref.shape
    right_copy_ref[...] = right_ref[...]
    other_copy_ref[...] = other_ref[...]
    step = 16
    for first in range(0, seqs, step):
        x = x_ref[first : first + step].astype(F32).reshape(step * rows, width)
        xhat, inverse, normalized = normalize(x, gain_ref[...], shift_ref[...])
        span = slice(first * rows, (first + step) * rows)
        normal_ref[span, :width] = normalized
        normal_ref[span, width:] = xhat.astype(BF16)
        inverse_ref[span, :] = inverse


def line_kernel(*refs):
    count = len(refs) // 2
    for k in range(count):
        refs[count + k][...] = refs[k][...]
    refs[-1][...] = jnp.zeros_like(refs[-1])


def place_kernel(index_ref, *refs):
    *blocks, out_ref = refs
    rows = blocks[0].shape[1]
    own = index_ref[0] >> 1
    for rel, ref in enumerate(blocks):
        out_ref[:, pl.ds(pl.multiple_of((own ^ rel) * rows, rows), rows), :] = ref[...]


def outer_columns(left_ref, right_ref, outer):
    proj_width, cols, seqs = right_ref.shape
    rows = left_ref.shape[0] // proj_width
    for e in range(0, proj_width, 2):
        pair = right_ref[e : e + 2].reshape(2 * cols, seqs)
        block = dot(left_ref[...], pair, LAST_DIMS).astype(BF16)
        for i in range(rows):
            for sub in range(2):
                outer[
                    i // 2,
                    (e + sub) * proj_width : (e + sub + 1) * proj_width,
                    (i % 2) * cols : (i % 2 + 1) * cols,
                ] = block[i * proj_width : (i + 1) * proj_width, sub * cols : (sub + 1) * cols]


def weight_columns(left_ref, right_ref, scaled_ref, w_ref, outer):
    rows, cols, chan = scaled_ref.shape
    outer_columns(left_ref, right_ref, outer)
    for p in range(rows // 2):
        w_ref[...] += dot(outer[p], scaled_ref[2 * p : 2 * p + 2].reshape(2 * cols, chan))


def left_columns(grad, right_ref, left_sum_ref):
    proj_width, cols, seqs = right_ref.shape
    for e in range(0, proj_width, 2):
        block = jnp.concatenate([grad[e], grad[e + 1]], 1)
        left_sum_ref[...] += dot(block, right_ref[e : e + 2].reshape(2 * cols, seqs))


def near_kernel(left_ref, scaled_ref, grad_ref, right_ref, w_sum_ref, left_sum_ref, outer_ref):
    w_sum_ref[...] = jnp.zeros_like(w_sum_ref)
    weight_columns(left_ref, right_ref, scaled_ref, w_sum_ref, outer_ref)
    left_sum_ref[...] = jnp.zeros_like(left_sum_ref)
    left_columns(grad_ref, right_ref, left_sum_ref)


def far_kernel(index_ref, left_ref, scaled_ref, w_sum_ref, right_ref, outer_ref, *refs):
    *quarter_refs, total = refs
    total[...] = w_sum_ref[...]
    weight_columns(left_ref, right_ref, scaled_ref, total, outer_ref)
    quarter = quarter_refs[0].shape[0]
    for m, ref in enumerate(quarter_refs):
        begin = pl.multiple_of(((index_ref[0] & 3) ^ m) * quarter, quarter)
        ref[...] = total[pl.ds(begin, quarter), :].astype(BF16)


def left_kernel(near_sum_ref, grad_ref, right_ref, left_sum_ref):
    left_sum_ref[...] = near_sum_ref[...]
    left_columns(grad_ref, right_ref, left_sum_ref)


def pair_kernel(
    index_ref, w2_ref, bias_ref, near_ref, far_ref, near_factor_ref, far_factor_ref, out_ref, w2_t
):
    rows = out_ref.shape[0]
    w2_t[...] = w2_ref[...].astype(F32).T.astype(BF16)
    bias = column_of(bias_ref[...])
    side = index_ref[0] & 1
    for half, outer, factor_ref in (
        (side, near_ref, near_factor_ref),
        (1 - side, far_ref, far_factor_ref),
    ):
        cols = outer.shape[2] // 2
        for p in range(rows // 2):
            projected = dot(w2_t[...], outer[p]) + bias
            for sub in range(2):
                i = 2 * p + sub
                block = projected[:, sub * cols : (sub + 1) * cols] * factor_ref[i : i + 1, :]
                block = block.T.astype(BF16)
                for q in range(cols // rows):
                    begin = pl.multiple_of((2 * q + half) * rows, rows)
                    out_ref[i, pl.ds(begin, rows), :] = block[q * rows : (q + 1) * rows]


def sums_kernel(
    right_own_ref, *refs
):
    *ins, grads_ref, pack_ref, right_sum, gathered = refs
    *right_refs, normal_ref, wl_ref, wr_ref, mask_own_ref, left_sum_ref, b_ref = ins
    seqs = mask_own_ref.shape[1]
    proj_width, rows, _ = right_own_ref.shape
    width = wl_ref.shape[1]
    total = right_own_ref[...]
    for ref in right_refs:
        total = total + ref[...].astype(F32)
    right_sum[...] = total.reshape(proj_width * rows, seqs)
    fill = jnp.zeros((LANES - 2 * proj_width, seqs), F32)
    bias_cols = jnp.zeros((LANES, seqs), F32)
    for i in range(rows):
        block = jnp.concatenate(
            [
                left_sum_ref[i * proj_width : (i + 1) * proj_width, :],
                right_sum[pl.ds(i, proj_width, stride=rows), :],
                fill,
            ],
            0,
        )
        block = (block * mask_own_ref[i : i + 1, :]).astype(BF16).astype(F32)
        bias_cols = bias_cols + block
        gathered[pl.ds(i, seqs, stride=rows), :] = block.T
    grads_ref[...] = gathered[...].astype(BF16)
    used = 2 * proj_width
    products = jnp.zeros((LANES, 2 * width), F32)
    step = 256
    for first in range(0, seqs * rows, step):
        products = products + dot(
            grads_ref[first : first + step, :], normal_ref[first : first + step, :], FIRST_DIMS
        )
    weights = jnp.concatenate([wl_ref[...], wr_ref[...]], 0).astype(F32)
    bias_sum = jnp.sum(bias_cols, 1, keepdims=True)
    gain_sum = jnp.sum(weights * products[:used, width:], 0, keepdims=True)
    shift_sum = jnp.sum(weights * bias_sum[:used], 0, keepdims=True)
    bias_row = jnp.broadcast_to(bias_sum, (LANES, LANES)).T[:1]
    pieces = [products[:used, k : k + LANES] for k in range(0, width, LANES)]
    pieces += [gain_sum[:, k : k + LANES] for k in range(0, width, LANES)]
    pieces += [shift_sum[:, k : k + LANES] for k in range(0, width, LANES)]
    pieces += [bias_row, b_ref[...]]
    pieces += [jnp.zeros((TAIL - 2 - 2 * (width // LANES), LANES), F32)]
    pack_ref[...] = jnp.concatenate(pieces, 0).astype(BF16)


def norm_kernel(normal_ref, inverse_ref, gain_ref, wl_ref, wr_ref, grads_ref, out_ref, weights):
    seqs, rows, width = out_ref.shape
    proj_width = wl_ref.shape[0]
    weights[...] = jnp.zeros_like(weights)
    weights[:proj_width, :] = wl_ref[...]
    weights[proj_width : 2 * proj_width, :] = wr_ref[...]
    step = 16
    for first in range(0, seqs, step):
        span = slice(first * rows, (first + step) * rows)
        xhat = normal_ref[span, width:].astype(F32)
        g = dot(grads_ref[span, :], weights[...]) * gain_ref[...]
        result = (
            g - jnp.mean(g, -1, keepdims=True) - xhat * jnp.mean(g * xhat, -1, keepdims=True)
        ) * inverse_ref[span, :]
        out_ref[first : first + step] = result.astype(BF16).reshape(step, rows, width)


def tree_sum(values):
    values = [value.astype(F32) for value in values]
    while len(values) > 1:
        values = [a + b for a, b in zip(values[::2], values[1::2])]
    return values[0]


def merge_kernel(*refs):
    *ins, out_ref = refs
    out_ref[...] = tree_sum([ref[...] for ref in ins]).astype(BF16)


def total_kernel(pack_ref, *refs):
    *quarter_refs, out_ref = refs
    head = pack_ref.shape[0]
    out_ref[:head, :] = pack_ref[...]
    out_ref[head:, :] = tree_sum([ref[...] for ref in quarter_refs]).astype(BF16)


def side_kernel(own_ref, other_ref, out_ref, *, head):
    rows = own_ref.shape[0]
    out_ref[:head, :] = tree_sum([own_ref[:head, :], other_ref[:head, :]]).astype(BF16)
    out_ref[head:rows, :] = own_ref[head:, :]
    out_ref[rows:, :] = other_ref[head:, :]


def unpack_kernel(index_ref, *refs):
    ins = refs[:2]
    wl_ref, bl_ref, wr_ref, br_ref, w_out_ref, b_ref, gain_ref, shift_ref, placed = refs[2:]
    proj_width, width = wl_ref.shape
    used = 2 * proj_width
    parts = width // LANES
    head = parts * used + TAIL
    total = tree_sum([ref[:head, :] for ref in ins])
    tail = total[parts * used :]
    for k in range(parts):
        span = slice(k * LANES, (k + 1) * LANES)
        wl_ref[:, span] = total[k * used : k * used + proj_width]
        wr_ref[:, span] = total[k * used + proj_width : (k + 1) * used]
        gain_ref[:, span] = tail[k : k + 1]
        shift_ref[:, span] = tail[parts + k : parts + k + 1]
    bl_ref[...] = tail[2 * parts : 2 * parts + 1, :proj_width]
    br_ref[...] = tail[2 * parts : 2 * parts + 1, proj_width:used]
    b_ref[...] = tail[2 * parts + 1 : 2 * parts + 2, :]
    quarter = placed.shape[0] // 4
    for core, ref in enumerate(ins):
        for side in range(2):
            begin = pl.multiple_of(((index_ref[0] & 3) ^ (core + 2 * side)) * quarter, quarter)
            span = slice(head + side * quarter, head + (side + 1) * quarter)
            placed[pl.ds(begin, quarter), :] = ref[span, :].astype(F32)
    for c in range(proj_width):
        w_out_ref[c * proj_width : (c + 1) * proj_width, :] = placed[
            pl.ds(c, proj_width, stride=proj_width), :
        ]


def body(
    devices,
    alignment_activations,
    alignment_row_mask,
    residue_mask_vector,
    layer_norm_gain,
    layer_norm_bias,
    left_weight,
    left_bias,
    right_weight,
    right_bias,
    output_weight,
    output_bias,
    pair_update_cotangent,
):
    seqs, rows, width = alignment_activations.shape
    cols = alignment_row_mask.shape[1]
    proj_width = left_weight.shape[1]
    pair_width, chan = output_weight.shape
    high = devices // 4
    half = cols // 2
    quarter = pair_width // 4
    flat = rows * proj_width
    index = lax.axis_index("res").astype(jnp.int32).reshape(1)
    gain = layer_norm_gain.reshape(1, width)
    shift = layer_norm_bias.reshape(1, width)
    wl, wr = left_weight.T, right_weight.T
    piece = (proj_width, rows, seqs)

    def swap(value, rel):
        return lax.ppermute(value, "res", [(d, d ^ rel) for d in range(devices)])

    slab = (high,) + piece
    left, right = call(
        project_kernel,
        (shape((flat, seqs), BF16), shape(piece, BF16)),
        (index, alignment_activations, alignment_row_mask, gain, shift, wl, wr)
        + (left_bias.reshape(1, proj_width), right_bias.reshape(1, proj_width)),
        (
            pltpu.VMEM((seqs * rows, LANES), F32),
            pltpu.VMEM((flat, seqs), F32),
            pltpu.VMEM((LANES, width), BF16),
            pltpu.VMEM((cols, seqs), F32),
        ),
        us=4,
        fetched=tuple(range(1, 9)),
        grant=60 * MIB,
    )
    blocks = {0: right, 2: swap(right, 2)}
    for k in range(2, high):
        blocks[4 * k] = swap(right, 4 * k)
    grad_shape = shape((proj_width, flat, half), BF16)
    outer_shape = shape((rows // 2, pair_width, 2 * half), BF16)
    send, far, near, far_factor, near_factor, w2, b_part, left_t, far_grad, mask_own = call(
        send_kernel,
        (
            shape((2 * high,) + piece, BF16),
            shape((rows, half, chan), BF16),
            shape((rows, half, chan), BF16),
            shape((rows, half), F32),
            shape((rows, half), F32),
            shape((pair_width, chan), BF16),
            shape((1, chan), F32),
            shape((seqs, flat), BF16),
            grad_shape,
            shape((rows, seqs), F32),
        ),
        (
            index,
            left,
            alignment_row_mask,
            residue_mask_vector.reshape(1, cols),
            pair_update_cotangent,
            output_weight,
        ),
        (
            pltpu.VMEM((pair_width, chan), F32),
            pltpu.VMEM((cols, LANES), F32),
            pltpu.VMEM((cols, seqs), F32),
        ),
        us=6,
    )
    keep, send, near_grad = call(
        keep_kernel,
        (shape(slab, F32), shape(slab, BF16), grad_shape),
        (index, left_t, w2, near, swap(send, 1)),
        (pltpu.VMEM((2 * high,) + piece, F32),),
        us=4,
    )
    normal, inverse, right_copy, other_copy, normal_token = call(
        normal_kernel,
        (shape((seqs * rows, 2 * width), BF16), shape((seqs * rows, 1), F32))
        + (shape(piece, BF16),) * 2,
        (alignment_activations, gain, shift, right, blocks[2]),
        scalars=0,
        us=10,
        after=(keep,),
        token=True,
    )
    blocks[4] = swap(right_copy, 4)
    blocks[6] = swap(other_copy, 4)
    blocks[10] = swap(other_copy, 8)
    line = call(
        line_kernel,
        (shape(piece, BF16),) * (high - 3) + (shape((8, LANES), F32),),
        tuple(blocks[4 * k] for k in range(3, high)),
        scalars=0,
        us=0.1,
        after=(normal_token, blocks[8]),
    )
    for k in range(3, high):
        blocks[4 * k + 2] = swap(line[k - 3], 2)
    right_own, *sends = call(
        high_kernel,
        (shape(piece, F32),) + (shape(piece, BF16),) * (high - 1),
        (keep, swap(send, 2)),
        scalars=0,
        us=10,
        after=(line[-1], blocks[4], blocks[10]),
    )
    right_parts = tuple(swap(sends[k - 1], 4 * k) for k in range(high - 1, 0, -1))
    right_near = call(
        place_kernel,
        shape((proj_width, half, seqs), BF16),
        (index,) + tuple(blocks[rel] for rel in range(0, devices, 2)),
        after=(right_own,),
    )
    right_far = swap(right_near, 1)
    near_w, near_left, near_outer = call(
        near_kernel,
        (shape((pair_width, chan), F32), shape((flat, seqs), F32), outer_shape),
        (left, near, near_grad, right_near),
        scalars=0,
        us=100,
    )
    far_outer, w_own, *w_sends = call(
        far_kernel,
        (outer_shape,) + (shape((quarter, chan), BF16),) * 4,
        (index, left, far, near_w, right_far),
        (pltpu.VMEM((pair_width, chan), F32),),
        us=0.02,
    )
    left_sum = call(
        left_kernel,
        shape((flat, seqs), F32),
        (near_left, far_grad, right_far),
        scalars=0,
        us=0.02,
        after=(w_own,),
    )
    pack_shape = shape((2 * proj_width * (width // LANES) + TAIL, LANES), BF16)
    grads, pack = call(
        sums_kernel,
        (shape((seqs * rows, LANES), BF16), pack_shape),
        (right_own,) + right_parts + (normal, wl, wr, mask_own, left_sum, b_part),
        (pltpu.VMEM((flat, seqs), F32), pltpu.VMEM((seqs * rows, LANES), F32)),
        scalars=0,
        us=2,
    )
    total_shape = shape((pack_shape.shape[0] + quarter, LANES), BF16)
    merged = call(
        total_kernel,
        total_shape,
        (pack, w_own) + tuple(swap(value, m + 1) for m, value in enumerate(w_sends)),
        scalars=0,
        us=0.1,
    )
    alignment_gradient, norm_token = call(
        norm_kernel,
        shape((seqs, rows, width), BF16),
        (normal, inverse, gain, wl, wr, grads),
        (pltpu.VMEM((LANES, width), BF16),),
        scalars=0,
        us=0.02,
        after=(merged,),
        token=True,
    )
    pair, pair_token = call(
        pair_kernel,
        shape((rows, cols, chan), BF16),
        (index, w2, output_bias.reshape(1, chan), near_outer, far_outer, near_factor, far_factor),
        (pltpu.VMEM((chan, pair_width), BF16),),
        us=0.02,
        after=(norm_token,),
        token=True,
    )
    distances = [devices // 2 >> n for n in range(high.bit_length() - 1)]
    for n, distance in enumerate(distances):
        merged = call(
            merge_kernel,
            total_shape,
            (merged, swap(merged, distance)),
            scalars=0,
            us=0.1,
            after=(pair_token if n else norm_token,),
        )
    merged = call(
        side_kernel,
        shape((total_shape.shape[0] + quarter, LANES), BF16),
        (merged, swap(merged, 2)),
        scalars=0,
        us=0.1,
        head=pack_shape.shape[0],
    )
    w_left, b_left, w_right, b_right, w_out_grad, b_out, gain_grad, shift_grad = call(
        unpack_kernel,
        (
            shape((proj_width, width), F32),
            shape((1, proj_width), F32),
            shape((proj_width, width), F32),
            shape((1, proj_width), F32),
            shape((pair_width, chan), F32),
            shape((1, chan), F32),
            shape((1, width), F32),
            shape((1, width), F32),
        ),
        (index, merged, swap(merged, 1)),
        (pltpu.VMEM((pair_width, chan), F32),),
    )
    return (
        pair,
        alignment_gradient,
        w_left.T,
        b_left.reshape(-1),
        w_right.T,
        b_right.reshape(-1),
        w_out_grad,
        b_out.reshape(-1),
        gain_grad.reshape(-1),
        shift_grad.reshape(-1),
    )


def solution(mesh):
    return jax.shard_map(
        functools.partial(body, mesh.shape["res"]),
        mesh=mesh,
        in_specs=(
            P(None, ("grp", "res"), None),
            P(None, "grp"),
            P("grp"),
            P(),
            P(),
            P(),
            P(),
            P(),
            P(),
            P(),
            P(),
            P(("grp", "res"), None, None),
        ),
        out_specs=(
            P(("grp", "res"), None, None),
            P(None, ("grp", "res"), None),
            P("grp", None),
            P("grp"),
            P("grp", None),
            P("grp"),
            P("grp", None),
            P("grp"),
            P("grp"),
            P("grp"),
        ),
        check_vma=False,
    )
```

```python
import functools
import math

import jax
import jax.numpy as jnp
from jax import lax
from jax.experimental import pallas as pl
from jax.experimental.pallas import tpu as pltpu
from jax.sharding import PartitionSpec as P

EPS = 1e-05
LAST_DIMS = (((1,), (1,)), ((), ()))
FIRST_DIMS = (((0,), (0,)), ((), ()))
MIB = 1024 * 1024
LANES = 128
TAIL = 16
F32 = jnp.float32
BF16 = jnp.bfloat16


def tiled_bytes(dims, dtype):
    dims = tuple(dims)
    lanes = -(-dims[-1] // LANES) * LANES
    sublanes = -(-(dims[-2] if len(dims) > 1 else 1) // 16) * 16
    return math.prod(dims[:-2]) * sublanes * lanes * jnp.dtype(dtype).itemsize


def call(
    kernel, out_shape, args, scratch=(), scalars=1, us=1.0, after=(), fetched=(), token=False, grant=0, **static
):
    count = len(args)
    specs = [pl.BlockSpec(memory_space=pl.ANY)] * len(after)
    specs += [pl.BlockSpec(memory_space=pltpu.SMEM)] * scalars
    for k in range(scalars, count):
        specs.append(pl.BlockSpec(memory_space=pltpu.HBM if k in fetched else pltpu.VMEM))
    outs = list(out_shape) if isinstance(out_shape, (tuple, list)) else [out_shape]
    if token:
        outs.append(shape((8, LANES), F32))
    held = list(args[scalars:]) + outs + list(scratch)
    need = sum(tiled_bytes(value.shape, value.dtype) for value in held)
    places = [pltpu.VMEM(args[k].shape, args[k].dtype) for k in fetched]
    semaphores = [pltpu.SemaphoreType.DMA((len(fetched),))] if fetched else []

    def run(*refs):
        ins = list(refs[len(after) : len(after) + count])
        rest = list(refs[len(after) + count :])
        if fetched:
            *rest, done = rest
            held_refs = rest[-len(fetched) :]
            rest = rest[: -len(fetched)]
            copies = [
                pltpu.make_async_copy(ins[k], ref, done.at[n])
                for n, (k, ref) in enumerate(zip(fetched, held_refs))
            ]
            for copy in copies:
                copy.start()
            for k, ref, copy in zip(fetched, held_refs, copies):
                ins[k] = Fetched(ref, copy)
        if token:
            rest.pop(len(outs) - 1)[...] = jnp.zeros((8, LANES), F32)
        kernel(*ins, *rest, **static)

    result = pl.pallas_call(
        run,
        name=kernel.__name__,
        out_shape=tuple(outs),
        in_specs=specs,
        out_specs=tuple([pl.BlockSpec(memory_space=pltpu.VMEM)] * len(outs)),
        scratch_shapes=list(scratch) + places + semaphores,
        compiler_params=pltpu.CompilerParams(vmem_limit_bytes=grant or min(need + 6 * MIB, 56 * MIB)),
        cost_estimate=pl.CostEstimate(
            flops=int(us * 1.1e9), bytes_accessed=int(us * 1e5), transcendentals=0
        ),
    )(*after, *args)
    return result if len(outs) > 1 else result[0]


class Fetched:
    def __init__(self, ref, copy):
        self.ref, self.copy, self.shape = ref, copy, ref.shape

    def __getitem__(self, index):
        if self.copy is not None:
            self.copy.wait()
            self.copy = None
        return self.ref[index]


def shape(dims, dtype):
    return jax.ShapeDtypeStruct(tuple(dims), dtype)


def dot(a, b, dims=(((1,), (0,)), ((), ()))):
    return lax.dot_general(a, b, dims, preferred_element_type=F32)


def normalize(x, gain, shift):
    centered = x - jnp.mean(x, -1, keepdims=True)
    inverse = lax.rsqrt(jnp.mean(centered * centered, -1, keepdims=True) + EPS)
    xhat = centered * inverse
    return xhat, inverse, (xhat * gain + shift).astype(BF16)


def column_of(row):
    return jnp.broadcast_to(row, (8, row.shape[1])).T[:, :1]


def project_kernel(
    index_ref, x_ref, mask_ref, gain_ref, shift_ref, wl_ref, wr_ref, bl_ref, br_ref,
    left_ref, right_ref, proj, right_rows, weights, mask_t,
):
    seqs, rows, width = x_ref.shape
    proj_width = right_ref.shape[0]
    begin = pl.multiple_of(index_ref[0] * rows, rows)
    weights[:proj_width, :] = wl_ref[...]
    weights[proj_width : 2 * proj_width, :] = wr_ref[...]
    weights[2 * proj_width :, :] = jnp.zeros((LANES - 2 * proj_width, width), BF16)
    bias_left = column_of(bl_ref[...])
    bias_right = column_of(br_ref[...])
    step = 16
    for first in range(0, seqs, step):
        x = x_ref[first : first + step].astype(F32).reshape(step * rows, width)
        normalized = normalize(x, gain_ref[...], shift_ref[...])[2]
        proj[first * rows : (first + step) * rows, :] = dot(normalized, weights[...], LAST_DIMS)
    mask_t[...] = mask_ref[...].astype(F32).T
    mask_own = mask_t[pl.ds(begin, rows), :]
    for i in range(rows):
        block = proj[pl.ds(i, seqs, stride=rows), :].T
        mask_row = mask_own[i : i + 1, :]
        span = slice(i * proj_width, (i + 1) * proj_width)
        left_ref[span, :] = ((block[:proj_width] + bias_left) * mask_row).astype(BF16)
        right_rows[span, :] = (block[proj_width : 2 * proj_width] + bias_right) * mask_row
    for e in range(proj_width):
        right_ref[e] = right_rows[pl.ds(e, rows, stride=proj_width), :].astype(BF16)


def grad_columns(w2_ref, scaled_ref, grad):
    rows, cols, chan = scaled_ref.shape
    proj_width = grad.shape[0]
    for i in range(0, rows, 2):
        pair = scaled_ref[i : i + 2].reshape(2 * cols, chan)
        block = dot(w2_ref[...], pair, LAST_DIMS).astype(BF16)
        for e in range(proj_width):
            for sub in range(2):
                grad[e, (i + sub) * proj_width : (i + sub + 1) * proj_width, :] = block[
                    e * proj_width : (e + 1) * proj_width, sub * cols : (sub + 1) * cols
                ]


def right_columns(index_ref, left_t, grad, emit):
    proj_width, _, cols = grad.shape
    rows = left_t.shape[1] // proj_width
    high = cols // rows // 2
    own = index_ref[0] >> 1
    for e in range(0, proj_width, 2):
        block = jnp.concatenate([grad[e], grad[e + 1]], 1)
        sums = dot(left_t[...], block)
        for sub in range(2):
            part = sums[:, sub * cols : (sub + 1) * cols].T
            for q in range(2 * high):
                rel = q ^ own
                emit(e + sub, (rel & 1) * high + (rel >> 1), part[q * rows : (q + 1) * rows])


def scale_columns(half, mask_t_ref, mask_own, resid_t, resid_own, cot_ref, scaled_ref, factor_ref):
    rows = cot_ref.shape[0]
    cols = scaled_ref.shape[1]
    starts = [
        pl.multiple_of((2 * q + half) * rows, rows) for q in range(cols // rows)
    ]
    mask_cols = jnp.concatenate([mask_t_ref[pl.ds(s, rows), :] for s in starts], 0)
    resid_cols = jnp.concatenate([resid_t[pl.ds(s, rows), :] for s in starts], 0)
    counted = dot(mask_cols.astype(BF16), mask_own.astype(BF16), LAST_DIMS)
    factor_t = resid_cols[:, :1] * resid_own / counted
    factor_ref[...] = factor_t.T
    bias_sum = jnp.zeros((1, cot_ref.shape[2]), F32)
    for i in range(rows):
        cot = jnp.concatenate([cot_ref[i, pl.ds(s, rows), :] for s in starts], 0)
        scaled = (cot.astype(F32) * factor_t[:, i : i + 1]).astype(BF16)
        scaled_ref[i] = scaled
        bias_sum = bias_sum + jnp.sum(scaled.astype(F32), 0, keepdims=True)
    return bias_sum


def send_kernel(
    index_ref, left_ref, mask_ref, resid_ref, cot_ref, w_ref,
    send_ref, far_ref, near_ref, far_factor_ref, near_factor_ref, w2_ref, b_ref, left_t_ref, grad,
    mask_own_ref, wide, resid_t, mask_t,
):
    rows, cols, chan = cot_ref.shape
    proj_width = left_ref.shape[0] // rows
    index = index_ref[0]
    wide[...] = w_ref[...].astype(F32)
    for e in range(proj_width):
        w2_ref[e * proj_width : (e + 1) * proj_width, :] = wide[
            pl.ds(e, proj_width, stride=proj_width), :
        ].astype(BF16)
    left_t_ref[...] = left_ref[...].astype(F32).T.astype(BF16)
    resid_t[...] = jnp.broadcast_to(resid_ref[...].astype(F32), (LANES, cols)).T
    begin = pl.multiple_of(index * rows, rows)
    mask_t[...] = mask_ref[...].astype(F32).T
    mask_own = mask_t[pl.ds(begin, rows), :]
    mask_own_ref[...] = mask_own
    resid_own = resid_t[pl.ds(begin, rows), :].T[:1]
    side = index & 1
    shared = (mask_t, mask_own, resid_t, resid_own, cot_ref)
    far_sum = scale_columns(1 - side, *shared, far_ref, far_factor_ref)
    near_sum = scale_columns(side, *shared, near_ref, near_factor_ref)
    b_ref[...] = far_sum + near_sum
    grad_columns(w2_ref, far_ref, grad)

    def emit(e, slot, value):
        send_ref[slot, e] = value.astype(BF16)

    right_columns(index_ref, left_t_ref, grad, emit)


def keep_kernel(
    index_ref, left_t_ref, w2_ref, near_ref, far_part_ref, keep_ref, send_ref, grad, total
):
    high = keep_ref.shape[0]
    grad_columns(w2_ref, near_ref, grad)

    def emit(e, slot, value):
        total[slot, e] = value

    right_columns(index_ref, left_t_ref, grad, emit)
    keep_ref[...] = total[:high] + far_part_ref[:high].astype(F32)
    send_ref[...] = (total[high:] + far_part_ref[high:].astype(F32)).astype(BF16)


def high_kernel(keep_ref, other_ref, own_ref, *send_refs):
    own_ref[...] = keep_ref[0] + other_ref[0].astype(F32)
    for k, ref in enumerate(send_refs):
        ref[...] = (keep_ref[k + 1] + other_ref[k + 1].astype(F32)).astype(BF16)


def normal_kernel(
    x_ref, gain_ref, shift_ref, right_ref, other_ref,
    normal_ref, inverse_ref, right_copy_ref, other_copy_ref,
):
    seqs, rows, width = x_ref.shape
    right_copy_ref[...] = right_ref[...]
    other_copy_ref[...] = other_ref[...]
    step = 16
    for first in range(0, seqs, step):
        x = x_ref[first : first + step].astype(F32).reshape(step * rows, width)
        xhat, inverse, normalized = normalize(x, gain_ref[...], shift_ref[...])
        span = slice(first * rows, (first + step) * rows)
        normal_ref[span, :width] = normalized
        normal_ref[span, width:] = xhat.astype(BF16)
        inverse_ref[span, :] = inverse


def line_kernel(*refs):
    count = len(refs) // 2
    for k in range(count):
        refs[count + k][...] = refs[k][...]
    refs[-1][...] = jnp.zeros_like(refs[-1])


def place_kernel(index_ref, *refs):
    *blocks, out_ref = refs
    rows = blocks[0].shape[1]
    own = index_ref[0] >> 1
    for rel, ref in enumerate(blocks):
        out_ref[:, pl.ds(pl.multiple_of((own ^ rel) * rows, rows), rows), :] = ref[...]


def outer_columns(left_ref, right_ref, outer):
    proj_width, cols, seqs = right_ref.shape
    rows = left_ref.shape[0] // proj_width
    for e in range(0, proj_width, 2):
        pair = right_ref[e : e + 2].reshape(2 * cols, seqs)
        block = dot(left_ref[...], pair, LAST_DIMS).astype(BF16)
        for i in range(rows):
            for sub in range(2):
                outer[
                    i // 2,
                    (e + sub) * proj_width : (e + sub + 1) * proj_width,
                    (i % 2) * cols : (i % 2 + 1) * cols,
                ] = block[i * proj_width : (i + 1) * proj_width, sub * cols : (sub + 1) * cols]


def weight_columns(left_ref, right_ref, scaled_ref, w_ref, outer):
    rows, cols, chan = scaled_ref.shape
    outer_columns(left_ref, right_ref, outer)
    for p in range(rows // 2):
        w_ref[...] += dot(outer[p], scaled_ref[2 * p : 2 * p + 2].reshape(2 * cols, chan))


def left_columns(grad, right_ref, left_sum_ref):
    proj_width, cols, seqs = right_ref.shape
    for e in range(0, proj_width, 2):
        block = jnp.concatenate([grad[e], grad[e + 1]], 1)
        left_sum_ref[...] += dot(block, right_ref[e : e + 2].reshape(2 * cols, seqs))


def near_kernel(left_ref, scaled_ref, grad_ref, right_ref, w_sum_ref, left_sum_ref, outer_ref):
    w_sum_ref[...] = jnp.zeros_like(w_sum_ref)
    weight_columns(left_ref, right_ref, scaled_ref, w_sum_ref, outer_ref)
    left_sum_ref[...] = jnp.zeros_like(left_sum_ref)
    left_columns(grad_ref, right_ref, left_sum_ref)


def far_kernel(index_ref, left_ref, scaled_ref, w_sum_ref, right_ref, outer_ref, *refs):
    *quarter_refs, total = refs
    total[...] = w_sum_ref[...]
    weight_columns(left_ref, right_ref, scaled_ref, total, outer_ref)
    quarter = quarter_refs[0].shape[0]
    for m, ref in enumerate(quarter_refs):
        begin = pl.multiple_of(((index_ref[0] & 3) ^ m) * quarter, quarter)
        ref[...] = total[pl.ds(begin, quarter), :].astype(BF16)


def left_kernel(near_sum_ref, grad_ref, right_ref, left_sum_ref):
    left_sum_ref[...] = near_sum_ref[...]
    left_columns(grad_ref, right_ref, left_sum_ref)


def pair_kernel(
    index_ref, w2_ref, bias_ref, near_ref, far_ref, near_factor_ref, far_factor_ref, out_ref, w2_t
):
    rows = out_ref.shape[0]
    w2_t[...] = w2_ref[...].astype(F32).T.astype(BF16)
    bias = column_of(bias_ref[...])
    side = index_ref[0] & 1
    for half, outer, factor_ref in (
        (side, near_ref, near_factor_ref),
        (1 - side, far_ref, far_factor_ref),
    ):
        cols = outer.shape[2] // 2
        for p in range(rows // 2):
            projected = dot(w2_t[...], outer[p]) + bias
            for sub in range(2):
                i = 2 * p + sub
                block = projected[:, sub * cols : (sub + 1) * cols] * factor_ref[i : i + 1, :]
                block = block.T.astype(BF16)
                for q in range(cols // rows):
                    begin = pl.multiple_of((2 * q + half) * rows, rows)
                    out_ref[i, pl.ds(begin, rows), :] = block[q * rows : (q + 1) * rows]


def sums_kernel(
    right_own_ref, *refs
):
    *ins, grads_ref, pack_ref, right_sum, gathered = refs
    *right_refs, normal_ref, wl_ref, wr_ref, mask_own_ref, left_sum_ref, b_ref = ins
    seqs = mask_own_ref.shape[1]
    proj_width, rows, _ = right_own_ref.shape
    width = wl_ref.shape[1]
    total = right_own_ref[...]
    for ref in right_refs:
        total = total + ref[...].astype(F32)
    right_sum[...] = total.reshape(proj_width * rows, seqs)
    fill = jnp.zeros((LANES - 2 * proj_width, seqs), F32)
    bias_cols = jnp.zeros((LANES, seqs), F32)
    for i in range(rows):
        block = jnp.concatenate(
            [
                left_sum_ref[i * proj_width : (i + 1) * proj_width, :],
                right_sum[pl.ds(i, proj_width, stride=rows), :],
                fill,
            ],
            0,
        )
        block = (block * mask_own_ref[i : i + 1, :]).astype(BF16).astype(F32)
        bias_cols = bias_cols + block
        gathered[pl.ds(i, seqs, stride=rows), :] = block.T
    grads_ref[...] = gathered[...].astype(BF16)
    used = 2 * proj_width
    products = jnp.zeros((LANES, 2 * width), F32)
    step = 256
    for first in range(0, seqs * rows, step):
        products = products + dot(
            grads_ref[first : first + step, :], normal_ref[first : first + step, :], FIRST_DIMS
        )
    weights = jnp.concatenate([wl_ref[...], wr_ref[...]], 0).astype(F32)
    bias_sum = jnp.sum(bias_cols, 1, keepdims=True)
    gain_sum = jnp.sum(weights * products[:used, width:], 0, keepdims=True)
    shift_sum = jnp.sum(weights * bias_sum[:used], 0, keepdims=True)
    bias_row = jnp.broadcast_to(bias_sum, (LANES, LANES)).T[:1]
    pieces = [products[:used, k : k + LANES] for k in range(0, width, LANES)]
    pieces += [gain_sum[:, k : k + LANES] for k in range(0, width, LANES)]
    pieces += [shift_sum[:, k : k + LANES] for k in range(0, width, LANES)]
    pieces += [bias_row, b_ref[...]]
    pieces += [jnp.zeros((TAIL - 2 - 2 * (width // LANES), LANES), F32)]
    pack_ref[...] = jnp.concatenate(pieces, 0).astype(BF16)


def norm_kernel(normal_ref, inverse_ref, gain_ref, wl_ref, wr_ref, grads_ref, out_ref, weights):
    seqs, rows, width = out_ref.shape
    proj_width = wl_ref.shape[0]
    weights[...] = jnp.zeros_like(weights)
    weights[:proj_width, :] = wl_ref[...]
    weights[proj_width : 2 * proj_width, :] = wr_ref[...]
    step = 16
    for first in range(0, seqs, step):
        span = slice(first * rows, (first + step) * rows)
        xhat = normal_ref[span, width:].astype(F32)
        g = dot(grads_ref[span, :], weights[...]) * gain_ref[...]
        result = (
            g - jnp.mean(g, -1, keepdims=True) - xhat * jnp.mean(g * xhat, -1, keepdims=True)
        ) * inverse_ref[span, :]
        out_ref[first : first + step] = result.astype(BF16).reshape(step, rows, width)


def tree_sum(values):
    values = [value.astype(F32) for value in values]
    while len(values) > 1:
        values = [a + b for a, b in zip(values[::2], values[1::2])]
    return values[0]


def merge_kernel(*refs):
    *ins, out_ref = refs
    out_ref[...] = tree_sum([ref[...] for ref in ins]).astype(BF16)


def total_kernel(pack_ref, *refs):
    *quarter_refs, out_ref = refs
    head = pack_ref.shape[0]
    out_ref[:head, :] = pack_ref[...]
    out_ref[head:, :] = tree_sum([ref[...] for ref in quarter_refs]).astype(BF16)


def side_kernel(own_ref, other_ref, out_ref, *, head):
    rows = own_ref.shape[0]
    out_ref[:head, :] = tree_sum([own_ref[:head, :], other_ref[:head, :]]).astype(BF16)
    out_ref[head:rows, :] = own_ref[head:, :]
    out_ref[rows:, :] = other_ref[head:, :]


def unpack_kernel(index_ref, *refs):
    ins = refs[:2]
    wl_ref, bl_ref, wr_ref, br_ref, w_out_ref, b_ref, gain_ref, shift_ref, placed = refs[2:]
    proj_width, width = wl_ref.shape
    used = 2 * proj_width
    parts = width // LANES
    head = parts * used + TAIL
    total = tree_sum([ref[:head, :] for ref in ins])
    tail = total[parts * used :]
    for k in range(parts):
        span = slice(k * LANES, (k + 1) * LANES)
        wl_ref[:, span] = total[k * used : k * used + proj_width]
        wr_ref[:, span] = total[k * used + proj_width : (k + 1) * used]
        gain_ref[:, span] = tail[k : k + 1]
        shift_ref[:, span] = tail[parts + k : parts + k + 1]
    bl_ref[...] = tail[2 * parts : 2 * parts + 1, :proj_width]
    br_ref[...] = tail[2 * parts : 2 * parts + 1, proj_width:used]
    b_ref[...] = tail[2 * parts + 1 : 2 * parts + 2, :]
    quarter = placed.shape[0] // 4
    for core, ref in enumerate(ins):
        for side in range(2):
            begin = pl.multiple_of(((index_ref[0] & 3) ^ (core + 2 * side)) * quarter, quarter)
            span = slice(head + side * quarter, head + (side + 1) * quarter)
            placed[pl.ds(begin, quarter), :] = ref[span, :].astype(F32)
    for c in range(proj_width):
        w_out_ref[c * proj_width : (c + 1) * proj_width, :] = placed[
            pl.ds(c, proj_width, stride=proj_width), :
        ]


def body(
    devices,
    alignment_activations,
    alignment_row_mask,
    residue_mask_vector,
    layer_norm_gain,
    layer_norm_bias,
    left_weight,
    left_bias,
    right_weight,
    right_bias,
    output_weight,
    output_bias,
    pair_update_cotangent,
):
    seqs, rows, width = alignment_activations.shape
    cols = alignment_row_mask.shape[1]
    proj_width = left_weight.shape[1]
    pair_width, chan = output_weight.shape
    high = devices // 4
    half = cols // 2
    quarter = pair_width // 4
    flat = rows * proj_width
    index = lax.axis_index("res").astype(jnp.int32).reshape(1)
    gain = layer_norm_gain.reshape(1, width)
    shift = layer_norm_bias.reshape(1, width)
    wl, wr = left_weight.T, right_weight.T
    piece = (proj_width, rows, seqs)

    def swap(value, rel):
        return lax.ppermute(value, "res", [(d, d ^ rel) for d in range(devices)])

    slab = (high,) + piece
    left, right = call(
        project_kernel,
        (shape((flat, seqs), BF16), shape(piece, BF16)),
        (index, alignment_activations, alignment_row_mask, gain, shift, wl, wr)
        + (left_bias.reshape(1, proj_width), right_bias.reshape(1, proj_width)),
        (
            pltpu.VMEM((seqs * rows, LANES), F32),
            pltpu.VMEM((flat, seqs), F32),
            pltpu.VMEM((LANES, width), BF16),
            pltpu.VMEM((cols, seqs), F32),
        ),
        us=4,
        fetched=tuple(range(1, 9)),
        grant=60 * MIB,
    )
    blocks = {0: right, 2: swap(right, 2)}
    for k in range(2, high):
        blocks[4 * k] = swap(right, 4 * k)
    grad_shape = shape((proj_width, flat, half), BF16)
    outer_shape = shape((rows // 2, pair_width, 2 * half), BF16)
    send, far, near, far_factor, near_factor, w2, b_part, left_t, far_grad, mask_own = call(
        send_kernel,
        (
            shape((2 * high,) + piece, BF16),
            shape((rows, half, chan), BF16),
            shape((rows, half, chan), BF16),
            shape((rows, half), F32),
            shape((rows, half), F32),
            shape((pair_width, chan), BF16),
            shape((1, chan), F32),
            shape((seqs, flat), BF16),
            grad_shape,
            shape((rows, seqs), F32),
        ),
        (
            index,
            left,
            alignment_row_mask,
            residue_mask_vector.reshape(1, cols),
            pair_update_cotangent,
            output_weight,
        ),
        (
            pltpu.VMEM((pair_width, chan), F32),
            pltpu.VMEM((cols, LANES), F32),
            pltpu.VMEM((cols, seqs), F32),
        ),
        us=6,
    )
    keep, send, near_grad = call(
        keep_kernel,
        (shape(slab, F32), shape(slab, BF16), grad_shape),
        (index, left_t, w2, near, swap(send, 1)),
        (pltpu.VMEM((2 * high,) + piece, F32),),
        us=4,
    )
    normal, inverse, right_copy, other_copy, normal_token = call(
        normal_kernel,
        (shape((seqs * rows, 2 * width), BF16), shape((seqs * rows, 1), F32))
        + (shape(piece, BF16),) * 2,
        (alignment_activations, gain, shift, right, blocks[2]),
        scalars=0,
        us=10,
        after=(keep,),
        token=True,
    )
    blocks[4] = swap(right_copy, 4)
    blocks[6] = swap(other_copy, 4)
    blocks[10] = swap(other_copy, 8)
    line = call(
        line_kernel,
        (shape(piece, BF16),) * (high - 3) + (shape((8, LANES), F32),),
        tuple(blocks[4 * k] for k in range(3, high)),
        scalars=0,
        us=0.1,
        after=(normal_token, blocks[8]),
    )
    for k in range(3, high):
        blocks[4 * k + 2] = swap(line[k - 3], 2)
    right_own, *sends = call(
        high_kernel,
        (shape(piece, F32),) + (shape(piece, BF16),) * (high - 1),
        (keep, swap(send, 2)),
        scalars=0,
        us=10,
        after=(line[-1], blocks[4], blocks[10]),
    )
    right_parts = tuple(swap(sends[k - 1], 4 * k) for k in range(high - 1, 0, -1))
    right_near = call(
        place_kernel,
        shape((proj_width, half, seqs), BF16),
        (index,) + tuple(blocks[rel] for rel in range(0, devices, 2)),
        after=(right_own,),
    )
    right_far = swap(right_near, 1)
    near_w, near_left, near_outer = call(
        near_kernel,
        (shape((pair_width, chan), F32), shape((flat, seqs), F32), outer_shape),
        (left, near, near_grad, right_near),
        scalars=0,
        us=100,
    )
    far_outer, w_own, *w_sends = call(
        far_kernel,
        (outer_shape,) + (shape((quarter, chan), BF16),) * 4,
        (index, left, far, near_w, right_far),
        (pltpu.VMEM((pair_width, chan), F32),),
        us=0.02,
    )
    left_sum = call(
        left_kernel,
        shape((flat, seqs), F32),
        (near_left, far_grad, right_far),
        scalars=0,
        us=0.02,
        after=(w_own,),
    )
    pack_shape = shape((2 * proj_width * (width // LANES) + TAIL, LANES), BF16)
    grads, pack = call(
        sums_kernel,
        (shape((seqs * rows, LANES), BF16), pack_shape),
        (right_own,) + right_parts + (normal, wl, wr, mask_own, left_sum, b_part),
        (pltpu.VMEM((flat, seqs), F32), pltpu.VMEM((seqs * rows, LANES), F32)),
        scalars=0,
        us=2,
    )
    total_shape = shape((pack_shape.shape[0] + quarter, LANES), BF16)
    merged = call(
        total_kernel,
        total_shape,
        (pack, w_own) + tuple(swap(w_sends[m - 1], m) for m in (3, 2, 1)),
        scalars=0,
        us=0.1,
    )
    alignment_gradient, norm_token = call(
        norm_kernel,
        shape((seqs, rows, width), BF16),
        (normal, inverse, gain, wl, wr, grads),
        (pltpu.VMEM((LANES, width), BF16),),
        scalars=0,
        us=0.02,
        after=(merged,),
        token=True,
    )
    pair, pair_token = call(
        pair_kernel,
        shape((rows, cols, chan), BF16),
        (index, w2, output_bias.reshape(1, chan), near_outer, far_outer, near_factor, far_factor),
        (pltpu.VMEM((chan, pair_width), BF16),),
        us=0.02,
        after=(norm_token,),
        token=True,
    )
    distances = [devices // 2 >> n for n in range(high.bit_length() - 1)]
    for n, distance in enumerate(distances):
        merged = call(
            merge_kernel,
            total_shape,
            (merged, swap(merged, distance)),
            scalars=0,
            us=0.1,
            after=(pair_token if n else norm_token,),
        )
    merged = call(
        side_kernel,
        shape((total_shape.shape[0] + quarter, LANES), BF16),
        (merged, swap(merged, 2)),
        scalars=0,
        us=0.1,
        head=pack_shape.shape[0],
    )
    w_left, b_left, w_right, b_right, w_out_grad, b_out, gain_grad, shift_grad = call(
        unpack_kernel,
        (
            shape((proj_width, width), F32),
            shape((1, proj_width), F32),
            shape((proj_width, width), F32),
            shape((1, proj_width), F32),
            shape((pair_width, chan), F32),
            shape((1, chan), F32),
            shape((1, width), F32),
            shape((1, width), F32),
        ),
        (index, merged, swap(merged, 1)),
        (pltpu.VMEM((pair_width, chan), F32),),
    )
    return (
        pair,
        alignment_gradient,
        w_left.T,
        b_left.reshape(-1),
        w_right.T,
        b_right.reshape(-1),
        w_out_grad,
        b_out.reshape(-1),
        gain_grad.reshape(-1),
        shift_grad.reshape(-1),
    )


def solution(mesh):
    return jax.shard_map(
        functools.partial(body, mesh.shape["res"]),
        mesh=mesh,
        in_specs=(
            P(None, ("grp", "res"), None),
            P(None, "grp"),
            P("grp"),
            P(),
            P(),
            P(),
            P(),
            P(),
            P(),
            P(),
            P(),
            P(("grp", "res"), None, None),
        ),
        out_specs=(
            P(("grp", "res"), None, None),
            P(None, ("grp", "res"), None),
            P("grp", None),
            P("grp"),
            P("grp", None),
            P("grp"),
            P("grp", None),
            P("grp"),
            P("grp"),
            P("grp"),
        ),
        check_vma=False,
    )
```

```python
import functools
import math

import jax
import jax.numpy as jnp
from jax import lax
from jax.experimental import pallas as pl
from jax.experimental.pallas import tpu as pltpu
from jax.sharding import PartitionSpec as P

EPS = 1e-05
LAST_DIMS = (((1,), (1,)), ((), ()))
FIRST_DIMS = (((0,), (0,)), ((), ()))
MIB = 1024 * 1024
LANES = 128
TAIL = 16
CHUNKS = 4
F32 = jnp.float32
BF16 = jnp.bfloat16


def tiled_bytes(dims, dtype):
    dims = tuple(dims)
    lanes = -(-dims[-1] // LANES) * LANES
    sublanes = -(-(dims[-2] if len(dims) > 1 else 1) // 16) * 16
    return math.prod(dims[:-2]) * sublanes * lanes * jnp.dtype(dtype).itemsize


def call(
    kernel, out_shape, args, scratch=(), scalars=1, us=1.0, after=(), fetched=(), token=False, grant=0, **static
):
    count = len(args)
    specs = [pl.BlockSpec(memory_space=pl.ANY)] * len(after)
    specs += [pl.BlockSpec(memory_space=pltpu.SMEM)] * scalars
    for k in range(scalars, count):
        specs.append(pl.BlockSpec(memory_space=pltpu.HBM if k in fetched else pltpu.VMEM))
    outs = list(out_shape) if isinstance(out_shape, (tuple, list)) else [out_shape]
    if token:
        outs.append(shape((8, LANES), F32))
    held = list(args[scalars:]) + outs + list(scratch)
    need = sum(tiled_bytes(value.shape, value.dtype) for value in held)
    places = [pltpu.VMEM(args[k].shape, args[k].dtype) for k in fetched]
    semaphores = [pltpu.SemaphoreType.DMA((len(fetched), CHUNKS))] if fetched else []

    def run(*refs):
        ins = list(refs[len(after) : len(after) + count])
        rest = list(refs[len(after) + count :])
        if fetched:
            *rest, done = rest
            held_refs = rest[-len(fetched) :]
            rest = rest[: -len(fetched)]
            for n, (k, ref) in enumerate(zip(fetched, held_refs)):
                size = ref.shape[0] // (CHUNKS if len(ref.shape) == 3 else 1)
                copies = []
                for c in range(ref.shape[0] // size):
                    part = pl.ds(c * size, size)
                    copies.append(
                        pltpu.make_async_copy(ins[k].at[part], ref.at[part], done.at[n, c])
                    )
                    copies[-1].start()
                ins[k] = Fetched(ref, copies, size)
        if token:
            rest.pop(len(outs) - 1)[...] = jnp.zeros((8, LANES), F32)
        kernel(*ins, *rest, **static)

    result = pl.pallas_call(
        run,
        name=kernel.__name__,
        out_shape=tuple(outs),
        in_specs=specs,
        out_specs=tuple([pl.BlockSpec(memory_space=pltpu.VMEM)] * len(outs)),
        scratch_shapes=list(scratch) + places + semaphores,
        compiler_params=pltpu.CompilerParams(vmem_limit_bytes=grant or min(need + 6 * MIB, 56 * MIB)),
        cost_estimate=pl.CostEstimate(
            flops=int(us * 1.1e9), bytes_accessed=int(us * 1e5), transcendentals=0
        ),
    )(*after, *args)
    return result if len(outs) > 1 else result[0]


class Fetched:
    def __init__(self, ref, copies, size):
        self.ref, self.copies, self.size, self.shape = ref, copies, size, ref.shape

    def __getitem__(self, index):
        last = len(self.copies) - 1
        if isinstance(index, slice):
            last = (index.stop - 1) // self.size
        for c in range(last + 1):
            if self.copies[c] is not None:
                self.copies[c].wait()
                self.copies[c] = None
        return self.ref[index]


def shape(dims, dtype):
    return jax.ShapeDtypeStruct(tuple(dims), dtype)


def dot(a, b, dims=(((1,), (0,)), ((), ()))):
    return lax.dot_general(a, b, dims, preferred_element_type=F32)


def normalize(x, gain, shift):
    centered = x - jnp.mean(x, -1, keepdims=True)
    inverse = lax.rsqrt(jnp.mean(centered * centered, -1, keepdims=True) + EPS)
    xhat = centered * inverse
    return xhat, inverse, (xhat * gain + shift).astype(BF16)


def column_of(row):
    return jnp.broadcast_to(row, (8, row.shape[1])).T[:, :1]


def project_kernel(
    index_ref, x_ref, mask_ref, gain_ref, shift_ref, wl_ref, wr_ref, bl_ref, br_ref,
    left_ref, right_ref, proj, right_rows, weights, mask_t,
):
    seqs, rows, width = x_ref.shape
    proj_width = right_ref.shape[0]
    begin = pl.multiple_of(index_ref[0] * rows, rows)
    weights[:proj_width, :] = wl_ref[...]
    weights[proj_width : 2 * proj_width, :] = wr_ref[...]
    weights[2 * proj_width :, :] = jnp.zeros((LANES - 2 * proj_width, width), BF16)
    mask_t[...] = mask_ref[...].astype(F32).T
    bias_left = column_of(bl_ref[...])
    bias_right = column_of(br_ref[...])
    step = 16
    for first in range(0, seqs, step):
        x = x_ref[first : first + step].astype(F32).reshape(step * rows, width)
        normalized = normalize(x, gain_ref[...], shift_ref[...])[2]
        proj[first * rows : (first + step) * rows, :] = dot(normalized, weights[...], LAST_DIMS)
    mask_own = mask_t[pl.ds(begin, rows), :]
    for i in range(rows):
        block = proj[pl.ds(i, seqs, stride=rows), :].T
        mask_row = mask_own[i : i + 1, :]
        span = slice(i * proj_width, (i + 1) * proj_width)
        left_ref[span, :] = ((block[:proj_width] + bias_left) * mask_row).astype(BF16)
        right_rows[span, :] = (block[proj_width : 2 * proj_width] + bias_right) * mask_row
    for e in range(proj_width):
        right_ref[e] = right_rows[pl.ds(e, rows, stride=proj_width), :].astype(BF16)


def grad_columns(w2_ref, scaled_ref, grad):
    rows, cols, chan = scaled_ref.shape
    proj_width = grad.shape[0]
    for i in range(0, rows, 2):
        pair = scaled_ref[i : i + 2].reshape(2 * cols, chan)
        block = dot(w2_ref[...], pair, LAST_DIMS).astype(BF16)
        for e in range(proj_width):
            for sub in range(2):
                grad[e, (i + sub) * proj_width : (i + sub + 1) * proj_width, :] = block[
                    e * proj_width : (e + 1) * proj_width, sub * cols : (sub + 1) * cols
                ]


def right_columns(index_ref, left_t, grad, emit):
    proj_width, _, cols = grad.shape
    rows = left_t.shape[1] // proj_width
    high = cols // rows // 2
    own = index_ref[0] >> 1
    for e in range(0, proj_width, 2):
        block = jnp.concatenate([grad[e], grad[e + 1]], 1)
        sums = dot(left_t[...], block)
        for sub in range(2):
            part = sums[:, sub * cols : (sub + 1) * cols].T
            for q in range(2 * high):
                rel = q ^ own
                emit(e + sub, (rel & 1) * high + (rel >> 1), part[q * rows : (q + 1) * rows])


def scale_columns(half, mask_t_ref, mask_own, resid_t, resid_own, cot_ref, scaled_ref, factor_ref):
    rows = cot_ref.shape[0]
    cols = scaled_ref.shape[1]
    starts = [
        pl.multiple_of((2 * q + half) * rows, rows) for q in range(cols // rows)
    ]
    mask_cols = jnp.concatenate([mask_t_ref[pl.ds(s, rows), :] for s in starts], 0)
    resid_cols = jnp.concatenate([resid_t[pl.ds(s, rows), :] for s in starts], 0)
    counted = dot(mask_cols.astype(BF16), mask_own.astype(BF16), LAST_DIMS)
    factor_t = resid_cols[:, :1] * resid_own / counted
    factor_ref[...] = factor_t.T
    bias_sum = jnp.zeros((1, cot_ref.shape[2]), F32)
    for i in range(rows):
        cot = jnp.concatenate([cot_ref[i, pl.ds(s, rows), :] for s in starts], 0)
        scaled = (cot.astype(F32) * factor_t[:, i : i + 1]).astype(BF16)
        scaled_ref[i] = scaled
        bias_sum = bias_sum + jnp.sum(scaled.astype(F32), 0, keepdims=True)
    return bias_sum


def send_kernel(
    index_ref, left_ref, mask_ref, resid_ref, cot_ref, w_ref,
    send_ref, far_ref, near_ref, far_factor_ref, near_factor_ref, w2_ref, b_ref, left_t_ref, grad,
    mask_own_ref, wide, resid_t, mask_t,
):
    rows, cols, chan = cot_ref.shape
    proj_width = left_ref.shape[0] // rows
    index = index_ref[0]
    wide[...] = w_ref[...].astype(F32)
    for e in range(proj_width):
        w2_ref[e * proj_width : (e + 1) * proj_width, :] = wide[
            pl.ds(e, proj_width, stride=proj_width), :
        ].astype(BF16)
    left_t_ref[...] = left_ref[...].astype(F32).T.astype(BF16)
    resid_t[...] = jnp.broadcast_to(resid_ref[...].astype(F32), (LANES, cols)).T
    begin = pl.multiple_of(index * rows, rows)
    mask_t[...] = mask_ref[...].astype(F32).T
    mask_own = mask_t[pl.ds(begin, rows), :]
    mask_own_ref[...] = mask_own
    resid_own = resid_t[pl.ds(begin, rows), :].T[:1]
    side = index & 1
    shared = (mask_t, mask_own, resid_t, resid_own, cot_ref)
    far_sum = scale_columns(1 - side, *shared, far_ref, far_factor_ref)
    near_sum = scale_columns(side, *shared, near_ref, near_factor_ref)
    b_ref[...] = far_sum + near_sum
    grad_columns(w2_ref, far_ref, grad)

    def emit(e, slot, value):
        send_ref[slot, e] = value.astype(BF16)

    right_columns(index_ref, left_t_ref, grad, emit)


def keep_kernel(
    index_ref, left_t_ref, w2_ref, near_ref, far_part_ref, keep_ref, send_ref, grad, total
):
    high = keep_ref.shape[0]
    grad_columns(w2_ref, near_ref, grad)

    def emit(e, slot, value):
        total[slot, e] = value

    right_columns(index_ref, left_t_ref, grad, emit)
    keep_ref[...] = total[:high] + far_part_ref[:high].astype(F32)
    send_ref[...] = (total[high:] + far_part_ref[high:].astype(F32)).astype(BF16)


def high_kernel(keep_ref, other_ref, own_ref, *send_refs):
    own_ref[...] = keep_ref[0] + other_ref[0].astype(F32)
    for k, ref in enumerate(send_refs):
        ref[...] = (keep_ref[k + 1] + other_ref[k + 1].astype(F32)).astype(BF16)


def normal_kernel(
    x_ref, gain_ref, shift_ref, right_ref, other_ref,
    normal_ref, inverse_ref, right_copy_ref, other_copy_ref,
):
    seqs, rows, width = x_ref.shape
    right_copy_ref[...] = right_ref[...]
    other_copy_ref[...] = other_ref[...]
    step = 16
    for first in range(0, seqs, step):
        x = x_ref[first : first + step].astype(F32).reshape(step * rows, width)
        xhat, inverse, normalized = normalize(x, gain_ref[...], shift_ref[...])
        span = slice(first * rows, (first + step) * rows)
        normal_ref[span, :width] = normalized
        normal_ref[span, width:] = xhat.astype(BF16)
        inverse_ref[span, :] = inverse


def line_kernel(*refs):
    count = len(refs) // 2
    for k in range(count):
        refs[count + k][...] = refs[k][...]
    refs[-1][...] = jnp.zeros_like(refs[-1])


def place_kernel(index_ref, *refs):
    *blocks, out_ref = refs
    rows = blocks[0].shape[1]
    own = index_ref[0] >> 1
    for rel, ref in enumerate(blocks):
        out_ref[:, pl.ds(pl.multiple_of((own ^ rel) * rows, rows), rows), :] = ref[...]


def outer_columns(left_ref, right_ref, outer):
    proj_width, cols, seqs = right_ref.shape
    rows = left_ref.shape[0] // proj_width
    for e in range(0, proj_width, 2):
        pair = right_ref[e : e + 2].reshape(2 * cols, seqs)
        block = dot(left_ref[...], pair, LAST_DIMS).astype(BF16)
        for i in range(rows):
            for sub in range(2):
                outer[
                    i // 2,
                    (e + sub) * proj_width : (e + sub + 1) * proj_width,
                    (i % 2) * cols : (i % 2 + 1) * cols,
                ] = block[i * proj_width : (i + 1) * proj_width, sub * cols : (sub + 1) * cols]


def weight_columns(left_ref, right_ref, scaled_ref, w_ref, outer):
    rows, cols, chan = scaled_ref.shape
    outer_columns(left_ref, right_ref, outer)
    for p in range(rows // 2):
        w_ref[...] += dot(outer[p], scaled_ref[2 * p : 2 * p + 2].reshape(2 * cols, chan))


def left_columns(grad, right_ref, left_sum_ref):
    proj_width, cols, seqs = right_ref.shape
    for e in range(0, proj_width, 2):
        block = jnp.concatenate([grad[e], grad[e + 1]], 1)
        left_sum_ref[...] += dot(block, right_ref[e : e + 2].reshape(2 * cols, seqs))


def near_kernel(left_ref, scaled_ref, grad_ref, right_ref, w_sum_ref, left_sum_ref, outer_ref):
    w_sum_ref[...] = jnp.zeros_like(w_sum_ref)
    weight_columns(left_ref, right_ref, scaled_ref, w_sum_ref, outer_ref)
    left_sum_ref[...] = jnp.zeros_like(left_sum_ref)
    left_columns(grad_ref, right_ref, left_sum_ref)


def far_kernel(index_ref, left_ref, scaled_ref, w_sum_ref, right_ref, outer_ref, *refs):
    *quarter_refs, total = refs
    total[...] = w_sum_ref[...]
    weight_columns(left_ref, right_ref, scaled_ref, total, outer_ref)
    quarter = quarter_refs[0].shape[0]
    for m, ref in enumerate(quarter_refs):
        begin = pl.multiple_of(((index_ref[0] & 3) ^ m) * quarter, quarter)
        ref[...] = total[pl.ds(begin, quarter), :].astype(BF16)


def left_kernel(near_sum_ref, grad_ref, right_ref, left_sum_ref):
    left_sum_ref[...] = near_sum_ref[...]
    left_columns(grad_ref, right_ref, left_sum_ref)


def pair_kernel(
    index_ref, w2_ref, bias_ref, near_ref, far_ref, near_factor_ref, far_factor_ref, out_ref, w2_t
):
    rows = out_ref.shape[0]
    w2_t[...] = w2_ref[...].astype(F32).T.astype(BF16)
    bias = column_of(bias_ref[...])
    side = index_ref[0] & 1
    for half, outer, factor_ref in (
        (side, near_ref, near_factor_ref),
        (1 - side, far_ref, far_factor_ref),
    ):
        cols = outer.shape[2] // 2
        for p in range(rows // 2):
            projected = dot(w2_t[...], outer[p]) + bias
            for sub in range(2):
                i = 2 * p + sub
                block = projected[:, sub * cols : (sub + 1) * cols] * factor_ref[i : i + 1, :]
                block = block.T.astype(BF16)
                for q in range(cols // rows):
                    begin = pl.multiple_of((2 * q + half) * rows, rows)
                    out_ref[i, pl.ds(begin, rows), :] = block[q * rows : (q + 1) * rows]


def sums_kernel(
    right_own_ref, *refs
):
    *ins, grads_ref, pack_ref, right_sum, gathered = refs
    *right_refs, normal_ref, wl_ref, wr_ref, mask_own_ref, left_sum_ref, b_ref = ins
    seqs = mask_own_ref.shape[1]
    proj_width, rows, _ = right_own_ref.shape
    width = wl_ref.shape[1]
    total = right_own_ref[...]
    for ref in right_refs:
        total = total + ref[...].astype(F32)
    right_sum[...] = total.reshape(proj_width * rows, seqs)
    fill = jnp.zeros((LANES - 2 * proj_width, seqs), F32)
    bias_cols = jnp.zeros((LANES, seqs), F32)
    for i in range(rows):
        block = jnp.concatenate(
            [
                left_sum_ref[i * proj_width : (i + 1) * proj_width, :],
                right_sum[pl.ds(i, proj_width, stride=rows), :],
                fill,
            ],
            0,
        )
        block = (block * mask_own_ref[i : i + 1, :]).astype(BF16).astype(F32)
        bias_cols = bias_cols + block
        gathered[pl.ds(i, seqs, stride=rows), :] = block.T
    grads_ref[...] = gathered[...].astype(BF16)
    used = 2 * proj_width
    products = jnp.zeros((LANES, 2 * width), F32)
    step = 256
    for first in range(0, seqs * rows, step):
        products = products + dot(
            grads_ref[first : first + step, :], normal_ref[first : first + step, :], FIRST_DIMS
        )
    weights = jnp.concatenate([wl_ref[...], wr_ref[...]], 0).astype(F32)
    bias_sum = jnp.sum(bias_cols, 1, keepdims=True)
    gain_sum = jnp.sum(weights * products[:used, width:], 0, keepdims=True)
    shift_sum = jnp.sum(weights * bias_sum[:used], 0, keepdims=True)
    bias_row = jnp.broadcast_to(bias_sum, (LANES, LANES)).T[:1]
    pieces = [products[:used, k : k + LANES] for k in range(0, width, LANES)]
    pieces += [gain_sum[:, k : k + LANES] for k in range(0, width, LANES)]
    pieces += [shift_sum[:, k : k + LANES] for k in range(0, width, LANES)]
    pieces += [bias_row, b_ref[...]]
    pieces += [jnp.zeros((TAIL - 2 - 2 * (width // LANES), LANES), F32)]
    pack_ref[...] = jnp.concatenate(pieces, 0).astype(BF16)


def norm_kernel(normal_ref, inverse_ref, gain_ref, wl_ref, wr_ref, grads_ref, out_ref, weights):
    seqs, rows, width = out_ref.shape
    proj_width = wl_ref.shape[0]
    weights[...] = jnp.zeros_like(weights)
    weights[:proj_width, :] = wl_ref[...]
    weights[proj_width : 2 * proj_width, :] = wr_ref[...]
    step = 16
    for first in range(0, seqs, step):
        span = slice(first * rows, (first + step) * rows)
        xhat = normal_ref[span, width:].astype(F32)
        g = dot(grads_ref[span, :], weights[...]) * gain_ref[...]
        result = (
            g - jnp.mean(g, -1, keepdims=True) - xhat * jnp.mean(g * xhat, -1, keepdims=True)
        ) * inverse_ref[span, :]
        out_ref[first : first + step] = result.astype(BF16).reshape(step, rows, width)


def tree_sum(values):
    values = [value.astype(F32) for value in values]
    while len(values) > 1:
        values = [a + b for a, b in zip(values[::2], values[1::2])]
    return values[0]


def merge_kernel(*refs):
    *ins, out_ref = refs
    out_ref[...] = tree_sum([ref[...] for ref in ins]).astype(BF16)


def total_kernel(pack_ref, *refs):
    *quarter_refs, out_ref = refs
    head = pack_ref.shape[0]
    out_ref[:head, :] = pack_ref[...]
    out_ref[head:, :] = tree_sum([ref[...] for ref in quarter_refs]).astype(BF16)


def side_kernel(own_ref, other_ref, out_ref, *, head):
    rows = own_ref.shape[0]
    out_ref[:head, :] = tree_sum([own_ref[:head, :], other_ref[:head, :]]).astype(BF16)
    out_ref[head:rows, :] = own_ref[head:, :]
    out_ref[rows:, :] = other_ref[head:, :]


def unpack_kernel(index_ref, *refs):
    ins = refs[:2]
    wl_ref, bl_ref, wr_ref, br_ref, w_out_ref, b_ref, gain_ref, shift_ref, placed = refs[2:]
    proj_width, width = wl_ref.shape
    used = 2 * proj_width
    parts = width // LANES
    head = parts * used + TAIL
    total = tree_sum([ref[:head, :] for ref in ins])
    tail = total[parts * used :]
    for k in range(parts):
        span = slice(k * LANES, (k + 1) * LANES)
        wl_ref[:, span] = total[k * used : k * used + proj_width]
        wr_ref[:, span] = total[k * used + proj_width : (k + 1) * used]
        gain_ref[:, span] = tail[k : k + 1]
        shift_ref[:, span] = tail[parts + k : parts + k + 1]
    bl_ref[...] = tail[2 * parts : 2 * parts + 1, :proj_width]
    br_ref[...] = tail[2 * parts : 2 * parts + 1, proj_width:used]
    b_ref[...] = tail[2 * parts + 1 : 2 * parts + 2, :]
    quarter = placed.shape[0] // 4
    for core, ref in enumerate(ins):
        for side in range(2):
            begin = pl.multiple_of(((index_ref[0] & 3) ^ (core + 2 * side)) * quarter, quarter)
            span = slice(head + side * quarter, head + (side + 1) * quarter)
            placed[pl.ds(begin, quarter), :] = ref[span, :].astype(F32)
    for c in range(proj_width):
        w_out_ref[c * proj_width : (c + 1) * proj_width, :] = placed[
            pl.ds(c, proj_width, stride=proj_width), :
        ]


def body(
    devices,
    alignment_activations,
    alignment_row_mask,
    residue_mask_vector,
    layer_norm_gain,
    layer_norm_bias,
    left_weight,
    left_bias,
    right_weight,
    right_bias,
    output_weight,
    output_bias,
    pair_update_cotangent,
):
    seqs, rows, width = alignment_activations.shape
    cols = alignment_row_mask.shape[1]
    proj_width = left_weight.shape[1]
    pair_width, chan = output_weight.shape
    high = devices // 4
    half = cols // 2
    quarter = pair_width // 4
    flat = rows * proj_width
    index = lax.axis_index("res").astype(jnp.int32).reshape(1)
    gain = layer_norm_gain.reshape(1, width)
    shift = layer_norm_bias.reshape(1, width)
    wl, wr = left_weight.T, right_weight.T
    piece = (proj_width, rows, seqs)

    def swap(value, rel):
        return lax.ppermute(value, "res", [(d, d ^ rel) for d in range(devices)])

    slab = (high,) + piece
    left, right = call(
        project_kernel,
        (shape((flat, seqs), BF16), shape(piece, BF16)),
        (index, alignment_activations, alignment_row_mask, gain, shift, wl, wr)
        + (left_bias.reshape(1, proj_width), right_bias.reshape(1, proj_width)),
        (
            pltpu.VMEM((seqs * rows, LANES), F32),
            pltpu.VMEM((flat, seqs), F32),
            pltpu.VMEM((LANES, width), BF16),
            pltpu.VMEM((cols, seqs), F32),
        ),
        us=4,
        fetched=tuple(range(1, 9)),
        grant=60 * MIB,
    )
    blocks = {0: right, 2: swap(right, 2)}
    for k in range(2, high):
        blocks[4 * k] = swap(right, 4 * k)
    grad_shape = shape((proj_width, flat, half), BF16)
    outer_shape = shape((rows // 2, pair_width, 2 * half), BF16)
    send, far, near, far_factor, near_factor, w2, b_part, left_t, far_grad, mask_own = call(
        send_kernel,
        (
            shape((2 * high,) + piece, BF16),
            shape((rows, half, chan), BF16),
            shape((rows, half, chan), BF16),
            shape((rows, half), F32),
            shape((rows, half), F32),
            shape((pair_width, chan), BF16),
            shape((1, chan), F32),
            shape((seqs, flat), BF16),
            grad_shape,
            shape((rows, seqs), F32),
        ),
        (
            index,
            left,
            alignment_row_mask,
            residue_mask_vector.reshape(1, cols),
            pair_update_cotangent,
            output_weight,
        ),
        (
            pltpu.VMEM((pair_width, chan), F32),
            pltpu.VMEM((cols, LANES), F32),
            pltpu.VMEM((cols, seqs), F32),
        ),
        us=6,
    )
    keep, send, near_grad = call(
        keep_kernel,
        (shape(slab, F32), shape(slab, BF16), grad_shape),
        (index, left_t, w2, near, swap(send, 1)),
        (pltpu.VMEM((2 * high,) + piece, F32),),
        us=4,
    )
    normal, inverse, right_copy, other_copy, normal_token = call(
        normal_kernel,
        (shape((seqs * rows, 2 * width), BF16), shape((seqs * rows, 1), F32))
        + (shape(piece, BF16),) * 2,
        (alignment_activations, gain, shift, right, blocks[2]),
        scalars=0,
        us=10,
        after=(keep,),
        token=True,
    )
    blocks[4] = swap(right_copy, 4)
    blocks[6] = swap(other_copy, 4)
    blocks[10] = swap(other_copy, 8)
    line = call(
        line_kernel,
        (shape(piece, BF16),) * (high - 3) + (shape((8, LANES), F32),),
        tuple(blocks[4 * k] for k in range(3, high)),
        scalars=0,
        us=0.1,
        after=(normal_token, blocks[8]),
    )
    for k in range(3, high):
        blocks[4 * k + 2] = swap(line[k - 3], 2)
    right_own, *sends = call(
        high_kernel,
        (shape(piece, F32),) + (shape(piece, BF16),) * (high - 1),
        (keep, swap(send, 2)),
        scalars=0,
        us=10,
        after=(line[-1], blocks[4], blocks[10]),
    )
    right_parts = tuple(swap(sends[k - 1], 4 * k) for k in range(high - 1, 0, -1))
    right_near = call(
        place_kernel,
        shape((proj_width, half, seqs), BF16),
        (index,) + tuple(blocks[rel] for rel in range(0, devices, 2)),
        after=(right_own,),
    )
    right_far = swap(right_near, 1)
    near_w, near_left, near_outer = call(
        near_kernel,
        (shape((pair_width, chan), F32), shape((flat, seqs), F32), outer_shape),
        (left, near, near_grad, right_near),
        scalars=0,
        us=100,
    )
    far_outer, w_own, *w_sends = call(
        far_kernel,
        (outer_shape,) + (shape((quarter, chan), BF16),) * 4,
        (index, left, far, near_w, right_far),
        (pltpu.VMEM((pair_width, chan), F32),),
        us=0.02,
    )
    left_sum = call(
        left_kernel,
        shape((flat, seqs), F32),
        (near_left, far_grad, right_far),
        scalars=0,
        us=0.02,
        after=(w_own,),
    )
    pack_shape = shape((2 * proj_width * (width // LANES) + TAIL, LANES), BF16)
    grads, pack = call(
        sums_kernel,
        (shape((seqs * rows, LANES), BF16), pack_shape),
        (right_own,) + right_parts + (normal, wl, wr, mask_own, left_sum, b_part),
        (pltpu.VMEM((flat, seqs), F32), pltpu.VMEM((seqs * rows, LANES), F32)),
        scalars=0,
        us=2,
    )
    total_shape = shape((pack_shape.shape[0] + quarter, LANES), BF16)
    merged = call(
        total_kernel,
        total_shape,
        (pack, w_own) + tuple(swap(w_sends[m - 1], m) for m in (3, 2, 1)),
        scalars=0,
        us=0.1,
    )
    alignment_gradient, norm_token = call(
        norm_kernel,
        shape((seqs, rows, width), BF16),
        (normal, inverse, gain, wl, wr, grads),
        (pltpu.VMEM((LANES, width), BF16),),
        scalars=0,
        us=0.02,
        after=(merged,),
        token=True,
    )
    pair, pair_token = call(
        pair_kernel,
        shape((rows, cols, chan), BF16),
        (index, w2, output_bias.reshape(1, chan), near_outer, far_outer, near_factor, far_factor),
        (pltpu.VMEM((chan, pair_width), BF16),),
        us=0.02,
        after=(norm_token,),
        token=True,
    )
    distances = [devices // 2 >> n for n in range(high.bit_length() - 1)]
    for n, distance in enumerate(distances):
        merged = call(
            merge_kernel,
            total_shape,
            (merged, swap(merged, distance)),
            scalars=0,
            us=0.1,
            after=(pair_token if n else norm_token,),
        )
    merged = call(
        side_kernel,
        shape((total_shape.shape[0] + quarter, LANES), BF16),
        (merged, swap(merged, 2)),
        scalars=0,
        us=0.1,
        head=pack_shape.shape[0],
    )
    w_left, b_left, w_right, b_right, w_out_grad, b_out, gain_grad, shift_grad = call(
        unpack_kernel,
        (
            shape((proj_width, width), F32),
            shape((1, proj_width), F32),
            shape((proj_width, width), F32),
            shape((1, proj_width), F32),
            shape((pair_width, chan), F32),
            shape((1, chan), F32),
            shape((1, width), F32),
            shape((1, width), F32),
        ),
        (index, merged, swap(merged, 1)),
        (pltpu.VMEM((pair_width, chan), F32),),
    )
    return (
        pair,
        alignment_gradient,
        w_left.T,
        b_left.reshape(-1),
        w_right.T,
        b_right.reshape(-1),
        w_out_grad,
        b_out.reshape(-1),
        gain_grad.reshape(-1),
        shift_grad.reshape(-1),
    )


def solution(mesh):
    return jax.shard_map(
        functools.partial(body, mesh.shape["res"]),
        mesh=mesh,
        in_specs=(
            P(None, ("grp", "res"), None),
            P(None, "grp"),
            P("grp"),
            P(),
            P(),
            P(),
            P(),
            P(),
            P(),
            P(),
            P(),
            P(("grp", "res"), None, None),
        ),
        out_specs=(
            P(("grp", "res"), None, None),
            P(None, ("grp", "res"), None),
            P("grp", None),
            P("grp"),
            P("grp", None),
            P("grp"),
            P("grp", None),
            P("grp"),
            P("grp"),
            P("grp"),
        ),
        check_vma=False,
    )
```
